256 devices in a mesh: row: 32 (over z, x_lo, core), col: 8 (over y, x_hi).
Axes of the slice: x: 4 (x_hi: 2, x_lo: 2; x = x_hi * 2 + x_lo), y: 4, z: 8, core: 2. Of those that a mesh axis runs over, the one named last changes fastest.
Arguments:
- noise_draw: bfloat16 [16384, 4096], P('row', 'col'), may hold values from -6 to 6
- latent_code: bfloat16 [4096, 4096], P('col', 'row'), may hold values from -6 to 6
- start_potential: float32 [4096], P('col'), may hold values from -0.6 to 0.6
Outputs:
- noise_potential: float32 [16384], P('row')
- latent_potential: float32 [4096], P('col')
- transported: float32 [4096, 4096], P('row', 'col')
The draws below stay inside these ranges and needn't reach their ends.
All inputs are finite; a program needn't handle non-finite values.
Results may differ from the reference program's by a relative error of at most 0.0028.
Values may be sent and summed in bfloat16 or wider, within the bound.
A program may use at most 128 MiB of HBM per device.

```python
import math
import jax
import jax.numpy as jnp

DIM = 4096
ITERS = 3
N = 16384
M = 4096


def block_scale(own_key, extent, cuts, least, high):
    loudness, own = 1.0, jax.random.fold_in(own_key, 6)
    for axis_at, blocks in cuts:
        heights = jnp.exp(jax.random.uniform(jax.random.fold_in(own, axis_at), (blocks,), jnp.float32, least / len(cuts), high / len(cuts)))
        loudness = loudness * jnp.repeat(heights, extent[axis_at] // blocks).reshape([-1 if axis == axis_at else 1 for axis in range(len(extent))])
    return loudness


def bell_draw(rng, dims, spread, bound, cuts=(), dtype=jnp.bfloat16):
    values = jax.random.normal(rng, dims, jnp.float32) * spread
    if len(cuts) > 0:
        values = block_scale(rng, dims, cuts, -0.22, 0.18) * values
    return jnp.clip(values, min=-bound, max=bound).astype(dtype)


def setup_inputs(seed: int = 0) -> dict:
    splits = jax.random.split(jax.random.key(seed), 4)
    return {
        "noise_draw": bell_draw(splits[0], (N, DIM), 1.0, 6.0, ((0, 32), (1, 8))),
        "latent_code": bell_draw(splits[1], (M, DIM), 1.0, 6.0, ((0, 8), (1, 32))),
        "start_potential": bell_draw(splits[2], (M,), 0.1, 0.6, ((0, 8),), jnp.float32),
    }


epsilon = 0.01


def log_sum_exp(scores, axis):
    top = jnp.max(scores, axis=axis, keepdims=True)
    total = jnp.sum(jnp.exp(scores - top), axis=axis)
    return jnp.squeeze(top, axis) + jnp.log(total)


def reference(noise_draw, latent_code, start_potential):
    noise_wide = noise_draw.astype(jnp.float32)
    latent_wide = latent_code.astype(jnp.float32)
    noise_sq = jnp.sum(noise_wide * noise_wide, axis=1)
    latent_sq = jnp.sum(latent_wide * latent_wide, axis=1)
    cross = jnp.dot(noise_draw, latent_code.T, preferred_element_type=jnp.float32)
    cost = (noise_sq[:, None] + latent_sq[None, :] - 2.0 * cross) / DIM
    latent_potential = start_potential
    noise_potential = jnp.zeros((N,), jnp.float32)
    for sweep in range(ITERS):
        noise_potential = -epsilon * (math.log(M) + log_sum_exp((latent_potential[None, :] - cost) / epsilon, 1))
        latent_potential = -epsilon * (math.log(N) + log_sum_exp((noise_potential[:, None] - cost) / epsilon, 0))
    weights = (M * jnp.exp((noise_potential[:, None] + latent_potential[None, :] - cost) / epsilon)).astype(jnp.bfloat16)
    transported = jnp.dot(noise_draw.T, weights, preferred_element_type=jnp.float32)
    return noise_potential, latent_potential, transported
```

```python
import math

import jax
import jax.numpy as jnp
from jax import lax
from jax.experimental import pallas as pl
from jax.experimental.pallas import tpu as pltpu
from jax.sharding import PartitionSpec as P

ITERS = 3
EPS = 0.01
MESH = pl.DeviceIdType.MESH
F32 = jnp.float32
BF16 = jnp.bfloat16

Z, Y = 8, 4
LANE = 128
BLK = 512
HALF = BLK // 2


def kernel(
    n_total, m_total, width,
    noise_ref, latent_ref, start_ref,
    npot_ref, lpot_ref, out_ref,
    nz, lt, no, cross, nsq, lsq, wt, part, stage, land, xs, xr, rowx, col1, col2,
    n_send, n_recv, l_send, l_recv, o_send, o_recv, w_send, w_recv,
    r_send, r_recv, c1_send, c1_recv, c2_send, c2_recv, s_send, s_recv, x_send, x_recv, loc,
):
    row = lax.axis_index("row")
    col = lax.axis_index("col")
    z = row // 4
    xl = (row // 2) % 2
    core = row % 2
    y = col // 2
    xh = col % 2
    quad = row % 4

    def ring_z(d):
        return (z + d + Z) % Z

    def ring_y(d):
        return (y + d + Y) % Y

    other_core = (row + 1 - 2 * core, col)
    other_xl = (row + 2 - 4 * xl, col)
    other_xh = (row, col + 1 - 2 * xh)
    z_up = (ring_z(1) * 4 + quad, col)
    z_dn = (ring_z(-1) * 4 + quad, col)
    y_up = (row, ring_y(1) * 2 + xh)
    y_dn = (row, ring_y(-1) * 2 + xh)
    col_peers = [(row, (col + d) % 8) for d in range(1, 8)]
    quad_peers = [(z * 4 + (quad + d) % 4, col) for d in range(1, 4)]
    z_peers = [(ring_z(d) * 4 + quad, col) for d in range(1, 8)]

    own_n = pltpu.make_async_copy(noise_ref, nz.at[col], loc.at[0])
    own_l = pltpu.make_async_copy(latent_ref, lt.at[z, core, xl], loc.at[1])
    own_n.start()
    own_l.start()

    barrier = pltpu.get_barrier_semaphore()
    for peer in col_peers + quad_peers + z_peers:
        pl.semaphore_signal(barrier, inc=1, device_id=peer, device_id_type=MESH)
    cross[...] = jnp.zeros_like(cross)
    nsq[...] = jnp.zeros_like(nsq)
    lsq[...] = jnp.zeros_like(lsq)
    own_n.wait()
    own_l.wait()
    pl.semaphore_wait(barrier, len(col_peers + quad_peers + z_peers))

    def rc(src, dst, ssem, rsem, dev):
        return pltpu.make_async_remote_copy(
            src_ref=src, dst_ref=dst, send_sem=ssem, recv_sem=rsem,
            device_id=dev, device_id_type=MESH,
        )

    def nsl(slot, h):
        return nz.at[slot, pl.ds(h * HALF, HALF), :]

    sent = []

    def nsend(slot, h, idx, dev):
        c = rc(nsl(slot, h), nsl(slot, h), n_send.at[idx], n_recv.at[idx], dev)
        c.start()
        sent.append(c)

    def nwait(slot, h, idx):
        rc(nsl(slot, h), nsl(slot, h), n_send.at[idx], n_recv.at[idx], y_up).wait_recv()

    def lsend(ref, idx, dev):
        c = rc(ref, ref, l_send.at[idx], l_recv.at[idx], dev)
        c.start()
        sent.append(c)

    def lwait(ref, idx):
        rc(ref, ref, l_send.at[idx], l_recv.at[idx], z_up).wait_recv()

    own_pair = lt.at[z, core]
    lsend(lt.at[z, core, xl], 0, other_xl)
    nsend(col, 0, 12, other_xh)
    nsend(col, 0, 0, y_up)
    nsend(col, 1, 3, y_dn)
    lsend(lt.at[z, core, xl], 1, z_up)
    lsend(lt.at[z, core, xl], 6, z_dn)
    nsend(col, 1, 13, other_xh)
    nsend(col, 1, 1, y_up)
    nsend(col, 0, 2, y_dn)

    lwait(lt.at[z, core, 1 - xl], 0)
    lsend(lt.at[z, core, 1 - xl], 2, z_up)
    lsend(lt.at[z, core, 1 - xl], 7, z_dn)
    lsend(own_pair, 11, other_core)

    for sgn, base, dev in ((-1, 1, z_up), (1, 6, z_dn)):
        zz = ring_z(sgn)
        lwait(lt.at[zz, core, xl], base)
        lwait(lt.at[zz, core, 1 - xl], base + 1)
        lsend(lt.at[zz, core], base + 2, dev)
        lsend(lt.at[zz, core], 12 + (base == 6), other_core)

    def slot_of(yy, s):
        return yy * 2 + (xh if s == 0 else 1 - xh)

    def forward_noise(s):
        dn, up = slot_of(ring_y(-1), s), slot_of(ring_y(1), s)
        nwait(dn, 0, 6 * s)
        nsend(dn, 0, 6 * s + 4, y_up)
        nwait(up, 1, 6 * s + 3)
        nsend(up, 1, 6 * s + 5, y_dn)

    forward_noise(0)

    for sgn, base, dev in ((-1, 1, z_up), (1, 6, z_dn)):
        zz = ring_z(2 * sgn)
        lwait(lt.at[zz, core], base + 2)
        lsend(lt.at[zz, core], base + 3, dev)
        lsend(lt.at[zz, core], 14 + (base == 6), other_core)

    partner = slot_of(y, 1)
    nwait(partner, 0, 12)
    nsend(partner, 0, 6, y_up)
    nwait(partner, 1, 13)
    nsend(partner, 1, 9, y_dn)
    nsend(partner, 1, 7, y_up)
    nsend(partner, 0, 8, y_dn)

    for sgn, base, dev in ((-1, 1, z_up), (1, 6, z_dn)):
        zz = ring_z(3 * sgn)
        lwait(lt.at[zz, core], base + 3)
        lsend(lt.at[zz, core, int(base == 6)], base + 4, dev)
        lsend(lt.at[zz, core], 16 + (base == 6), other_core)
    far = ring_z(4)
    lwait(lt.at[far, core, 0], 5)
    lwait(lt.at[far, core, 1], 10)
    lsend(lt.at[far, core], 18, other_core)
    for j, d in enumerate((0, -1, 1, -2, 2, -3, 3, 4)):
        lwait(lt.at[ring_z(d), 1 - core], 11 + j)

    def accumulate(slot):
        a = nz[slot]
        b = jnp.concatenate([lt[slot, 0, 0], lt[slot, 1, 0], lt[slot, 0, 1], lt[slot, 1, 1]], axis=1)
        cross[...] += lax.dot_general(a, b, (((1,), (1,)), ((), ())), preferred_element_type=F32)
        a2 = jnp.square(a.astype(F32))
        nsq[...] += (a2[:, 0:128] + a2[:, 128:256]) + (a2[:, 256:384] + a2[:, 384:512])
        b2 = jnp.square(b.astype(F32))
        lsq[...] += (b2[:, 0:128] + b2[:, 128:256]) + (b2[:, 256:384] + b2[:, 384:512])

    def wait_rest(s):
        dn, up = slot_of(ring_y(-1), s), slot_of(ring_y(1), s)
        nwait(dn, 1, 6 * s + 1)
        nwait(up, 0, 6 * s + 2)

    def wait_far(s):
        fr = slot_of(ring_y(2), s)
        nwait(fr, 0, 6 * s + 4)
        nwait(fr, 1, 6 * s + 5)

    wait_rest(0)
    wait_far(0)

    def set0(k, carry):
        accumulate(((y + k) % Y) * 2 + xh)
        return carry

    lax.fori_loop(0, Y, set0, 0)
    forward_noise(1)
    wait_rest(1)

    def set1(k, carry):
        accumulate(((y + Y - 1 + k) % Y) * 2 + 1 - xh)
        return carry

    lax.fori_loop(0, 3, set1, 0)
    wait_far(1)
    accumulate(slot_of(ring_y(2), 1))

    for q in range(2):
        c = rc(
            nz.at[:, :, pl.ds(pl.multiple_of(q * 256 + (1 - core) * LANE, LANE), LANE)],
            no.at[:, :, pl.ds(q * LANE, LANE)],
            o_send.at[q], o_recv.at[q], other_core,
        )
        c.start()
        sent.append(c)

    eye = (
        lax.broadcasted_iota(jnp.int32, (LANE, LANE), 0)
        == lax.broadcasted_iota(jnp.int32, (LANE, LANE), 1)
    )

    def to_lanes(v):
        return jnp.sum(jnp.where(eye, v, 0.0), axis=0, keepdims=True)

    def to_rows(v):
        return jnp.sum(jnp.where(eye, v, 0.0), axis=1, keepdims=True)

    def wide(v):
        return jnp.concatenate([v[q:q + 1, :] for q in range(4)], axis=1)

    scale = 1.0 / (width * EPS)
    lq = jnp.concatenate(
        [to_lanes(jnp.sum(lsq[q * LANE:(q + 1) * LANE, :], axis=1, keepdims=True)) for q in range(4)],
        axis=1,
    )
    for b in range(4):
        rows = slice(b * LANE, (b + 1) * LANE)
        nq = jnp.sum(nsq[rows, :], axis=1, keepdims=True)
        cross[rows, :] = (nq + lq - 2.0 * cross[rows, :]) * scale

    def merge(top, total):
        best = jnp.max(top, axis=0)
        return best, jnp.sum(total * jnp.exp(top - best[None]), axis=0)

    def exchange(buf, mine, peers, ssem, rsem):
        for peer in peers:
            rc(buf.at[mine], buf.at[mine], ssem, rsem, peer).start()
        k = len(peers)
        rc(buf.at[pl.ds(0, k)], buf.at[pl.ds(0, k)], ssem, rsem, peers[0]).wait_recv()

    g = start_ref[...] * (1.0 / EPS)
    f = None
    f_rows = None
    for it in range(ITERS):
        gw = wide(g)
        for b in range(4):
            s = gw - cross[b * LANE:(b + 1) * LANE, :]
            top = jnp.max(s, axis=1, keepdims=True)
            tot = jnp.sum(jnp.exp(s - top), axis=1, keepdims=True)
            rowx[it, col, b:b + 1, :] = to_lanes(top)
            rowx[it, col, 4 + b:5 + b, :] = to_lanes(tot)
        exchange(rowx.at[it], col, col_peers, r_send.at[it], r_recv.at[it])
        top, tot = merge(rowx[it, :, 0:4, :], rowx[it, :, 4:8, :])
        f = -(math.log(m_total) + (top + jnp.log(tot)))
        f_rows = [to_rows(f[b:b + 1, :]) for b in range(4)]
        tops, tots = [], []
        for b in range(4):
            s = f_rows[b] - cross[b * LANE:(b + 1) * LANE, :]
            top = jnp.max(s, axis=0, keepdims=True)
            tops.append(top)
            tots.append(jnp.sum(jnp.exp(s - top), axis=0, keepdims=True))
        top = jnp.maximum(jnp.maximum(tops[0], tops[1]), jnp.maximum(tops[2], tops[3]))
        tot = sum(tots[b] * jnp.exp(tops[b] - top) for b in range(4))
        for q in range(4):
            col1[it, quad, q:q + 1, :] = top[:, q * LANE:(q + 1) * LANE]
            col1[it, quad, 4 + q:5 + q, :] = tot[:, q * LANE:(q + 1) * LANE]
        exchange(col1.at[it], quad, quad_peers, c1_send.at[it], c1_recv.at[it])
        top, tot = merge(col1[it, :, 0:4, :], col1[it, :, 4:8, :])
        col2[it, z, 0:4, :] = top
        col2[it, z, 4:8, :] = tot
        exchange(col2.at[it], z, z_peers, c2_send.at[it], c2_recv.at[it])
        top, tot = merge(col2[it, :, 0:4, :], col2[it, :, 4:8, :])
        g = -(math.log(n_total) + (top + jnp.log(tot)))

    npot_ref[...] = f * EPS
    lpot_ref[...] = g * EPS

    gw = wide(g)
    for b in range(4):
        rows = slice(b * LANE, (b + 1) * LANE)
        w = m_total * jnp.exp((f_rows[b] + gw) - cross[rows, :])
        wt[core, :, rows] = w.T.astype(BF16)
    wc = rc(wt.at[core], wt.at[core], w_send.at[0], w_recv.at[0], other_core)
    wc.start()
    sent.append(wc)
    for q in range(2):
        rc(no.at[:, :, pl.ds(q * LANE, LANE)], no.at[:, :, pl.ds(q * LANE, LANE)],
           o_send.at[q], o_recv.at[q], other_core).wait_recv()
    rc(wt.at[core], wt.at[1 - core], w_send.at[0], w_recv.at[0], other_core).wait_recv()

    def partial(rel):
        d = (z + rel) % Z
        mine = jnp.concatenate(
            [nz[d, :, pl.ds(pl.multiple_of(q * 256 + core * LANE, LANE), LANE)] for q in (1 - xl, xl)],
            axis=1,
        )
        theirs = jnp.concatenate(
            [no[d, :, pl.ds(pl.multiple_of(q * LANE, LANE), LANE)] for q in (1 - xl, xl)], axis=1
        )
        part[rel] = jnp.dot(wt[core], mine, preferred_element_type=F32) + jnp.dot(
            wt[1 - core], theirs, preferred_element_type=F32
        )

    def piece(buf, dr, s, k):
        if s == 4:
            return buf.at[dr, 0, k, pl.ds(dr * HALF, HALF), :]
        return buf.at[dr, 4 - s, k]

    def ring_copy(dr, s, k):
        return rc(
            piece(stage, dr, s, k), piece(land, dr, s, k),
            s_send.at[dr, 4 - s, k], s_recv.at[dr, 4 - s, k], z_dn if dr == 0 else z_up,
        )

    def ring_send(dr, s, k):
        c = ring_copy(dr, s, k)
        c.start()
        sent.append(c)

    partial(4)
    for k in range(2):
        for dr in range(2):
            half = slice(dr * HALF, (dr + 1) * HALF)
            stage[dr, 0, k, half, :] = part[4, half, k * LANE:(k + 1) * LANE].astype(BF16)
            ring_send(dr, 4, k)

    def rest(i, carry):
        rel = jnp.where(i % 2 == 0, 3 - i // 2, 5 + i // 2)
        partial((rel + Z) % Z)
        return carry

    lax.fori_loop(0, 7, rest, 0)

    for s in (3, 2, 1):
        for k in range(2):
            lanes = slice(k * LANE, (k + 1) * LANE)
            for dr in range(2):
                rel = Z - s if dr == 0 else s
                ring_copy(dr, s + 1, k).wait_recv()
                if s == 3:
                    half = slice(dr * HALF, (dr + 1) * HALF)
                    rest_rows = slice((1 - dr) * HALF, (2 - dr) * HALF)
                    stage[dr, 1, k, half, :] = (
                        part[rel, half, lanes] + land[dr, 0, k, half, :].astype(F32)
                    ).astype(BF16)
                    stage[dr, 1, k, rest_rows, :] = part[rel, rest_rows, lanes].astype(BF16)
                else:
                    stage[dr, 4 - s, k] = (
                        part[rel, :, lanes] + land[dr, 3 - s, k].astype(F32)
                    ).astype(BF16)
                ring_send(dr, s, k)

    def total(k):
        for dr in range(2):
            ring_copy(dr, 1, k).wait_recv()
        return part[0, :, k * LANE:(k + 1) * LANE] + (
            land[0, 3, k].astype(F32) + land[1, 3, k].astype(F32)
        )

    xs[...] = total(0)
    xc = rc(xs, xr, x_send.at[0], x_recv.at[0], other_xl)
    xc.start()
    sent.append(xc)
    kept = total(1)
    xc.wait_recv()
    out_ref[...] = (kept + xr[...]).T

    for c in sent:
        c.wait_send()
    for it in range(ITERS):
        for buf, k, ssem, rsem in (
            (rowx, 7, r_send, r_recv), (col1, 3, c1_send, c1_recv), (col2, 7, c2_send, c2_recv)
        ):
            ref = buf.at[it, pl.ds(0, k)]
            rc(ref, ref, ssem.at[it], rsem.at[it], z_up).wait_send()


def per_device(n_total, m_total, noise_draw, latent_code, start_potential):
    anyspace = pl.BlockSpec(memory_space=pl.ANY)
    vmem = pl.BlockSpec(memory_space=pltpu.VMEM)
    width = 4096
    dma = pltpu.SemaphoreType.DMA

    def body(*refs):
        kernel(n_total, m_total, width, *refs)

    npot, lpot, out = pl.pallas_call(
        body,
        out_shape=(
            jax.ShapeDtypeStruct((4, LANE), F32),
            jax.ShapeDtypeStruct((4, LANE), F32),
            jax.ShapeDtypeStruct((LANE, BLK), F32),
        ),
        in_specs=[anyspace, anyspace, vmem],
        out_specs=(vmem, vmem, vmem),
        scratch_shapes=[
            pltpu.VMEM((8, BLK, BLK), BF16),
            pltpu.VMEM((Z, 2, 2, BLK, LANE), BF16),
            pltpu.VMEM((8, BLK, 2 * LANE), BF16),
            pltpu.VMEM((BLK, BLK), F32),
            pltpu.VMEM((BLK, LANE), F32),
            pltpu.VMEM((BLK, LANE), F32),
            pltpu.VMEM((2, BLK, BLK), BF16),
            pltpu.VMEM((8, BLK, 2 * LANE), F32),
            pltpu.VMEM((2, 4, 2, BLK, LANE), BF16),
            pltpu.VMEM((2, 4, 2, BLK, LANE), BF16),
            pltpu.VMEM((BLK, LANE), F32),
            pltpu.VMEM((BLK, LANE), F32),
            pltpu.VMEM((ITERS, 8, 8, LANE), F32),
            pltpu.VMEM((ITERS, 4, 8, LANE), F32),
            pltpu.VMEM((ITERS, 8, 8, LANE), F32),
            dma((14,)), dma((14,)),
            dma((19,)), dma((19,)),
            dma((2,)), dma((2,)),
            dma((1,)), dma((1,)),
            dma((ITERS,)), dma((ITERS,)),
            dma((ITERS,)), dma((ITERS,)),
            dma((ITERS,)), dma((ITERS,)),
            dma((2, 4, 2)), dma((2, 4, 2)),
            dma((1,)), dma((1,)),
            dma((2,)),
        ],
        compiler_params=pltpu.CompilerParams(
            collective_id=0, has_side_effects=True, vmem_limit_bytes=48 * 1024 * 1024
        ),
    )(noise_draw, latent_code, start_potential.reshape(4, LANE))
    return npot.reshape(BLK), lpot.reshape(BLK), out


def solution(mesh):
    in_specs = (P("row", "col"), P("col", "row"), P("col"))
    out_specs = (P("row"), P("col"), P("row", "col"))

    def whole(noise_draw, latent_code, start_potential):
        def block(a, b, c):
            return per_device(noise_draw.shape[0], latent_code.shape[0], a, b, c)

        return jax.shard_map(
            block, mesh=mesh, in_specs=in_specs, out_specs=out_specs, check_vma=False
        )(noise_draw, latent_code, start_potential)

    return whole
```

```python
import math

import jax
import jax.numpy as jnp
from jax import lax
from jax.experimental import pallas as pl
from jax.experimental.pallas import tpu as pltpu
from jax.sharding import PartitionSpec as P

ITERS = 3
EPS = 0.01
MESH = pl.DeviceIdType.MESH
F32 = jnp.float32
BF16 = jnp.bfloat16

Z, Y = 8, 4
LANE = 128
BLK = 512
HALF = BLK // 2


def kernel(
    n_total, m_total, width,
    noise_ref, latent_ref, start_ref,
    npot_ref, lpot_ref, out_ref,
    nz, lt, no, relay, cross, nsq, lsq, wt, part, stage, land, xs, xr, rowx, col1, col2,
    n_send, n_recv, h_send, h_recv, l_send, l_recv, o_send, o_recv, w_send, w_recv,
    r_send, r_recv, c1_send, c1_recv, c2_send, c2_recv, s_send, s_recv, x_send, x_recv, loc,
):
    row = lax.axis_index("row")
    col = lax.axis_index("col")
    z = row // 4
    xl = (row // 2) % 2
    core = row % 2
    y = col // 2
    xh = col % 2
    quad = row % 4

    def ring_z(d):
        return (z + d + Z) % Z

    def ring_y(d):
        return (y + d + Y) % Y

    other_core = (row + 1 - 2 * core, col)
    other_xl = (row + 2 - 4 * xl, col)
    flip_col = col + 1 - 2 * xh
    diagonal = (row + 2 - 4 * xl, flip_col)
    z_up = (ring_z(1) * 4 + quad, col)
    z_dn = (ring_z(-1) * 4 + quad, col)
    y_up = (row, ring_y(1) * 2 + xh)
    y_dn = (row, ring_y(-1) * 2 + xh)
    col_peers = [(row, (col + d) % 8) for d in range(1, 8)]
    quad_peers = [(z * 4 + (quad + d) % 4, col) for d in range(1, 4)]
    z_peers = [(ring_z(d) * 4 + quad, col) for d in range(1, 8)]

    peers = col_peers + quad_peers + z_peers + [diagonal]

    own_n = pltpu.make_async_copy(noise_ref, nz.at[col], loc.at[0])
    own_l = pltpu.make_async_copy(latent_ref, lt.at[z, core, xl], loc.at[1])
    own_n.start()
    own_l.start()

    barrier = pltpu.get_barrier_semaphore()
    for peer in peers:
        pl.semaphore_signal(barrier, inc=1, device_id=peer, device_id_type=MESH)
    cross[...] = jnp.zeros_like(cross)
    nsq[...] = jnp.zeros_like(nsq)
    lsq[...] = jnp.zeros_like(lsq)
    own_n.wait()
    own_l.wait()
    pl.semaphore_wait(barrier, len(peers))

    def rc(src, dst, ssem, rsem, dev):
        return pltpu.make_async_remote_copy(
            src_ref=src, dst_ref=dst, send_sem=ssem, recv_sem=rsem,
            device_id=dev, device_id_type=MESH,
        )

    def nsl(slot, h):
        return nz.at[slot, pl.ds(h * HALF, HALF), :]

    sent = []

    def nsend(slot, h, idx, dev):
        c = rc(nsl(slot, h), nsl(slot, h), n_send.at[idx], n_recv.at[idx], dev)
        c.start()
        sent.append(c)

    def nwait(slot, h, idx):
        rc(nsl(slot, h), nsl(slot, h), n_send.at[idx], n_recv.at[idx], y_up).wait_recv()

    def lsend(ref, idx, dev):
        c = rc(ref, ref, l_send.at[idx], l_recv.at[idx], dev)
        c.start()
        sent.append(c)

    def lwait(ref, idx):
        rc(ref, ref, l_send.at[idx], l_recv.at[idx], z_up).wait_recv()

    QUART = HALF // 2

    def quarter(slot, path, p):
        return nz.at[slot, pl.ds(path * HALF + p * QUART, QUART), :]

    def relay_start(path, p):
        c = rc(quarter(col, path, p), relay.at[path, p], h_send.at[0, path, p], h_recv.at[0, path, p],
               other_xl if path == 0 else diagonal)
        c.start()
        sent.append(c)

    def relay_forward(path, p):
        slot = col if path == 0 else flip_col
        dev = diagonal if path == 0 else other_xl
        rc(relay.at[path, p], relay.at[path, p], h_send.at[0, path, p], h_recv.at[0, path, p], dev).wait_recv()
        c = rc(relay.at[path, p], quarter(slot, path, p), h_send.at[1, path, p], h_recv.at[1, path, p], dev)
        c.start()
        sent.append(c)

    def relay_end(path):
        for p in range(2):
            ref = quarter(flip_col, path, p)
            rc(ref, ref, h_send.at[1, path, p], h_recv.at[1, path, p], diagonal).wait_recv()

    def slot_of(yy, s):
        return yy * 2 + (xh if s == 0 else 1 - xh)

    def forward_noise(s):
        dn, up = slot_of(ring_y(-1), s), slot_of(ring_y(1), s)
        nwait(dn, 0, 6 * s)
        nsend(dn, 0, 6 * s + 4, y_up)
        nwait(up, 1, 6 * s + 3)
        nsend(up, 1, 6 * s + 5, y_dn)

    own_pair = lt.at[z, core]
    lsend(lt.at[z, core, xl], 0, other_xl)
    relay_start(0, 0)
    relay_start(1, 0)
    nsend(col, 0, 0, y_up)
    nsend(col, 1, 3, y_dn)
    lsend(lt.at[z, core, xl], 1, z_up)
    lsend(lt.at[z, core, xl], 6, z_dn)
    relay_start(0, 1)
    relay_start(1, 1)
    nsend(col, 1, 1, y_up)
    nsend(col, 0, 2, y_dn)

    lwait(lt.at[z, core, 1 - xl], 0)
    lsend(lt.at[z, core, 1 - xl], 2, z_up)
    lsend(lt.at[z, core, 1 - xl], 7, z_dn)
    lsend(own_pair, 11, other_core)
    relay_forward(0, 0)
    relay_forward(1, 0)

    for sgn, base, dev in ((-1, 1, z_up), (1, 6, z_dn)):
        zz = ring_z(sgn)
        lwait(lt.at[zz, core, xl], base)
        lwait(lt.at[zz, core, 1 - xl], base + 1)
        lsend(lt.at[zz, core], base + 2, dev)
        lsend(lt.at[zz, core], 12 + (base == 6), other_core)

    relay_forward(0, 1)
    relay_forward(1, 1)
    forward_noise(0)

    for sgn, base, dev in ((-1, 1, z_up), (1, 6, z_dn)):
        zz = ring_z(2 * sgn)
        lwait(lt.at[zz, core], base + 2)
        lsend(lt.at[zz, core], base + 3, dev)
        lsend(lt.at[zz, core], 14 + (base == 6), other_core)

    relay_end(0)
    nsend(flip_col, 0, 6, y_up)
    nsend(flip_col, 0, 8, y_dn)
    relay_end(1)
    nsend(flip_col, 1, 9, y_dn)
    nsend(flip_col, 1, 7, y_up)

    for sgn, base, dev in ((-1, 1, z_up), (1, 6, z_dn)):
        zz = ring_z(3 * sgn)
        lwait(lt.at[zz, core], base + 3)
        lsend(lt.at[zz, core, int(base == 6)], base + 4, dev)
        lsend(lt.at[zz, core], 16 + (base == 6), other_core)
    far = ring_z(4)
    lwait(lt.at[far, core, 0], 5)
    lwait(lt.at[far, core, 1], 10)
    lsend(lt.at[far, core], 18, other_core)
    for j, d in enumerate((0, -1, 1, -2, 2, -3, 3, 4)):
        lwait(lt.at[ring_z(d), 1 - core], 11 + j)

    def accumulate(slot):
        a = nz[slot]
        b = jnp.concatenate([lt[slot, 0, 0], lt[slot, 1, 0], lt[slot, 0, 1], lt[slot, 1, 1]], axis=1)
        cross[...] += lax.dot_general(a, b, (((1,), (1,)), ((), ())), preferred_element_type=F32)
        a2 = jnp.square(a.astype(F32))
        nsq[...] += (a2[:, 0:128] + a2[:, 128:256]) + (a2[:, 256:384] + a2[:, 384:512])
        b2 = jnp.square(b.astype(F32))
        lsq[...] += (b2[:, 0:128] + b2[:, 128:256]) + (b2[:, 256:384] + b2[:, 384:512])

    def wait_rest(s):
        dn, up = slot_of(ring_y(-1), s), slot_of(ring_y(1), s)
        nwait(dn, 1, 6 * s + 1)
        nwait(up, 0, 6 * s + 2)

    def wait_far(s):
        fr = slot_of(ring_y(2), s)
        nwait(fr, 0, 6 * s + 4)
        nwait(fr, 1, 6 * s + 5)

    wait_rest(0)
    wait_far(0)

    def set0(k, carry):
        accumulate(((y + k) % Y) * 2 + xh)
        return carry

    lax.fori_loop(0, Y, set0, 0)
    forward_noise(1)
    wait_rest(1)

    def set1(k, carry):
        accumulate(((y + Y - 1 + k) % Y) * 2 + 1 - xh)
        return carry

    lax.fori_loop(0, 3, set1, 0)
    wait_far(1)
    accumulate(slot_of(ring_y(2), 1))

    for q in range(2):
        c = rc(
            nz.at[:, :, pl.ds(pl.multiple_of(q * 256 + (1 - core) * LANE, LANE), LANE)],
            no.at[:, :, pl.ds(q * LANE, LANE)],
            o_send.at[q], o_recv.at[q], other_core,
        )
        c.start()
        sent.append(c)

    eye = (
        lax.broadcasted_iota(jnp.int32, (LANE, LANE), 0)
        == lax.broadcasted_iota(jnp.int32, (LANE, LANE), 1)
    )

    def to_lanes(v):
        return jnp.sum(jnp.where(eye, v, 0.0), axis=0, keepdims=True)

    def to_rows(v):
        return jnp.sum(jnp.where(eye, v, 0.0), axis=1, keepdims=True)

    def wide(v):
        return jnp.concatenate([v[q:q + 1, :] for q in range(4)], axis=1)

    scale = 1.0 / (width * EPS)
    lq = jnp.concatenate(
        [to_lanes(jnp.sum(lsq[q * LANE:(q + 1) * LANE, :], axis=1, keepdims=True)) for q in range(4)],
        axis=1,
    )
    for b in range(4):
        rows = slice(b * LANE, (b + 1) * LANE)
        nq = jnp.sum(nsq[rows, :], axis=1, keepdims=True)
        cross[rows, :] = (nq + lq - 2.0 * cross[rows, :]) * scale

    def merge(top, total):
        best = jnp.max(top, axis=0)
        return best, jnp.sum(total * jnp.exp(top - best[None]), axis=0)

    def exchange(buf, mine, peers, ssem, rsem):
        for peer in peers:
            rc(buf.at[mine], buf.at[mine], ssem, rsem, peer).start()
        k = len(peers)
        rc(buf.at[pl.ds(0, k)], buf.at[pl.ds(0, k)], ssem, rsem, peers[0]).wait_recv()

    g = start_ref[...] * (1.0 / EPS)
    f = None
    f_rows = None
    for it in range(ITERS):
        gw = wide(g)
        for b in range(4):
            s = gw - cross[b * LANE:(b + 1) * LANE, :]
            top = jnp.max(s, axis=1, keepdims=True)
            tot = jnp.sum(jnp.exp(s - top), axis=1, keepdims=True)
            rowx[it, col, b:b + 1, :] = to_lanes(top)
            rowx[it, col, 4 + b:5 + b, :] = to_lanes(tot)
        exchange(rowx.at[it], col, col_peers, r_send.at[it], r_recv.at[it])
        top, tot = merge(rowx[it, :, 0:4, :], rowx[it, :, 4:8, :])
        f = -(math.log(m_total) + (top + jnp.log(tot)))
        f_rows = [to_rows(f[b:b + 1, :]) for b in range(4)]
        tops, tots = [], []
        for b in range(4):
            s = f_rows[b] - cross[b * LANE:(b + 1) * LANE, :]
            top = jnp.max(s, axis=0, keepdims=True)
            tops.append(top)
            tots.append(jnp.sum(jnp.exp(s - top), axis=0, keepdims=True))
        top = jnp.maximum(jnp.maximum(tops[0], tops[1]), jnp.maximum(tops[2], tops[3]))
        tot = sum(tots[b] * jnp.exp(tops[b] - top) for b in range(4))
        for q in range(4):
            col1[it, quad, q:q + 1, :] = top[:, q * LANE:(q + 1) * LANE]
            col1[it, quad, 4 + q:5 + q, :] = tot[:, q * LANE:(q + 1) * LANE]
        exchange(col1.at[it], quad, quad_peers, c1_send.at[it], c1_recv.at[it])
        top, tot = merge(col1[it, :, 0:4, :], col1[it, :, 4:8, :])
        col2[it, z, 0:4, :] = top
        col2[it, z, 4:8, :] = tot
        exchange(col2.at[it], z, z_peers, c2_send.at[it], c2_recv.at[it])
        top, tot = merge(col2[it, :, 0:4, :], col2[it, :, 4:8, :])
        g = -(math.log(n_total) + (top + jnp.log(tot)))

    npot_ref[...] = f * EPS
    lpot_ref[...] = g * EPS

    gw = wide(g)
    for b in range(4):
        rows = slice(b * LANE, (b + 1) * LANE)
        w = m_total * jnp.exp((f_rows[b] + gw) - cross[rows, :])
        wt[core, :, rows] = w.T.astype(BF16)
    wc = rc(wt.at[core], wt.at[core], w_send.at[0], w_recv.at[0], other_core)
    wc.start()
    sent.append(wc)
    for q in range(2):
        rc(no.at[:, :, pl.ds(q * LANE, LANE)], no.at[:, :, pl.ds(q * LANE, LANE)],
           o_send.at[q], o_recv.at[q], other_core).wait_recv()
    rc(wt.at[core], wt.at[1 - core], w_send.at[0], w_recv.at[0], other_core).wait_recv()

    def partial(rel):
        d = (z + rel) % Z
        mine = jnp.concatenate(
            [nz[d, :, pl.ds(pl.multiple_of(q * 256 + core * LANE, LANE), LANE)] for q in (1 - xl, xl)],
            axis=1,
        )
        theirs = jnp.concatenate(
            [no[d, :, pl.ds(pl.multiple_of(q * LANE, LANE), LANE)] for q in (1 - xl, xl)], axis=1
        )
        part[rel] = jnp.dot(wt[core], mine, preferred_element_type=F32) + jnp.dot(
            wt[1 - core], theirs, preferred_element_type=F32
        )

    def piece(buf, dr, s, k):
        if s == 4:
            return buf.at[dr, 0, k, pl.ds(dr * HALF, HALF), :]
        return buf.at[dr, 4 - s, k]

    def ring_copy(dr, s, k):
        return rc(
            piece(stage, dr, s, k), piece(land, dr, s, k),
            s_send.at[dr, 4 - s, k], s_recv.at[dr, 4 - s, k], z_dn if dr == 0 else z_up,
        )

    def ring_send(dr, s, k):
        c = ring_copy(dr, s, k)
        c.start()
        sent.append(c)

    partial(4)
    for k in range(2):
        for dr in range(2):
            half = slice(dr * HALF, (dr + 1) * HALF)
            stage[dr, 0, k, half, :] = part[4, half, k * LANE:(k + 1) * LANE].astype(BF16)
            ring_send(dr, 4, k)

    def rest(i, carry):
        rel = jnp.where(i % 2 == 0, 3 - i // 2, 5 + i // 2)
        partial((rel + Z) % Z)
        return carry

    lax.fori_loop(0, 7, rest, 0)

    for s in (3, 2, 1):
        for k in range(2):
            lanes = slice(k * LANE, (k + 1) * LANE)
            for dr in range(2):
                rel = Z - s if dr == 0 else s
                ring_copy(dr, s + 1, k).wait_recv()
                if s == 3:
                    half = slice(dr * HALF, (dr + 1) * HALF)
                    rest_rows = slice((1 - dr) * HALF, (2 - dr) * HALF)
                    stage[dr, 1, k, half, :] = (
                        part[rel, half, lanes] + land[dr, 0, k, half, :].astype(F32)
                    ).astype(BF16)
                    stage[dr, 1, k, rest_rows, :] = part[rel, rest_rows, lanes].astype(BF16)
                else:
                    stage[dr, 4 - s, k] = (
                        part[rel, :, lanes] + land[dr, 3 - s, k].astype(F32)
                    ).astype(BF16)
                ring_send(dr, s, k)

    def total(k):
        for dr in range(2):
            ring_copy(dr, 1, k).wait_recv()
        return part[0, :, k * LANE:(k + 1) * LANE] + (
            land[0, 3, k].astype(F32) + land[1, 3, k].astype(F32)
        )

    xs[...] = total(0)
    xc = rc(xs, xr, x_send.at[0], x_recv.at[0], other_xl)
    xc.start()
    sent.append(xc)
    kept = total(1)
    xc.wait_recv()
    out_ref[...] = (kept + xr[...]).T

    for c in sent:
        c.wait_send()
    for it in range(ITERS):
        for buf, k, ssem, rsem in (
            (rowx, 7, r_send, r_recv), (col1, 3, c1_send, c1_recv), (col2, 7, c2_send, c2_recv)
        ):
            ref = buf.at[it, pl.ds(0, k)]
            rc(ref, ref, ssem.at[it], rsem.at[it], z_up).wait_send()


def per_device(n_total, m_total, noise_draw, latent_code, start_potential):
    anyspace = pl.BlockSpec(memory_space=pl.ANY)
    vmem = pl.BlockSpec(memory_space=pltpu.VMEM)
    width = 4096
    dma = pltpu.SemaphoreType.DMA

    def body(*refs):
        kernel(n_total, m_total, width, *refs)

    npot, lpot, out = pl.pallas_call(
        body,
        out_shape=(
            jax.ShapeDtypeStruct((4, LANE), F32),
            jax.ShapeDtypeStruct((4, LANE), F32),
            jax.ShapeDtypeStruct((LANE, BLK), F32),
        ),
        in_specs=[anyspace, anyspace, vmem],
        out_specs=(vmem, vmem, vmem),
        scratch_shapes=[
            pltpu.VMEM((8, BLK, BLK), BF16),
            pltpu.VMEM((Z, 2, 2, BLK, LANE), BF16),
            pltpu.VMEM((8, BLK, 2 * LANE), BF16),
            pltpu.VMEM((2, 2, BLK // 4, BLK), BF16),
            pltpu.VMEM((BLK, BLK), F32),
            pltpu.VMEM((BLK, LANE), F32),
            pltpu.VMEM((BLK, LANE), F32),
            pltpu.VMEM((2, BLK, BLK), BF16),
            pltpu.VMEM((8, BLK, 2 * LANE), F32),
            pltpu.VMEM((2, 4, 2, BLK, LANE), BF16),
            pltpu.VMEM((2, 4, 2, BLK, LANE), BF16),
            pltpu.VMEM((BLK, LANE), F32),
            pltpu.VMEM((BLK, LANE), F32),
            pltpu.VMEM((ITERS, 8, 8, LANE), F32),
            pltpu.VMEM((ITERS, 4, 8, LANE), F32),
            pltpu.VMEM((ITERS, 8, 8, LANE), F32),
            dma((12,)), dma((12,)),
            dma((2, 2, 2)), dma((2, 2, 2)),
            dma((19,)), dma((19,)),
            dma((2,)), dma((2,)),
            dma((1,)), dma((1,)),
            dma((ITERS,)), dma((ITERS,)),
            dma((ITERS,)), dma((ITERS,)),
            dma((ITERS,)), dma((ITERS,)),
            dma((2, 4, 2)), dma((2, 4, 2)),
            dma((1,)), dma((1,)),
            dma((2,)),
        ],
        compiler_params=pltpu.CompilerParams(
            collective_id=0, has_side_effects=True, vmem_limit_bytes=60 * 1024 * 1024
        ),
    )(noise_draw, latent_code, start_potential.reshape(4, LANE))
    return npot.reshape(BLK), lpot.reshape(BLK), out


def solution(mesh):
    in_specs = (P("row", "col"), P("col", "row"), P("col"))
    out_specs = (P("row"), P("col"), P("row", "col"))

    def whole(noise_draw, latent_code, start_potential):
        def block(a, b, c):
            return per_device(noise_draw.shape[0], latent_code.shape[0], a, b, c)

        return jax.shard_map(
            block, mesh=mesh, in_specs=in_specs, out_specs=out_specs, check_vma=False
        )(noise_draw, latent_code, start_potential)

    return whole
```

```python
import math

import jax
import jax.numpy as jnp
from jax import lax
from jax.experimental import pallas as pl
from jax.experimental.pallas import tpu as pltpu
from jax.sharding import PartitionSpec as P

ITERS = 3
EPS = 0.01
MESH = pl.DeviceIdType.MESH
F32 = jnp.float32
BF16 = jnp.bfloat16

Z, Y = 8, 4
LANE = 128
BLK = 512
HALF = BLK // 2


def kernel(
    n_total, m_total, width,
    noise_ref, latent_ref, start_ref,
    npot_ref, lpot_ref, out_ref,
    nz, lt, no, relay, cross, nsq, lsq, wt, part, stage, land, xs, xr, rowx, col1, col2,
    n_send, n_recv, h_send, h_recv, l_send, l_recv, o_send, o_recv, w_send, w_recv,
    r_send, r_recv, c1_send, c1_recv, c2_send, c2_recv, s_send, s_recv, x_send, x_recv, loc,
):
    row = lax.axis_index("row")
    col = lax.axis_index("col")
    z = row // 4
    xl = (row // 2) % 2
    core = row % 2
    y = col // 2
    xh = col % 2
    quad = row % 4

    def ring_z(d):
        return (z + d + Z) % Z

    def ring_y(d):
        return (y + d + Y) % Y

    other_core = (row + 1 - 2 * core, col)
    other_xl = (row + 2 - 4 * xl, col)
    flip_col = col + 1 - 2 * xh
    diagonal = (row + 2 - 4 * xl, flip_col)
    z_up = (ring_z(1) * 4 + quad, col)
    z_dn = (ring_z(-1) * 4 + quad, col)
    y_up = (row, ring_y(1) * 2 + xh)
    y_dn = (row, ring_y(-1) * 2 + xh)
    col_peers = [(row, (col + d) % 8) for d in range(1, 8)]
    quad_peers = [(z * 4 + (quad + d) % 4, col) for d in range(1, 4)]
    z_peers = [(ring_z(d) * 4 + quad, col) for d in range(1, 8)]

    peers = col_peers + quad_peers + z_peers + [diagonal]

    own_n = pltpu.make_async_copy(noise_ref, nz.at[col], loc.at[0])
    own_l = pltpu.make_async_copy(latent_ref, lt.at[z, core, xl], loc.at[1])
    own_n.start()
    own_l.start()

    barrier = pltpu.get_barrier_semaphore()
    for peer in peers:
        pl.semaphore_signal(barrier, inc=1, device_id=peer, device_id_type=MESH)
    cross[...] = jnp.zeros_like(cross)
    nsq[...] = jnp.zeros_like(nsq)
    lsq[...] = jnp.zeros_like(lsq)
    own_n.wait()
    own_l.wait()
    pl.semaphore_wait(barrier, len(peers))

    def rc(src, dst, ssem, rsem, dev):
        return pltpu.make_async_remote_copy(
            src_ref=src, dst_ref=dst, send_sem=ssem, recv_sem=rsem,
            device_id=dev, device_id_type=MESH,
        )

    def nsl(slot, h):
        return nz.at[slot, pl.ds(h * HALF, HALF), :]

    sent = []

    def nsend(slot, h, idx, dev):
        c = rc(nsl(slot, h), nsl(slot, h), n_send.at[idx], n_recv.at[idx], dev)
        c.start()
        sent.append(c)

    def nwait(slot, h, idx):
        rc(nsl(slot, h), nsl(slot, h), n_send.at[idx], n_recv.at[idx], y_up).wait_recv()

    def lsend(ref, idx, dev):
        c = rc(ref, ref, l_send.at[idx], l_recv.at[idx], dev)
        c.start()
        sent.append(c)

    def lwait(ref, idx):
        rc(ref, ref, l_send.at[idx], l_recv.at[idx], z_up).wait_recv()

    QUART = HALF // 2

    def quarter(slot, path, p):
        return nz.at[slot, pl.ds(path * HALF + p * QUART, QUART), :]

    def relay_start(path, p):
        c = rc(quarter(col, path, p), relay.at[path, p], h_send.at[0, path, p], h_recv.at[0, path, p],
               other_xl if path == 0 else diagonal)
        c.start()
        sent.append(c)

    def relay_forward(path, p):
        slot = col if path == 0 else flip_col
        dev = diagonal if path == 0 else other_xl
        rc(relay.at[path, p], relay.at[path, p], h_send.at[0, path, p], h_recv.at[0, path, p], dev).wait_recv()
        c = rc(relay.at[path, p], quarter(slot, path, p), h_send.at[1, path, p], h_recv.at[1, path, p], dev)
        c.start()
        sent.append(c)

    def relay_end(path):
        for p in range(2):
            ref = quarter(flip_col, path, p)
            rc(ref, ref, h_send.at[1, path, p], h_recv.at[1, path, p], diagonal).wait_recv()

    def slot_of(yy, s):
        return yy * 2 + (xh if s == 0 else 1 - xh)

    def forward_noise(s):
        dn, up = slot_of(ring_y(-1), s), slot_of(ring_y(1), s)
        nwait(dn, 0, 6 * s)
        nsend(dn, 0, 6 * s + 4, y_up)
        nwait(up, 1, 6 * s + 3)
        nsend(up, 1, 6 * s + 5, y_dn)

    own_pair = lt.at[z, core]
    lsend(lt.at[z, core, xl], 0, other_xl)
    relay_start(0, 0)
    relay_start(1, 0)
    nsend(col, 0, 0, y_up)
    nsend(col, 1, 3, y_dn)
    lsend(lt.at[z, core, xl], 1, z_up)
    lsend(lt.at[z, core, xl], 6, z_dn)
    relay_start(0, 1)
    relay_start(1, 1)
    nsend(col, 1, 1, y_up)
    nsend(col, 0, 2, y_dn)

    lwait(lt.at[z, core, 1 - xl], 0)
    lsend(lt.at[z, core, 1 - xl], 2, z_up)
    lsend(lt.at[z, core, 1 - xl], 7, z_dn)
    lsend(own_pair, 11, other_core)
    relay_forward(0, 0)
    relay_forward(1, 0)

    for sgn, base, dev in ((-1, 1, z_up), (1, 6, z_dn)):
        zz = ring_z(sgn)
        lwait(lt.at[zz, core, xl], base)
        lwait(lt.at[zz, core, 1 - xl], base + 1)
        lsend(lt.at[zz, core], base + 2, dev)
        lsend(lt.at[zz, core], 12 + (base == 6), other_core)

    relay_forward(0, 1)
    relay_forward(1, 1)
    forward_noise(0)

    for sgn, base, dev in ((-1, 1, z_up), (1, 6, z_dn)):
        zz = ring_z(2 * sgn)
        lwait(lt.at[zz, core], base + 2)
        lsend(lt.at[zz, core], base + 3, dev)
        lsend(lt.at[zz, core], 14 + (base == 6), other_core)

    relay_end(0)
    nsend(flip_col, 0, 6, y_up)
    nsend(flip_col, 0, 8, y_dn)
    relay_end(1)
    nsend(flip_col, 1, 9, y_dn)
    nsend(flip_col, 1, 7, y_up)

    for sgn, base, dev in ((-1, 1, z_up), (1, 6, z_dn)):
        zz = ring_z(3 * sgn)
        lwait(lt.at[zz, core], base + 3)
        lsend(lt.at[zz, core, int(base == 6)], base + 4, dev)
        lsend(lt.at[zz, core], 16 + (base == 6), other_core)
    far = ring_z(4)
    lwait(lt.at[far, core, 0], 5)
    lwait(lt.at[far, core, 1], 10)
    lsend(lt.at[far, core], 18, other_core)
    for j, d in enumerate((0, -1, 1, -2, 2, -3, 3, 4)):
        lwait(lt.at[ring_z(d), 1 - core], 11 + j)

    def accumulate(slot):
        a = nz[slot]
        b = jnp.concatenate([lt[slot, 0, 0], lt[slot, 1, 0], lt[slot, 0, 1], lt[slot, 1, 1]], axis=1)
        cross[...] += lax.dot_general(a, b, (((1,), (1,)), ((), ())), preferred_element_type=F32)
        a2 = jnp.square(a.astype(F32))
        nsq[...] += (a2[:, 0:128] + a2[:, 128:256]) + (a2[:, 256:384] + a2[:, 384:512])
        b2 = jnp.square(b.astype(F32))
        lsq[...] += (b2[:, 0:128] + b2[:, 128:256]) + (b2[:, 256:384] + b2[:, 384:512])

    def wait_rest(s):
        dn, up = slot_of(ring_y(-1), s), slot_of(ring_y(1), s)
        nwait(dn, 1, 6 * s + 1)
        nwait(up, 0, 6 * s + 2)

    def wait_far(s):
        fr = slot_of(ring_y(2), s)
        nwait(fr, 0, 6 * s + 4)
        nwait(fr, 1, 6 * s + 5)

    wait_rest(0)
    wait_far(0)

    def set0(k, carry):
        accumulate(((y + k) % Y) * 2 + xh)
        return carry

    lax.fori_loop(0, Y, set0, 0)
    forward_noise(1)
    wait_rest(1)

    def set1(k, carry):
        accumulate(((y + Y - 1 + k) % Y) * 2 + 1 - xh)
        return carry

    lax.fori_loop(0, 3, set1, 0)
    wait_far(1)
    accumulate(slot_of(ring_y(2), 1))

    for q in range(2):
        c = rc(
            nz.at[:, :, pl.ds(pl.multiple_of(q * 256 + (1 - core) * LANE, LANE), LANE)],
            no.at[:, :, pl.ds(q * LANE, LANE)],
            o_send.at[q], o_recv.at[q], other_core,
        )
        c.start()
        sent.append(c)

    eye = (
        lax.broadcasted_iota(jnp.int32, (LANE, LANE), 0)
        == lax.broadcasted_iota(jnp.int32, (LANE, LANE), 1)
    )

    def to_lanes(v):
        return jnp.sum(jnp.where(eye, v, 0.0), axis=0, keepdims=True)

    def to_rows(v):
        return jnp.sum(jnp.where(eye, v, 0.0), axis=1, keepdims=True)

    def wide(v):
        return jnp.concatenate([v[q:q + 1, :] for q in range(4)], axis=1)

    scale = 1.0 / (width * EPS)
    lq = jnp.concatenate(
        [to_lanes(jnp.sum(lsq[q * LANE:(q + 1) * LANE, :], axis=1, keepdims=True)) for q in range(4)],
        axis=1,
    )
    for b in range(4):
        rows = slice(b * LANE, (b + 1) * LANE)
        nq = jnp.sum(nsq[rows, :], axis=1, keepdims=True)
        cross[rows, :] = (nq + lq - 2.0 * cross[rows, :]) * scale

    def merge(top, total):
        best = jnp.max(top, axis=0)
        return best, jnp.sum(total * jnp.exp(top - best[None]), axis=0)

    def exchange(buf, mine, peers, ssem, rsem):
        for peer in peers:
            rc(buf.at[mine], buf.at[mine], ssem, rsem, peer).start()
        k = len(peers)
        rc(buf.at[pl.ds(0, k)], buf.at[pl.ds(0, k)], ssem, rsem, peers[0]).wait_recv()

    g = start_ref[...] * (1.0 / EPS)
    f = None
    f_rows = None
    for it in range(ITERS):
        gw = wide(g)
        for b in range(4):
            s = gw - cross[b * LANE:(b + 1) * LANE, :]
            top = jnp.max(s, axis=1, keepdims=True)
            tot = jnp.sum(jnp.exp(s - top), axis=1, keepdims=True)
            rowx[it, col, b:b + 1, :] = to_lanes(top)
            rowx[it, col, 4 + b:5 + b, :] = to_lanes(tot)
        exchange(rowx.at[it], col, col_peers, r_send.at[it], r_recv.at[it])
        top, tot = merge(rowx[it, :, 0:4, :], rowx[it, :, 4:8, :])
        f = -(math.log(m_total) + (top + jnp.log(tot)))
        f_rows = [to_rows(f[b:b + 1, :]) for b in range(4)]
        tops, tots = [], []
        for b in range(4):
            s = f_rows[b] - cross[b * LANE:(b + 1) * LANE, :]
            top = jnp.max(s, axis=0, keepdims=True)
            tops.append(top)
            tots.append(jnp.sum(jnp.exp(s - top), axis=0, keepdims=True))
        top = jnp.maximum(jnp.maximum(tops[0], tops[1]), jnp.maximum(tops[2], tops[3]))
        tot = sum(tots[b] * jnp.exp(tops[b] - top) for b in range(4))
        for q in range(4):
            col1[it, quad, q:q + 1, :] = top[:, q * LANE:(q + 1) * LANE]
            col1[it, quad, 4 + q:5 + q, :] = tot[:, q * LANE:(q + 1) * LANE]
        exchange(col1.at[it], quad, quad_peers, c1_send.at[it], c1_recv.at[it])
        top, tot = merge(col1[it, :, 0:4, :], col1[it, :, 4:8, :])
        col2[it, z, 0:4, :] = top
        col2[it, z, 4:8, :] = tot
        exchange(col2.at[it], z, z_peers, c2_send.at[it], c2_recv.at[it])
        top, tot = merge(col2[it, :, 0:4, :], col2[it, :, 4:8, :])
        g = -(math.log(n_total) + (top + jnp.log(tot)))

    npot_ref[...] = f * EPS
    lpot_ref[...] = g * EPS

    gw = wide(g)
    for b in range(4):
        rows = slice(b * LANE, (b + 1) * LANE)
        w = m_total * jnp.exp((f_rows[b] + gw) - cross[rows, :])
        wt[core, :, rows] = w.T.astype(BF16)
    wc = rc(wt.at[core], wt.at[core], w_send.at[0], w_recv.at[0], other_core)
    wc.start()
    sent.append(wc)
    for q in range(2):
        rc(no.at[:, :, pl.ds(q * LANE, LANE)], no.at[:, :, pl.ds(q * LANE, LANE)],
           o_send.at[q], o_recv.at[q], other_core).wait_recv()
    rc(wt.at[core], wt.at[1 - core], w_send.at[0], w_recv.at[0], other_core).wait_recv()

    def partial(rel):
        d = (z + rel) % Z
        mine = jnp.concatenate(
            [nz[d, :, pl.ds(pl.multiple_of(q * 256 + core * LANE, LANE), LANE)] for q in (1 - xl, xl)],
            axis=1,
        )
        theirs = jnp.concatenate(
            [no[d, :, pl.ds(pl.multiple_of(q * LANE, LANE), LANE)] for q in (1 - xl, xl)], axis=1
        )
        part[rel] = jnp.dot(wt[core], mine, preferred_element_type=F32) + jnp.dot(
            wt[1 - core], theirs, preferred_element_type=F32
        )

    def piece(buf, dr, s, k):
        if s == 4:
            return buf.at[dr, 0, k, pl.ds(dr * HALF, HALF), :]
        return buf.at[dr, 4 - s, k]

    def ring_copy(dr, s, k):
        return rc(
            piece(stage, dr, s, k), piece(land, dr, s, k),
            s_send.at[dr, 4 - s, k], s_recv.at[dr, 4 - s, k], z_dn if dr == 0 else z_up,
        )

    def ring_send(dr, s, k):
        c = ring_copy(dr, s, k)
        c.start()
        sent.append(c)

    partial(4)
    for k in range(2):
        for dr in range(2):
            half = slice(dr * HALF, (dr + 1) * HALF)
            stage[dr, 0, k, half, :] = part[4, half, k * LANE:(k + 1) * LANE].astype(BF16)
            ring_send(dr, 4, k)

    for s in (3, 2, 1):
        partial(Z - s)
        partial(s)
        for k in range(2):
            lanes = slice(k * LANE, (k + 1) * LANE)
            for dr in range(2):
                rel = Z - s if dr == 0 else s
                ring_copy(dr, s + 1, k).wait_recv()
                if s == 3:
                    half = slice(dr * HALF, (dr + 1) * HALF)
                    rest_rows = slice((1 - dr) * HALF, (2 - dr) * HALF)
                    stage[dr, 1, k, half, :] = (
                        part[rel, half, lanes] + land[dr, 0, k, half, :].astype(F32)
                    ).astype(BF16)
                    stage[dr, 1, k, rest_rows, :] = part[rel, rest_rows, lanes].astype(BF16)
                else:
                    stage[dr, 4 - s, k] = (
                        part[rel, :, lanes] + land[dr, 3 - s, k].astype(F32)
                    ).astype(BF16)
                ring_send(dr, s, k)

    def total(k):
        for dr in range(2):
            ring_copy(dr, 1, k).wait_recv()
        return part[0, :, k * LANE:(k + 1) * LANE] + (
            land[0, 3, k].astype(F32) + land[1, 3, k].astype(F32)
        )

    partial(0)
    xs[...] = total(0)
    xc = rc(xs, xr, x_send.at[0], x_recv.at[0], other_xl)
    xc.start()
    sent.append(xc)
    kept = total(1)
    xc.wait_recv()
    out_ref[...] = (kept + xr[...]).T

    for c in sent:
        c.wait_send()
    for it in range(ITERS):
        for buf, k, ssem, rsem in (
            (rowx, 7, r_send, r_recv), (col1, 3, c1_send, c1_recv), (col2, 7, c2_send, c2_recv)
        ):
            ref = buf.at[it, pl.ds(0, k)]
            rc(ref, ref, ssem.at[it], rsem.at[it], z_up).wait_send()


def per_device(n_total, m_total, noise_draw, latent_code, start_potential):
    anyspace = pl.BlockSpec(memory_space=pltpu.HBM)
    vmem = pl.BlockSpec(memory_space=pltpu.VMEM)
    width = 4096
    dma = pltpu.SemaphoreType.DMA

    def body(*refs):
        kernel(n_total, m_total, width, *refs)

    npot, lpot, out = pl.pallas_call(
        body,
        out_shape=(
            jax.ShapeDtypeStruct((4, LANE), F32),
            jax.ShapeDtypeStruct((4, LANE), F32),
            jax.ShapeDtypeStruct((LANE, BLK), F32),
        ),
        in_specs=[anyspace, anyspace, vmem],
        out_specs=(vmem, vmem, vmem),
        scratch_shapes=[
            pltpu.VMEM((8, BLK, BLK), BF16),
            pltpu.VMEM((Z, 2, 2, BLK, LANE), BF16),
            pltpu.VMEM((8, BLK, 2 * LANE), BF16),
            pltpu.VMEM((2, 2, BLK // 4, BLK), BF16),
            pltpu.VMEM((BLK, BLK), F32),
            pltpu.VMEM((BLK, LANE), F32),
            pltpu.VMEM((BLK, LANE), F32),
            pltpu.VMEM((2, BLK, BLK), BF16),
            pltpu.VMEM((8, BLK, 2 * LANE), F32),
            pltpu.VMEM((2, 4, 2, BLK, LANE), BF16),
            pltpu.VMEM((2, 4, 2, BLK, LANE), BF16),
            pltpu.VMEM((BLK, LANE), F32),
            pltpu.VMEM((BLK, LANE), F32),
            pltpu.VMEM((ITERS, 8, 8, LANE), F32),
            pltpu.VMEM((ITERS, 4, 8, LANE), F32),
            pltpu.VMEM((ITERS, 8, 8, LANE), F32),
            dma((12,)), dma((12,)),
            dma((2, 2, 2)), dma((2, 2, 2)),
            dma((19,)), dma((19,)),
            dma((2,)), dma((2,)),
            dma((1,)), dma((1,)),
            dma((ITERS,)), dma((ITERS,)),
            dma((ITERS,)), dma((ITERS,)),
            dma((ITERS,)), dma((ITERS,)),
            dma((2, 4, 2)), dma((2, 4, 2)),
            dma((1,)), dma((1,)),
            dma((2,)),
        ],
        compiler_params=pltpu.CompilerParams(
            collective_id=0, has_side_effects=True, vmem_limit_bytes=32 * 1024 * 1024
        ),
    )(noise_draw, latent_code, start_potential.reshape(4, LANE))
    return npot.reshape(BLK), lpot.reshape(BLK), out


def solution(mesh):
    in_specs = (P("row", "col"), P("col", "row"), P("col"))
    out_specs = (P("row"), P("col"), P("row", "col"))

    def whole(noise_draw, latent_code, start_potential):
        def block(a, b, c):
            return per_device(noise_draw.shape[0], latent_code.shape[0], a, b, c)

        return jax.shard_map(
            block, mesh=mesh, in_specs=in_specs, out_specs=out_specs, check_vma=False
        )(noise_draw, latent_code, start_potential)

    return whole
```

```python
import math

import jax
import jax.numpy as jnp
from jax import lax
from jax.experimental import pallas as pl
from jax.experimental.pallas import tpu as pltpu
from jax.sharding import PartitionSpec as P

ITERS = 3
EPS = 0.01
LOG2E = math.log2(math.e)
MESH = pl.DeviceIdType.MESH
F32 = jnp.float32
BF16 = jnp.bfloat16

Z, Y = 8, 4
LANE = 128
BLK = 512
HALF = BLK // 2


def kernel(
    n_total, m_total, width,
    noise_ref, latent_ref, start_ref,
    npot_ref, lpot_ref, out_ref,
    nz, lt, no, relay, cross, nsq, lsq, wt, part, stage, land, xs, xr, rowx, col1, col2,
    n_send, n_recv, h_send, h_recv, l_send, l_recv, o_send, o_recv, w_send, w_recv,
    r_send, r_recv, c1_send, c1_recv, c2_send, c2_recv, s_send, s_recv, x_send, x_recv, loc,
):
    row = lax.axis_index("row")
    col = lax.axis_index("col")
    z = row // 4
    xl = (row // 2) % 2
    core = row % 2
    y = col // 2
    xh = col % 2
    quad = row % 4

    def ring_z(d):
        return (z + d + Z) % Z

    def ring_y(d):
        return (y + d + Y) % Y

    other_core = (row + 1 - 2 * core, col)
    other_xl = (row + 2 - 4 * xl, col)
    flip_col = col + 1 - 2 * xh
    diagonal = (row + 2 - 4 * xl, flip_col)
    z_up = (ring_z(1) * 4 + quad, col)
    z_dn = (ring_z(-1) * 4 + quad, col)
    y_up = (row, ring_y(1) * 2 + xh)
    y_dn = (row, ring_y(-1) * 2 + xh)
    col_peers = [(row, (col + d) % 8) for d in range(1, 8)]
    quad_peers = [(z * 4 + (quad + d) % 4, col) for d in range(1, 4)]
    z_peers = [(ring_z(d) * 4 + quad, col) for d in range(1, 8)]

    peers = col_peers + quad_peers + z_peers + [diagonal]

    own_n = pltpu.make_async_copy(noise_ref, nz.at[col], loc.at[0])
    own_l = pltpu.make_async_copy(latent_ref, lt.at[z, core, xl], loc.at[1])
    own_n.start()
    own_l.start()

    barrier = pltpu.get_barrier_semaphore()
    for peer in peers:
        pl.semaphore_signal(barrier, inc=1, device_id=peer, device_id_type=MESH)
    cross[...] = jnp.zeros_like(cross)
    nsq[...] = jnp.zeros_like(nsq)
    lsq[...] = jnp.zeros_like(lsq)
    own_n.wait()
    own_l.wait()
    pl.semaphore_wait(barrier, len(peers))

    def rc(src, dst, ssem, rsem, dev):
        return pltpu.make_async_remote_copy(
            src_ref=src, dst_ref=dst, send_sem=ssem, recv_sem=rsem,
            device_id=dev, device_id_type=MESH,
        )

    def nsl(slot, h):
        return nz.at[slot, pl.ds(h * HALF, HALF), :]

    sent = []

    def nsend(slot, h, idx, dev):
        c = rc(nsl(slot, h), nsl(slot, h), n_send.at[idx], n_recv.at[idx], dev)
        c.start()
        sent.append(c)

    def nwait(slot, h, idx):
        rc(nsl(slot, h), nsl(slot, h), n_send.at[idx], n_recv.at[idx], y_up).wait_recv()

    def lsend(ref, idx, dev):
        c = rc(ref, ref, l_send.at[idx], l_recv.at[idx], dev)
        c.start()
        sent.append(c)

    def lwait(ref, idx):
        rc(ref, ref, l_send.at[idx], l_recv.at[idx], z_up).wait_recv()

    QUART = HALF // 2

    def quarter(slot, path, p):
        return nz.at[slot, pl.ds(path * HALF + p * QUART, QUART), :]

    def relay_start(path, p):
        c = rc(quarter(col, path, p), relay.at[path, p], h_send.at[0, path, p], h_recv.at[0, path, p],
               other_xl if path == 0 else diagonal)
        c.start()
        sent.append(c)

    def relay_forward(path, p):
        slot = col if path == 0 else flip_col
        dev = diagonal if path == 0 else other_xl
        rc(relay.at[path, p], relay.at[path, p], h_send.at[0, path, p], h_recv.at[0, path, p], dev).wait_recv()
        c = rc(relay.at[path, p], quarter(slot, path, p), h_send.at[1, path, p], h_recv.at[1, path, p], dev)
        c.start()
        sent.append(c)

    def relay_end(path):
        for p in range(2):
            ref = quarter(flip_col, path, p)
            rc(ref, ref, h_send.at[1, path, p], h_recv.at[1, path, p], diagonal).wait_recv()

    def slot_of(yy, s):
        return yy * 2 + (xh if s == 0 else 1 - xh)

    def forward_noise(s):
        dn, up = slot_of(ring_y(-1), s), slot_of(ring_y(1), s)
        nwait(dn, 0, 6 * s)
        nsend(dn, 0, 6 * s + 4, y_up)
        nwait(up, 1, 6 * s + 3)
        nsend(up, 1, 6 * s + 5, y_dn)

    own_pair = lt.at[z, core]
    lsend(lt.at[z, core, xl], 0, other_xl)
    relay_start(0, 0)
    relay_start(1, 0)
    nsend(col, 0, 0, y_up)
    nsend(col, 1, 3, y_dn)
    lsend(lt.at[z, core, xl], 1, z_up)
    lsend(lt.at[z, core, xl], 6, z_dn)
    relay_start(0, 1)
    relay_start(1, 1)
    nsend(col, 1, 1, y_up)
    nsend(col, 0, 2, y_dn)

    lwait(lt.at[z, core, 1 - xl], 0)
    lsend(lt.at[z, core, 1 - xl], 2, z_up)
    lsend(lt.at[z, core, 1 - xl], 7, z_dn)
    lsend(own_pair, 11, other_core)
    relay_forward(0, 0)
    relay_forward(1, 0)

    for sgn, base, dev in ((-1, 1, z_up), (1, 6, z_dn)):
        zz = ring_z(sgn)
        lwait(lt.at[zz, core, xl], base)
        lwait(lt.at[zz, core, 1 - xl], base + 1)
        lsend(lt.at[zz, core], base + 2, dev)
        lsend(lt.at[zz, core], 12 + (base == 6), other_core)

    relay_forward(0, 1)
    relay_forward(1, 1)
    forward_noise(0)

    for sgn, base, dev in ((-1, 1, z_up), (1, 6, z_dn)):
        zz = ring_z(2 * sgn)
        lwait(lt.at[zz, core], base + 2)
        lsend(lt.at[zz, core], base + 3, dev)
        lsend(lt.at[zz, core], 14 + (base == 6), other_core)

    relay_end(0)
    nsend(flip_col, 0, 6, y_up)
    nsend(flip_col, 0, 8, y_dn)
    relay_end(1)
    nsend(flip_col, 1, 9, y_dn)
    nsend(flip_col, 1, 7, y_up)

    for sgn, base, dev in ((-1, 1, z_up), (1, 6, z_dn)):
        zz = ring_z(3 * sgn)
        lwait(lt.at[zz, core], base + 3)
        lsend(lt.at[zz, core, int(base == 6)], base + 4, dev)
        lsend(lt.at[zz, core], 16 + (base == 6), other_core)
    far = ring_z(4)
    lwait(lt.at[far, core, 0], 5)
    lwait(lt.at[far, core, 1], 10)
    lsend(lt.at[far, core], 18, other_core)
    for j, d in enumerate((0, -1, 1, -2, 2, -3, 3, 4)):
        lwait(lt.at[ring_z(d), 1 - core], 11 + j)

    def accumulate(slot):
        a = nz[slot]
        b = jnp.concatenate([lt[slot, 0, 0], lt[slot, 1, 0], lt[slot, 0, 1], lt[slot, 1, 1]], axis=1)
        cross[...] += lax.dot_general(a, b, (((1,), (1,)), ((), ())), preferred_element_type=F32)
        a2 = jnp.square(a.astype(F32))
        nsq[...] += (a2[:, 0:128] + a2[:, 128:256]) + (a2[:, 256:384] + a2[:, 384:512])
        b2 = jnp.square(b.astype(F32))
        lsq[...] += (b2[:, 0:128] + b2[:, 128:256]) + (b2[:, 256:384] + b2[:, 384:512])

    def wait_rest(s):
        dn, up = slot_of(ring_y(-1), s), slot_of(ring_y(1), s)
        nwait(dn, 1, 6 * s + 1)
        nwait(up, 0, 6 * s + 2)

    def wait_far(s):
        fr = slot_of(ring_y(2), s)
        nwait(fr, 0, 6 * s + 4)
        nwait(fr, 1, 6 * s + 5)

    wait_rest(0)
    wait_far(0)

    def set0(k, carry):
        accumulate(((y + k) % Y) * 2 + xh)
        return carry

    lax.fori_loop(0, Y, set0, 0)
    forward_noise(1)
    wait_rest(1)

    def set1(k, carry):
        accumulate(((y + Y - 1 + k) % Y) * 2 + 1 - xh)
        return carry

    lax.fori_loop(0, 3, set1, 0)
    wait_far(1)
    accumulate(slot_of(ring_y(2), 1))

    for q in range(2):
        c = rc(
            nz.at[:, :, pl.ds(pl.multiple_of(q * 256 + (1 - core) * LANE, LANE), LANE)],
            no.at[:, :, pl.ds(q * LANE, LANE)],
            o_send.at[q], o_recv.at[q], other_core,
        )
        c.start()
        sent.append(c)

    eye = (
        lax.broadcasted_iota(jnp.int32, (LANE, LANE), 0)
        == lax.broadcasted_iota(jnp.int32, (LANE, LANE), 1)
    )

    def to_lanes(v):
        return jnp.sum(jnp.where(eye, v, 0.0), axis=0, keepdims=True)

    def to_rows(v):
        return jnp.sum(jnp.where(eye, v, 0.0), axis=1, keepdims=True)

    def wide(v):
        return jnp.concatenate([v[q:q + 1, :] for q in range(4)], axis=1)

    scale = LOG2E / (width * EPS)
    lq = jnp.concatenate(
        [to_lanes(jnp.sum(lsq[q * LANE:(q + 1) * LANE, :], axis=1, keepdims=True)) for q in range(4)],
        axis=1,
    )
    for b in range(4):
        rows = slice(b * LANE, (b + 1) * LANE)
        nq = jnp.sum(nsq[rows, :], axis=1, keepdims=True)
        cross[rows, :] = (nq + lq - 2.0 * cross[rows, :]) * scale

    def merge(parts):
        best = jnp.max(parts, axis=0)
        return best + jnp.log2(jnp.sum(jnp.exp2(parts - best[None]), axis=0))

    def exchange(buf, mine, peers, ssem, rsem):
        for peer in peers:
            rc(buf.at[mine], buf.at[mine], ssem, rsem, peer).start()
        k = len(peers)
        rc(buf.at[pl.ds(0, k)], buf.at[pl.ds(0, k)], ssem, rsem, peers[0]).wait_recv()

    g = start_ref[...] * (LOG2E / EPS)
    f = None
    f_rows = None
    for it in range(ITERS):
        gw = wide(g)
        for b in range(4):
            s = gw - cross[b * LANE:(b + 1) * LANE, :]
            top = jnp.max(s, axis=1, keepdims=True)
            tot = jnp.sum(jnp.exp2(s - top), axis=1, keepdims=True)
            rowx[it, col, b:b + 1, :] = to_lanes(top) + jnp.log2(to_lanes(tot))
        exchange(rowx.at[it], col, col_peers, r_send.at[it], r_recv.at[it])
        f = -(math.log2(m_total) + merge(rowx[it]))
        f_rows = [to_rows(f[b:b + 1, :]) for b in range(4)]
        tops, tots = [], []
        for b in range(4):
            s = f_rows[b] - cross[b * LANE:(b + 1) * LANE, :]
            top = jnp.max(s, axis=0, keepdims=True)
            tops.append(top)
            tots.append(jnp.sum(jnp.exp2(s - top), axis=0, keepdims=True))
        top = jnp.maximum(jnp.maximum(tops[0], tops[1]), jnp.maximum(tops[2], tops[3]))
        own = top + jnp.log2(sum(tots[b] * jnp.exp2(tops[b] - top) for b in range(4)))
        for q in range(4):
            col1[it, quad, q:q + 1, :] = own[:, q * LANE:(q + 1) * LANE]
        exchange(col1.at[it], quad, quad_peers, c1_send.at[it], c1_recv.at[it])
        col2[it, z] = merge(col1[it])
        exchange(col2.at[it], z, z_peers, c2_send.at[it], c2_recv.at[it])
        g = -(math.log2(n_total) + merge(col2[it]))

    npot_ref[...] = f * (EPS / LOG2E)
    lpot_ref[...] = g * (EPS / LOG2E)

    gw = wide(g)
    for b in range(4):
        rows = slice(b * LANE, (b + 1) * LANE)
        w = m_total * jnp.exp2((f_rows[b] + gw) - cross[rows, :])
        wt[core, :, rows] = w.T.astype(BF16)
    wc = rc(wt.at[core], wt.at[core], w_send.at[0], w_recv.at[0], other_core)
    wc.start()
    sent.append(wc)
    for q in range(2):
        rc(no.at[:, :, pl.ds(q * LANE, LANE)], no.at[:, :, pl.ds(q * LANE, LANE)],
           o_send.at[q], o_recv.at[q], other_core).wait_recv()
    rc(wt.at[core], wt.at[1 - core], w_send.at[0], w_recv.at[0], other_core).wait_recv()

    def partial(rel):
        d = (z + rel) % Z
        mine = jnp.concatenate(
            [nz[d, :, pl.ds(pl.multiple_of(q * 256 + core * LANE, LANE), LANE)] for q in (1 - xl, xl)],
            axis=1,
        )
        theirs = jnp.concatenate(
            [no[d, :, pl.ds(pl.multiple_of(q * LANE, LANE), LANE)] for q in (1 - xl, xl)], axis=1
        )
        part[rel] = jnp.dot(wt[core], mine, preferred_element_type=F32) + jnp.dot(
            wt[1 - core], theirs, preferred_element_type=F32
        )

    def piece(buf, dr, s, k):
        if s == 4:
            return buf.at[dr, 0, k, pl.ds(dr * HALF, HALF), :]
        return buf.at[dr, 4 - s, k]

    def ring_copy(dr, s, k):
        return rc(
            piece(stage, dr, s, k), piece(land, dr, s, k),
            s_send.at[dr, 4 - s, k], s_recv.at[dr, 4 - s, k], z_dn if dr == 0 else z_up,
        )

    def ring_send(dr, s, k):
        c = ring_copy(dr, s, k)
        c.start()
        sent.append(c)

    partial(4)
    for k in range(2):
        for dr in range(2):
            half = slice(dr * HALF, (dr + 1) * HALF)
            stage[dr, 0, k, half, :] = part[4, half, k * LANE:(k + 1) * LANE].astype(BF16)
            ring_send(dr, 4, k)

    for s in (3, 2, 1):
        partial(Z - s)
        partial(s)
        for k in range(2):
            lanes = slice(k * LANE, (k + 1) * LANE)
            for dr in range(2):
                rel = Z - s if dr == 0 else s
                ring_copy(dr, s + 1, k).wait_recv()
                if s == 3:
                    half = slice(dr * HALF, (dr + 1) * HALF)
                    rest_rows = slice((1 - dr) * HALF, (2 - dr) * HALF)
                    stage[dr, 1, k, half, :] = (
                        part[rel, half, lanes] + land[dr, 0, k, half, :].astype(F32)
                    ).astype(BF16)
                    stage[dr, 1, k, rest_rows, :] = part[rel, rest_rows, lanes].astype(BF16)
                else:
                    stage[dr, 4 - s, k] = (
                        part[rel, :, lanes] + land[dr, 3 - s, k].astype(F32)
                    ).astype(BF16)
                ring_send(dr, s, k)

    def total(k):
        for dr in range(2):
            ring_copy(dr, 1, k).wait_recv()
        return part[0, :, k * LANE:(k + 1) * LANE] + (
            land[0, 3, k].astype(F32) + land[1, 3, k].astype(F32)
        )

    partial(0)
    xs[...] = total(0)
    xc = rc(xs, xr, x_send.at[0], x_recv.at[0], other_xl)
    xc.start()
    sent.append(xc)
    kept = total(1)
    xc.wait_recv()
    out_ref[...] = (kept + xr[...]).T

    for c in sent:
        c.wait_send()
    for it in range(ITERS):
        for buf, k, ssem, rsem in (
            (rowx, 7, r_send, r_recv), (col1, 3, c1_send, c1_recv), (col2, 7, c2_send, c2_recv)
        ):
            ref = buf.at[it, pl.ds(0, k)]
            rc(ref, ref, ssem.at[it], rsem.at[it], z_up).wait_send()


def per_device(n_total, m_total, noise_draw, latent_code, start_potential):
    anyspace = pl.BlockSpec(memory_space=pltpu.HBM)
    vmem = pl.BlockSpec(memory_space=pltpu.VMEM)
    width = 4096
    dma = pltpu.SemaphoreType.DMA

    def body(*refs):
        kernel(n_total, m_total, width, *refs)

    npot, lpot, out = pl.pallas_call(
        body,
        out_shape=(
            jax.ShapeDtypeStruct((4, LANE), F32),
            jax.ShapeDtypeStruct((4, LANE), F32),
            jax.ShapeDtypeStruct((LANE, BLK), F32),
        ),
        in_specs=[anyspace, anyspace, vmem],
        out_specs=(vmem, vmem, vmem),
        scratch_shapes=[
            pltpu.VMEM((8, BLK, BLK), BF16),
            pltpu.VMEM((Z, 2, 2, BLK, LANE), BF16),
            pltpu.VMEM((8, BLK, 2 * LANE), BF16),
            pltpu.VMEM((2, 2, BLK // 4, BLK), BF16),
            pltpu.VMEM((BLK, BLK), F32),
            pltpu.VMEM((BLK, LANE), F32),
            pltpu.VMEM((BLK, LANE), F32),
            pltpu.VMEM((2, BLK, BLK), BF16),
            pltpu.VMEM((8, BLK, 2 * LANE), F32),
            pltpu.VMEM((2, 4, 2, BLK, LANE), BF16),
            pltpu.VMEM((2, 4, 2, BLK, LANE), BF16),
            pltpu.VMEM((BLK, LANE), F32),
            pltpu.VMEM((BLK, LANE), F32),
            pltpu.VMEM((ITERS, 8, 4, LANE), F32),
            pltpu.VMEM((ITERS, 4, 4, LANE), F32),
            pltpu.VMEM((ITERS, 8, 4, LANE), F32),
            dma((12,)), dma((12,)),
            dma((2, 2, 2)), dma((2, 2, 2)),
            dma((19,)), dma((19,)),
            dma((2,)), dma((2,)),
            dma((1,)), dma((1,)),
            dma((ITERS,)), dma((ITERS,)),
            dma((ITERS,)), dma((ITERS,)),
            dma((ITERS,)), dma((ITERS,)),
            dma((2, 4, 2)), dma((2, 4, 2)),
            dma((1,)), dma((1,)),
            dma((2,)),
        ],
        compiler_params=pltpu.CompilerParams(
            collective_id=0, has_side_effects=True, vmem_limit_bytes=32 * 1024 * 1024
        ),
    )(noise_draw, latent_code, start_potential.reshape(4, LANE))
    return npot.reshape(BLK), lpot.reshape(BLK), out


def solution(mesh):
    in_specs = (P("row", "col"), P("col", "row"), P("col"))
    out_specs = (P("row"), P("col"), P("row", "col"))

    def whole(noise_draw, latent_code, start_potential):
        def block(a, b, c):
            return per_device(noise_draw.shape[0], latent_code.shape[0], a, b, c)

        return jax.shard_map(
            block, mesh=mesh, in_specs=in_specs, out_specs=out_specs, check_vma=False
        )(noise_draw, latent_code, start_potential)

    return whole
```

```python
import math

import jax
import jax.numpy as jnp
from jax import lax
from jax.experimental import pallas as pl
from jax.experimental.pallas import tpu as pltpu
from jax.sharding import PartitionSpec as P

ITERS = 3
EPS = 0.01
LOG2E = math.log2(math.e)
MESH = pl.DeviceIdType.MESH
F32 = jnp.float32
BF16 = jnp.bfloat16

Z, Y = 8, 4
LANE = 128
BLK = 512
HALF = BLK // 2


def kernel(
    n_total, m_total, width,
    noise_ref, latent_ref, start_ref,
    npot_ref, lpot_ref, out_ref,
    nz, lt, no, relay, cross, nsq, lsq, wt, wx, nx, part, parth, stage, land, stageh, landh, xs, xr, rowx, col1, col2,
    n_send, n_recv, h_send, h_recv, l_send, l_recv, o_send, o_recv, w_send, w_recv,
    p_send, p_recv, r_send, r_recv, c1_send, c1_recv, c2_send, c2_recv,
    s_send, s_recv, t_send, t_recv, x_send, x_recv, loc,
):
    row = lax.axis_index("row")
    col = lax.axis_index("col")
    z = row // 4
    xl = (row // 2) % 2
    core = row % 2
    y = col // 2
    xh = col % 2
    quad = row % 4

    def ring_z(d):
        return (z + d + Z) % Z

    def ring_y(d):
        return (y + d + Y) % Y

    other_core = (row + 1 - 2 * core, col)
    other_xl = (row + 2 - 4 * xl, col)
    flip_col = col + 1 - 2 * xh
    diagonal = (row + 2 - 4 * xl, flip_col)
    z_up = (ring_z(1) * 4 + quad, col)
    z_dn = (ring_z(-1) * 4 + quad, col)
    y_up = (row, ring_y(1) * 2 + xh)
    y_dn = (row, ring_y(-1) * 2 + xh)
    col_peers = [
        (row, ring_y(dy) * 2 + (1 - xh if dx else xh))
        for dy, dx in ((2, 1), (1, 1), (-1, 1), (2, 0), (0, 1), (1, 0), (-1, 0))
    ]
    across = (row + 2 - 4 * xl) // 2 * 2
    quad_peers = [(across + 1 - core, col), (across + core, col), other_core]
    z_peers = [(ring_z(d) * 4 + quad, col) for d in (4, 3, -3, 2, -2, 1, -1)]
    peers = col_peers + quad_peers + z_peers + [(across, flip_col), (across + 1, flip_col)]

    own_n = pltpu.make_async_copy(noise_ref, nz.at[col], loc.at[0])
    own_l = pltpu.make_async_copy(latent_ref, lt.at[z, core, xl], loc.at[1])
    own_n.start()
    own_l.start()

    barrier = pltpu.get_barrier_semaphore()
    for peer in peers:
        pl.semaphore_signal(barrier, inc=1, device_id=peer, device_id_type=MESH)
    cross[...] = jnp.zeros_like(cross)
    nsq[...] = jnp.zeros_like(nsq)
    lsq[...] = jnp.zeros_like(lsq)
    own_n.wait()
    own_l.wait()
    pl.semaphore_wait(barrier, len(peers))

    def rc(src, dst, ssem, rsem, dev):
        return pltpu.make_async_remote_copy(
            src_ref=src, dst_ref=dst, send_sem=ssem, recv_sem=rsem,
            device_id=dev, device_id_type=MESH,
        )

    def nsl(slot, h):
        return nz.at[slot, pl.ds(h * HALF, HALF), :]

    sent = []

    def nsend(slot, h, idx, dev):
        c = rc(nsl(slot, h), nsl(slot, h), n_send.at[idx], n_recv.at[idx], dev)
        c.start()
        sent.append(c)

    def nwait(slot, h, idx):
        rc(nsl(slot, h), nsl(slot, h), n_send.at[idx], n_recv.at[idx], y_up).wait_recv()

    def lsend(ref, idx, dev):
        c = rc(ref, ref, l_send.at[idx], l_recv.at[idx], dev)
        c.start()
        sent.append(c)

    def lwait(ref, idx):
        rc(ref, ref, l_send.at[idx], l_recv.at[idx], z_up).wait_recv()

    QUART = HALF // 2

    def quarter(slot, path, p):
        return nz.at[slot, pl.ds(path * HALF + p * QUART, QUART), :]

    def relay_start(path, p):
        c = rc(quarter(col, path, p), relay.at[path, p], h_send.at[0, path, p], h_recv.at[0, path, p],
               other_xl if path == 0 else diagonal)
        c.start()
        sent.append(c)

    def relay_forward(path, p):
        slot = col if path == 0 else flip_col
        dev = diagonal if path == 0 else other_xl
        rc(relay.at[path, p], relay.at[path, p], h_send.at[0, path, p], h_recv.at[0, path, p], dev).wait_recv()
        c = rc(relay.at[path, p], quarter(slot, path, p), h_send.at[1, path, p], h_recv.at[1, path, p], dev)
        c.start()
        sent.append(c)

    def relay_end(path):
        for p in range(2):
            ref = quarter(flip_col, path, p)
            rc(ref, ref, h_send.at[1, path, p], h_recv.at[1, path, p], diagonal).wait_recv()

    def slot_of(yy, s):
        return yy * 2 + (xh if s == 0 else 1 - xh)

    def forward_noise(s):
        dn, up = slot_of(ring_y(-1), s), slot_of(ring_y(1), s)
        nwait(dn, 0, 6 * s)
        nsend(dn, 0, 6 * s + 4, y_up)
        nwait(up, 1, 6 * s + 3)
        nsend(up, 1, 6 * s + 5, y_dn)

    own_pair = lt.at[z, core]
    lsend(lt.at[z, core, xl], 0, other_xl)
    relay_start(0, 0)
    relay_start(1, 0)
    nsend(col, 0, 0, y_up)
    nsend(col, 1, 3, y_dn)
    lsend(lt.at[z, core, xl], 1, z_up)
    lsend(lt.at[z, core, xl], 6, z_dn)
    relay_start(0, 1)
    relay_start(1, 1)
    nsend(col, 1, 1, y_up)
    nsend(col, 0, 2, y_dn)

    lwait(lt.at[z, core, 1 - xl], 0)
    lsend(lt.at[z, core, 1 - xl], 2, z_up)
    lsend(lt.at[z, core, 1 - xl], 7, z_dn)
    lsend(own_pair, 11, other_core)
    relay_forward(0, 0)
    relay_forward(1, 0)

    for sgn, base, dev in ((-1, 1, z_up), (1, 6, z_dn)):
        zz = ring_z(sgn)
        lwait(lt.at[zz, core, xl], base)
        lwait(lt.at[zz, core, 1 - xl], base + 1)
        lsend(lt.at[zz, core], base + 2, dev)
        lsend(lt.at[zz, core], 12 + (base == 6), other_core)

    relay_forward(0, 1)
    relay_forward(1, 1)
    forward_noise(0)

    for sgn, base, dev in ((-1, 1, z_up), (1, 6, z_dn)):
        zz = ring_z(2 * sgn)
        lwait(lt.at[zz, core], base + 2)
        lsend(lt.at[zz, core], base + 3, dev)
        lsend(lt.at[zz, core], 14 + (base == 6), other_core)

    relay_end(0)
    nsend(flip_col, 0, 6, y_up)
    nsend(flip_col, 0, 8, y_dn)
    relay_end(1)
    nsend(flip_col, 1, 9, y_dn)
    nsend(flip_col, 1, 7, y_up)

    for sgn, base, dev in ((-1, 1, z_up), (1, 6, z_dn)):
        zz = ring_z(3 * sgn)
        lwait(lt.at[zz, core], base + 3)
        lsend(lt.at[zz, core, int(base == 6)], base + 4, dev)
        lsend(lt.at[zz, core], 16 + (base == 6), other_core)
    far = ring_z(4)
    lwait(lt.at[far, core, 0], 5)
    lwait(lt.at[far, core, 1], 10)
    lsend(lt.at[far, core], 18, other_core)
    for j, d in enumerate((0, -1, 1, -2, 2, -3, 3, 4)):
        lwait(lt.at[ring_z(d), 1 - core], 11 + j)

    def accumulate(slot):
        a = nz[slot]
        b = jnp.concatenate([lt[slot, 0, 0], lt[slot, 1, 0], lt[slot, 0, 1], lt[slot, 1, 1]], axis=1)
        cross[...] += lax.dot_general(a, b, (((1,), (1,)), ((), ())), preferred_element_type=F32)
        a2 = jnp.square(a.astype(F32))
        nsq[...] += (a2[:, 0:128] + a2[:, 128:256]) + (a2[:, 256:384] + a2[:, 384:512])
        b2 = jnp.square(b.astype(F32))
        lsq[...] += (b2[:, 0:128] + b2[:, 128:256]) + (b2[:, 256:384] + b2[:, 384:512])

    def wait_rest(s):
        dn, up = slot_of(ring_y(-1), s), slot_of(ring_y(1), s)
        nwait(dn, 1, 6 * s + 1)
        nwait(up, 0, 6 * s + 2)

    def wait_far(s):
        fr = slot_of(ring_y(2), s)
        nwait(fr, 0, 6 * s + 4)
        nwait(fr, 1, 6 * s + 5)

    wait_rest(0)
    wait_far(0)

    def set0(k, carry):
        accumulate(((y + k) % Y) * 2 + xh)
        return carry

    lax.fori_loop(0, Y, set0, 0)
    forward_noise(1)
    wait_rest(1)

    def set1(k, carry):
        accumulate(((y + Y - 1 + k) % Y) * 2 + 1 - xh)
        return carry

    lax.fori_loop(0, 3, set1, 0)
    wait_far(1)
    accumulate(slot_of(ring_y(2), 1))

    for q in range(2):
        c = rc(
            nz.at[:, :, pl.ds(pl.multiple_of(q * 256 + (1 - core) * LANE, LANE), LANE)],
            no.at[:, :, pl.ds(q * LANE, LANE)],
            o_send.at[q], o_recv.at[q], other_core,
        )
        c.start()
        sent.append(c)

    eye = (
        lax.broadcasted_iota(jnp.int32, (LANE, LANE), 0)
        == lax.broadcasted_iota(jnp.int32, (LANE, LANE), 1)
    )

    def to_lanes(v):
        return jnp.sum(jnp.where(eye, v, 0.0), axis=0, keepdims=True)

    def to_rows(v):
        return jnp.sum(jnp.where(eye, v, 0.0), axis=1, keepdims=True)

    def wide(v):
        return jnp.concatenate([v[q:q + 1, :] for q in range(4)], axis=1)

    scale = LOG2E / (width * EPS)
    lq = jnp.concatenate(
        [to_lanes(jnp.sum(lsq[q * LANE:(q + 1) * LANE, :], axis=1, keepdims=True)) for q in range(4)],
        axis=1,
    )
    for b in range(4):
        rows = slice(b * LANE, (b + 1) * LANE)
        nq = jnp.sum(nsq[rows, :], axis=1, keepdims=True)
        cross[rows, :] = (nq + lq - 2.0 * cross[rows, :]) * scale

    def merge(parts):
        best = jnp.max(parts, axis=0)
        return best + jnp.log2(jnp.sum(jnp.exp2(parts - best[None]), axis=0))

    def lend(step):
        k, zz = step % 2, step // 2
        lanes = pl.ds(pl.multiple_of((1 - xl) * 256 + k * LANE, LANE), LANE)
        for slot, dev in ((zz, (across + k, col)), (zz + 4, (across + k, flip_col))):
            c = rc(nz.at[slot, :, lanes], nx.at[core, slot], p_send.at[k, slot], p_recv.at[core, slot], dev)
            c.start()
            sent.append(c)

    steps = iter(range(9))

    def exchange(buf, mine, peers, ssem, rsem):
        for peer in peers:
            rc(buf.at[mine], buf.at[mine], ssem, rsem, peer).start()
        step = next(steps)
        if step < 8:
            lend(step)
        k = len(peers)
        rc(buf.at[pl.ds(0, k)], buf.at[pl.ds(0, k)], ssem, rsem, peers[0]).wait_recv()

    g = start_ref[...] * (LOG2E / EPS)
    f = None
    f_rows = None
    for it in range(ITERS):
        gw = wide(g)
        for b in range(4):
            s = gw - cross[b * LANE:(b + 1) * LANE, :]
            top = jnp.max(s, axis=1, keepdims=True)
            tot = jnp.sum(jnp.exp2(s - top), axis=1, keepdims=True)
            rowx[it, col, b:b + 1, :] = to_lanes(top) + jnp.log2(to_lanes(tot))
        exchange(rowx.at[it], col, col_peers, r_send.at[it], r_recv.at[it])
        f = -(math.log2(m_total) + merge(rowx[it]))
        f_rows = [to_rows(f[b:b + 1, :]) for b in range(4)]
        tops, tots = [], []
        for b in range(4):
            s = f_rows[b] - cross[b * LANE:(b + 1) * LANE, :]
            top = jnp.max(s, axis=0, keepdims=True)
            tops.append(top)
            tots.append(jnp.sum(jnp.exp2(s - top), axis=0, keepdims=True))
        top = jnp.maximum(jnp.maximum(tops[0], tops[1]), jnp.maximum(tops[2], tops[3]))
        own = top + jnp.log2(sum(tots[b] * jnp.exp2(tops[b] - top) for b in range(4)))
        for q in range(4):
            col1[it, quad, q:q + 1, :] = own[:, q * LANE:(q + 1) * LANE]
        exchange(col1.at[it], quad, quad_peers, c1_send.at[it], c1_recv.at[it])
        col2[it, z] = merge(col1[it])
        exchange(col2.at[it], z, z_peers, c2_send.at[it], c2_recv.at[it])
        g = -(math.log2(n_total) + merge(col2[it]))

    npot_ref[...] = f * (EPS / LOG2E)
    lpot_ref[...] = g * (EPS / LOG2E)

    LOW, HIGH = slice(0, HALF), slice(HALF, BLK)
    gw = wide(g)

    def weights(cols):
        for b in range(4):
            rows = slice(b * LANE, (b + 1) * LANE)
            w = m_total * jnp.exp2((f_rows[b] + gw[:, cols]) - cross[rows, cols])
            wt[core, cols, rows] = w.T.astype(BF16)

    def wcopy(j, src, dst, dev):
        return rc(src, dst, w_send.at[j], w_recv.at[j], dev)

    low, high = pl.ds(0, HALF), pl.ds(HALF, HALF)
    copies = []
    weights(HIGH)
    copies.append(wcopy(0, wt.at[core, high], wx.at[core], other_xl))
    copies[-1].start()
    weights(LOW)
    copies.append(wcopy(1, wt.at[core, low], wt.at[core, low], other_core))
    copies[-1].start()
    copies.append(wcopy(2, wt.at[core, high], wt.at[core, high], other_core))
    copies[-1].start()
    for q in range(2):
        rc(no.at[:, :, pl.ds(q * LANE, LANE)], no.at[:, :, pl.ds(q * LANE, LANE)],
           o_send.at[q], o_recv.at[q], other_core).wait_recv()
    wcopy(1, wt.at[core, low], wt.at[1 - core, low], other_core).wait_recv()

    def mine(d, q):
        return nz[d, :, pl.ds(pl.multiple_of(q * 256 + core * LANE, LANE), LANE)]

    def theirs(d, q):
        return no[d, :, pl.ds(pl.multiple_of(q * LANE, LANE), LANE)]

    def partial(rel):
        d = (z + rel) % Z
        part[rel] = jnp.dot(
            wt[core, LOW, :], jnp.concatenate([mine(d, q) for q in (1 - xl, xl)], axis=1),
            preferred_element_type=F32,
        ) + jnp.dot(
            wt[1 - core, LOW, :], jnp.concatenate([theirs(d, q) for q in (1 - xl, xl)], axis=1),
            preferred_element_type=F32,
        )

    def partial_high(rel):
        d = (z + rel) % Z
        parth[rel] = (
            jnp.dot(wt[core, HIGH, :], mine(d, xl), preferred_element_type=F32)
            + jnp.dot(wt[1 - core, HIGH, :], theirs(d, xl), preferred_element_type=F32)
        ) + (
            jnp.dot(wx[0], nx[0, d], preferred_element_type=F32)
            + jnp.dot(wx[1], nx[1, d], preferred_element_type=F32)
        )

    def piece(k, bufs, dr, s):
        ref = bufs[1].at[dr, 4 - s] if k == 2 else bufs[0].at[dr, 4 - s, k]
        return ref.at[pl.ds(dr * LANE, LANE)] if s == 4 else ref

    def ring_copy(k, dr, s):
        ss, rs = (t_send.at[dr, 4 - s], t_recv.at[dr, 4 - s]) if k == 2 else (
            s_send.at[dr, 4 - s, k], s_recv.at[dr, 4 - s, k])
        return rc(
            piece(k, (stage, stageh), dr, s), piece(k, (land, landh), dr, s), ss, rs,
            z_dn if dr == 0 else z_up,
        )

    def own_part(k, rel, rows):
        return parth[rel, rows, :] if k == 2 else part[rel, rows, k * LANE:(k + 1) * LANE]

    def got(k, dr, s, rows):
        v = landh[dr, 4 - s, rows, :] if k == 2 else land[dr, 4 - s, k, rows, :]
        return v.astype(F32)

    def put(k, dr, s, rows, v):
        if k == 2:
            stageh[dr, 4 - s, rows, :] = v.astype(BF16)
        else:
            stage[dr, 4 - s, k, rows, :] = v.astype(BF16)

    ALL = slice(0, HALF)

    def ring_step(k, s):
        for dr in range(2):
            rel = Z - s if dr == 0 else s
            first = slice(dr * LANE, (dr + 1) * LANE)
            other = slice((1 - dr) * LANE, (2 - dr) * LANE)
            if s == 4:
                put(k, dr, s, first, own_part(k, 4, first))
            else:
                ring_copy(k, dr, s + 1).wait_recv()
                if s == 3:
                    put(k, dr, s, first, own_part(k, rel, first) + got(k, dr, 4, first))
                    put(k, dr, s, other, own_part(k, rel, other))
                else:
                    put(k, dr, s, ALL, own_part(k, rel, ALL) + got(k, dr, s + 1, ALL))
            c = ring_copy(k, dr, s)
            c.start()
            sent.append(c)

    def total(k):
        for dr in range(2):
            ring_copy(k, dr, 1).wait_recv()
        return own_part(k, 0, ALL) + (got(k, 0, 1, ALL) + got(k, 1, 1, ALL))

    partial(4)
    ring_step(0, 4)
    ring_step(1, 4)
    partial(5)
    partial(3)
    ring_step(0, 3)
    ring_step(1, 3)
    partial(6)
    partial(2)
    ring_step(0, 2)
    ring_step(1, 2)
    wcopy(0, wt.at[core, high], wx.at[core], other_xl).wait_recv()
    copies.append(wcopy(3, wx.at[core], wx.at[core], other_core))
    copies[-1].start()
    partial(7)
    partial(1)
    wcopy(2, wt.at[core, high], wt.at[1 - core, high], other_core).wait_recv()
    for c in range(2):
        for slot in range(Z):
            rc(nx.at[c, slot], nx.at[c, slot], p_send.at[0, slot], p_recv.at[c, slot], other_xl).wait_recv()
    wcopy(3, wx.at[core], wx.at[1 - core], other_core).wait_recv()
    partial_high(4)
    ring_step(2, 4)
    ring_step(0, 1)
    ring_step(1, 1)
    partial_high(5)
    partial_high(3)
    ring_step(2, 3)
    partial_high(6)
    partial_high(2)
    ring_step(2, 2)
    partial(0)
    xs[...] = total(0)
    xc = rc(xs, xr, x_send.at[0], x_recv.at[0], other_xl)
    xc.start()
    copies.append(xc)
    partial_high(7)
    partial_high(1)
    ring_step(2, 1)
    partial_high(0)
    kept = total(1)
    xc.wait_recv()
    out_ref[:, LOW] = (kept + xr[...]).T
    out_ref[:, HIGH] = total(2).T
    sent.extend(copies)

    for c in sent:
        c.wait_send()
    for it in range(ITERS):
        for buf, k, ssem, rsem in (
            (rowx, 7, r_send, r_recv), (col1, 3, c1_send, c1_recv), (col2, 7, c2_send, c2_recv)
        ):
            ref = buf.at[it, pl.ds(0, k)]
            rc(ref, ref, ssem.at[it], rsem.at[it], z_up).wait_send()


def per_device(n_total, m_total, noise_draw, latent_code, start_potential):
    anyspace = pl.BlockSpec(memory_space=pltpu.HBM)
    vmem = pl.BlockSpec(memory_space=pltpu.VMEM)
    width = 4096
    dma = pltpu.SemaphoreType.DMA

    def body(*refs):
        kernel(n_total, m_total, width, *refs)

    npot, lpot, out = pl.pallas_call(
        body,
        out_shape=(
            jax.ShapeDtypeStruct((4, LANE), F32),
            jax.ShapeDtypeStruct((4, LANE), F32),
            jax.ShapeDtypeStruct((LANE, BLK), F32),
        ),
        in_specs=[anyspace, anyspace, vmem],
        out_specs=(vmem, vmem, vmem),
        scratch_shapes=[
            pltpu.VMEM((8, BLK, BLK), BF16),
            pltpu.VMEM((Z, 2, 2, BLK, LANE), BF16),
            pltpu.VMEM((8, BLK, 2 * LANE), BF16),
            pltpu.VMEM((2, 2, BLK // 4, BLK), BF16),
            pltpu.VMEM((BLK, BLK), F32),
            pltpu.VMEM((BLK, LANE), F32),
            pltpu.VMEM((BLK, LANE), F32),
            pltpu.VMEM((2, BLK, BLK), BF16),
            pltpu.VMEM((2, HALF, BLK), BF16),
            pltpu.VMEM((2, Z, BLK, LANE), BF16),
            pltpu.VMEM((Z, HALF, 2 * LANE), F32),
            pltpu.VMEM((Z, HALF, LANE), F32),
            pltpu.VMEM((2, 4, 2, HALF, LANE), BF16),
            pltpu.VMEM((2, 4, 2, HALF, LANE), BF16),
            pltpu.VMEM((2, 4, HALF, LANE), BF16),
            pltpu.VMEM((2, 4, HALF, LANE), BF16),
            pltpu.VMEM((HALF, LANE), F32),
            pltpu.VMEM((HALF, LANE), F32),
            pltpu.VMEM((ITERS, 8, 4, LANE), F32),
            pltpu.VMEM((ITERS, 4, 4, LANE), F32),
            pltpu.VMEM((ITERS, 8, 4, LANE), F32),
            dma((12,)), dma((12,)),
            dma((2, 2, 2)), dma((2, 2, 2)),
            dma((19,)), dma((19,)),
            dma((2,)), dma((2,)),
            dma((4,)), dma((4,)),
            dma((2, Z)), dma((2, Z)),
            dma((ITERS,)), dma((ITERS,)),
            dma((ITERS,)), dma((ITERS,)),
            dma((ITERS,)), dma((ITERS,)),
            dma((2, 4, 2)), dma((2, 4, 2)),
            dma((2, 4)), dma((2, 4)),
            dma((1,)), dma((1,)),
            dma((2,)),
        ],
        compiler_params=pltpu.CompilerParams(
            collective_id=0, has_side_effects=True, vmem_limit_bytes=32 * 1024 * 1024
        ),
    )(noise_draw, latent_code, start_potential.reshape(4, LANE))
    return npot.reshape(BLK), lpot.reshape(BLK), out


def solution(mesh):
    in_specs = (P("row", "col"), P("col", "row"), P("col"))
    out_specs = (P("row"), P("col"), P("row", "col"))

    def whole(noise_draw, latent_code, start_potential):
        def block(a, b, c):
            return per_device(noise_draw.shape[0], latent_code.shape[0], a, b, c)

        return jax.shard_map(
            block, mesh=mesh, in_specs=in_specs, out_specs=out_specs, check_vma=False
        )(noise_draw, latent_code, start_potential)

    return whole
```

```python
import math

import jax
import jax.numpy as jnp
from jax import lax
from jax.experimental import pallas as pl
from jax.experimental.pallas import tpu as pltpu
from jax.sharding import PartitionSpec as P

ITERS = 3
EPS = 0.01
LOG2E = math.log2(math.e)
MESH = pl.DeviceIdType.MESH
F32 = jnp.float32
BF16 = jnp.bfloat16

Z, Y = 8, 4
LANE = 128
BLK = 512
HALF = BLK // 2


def kernel(
    n_total, m_total, width,
    noise_ref, latent_ref, start_ref,
    npot_ref, lpot_ref, out_ref,
    nz, lt, no, relay, cross, nsq, lsq, wt, wx, nx, part, parth, stage, land, stageh, landh, xs, xr, rowx, col1, col2,
    n_send, n_recv, h_send, h_recv, l_send, l_recv, o_send, o_recv, w_send, w_recv,
    p_send, p_recv, r_send, r_recv, c1_send, c1_recv, c2_send, c2_recv,
    s_send, s_recv, t_send, t_recv, x_send, x_recv, loc,
):
    row = lax.axis_index("row")
    col = lax.axis_index("col")
    z = row // 4
    xl = (row // 2) % 2
    core = row % 2
    y = col // 2
    xh = col % 2
    quad = row % 4

    def ring_z(d):
        return (z + d + Z) % Z

    def ring_y(d):
        return (y + d + Y) % Y

    other_core = (row + 1 - 2 * core, col)
    other_xl = (row + 2 - 4 * xl, col)
    flip_col = col + 1 - 2 * xh
    diagonal = (row + 2 - 4 * xl, flip_col)
    z_up = (ring_z(1) * 4 + quad, col)
    z_dn = (ring_z(-1) * 4 + quad, col)
    y_up = (row, ring_y(1) * 2 + xh)
    y_dn = (row, ring_y(-1) * 2 + xh)
    col_peers = [
        (row, ring_y(dy) * 2 + (1 - xh if dx else xh))
        for dy, dx in ((2, 1), (1, 1), (-1, 1), (2, 0), (0, 1), (1, 0), (-1, 0))
    ]
    across = (row + 2 - 4 * xl) // 2 * 2
    quad_peers = [(across + 1 - core, col), (across + core, col), other_core]
    z_peers = [(ring_z(d) * 4 + quad, col) for d in (4, 3, -3, 2, -2, 1, -1)]
    peers = col_peers + quad_peers + z_peers + [(across, flip_col), (across + 1, flip_col)]

    own_n = pltpu.make_async_copy(noise_ref, nz.at[col], loc.at[0])
    own_l = pltpu.make_async_copy(latent_ref, lt.at[z, core, xl], loc.at[1])
    own_n.start()
    own_l.start()

    barrier = pltpu.get_barrier_semaphore()
    for peer in peers:
        pl.semaphore_signal(barrier, inc=1, device_id=peer, device_id_type=MESH)
    cross[...] = jnp.zeros_like(cross)
    nsq[...] = jnp.zeros_like(nsq)
    lsq[...] = jnp.zeros_like(lsq)
    own_n.wait()
    own_l.wait()
    pl.semaphore_wait(barrier, len(peers))

    def rc(src, dst, ssem, rsem, dev):
        return pltpu.make_async_remote_copy(
            src_ref=src, dst_ref=dst, send_sem=ssem, recv_sem=rsem,
            device_id=dev, device_id_type=MESH,
        )

    def nsl(slot, h):
        return nz.at[slot, pl.ds(h * HALF, HALF), :]

    sent = []

    def nsend(slot, h, idx, dev):
        c = rc(nsl(slot, h), nsl(slot, h), n_send.at[idx], n_recv.at[idx], dev)
        c.start()
        sent.append(c)

    def nwait(slot, h, idx):
        rc(nsl(slot, h), nsl(slot, h), n_send.at[idx], n_recv.at[idx], y_up).wait_recv()

    def lsend(ref, idx, dev):
        c = rc(ref, ref, l_send.at[idx], l_recv.at[idx], dev)
        c.start()
        sent.append(c)

    def lwait(ref, idx):
        rc(ref, ref, l_send.at[idx], l_recv.at[idx], z_up).wait_recv()

    QUART = HALF // 2

    def slot_of(yy, s):
        return yy * 2 + (xh if s == 0 else 1 - xh)

    def quarter(slot, path, p):
        return nz.at[slot, pl.ds(path * HALF + p * QUART, QUART), :]

    def relay_start(t, path, p):
        ref = quarter(slot_of(ring_y(2 * t), 0), path, p)
        c = rc(ref, relay.at[t, path, p], h_send.at[0, t, path, p], h_recv.at[0, t, path, p],
               other_xl if path == 0 else diagonal)
        c.start()
        sent.append(c)

    def relay_forward(t, path, p):
        ref = quarter(slot_of(ring_y(2 * t), path), path, p)
        dev = diagonal if path == 0 else other_xl
        buf = relay.at[t, path, p]
        rc(buf, buf, h_send.at[0, t, path, p], h_recv.at[0, t, path, p], dev).wait_recv()
        c = rc(buf, ref, h_send.at[1, t, path, p], h_recv.at[1, t, path, p], dev)
        c.start()
        sent.append(c)

    def relay_end(t, path):
        for p in range(2):
            ref = quarter(slot_of(ring_y(2 * t), 1), path, p)
            rc(ref, ref, h_send.at[1, t, path, p], h_recv.at[1, t, path, p], diagonal).wait_recv()

    own_pair = lt.at[z, core]
    lsend(lt.at[z, core, xl], 0, other_xl)
    relay_start(0, 0, 0)
    relay_start(0, 1, 0)
    nsend(col, 0, 0, y_up)
    nsend(col, 1, 3, y_dn)
    lsend(lt.at[z, core, xl], 1, z_up)
    lsend(lt.at[z, core, xl], 6, z_dn)
    relay_start(0, 0, 1)
    relay_start(0, 1, 1)
    nsend(col, 1, 1, y_up)
    nsend(col, 0, 2, y_dn)

    lwait(lt.at[z, core, 1 - xl], 0)
    lsend(lt.at[z, core, 1 - xl], 2, z_up)
    lsend(lt.at[z, core, 1 - xl], 7, z_dn)
    lsend(own_pair, 11, other_core)
    relay_forward(0, 0, 0)
    relay_forward(0, 1, 0)

    for sgn, base, dev in ((-1, 1, z_up), (1, 6, z_dn)):
        zz = ring_z(sgn)
        lwait(lt.at[zz, core, xl], base)
        lwait(lt.at[zz, core, 1 - xl], base + 1)
        lsend(lt.at[zz, core], base + 2, dev)
        lsend(lt.at[zz, core], 12 + (base == 6), other_core)

    relay_forward(0, 0, 1)
    relay_forward(0, 1, 1)
    dn, up = slot_of(ring_y(-1), 0), slot_of(ring_y(1), 0)
    nwait(dn, 0, 0)
    nsend(dn, 0, 4, y_up)
    nwait(up, 1, 3)
    nsend(up, 1, 5, y_dn)

    for sgn, base, dev in ((-1, 1, z_up), (1, 6, z_dn)):
        zz = ring_z(2 * sgn)
        lwait(lt.at[zz, core], base + 2)
        lsend(lt.at[zz, core], base + 3, dev)
        lsend(lt.at[zz, core], 14 + (base == 6), other_core)

    relay_end(0, 0)
    nsend(flip_col, 0, 6, y_up)
    nsend(flip_col, 0, 8, y_dn)
    relay_end(0, 1)
    nsend(flip_col, 1, 9, y_dn)
    nsend(flip_col, 1, 7, y_up)

    nwait(slot_of(ring_y(2), 0), 0, 4)
    relay_start(1, 0, 0)
    relay_start(1, 0, 1)
    nwait(slot_of(ring_y(2), 0), 1, 5)
    relay_start(1, 1, 0)
    relay_start(1, 1, 1)

    for sgn, base, dev in ((-1, 1, z_up), (1, 6, z_dn)):
        zz = ring_z(3 * sgn)
        lwait(lt.at[zz, core], base + 3)
        lsend(lt.at[zz, core, int(base == 6)], base + 4, dev)
        lsend(lt.at[zz, core], 16 + (base == 6), other_core)
    far = ring_z(4)
    lwait(lt.at[far, core, 0], 5)
    lwait(lt.at[far, core, 1], 10)
    lsend(lt.at[far, core], 18, other_core)
    for p in range(2):
        for path in range(2):
            relay_forward(1, path, p)
    for j, d in enumerate((0, -1, 1, -2, 2, -3, 3, 4)):
        lwait(lt.at[ring_z(d), 1 - core], 11 + j)

    def accumulate(slot):
        a = nz[slot]
        b = jnp.concatenate([lt[slot, 0, 0], lt[slot, 1, 0], lt[slot, 0, 1], lt[slot, 1, 1]], axis=1)
        cross[...] += lax.dot_general(a, b, (((1,), (1,)), ((), ())), preferred_element_type=F32)
        a2 = jnp.square(a.astype(F32))
        nsq[...] += (a2[:, 0:128] + a2[:, 128:256]) + (a2[:, 256:384] + a2[:, 384:512])
        b2 = jnp.square(b.astype(F32))
        lsq[...] += (b2[:, 0:128] + b2[:, 128:256]) + (b2[:, 256:384] + b2[:, 384:512])

    def wait_rest(s):
        dn, up = slot_of(ring_y(-1), s), slot_of(ring_y(1), s)
        nwait(dn, 1, 6 * s + 1)
        nwait(up, 0, 6 * s + 2)

    wait_rest(0)

    def set0(k, carry):
        accumulate(((y + k) % Y) * 2 + xh)
        return carry

    lax.fori_loop(0, Y, set0, 0)
    accumulate(flip_col)
    dn, up = slot_of(ring_y(-1), 1), slot_of(ring_y(1), 1)
    nwait(dn, 0, 6)
    nwait(up, 1, 9)
    wait_rest(1)
    accumulate(dn)
    accumulate(up)
    relay_end(1, 0)
    relay_end(1, 1)
    accumulate(slot_of(ring_y(2), 1))

    for q in range(2):
        c = rc(
            nz.at[:, :, pl.ds(pl.multiple_of(q * 256 + (1 - core) * LANE, LANE), LANE)],
            no.at[:, :, pl.ds(q * LANE, LANE)],
            o_send.at[q], o_recv.at[q], other_core,
        )
        c.start()
        sent.append(c)

    eye = (
        lax.broadcasted_iota(jnp.int32, (LANE, LANE), 0)
        == lax.broadcasted_iota(jnp.int32, (LANE, LANE), 1)
    )

    def to_lanes(v):
        return jnp.sum(jnp.where(eye, v, 0.0), axis=0, keepdims=True)

    def to_rows(v):
        return jnp.sum(jnp.where(eye, v, 0.0), axis=1, keepdims=True)

    def wide(v):
        return jnp.concatenate([v[q:q + 1, :] for q in range(4)], axis=1)

    scale = LOG2E / (width * EPS)
    lq = jnp.concatenate(
        [to_lanes(jnp.sum(lsq[q * LANE:(q + 1) * LANE, :], axis=1, keepdims=True)) for q in range(4)],
        axis=1,
    )
    for b in range(4):
        rows = slice(b * LANE, (b + 1) * LANE)
        nq = jnp.sum(nsq[rows, :], axis=1, keepdims=True)
        cross[rows, :] = (nq + lq - 2.0 * cross[rows, :]) * scale

    def merge(parts):
        best = jnp.max(parts, axis=0)
        return best + jnp.log2(jnp.sum(jnp.exp2(parts - best[None]), axis=0))

    def lend(step):
        k, zz = step % 2, step // 2
        lanes = pl.ds(pl.multiple_of((1 - xl) * 256 + k * LANE, LANE), LANE)
        for slot, dev in ((zz, (across + k, col)), (zz + 4, (across + k, flip_col))):
            c = rc(nz.at[slot, :, lanes], nx.at[core, slot], p_send.at[k, slot], p_recv.at[core, slot], dev)
            c.start()
            sent.append(c)

    steps = iter(range(9))

    def exchange(buf, mine, peers, ssem, rsem):
        for peer in peers:
            rc(buf.at[mine], buf.at[mine], ssem, rsem, peer).start()
        step = next(steps)
        if step < 8:
            lend(step)
        k = len(peers)
        rc(buf.at[pl.ds(0, k)], buf.at[pl.ds(0, k)], ssem, rsem, peers[0]).wait_recv()

    g = start_ref[...] * (LOG2E / EPS)
    f = None
    f_rows = None
    for it in range(ITERS):
        gw = wide(g)
        for b in range(4):
            s = gw - cross[b * LANE:(b + 1) * LANE, :]
            top = jnp.max(s, axis=1, keepdims=True)
            tot = jnp.sum(jnp.exp2(s - top), axis=1, keepdims=True)
            rowx[it, col, b:b + 1, :] = to_lanes(top) + jnp.log2(to_lanes(tot))
        exchange(rowx.at[it], col, col_peers, r_send.at[it], r_recv.at[it])
        f = -(math.log2(m_total) + merge(rowx[it]))
        f_rows = [to_rows(f[b:b + 1, :]) for b in range(4)]
        tops, tots = [], []
        for b in range(4):
            s = f_rows[b] - cross[b * LANE:(b + 1) * LANE, :]
            top = jnp.max(s, axis=0, keepdims=True)
            tops.append(top)
            tots.append(jnp.sum(jnp.exp2(s - top), axis=0, keepdims=True))
        top = jnp.maximum(jnp.maximum(tops[0], tops[1]), jnp.maximum(tops[2], tops[3]))
        own = top + jnp.log2(sum(tots[b] * jnp.exp2(tops[b] - top) for b in range(4)))
        for q in range(4):
            col1[it, quad, q:q + 1, :] = own[:, q * LANE:(q + 1) * LANE]
        exchange(col1.at[it], quad, quad_peers, c1_send.at[it], c1_recv.at[it])
        col2[it, z] = merge(col1[it])
        exchange(col2.at[it], z, z_peers, c2_send.at[it], c2_recv.at[it])
        g = -(math.log2(n_total) + merge(col2[it]))

    npot_ref[...] = f * (EPS / LOG2E)
    lpot_ref[...] = g * (EPS / LOG2E)

    LOW, HIGH = slice(0, HALF), slice(HALF, BLK)
    gw = wide(g)

    def weights(cols):
        for b in range(4):
            rows = slice(b * LANE, (b + 1) * LANE)
            w = m_total * jnp.exp2((f_rows[b] + gw[:, cols]) - cross[rows, cols])
            wt[core, cols, rows] = w.T.astype(BF16)

    def wcopy(j, src, dst, dev):
        return rc(src, dst, w_send.at[j], w_recv.at[j], dev)

    low, high = pl.ds(0, HALF), pl.ds(HALF, HALF)
    copies = []
    weights(HIGH)
    copies.append(wcopy(0, wt.at[core, high], wx.at[core], other_xl))
    copies[-1].start()
    weights(LOW)
    copies.append(wcopy(1, wt.at[core, low], wt.at[core, low], other_core))
    copies[-1].start()
    copies.append(wcopy(2, wt.at[core, high], wt.at[core, high], other_core))
    copies[-1].start()
    for q in range(2):
        rc(no.at[:, :, pl.ds(q * LANE, LANE)], no.at[:, :, pl.ds(q * LANE, LANE)],
           o_send.at[q], o_recv.at[q], other_core).wait_recv()
    wcopy(1, wt.at[core, low], wt.at[1 - core, low], other_core).wait_recv()

    def mine(d, q):
        return nz[d, :, pl.ds(pl.multiple_of(q * 256 + core * LANE, LANE), LANE)]

    def theirs(d, q):
        return no[d, :, pl.ds(pl.multiple_of(q * LANE, LANE), LANE)]

    def partial(rel):
        d = (z + rel) % Z
        part[rel] = jnp.dot(
            wt[core, LOW, :], jnp.concatenate([mine(d, q) for q in (1 - xl, xl)], axis=1),
            preferred_element_type=F32,
        ) + jnp.dot(
            wt[1 - core, LOW, :], jnp.concatenate([theirs(d, q) for q in (1 - xl, xl)], axis=1),
            preferred_element_type=F32,
        )

    def partial_high(rel):
        d = (z + rel) % Z
        parth[rel] = (
            jnp.dot(wt[core, HIGH, :], mine(d, xl), preferred_element_type=F32)
            + jnp.dot(wt[1 - core, HIGH, :], theirs(d, xl), preferred_element_type=F32)
        ) + (
            jnp.dot(wx[0], nx[0, d], preferred_element_type=F32)
            + jnp.dot(wx[1], nx[1, d], preferred_element_type=F32)
        )

    def piece(k, bufs, dr, s):
        ref = bufs[1].at[dr, 4 - s] if k == 2 else bufs[0].at[dr, 4 - s, k]
        return ref.at[pl.ds(dr * LANE, LANE)] if s == 4 else ref

    def ring_copy(k, dr, s):
        ss, rs = (t_send.at[dr, 4 - s], t_recv.at[dr, 4 - s]) if k == 2 else (
            s_send.at[dr, 4 - s, k], s_recv.at[dr, 4 - s, k])
        return rc(
            piece(k, (stage, stageh), dr, s), piece(k, (land, landh), dr, s), ss, rs,
            z_dn if dr == 0 else z_up,
        )

    def own_part(k, rel, rows):
        return parth[rel, rows, :] if k == 2 else part[rel, rows, k * LANE:(k + 1) * LANE]

    def got(k, dr, s, rows):
        v = landh[dr, 4 - s, rows, :] if k == 2 else land[dr, 4 - s, k, rows, :]
        return v.astype(F32)

    def put(k, dr, s, rows, v):
        if k == 2:
            stageh[dr, 4 - s, rows, :] = v.astype(BF16)
        else:
            stage[dr, 4 - s, k, rows, :] = v.astype(BF16)

    ALL = slice(0, HALF)

    def ring_step(k, s):
        for dr in range(2):
            rel = Z - s if dr == 0 else s
            first = slice(dr * LANE, (dr + 1) * LANE)
            other = slice((1 - dr) * LANE, (2 - dr) * LANE)
            if s == 4:
                put(k, dr, s, first, own_part(k, 4, first))
            else:
                ring_copy(k, dr, s + 1).wait_recv()
                if s == 3:
                    put(k, dr, s, first, own_part(k, rel, first) + got(k, dr, 4, first))
                    put(k, dr, s, other, own_part(k, rel, other))
                else:
                    put(k, dr, s, ALL, own_part(k, rel, ALL) + got(k, dr, s + 1, ALL))
            c = ring_copy(k, dr, s)
            c.start()
            sent.append(c)

    def total(k):
        for dr in range(2):
            ring_copy(k, dr, 1).wait_recv()
        return own_part(k, 0, ALL) + (got(k, 0, 1, ALL) + got(k, 1, 1, ALL))

    partial(4)
    ring_step(0, 4)
    ring_step(1, 4)
    partial(5)
    partial(3)
    ring_step(0, 3)
    ring_step(1, 3)
    partial(6)
    partial(2)
    ring_step(0, 2)
    ring_step(1, 2)
    wcopy(0, wt.at[core, high], wx.at[core], other_xl).wait_recv()
    copies.append(wcopy(3, wx.at[core], wx.at[core], other_core))
    copies[-1].start()
    partial(7)
    partial(1)
    wcopy(2, wt.at[core, high], wt.at[1 - core, high], other_core).wait_recv()
    for c in range(2):
        for slot in range(Z):
            rc(nx.at[c, slot], nx.at[c, slot], p_send.at[0, slot], p_recv.at[c, slot], other_xl).wait_recv()
    wcopy(3, wx.at[core], wx.at[1 - core], other_core).wait_recv()
    partial_high(4)
    ring_step(2, 4)
    ring_step(0, 1)
    ring_step(1, 1)
    partial_high(5)
    partial_high(3)
    ring_step(2, 3)
    partial_high(6)
    partial_high(2)
    ring_step(2, 2)
    partial(0)
    xs[...] = total(0)
    xc = rc(xs, xr, x_send.at[0], x_recv.at[0], other_xl)
    xc.start()
    copies.append(xc)
    partial_high(7)
    partial_high(1)
    ring_step(2, 1)
    partial_high(0)
    kept = total(1)
    xc.wait_recv()
    out_ref[:, LOW] = (kept + xr[...]).T
    out_ref[:, HIGH] = total(2).T
    sent.extend(copies)

    for c in sent:
        c.wait_send()
    for it in range(ITERS):
        for buf, k, ssem, rsem in (
            (rowx, 7, r_send, r_recv), (col1, 3, c1_send, c1_recv), (col2, 7, c2_send, c2_recv)
        ):
            ref = buf.at[it, pl.ds(0, k)]
            rc(ref, ref, ssem.at[it], rsem.at[it], z_up).wait_send()


def per_device(n_total, m_total, noise_draw, latent_code, start_potential):
    anyspace = pl.BlockSpec(memory_space=pltpu.HBM)
    vmem = pl.BlockSpec(memory_space=pltpu.VMEM)
    width = 4096
    dma = pltpu.SemaphoreType.DMA

    def body(*refs):
        kernel(n_total, m_total, width, *refs)

    npot, lpot, out = pl.pallas_call(
        body,
        out_shape=(
            jax.ShapeDtypeStruct((4, LANE), F32),
            jax.ShapeDtypeStruct((4, LANE), F32),
            jax.ShapeDtypeStruct((LANE, BLK), F32),
        ),
        in_specs=[anyspace, anyspace, vmem],
        out_specs=(vmem, vmem, vmem),
        scratch_shapes=[
            pltpu.VMEM((8, BLK, BLK), BF16),
            pltpu.VMEM((Z, 2, 2, BLK, LANE), BF16),
            pltpu.VMEM((8, BLK, 2 * LANE), BF16),
            pltpu.VMEM((2, 2, 2, BLK // 4, BLK), BF16),
            pltpu.VMEM((BLK, BLK), F32),
            pltpu.VMEM((BLK, LANE), F32),
            pltpu.VMEM((BLK, LANE), F32),
            pltpu.VMEM((2, BLK, BLK), BF16),
            pltpu.VMEM((2, HALF, BLK), BF16),
            pltpu.VMEM((2, Z, BLK, LANE), BF16),
            pltpu.VMEM((Z, HALF, 2 * LANE), F32),
            pltpu.VMEM((Z, HALF, LANE), F32),
            pltpu.VMEM((2, 4, 2, HALF, LANE), BF16),
            pltpu.VMEM((2, 4, 2, HALF, LANE), BF16),
            pltpu.VMEM((2, 4, HALF, LANE), BF16),
            pltpu.VMEM((2, 4, HALF, LANE), BF16),
            pltpu.VMEM((HALF, LANE), F32),
            pltpu.VMEM((HALF, LANE), F32),
            pltpu.VMEM((ITERS, 8, 4, LANE), F32),
            pltpu.VMEM((ITERS, 4, 4, LANE), F32),
            pltpu.VMEM((ITERS, 8, 4, LANE), F32),
            dma((10,)), dma((10,)),
            dma((2, 2, 2, 2)), dma((2, 2, 2, 2)),
            dma((19,)), dma((19,)),
            dma((2,)), dma((2,)),
            dma((4,)), dma((4,)),
            dma((2, Z)), dma((2, Z)),
            dma((ITERS,)), dma((ITERS,)),
            dma((ITERS,)), dma((ITERS,)),
            dma((ITERS,)), dma((ITERS,)),
            dma((2, 4, 2)), dma((2, 4, 2)),
            dma((2, 4)), dma((2, 4)),
            dma((1,)), dma((1,)),
            dma((2,)),
        ],
        compiler_params=pltpu.CompilerParams(
            collective_id=0, has_side_effects=True, vmem_limit_bytes=32 * 1024 * 1024
        ),
    )(noise_draw, latent_code, start_potential.reshape(4, LANE))
    return npot.reshape(BLK), lpot.reshape(BLK), out


def solution(mesh):
    in_specs = (P("row", "col"), P("col", "row"), P("col"))
    out_specs = (P("row"), P("col"), P("row", "col"))

    def whole(noise_draw, latent_code, start_potential):
        def block(a, b, c):
            return per_device(noise_draw.shape[0], latent_code.shape[0], a, b, c)

        return jax.shard_map(
            block, mesh=mesh, in_specs=in_specs, out_specs=out_specs, check_vma=False
        )(noise_draw, latent_code, start_potential)

    return whole
```

```python
import math

import jax
import jax.numpy as jnp
from jax import lax
from jax.experimental import pallas as pl
from jax.experimental.pallas import tpu as pltpu
from jax.sharding import PartitionSpec as P

ITERS = 3
EPS = 0.01
LOG2E = math.log2(math.e)
MESH = pl.DeviceIdType.MESH
F32 = jnp.float32
BF16 = jnp.bfloat16

Z, Y = 8, 4
LANE = 128
BLK = 512
HALF = BLK // 2


def kernel(
    n_total, m_total, width,
    noise_ref, latent_ref, start_ref,
    npot_ref, lpot_ref, out_ref,
    nz, lt, no, relay, cross, nsq, lsq, wt, wx, nx, part, parth, stage, land, stageh, landh, xs, xr, rowx, col1, col2,
    n_send, n_recv, h_send, h_recv, l_send, l_recv, o_send, o_recv, w_send, w_recv,
    p_send, p_recv, r_send, r_recv, c1_send, c1_recv, c2_send, c2_recv,
    s_send, s_recv, t_send, t_recv, x_send, x_recv, loc,
):
    row = lax.axis_index("row")
    col = lax.axis_index("col")
    z = row // 4
    xl = (row // 2) % 2
    core = row % 2
    y = col // 2
    xh = col % 2
    quad = row % 4

    def ring_z(d):
        return (z + d + Z) % Z

    def ring_y(d):
        return (y + d + Y) % Y

    other_core = (row + 1 - 2 * core, col)
    other_xl = (row + 2 - 4 * xl, col)
    flip_col = col + 1 - 2 * xh
    diagonal = (row + 2 - 4 * xl, flip_col)
    z_up = (ring_z(1) * 4 + quad, col)
    z_dn = (ring_z(-1) * 4 + quad, col)
    y_up = (row, ring_y(1) * 2 + xh)
    y_dn = (row, ring_y(-1) * 2 + xh)
    col_peers = [
        (row, ring_y(dy) * 2 + (1 - xh if dx else xh))
        for dy, dx in ((2, 1), (1, 1), (-1, 1), (2, 0), (0, 1), (1, 0), (-1, 0))
    ]
    across = (row + 2 - 4 * xl) // 2 * 2
    quad_peers = [(across + 1 - core, col), (across + core, col), other_core]
    z_peers = [(ring_z(d) * 4 + quad, col) for d in (4, 3, -3, 2, -2, 1, -1)]
    peers = col_peers + quad_peers + z_peers + [(across, flip_col), (across + 1, flip_col)]

    own_n = pltpu.make_async_copy(noise_ref, nz.at[col], loc.at[0])
    own_l = pltpu.make_async_copy(latent_ref, lt.at[z, core, xl], loc.at[1])
    own_n.start()
    own_l.start()

    barrier = pltpu.get_barrier_semaphore()
    for peer in peers:
        pl.semaphore_signal(barrier, inc=1, device_id=peer, device_id_type=MESH)
    cross[...] = jnp.zeros_like(cross)
    nsq[...] = jnp.zeros_like(nsq)
    lsq[...] = jnp.zeros_like(lsq)
    own_n.wait()
    own_l.wait()
    pl.semaphore_wait(barrier, len(peers))

    def rc(src, dst, ssem, rsem, dev):
        return pltpu.make_async_remote_copy(
            src_ref=src, dst_ref=dst, send_sem=ssem, recv_sem=rsem,
            device_id=dev, device_id_type=MESH,
        )

    def nsl(slot, h):
        return nz.at[slot, pl.ds(h * HALF, HALF), :]

    sent = []

    def nsend(slot, h, idx, dev):
        c = rc(nsl(slot, h), nsl(slot, h), n_send.at[idx], n_recv.at[idx], dev)
        c.start()
        sent.append(c)

    def nwait(slot, h, idx):
        rc(nsl(slot, h), nsl(slot, h), n_send.at[idx], n_recv.at[idx], y_up).wait_recv()

    def lsend(ref, idx, dev):
        c = rc(ref, ref, l_send.at[idx], l_recv.at[idx], dev)
        c.start()
        sent.append(c)

    def lwait(ref, idx):
        rc(ref, ref, l_send.at[idx], l_recv.at[idx], z_up).wait_recv()

    QUART = HALF // 2

    def slot_of(yy, s):
        return yy * 2 + (xh if s == 0 else 1 - xh)

    def quarter(slot, path, p):
        return nz.at[slot, pl.ds(path * HALF + p * QUART, QUART), :]

    def relay_start(t, path, p):
        ref = quarter(slot_of(ring_y(2 * t), 0), path, p)
        c = rc(ref, relay.at[t, path, p], h_send.at[0, t, path, p], h_recv.at[0, t, path, p],
               other_xl if path == 0 else diagonal)
        c.start()
        sent.append(c)

    def relay_forward(t, path, p):
        ref = quarter(slot_of(ring_y(2 * t), path), path, p)
        dev = diagonal if path == 0 else other_xl
        buf = relay.at[t, path, p]
        rc(buf, buf, h_send.at[0, t, path, p], h_recv.at[0, t, path, p], dev).wait_recv()
        c = rc(buf, ref, h_send.at[1, t, path, p], h_recv.at[1, t, path, p], dev)
        c.start()
        sent.append(c)

    def relay_end(t, path):
        for p in range(2):
            ref = quarter(slot_of(ring_y(2 * t), 1), path, p)
            rc(ref, ref, h_send.at[1, t, path, p], h_recv.at[1, t, path, p], diagonal).wait_recv()

    own_pair = lt.at[z, core]
    lsend(lt.at[z, core, xl], 0, other_xl)
    relay_start(0, 0, 0)
    relay_start(0, 1, 0)
    nsend(col, 0, 0, y_up)
    nsend(col, 1, 3, y_dn)
    lsend(lt.at[z, core, xl], 1, z_up)
    lsend(lt.at[z, core, xl], 6, z_dn)
    relay_start(0, 0, 1)
    relay_start(0, 1, 1)
    nsend(col, 1, 1, y_up)
    nsend(col, 0, 2, y_dn)

    lwait(lt.at[z, core, 1 - xl], 0)
    lsend(lt.at[z, core, 1 - xl], 2, z_up)
    lsend(lt.at[z, core, 1 - xl], 7, z_dn)
    lsend(own_pair, 11, other_core)
    relay_forward(0, 0, 0)
    relay_forward(0, 1, 0)

    for sgn, base, dev in ((-1, 1, z_up), (1, 6, z_dn)):
        zz = ring_z(sgn)
        lwait(lt.at[zz, core, xl], base)
        lwait(lt.at[zz, core, 1 - xl], base + 1)
        lsend(lt.at[zz, core], base + 2, dev)
        lsend(lt.at[zz, core], 12 + (base == 6), other_core)

    relay_forward(0, 0, 1)
    relay_forward(0, 1, 1)
    dn, up = slot_of(ring_y(-1), 0), slot_of(ring_y(1), 0)
    nwait(dn, 0, 0)
    nsend(dn, 0, 4, y_up)
    nwait(up, 1, 3)
    nsend(up, 1, 5, y_dn)

    for sgn, base, dev in ((-1, 1, z_up), (1, 6, z_dn)):
        zz = ring_z(2 * sgn)
        lwait(lt.at[zz, core], base + 2)
        lsend(lt.at[zz, core], base + 3, dev)
        lsend(lt.at[zz, core], 14 + (base == 6), other_core)

    relay_end(0, 0)
    nsend(flip_col, 0, 6, y_up)
    nsend(flip_col, 0, 8, y_dn)
    relay_end(0, 1)
    nsend(flip_col, 1, 9, y_dn)
    nsend(flip_col, 1, 7, y_up)

    nwait(slot_of(ring_y(2), 0), 0, 4)
    relay_start(1, 0, 0)
    relay_start(1, 0, 1)
    nwait(slot_of(ring_y(2), 0), 1, 5)
    relay_start(1, 1, 0)
    relay_start(1, 1, 1)

    for sgn, base, dev in ((-1, 1, z_up), (1, 6, z_dn)):
        zz = ring_z(3 * sgn)
        lwait(lt.at[zz, core], base + 3)
        lsend(lt.at[zz, core, int(base == 6)], base + 4, dev)
        lsend(lt.at[zz, core], 16 + (base == 6), other_core)
    far = ring_z(4)
    lwait(lt.at[far, core, 0], 5)
    lwait(lt.at[far, core, 1], 10)
    lsend(lt.at[far, core], 18, other_core)
    for p in range(2):
        for path in range(2):
            relay_forward(1, path, p)
    for j, d in enumerate((0, -1, 1, -2, 2, -3, 3, 4)):
        lwait(lt.at[ring_z(d), 1 - core], 11 + j)

    def accumulate(slot):
        a = nz[slot]
        b = jnp.concatenate([lt[slot, 0, 0], lt[slot, 1, 0], lt[slot, 0, 1], lt[slot, 1, 1]], axis=1)
        cross[...] += lax.dot_general(a, b, (((1,), (1,)), ((), ())), preferred_element_type=F32)
        a2 = jnp.square(a.astype(F32))
        nsq[...] += (a2[:, 0:128] + a2[:, 128:256]) + (a2[:, 256:384] + a2[:, 384:512])
        b2 = jnp.square(b.astype(F32))
        lsq[...] += (b2[:, 0:128] + b2[:, 128:256]) + (b2[:, 256:384] + b2[:, 384:512])

    def wait_rest(s):
        dn, up = slot_of(ring_y(-1), s), slot_of(ring_y(1), s)
        nwait(dn, 1, 6 * s + 1)
        nwait(up, 0, 6 * s + 2)

    wait_rest(0)

    def set0(k, carry):
        accumulate(((y + k) % Y) * 2 + xh)
        return carry

    lax.fori_loop(0, Y, set0, 0)
    accumulate(flip_col)
    dn, up = slot_of(ring_y(-1), 1), slot_of(ring_y(1), 1)
    nwait(dn, 0, 6)
    nwait(up, 1, 9)
    wait_rest(1)
    accumulate(dn)
    accumulate(up)
    relay_end(1, 0)
    relay_end(1, 1)
    accumulate(slot_of(ring_y(2), 1))

    for q in range(2):
        c = rc(
            nz.at[:, :, pl.ds(pl.multiple_of(q * 256 + (1 - core) * LANE, LANE), LANE)],
            no.at[:, :, pl.ds(q * LANE, LANE)],
            o_send.at[q], o_recv.at[q], other_core,
        )
        c.start()
        sent.append(c)

    eye = (
        lax.broadcasted_iota(jnp.int32, (LANE, LANE), 0)
        == lax.broadcasted_iota(jnp.int32, (LANE, LANE), 1)
    )

    def to_lanes(v):
        return jnp.sum(jnp.where(eye, v, 0.0), axis=0, keepdims=True)

    def to_rows(v):
        return jnp.sum(jnp.where(eye, v, 0.0), axis=1, keepdims=True)

    def wide(v):
        return jnp.concatenate([v[q:q + 1, :] for q in range(4)], axis=1)

    scale = LOG2E / (width * EPS)
    lq = jnp.concatenate(
        [to_lanes(jnp.sum(lsq[q * LANE:(q + 1) * LANE, :], axis=1, keepdims=True)) for q in range(4)],
        axis=1,
    )
    for b in range(4):
        rows = slice(b * LANE, (b + 1) * LANE)
        nq = jnp.sum(nsq[rows, :], axis=1, keepdims=True)
        cross[rows, :] = (nq + lq - 2.0 * cross[rows, :]) * scale

    def merge(parts):
        best = jnp.max(parts, axis=0)
        return best + jnp.log2(jnp.sum(jnp.exp2(parts - best[None]), axis=0))

    def merge_rows(parts):
        best = jnp.max(parts, axis=0, keepdims=True)
        return best + jnp.log2(jnp.sum(jnp.exp2(parts - best), axis=0, keepdims=True))

    def lend(step):
        k, zz = step % 2, step // 2
        lanes = pl.ds(pl.multiple_of((1 - xl) * 256 + k * LANE, LANE), LANE)
        for slot, dev in ((zz, (across + k, col)), (zz + 4, (across + k, flip_col))):
            c = rc(nz.at[slot, :, lanes], nx.at[core, slot], p_send.at[k, slot], p_recv.at[core, slot], dev)
            c.start()
            sent.append(c)

    steps = iter(range(9))

    def exchange(buf, mine, peers, ssem, rsem):
        for peer in peers:
            rc(buf.at[mine], buf.at[mine], ssem, rsem, peer).start()
        step = next(steps)
        if step < 8:
            lend(step)
        k = len(peers)
        rc(buf.at[pl.ds(0, k)], buf.at[pl.ds(0, k)], ssem, rsem, peers[0]).wait_recv()

    g = start_ref[...] * (LOG2E / EPS)
    f = None
    f_rows = None
    for it in range(ITERS):
        for b in range(4):
            parts = []
            for r in range(b * LANE, (b + 1) * LANE, 32):
                s = [g[q:q + 1, :] - cross[r:r + 32, q * LANE:(q + 1) * LANE] for q in range(4)]
                top = jnp.maximum(jnp.maximum(s[0], s[1]), jnp.maximum(s[2], s[3]))
                e = [jnp.exp2(v - top) for v in s]
                parts.append(top + jnp.log2((e[0] + e[1]) + (e[2] + e[3])))
            rowx[it, col, b:b + 1, :] = merge_rows(jnp.concatenate(parts, axis=0).T)
        exchange(rowx.at[it], col, col_peers, r_send.at[it], r_recv.at[it])
        f = -(math.log2(m_total) + merge(rowx[it]))
        f_rows = [to_rows(f[b:b + 1, :]) for b in range(4)]
        parts = []
        for r in range(0, BLK, 64):
            fr = f_rows[r // LANE][r % LANE:r % LANE + 64]
            s = (fr - cross[r:r + 64, :]).reshape(8, 8, BLK)
            top = jnp.max(s, axis=0)
            parts.append(top + jnp.log2(jnp.sum(jnp.exp2(s - top[None]), axis=0)))
        top = parts[0]
        for v in parts[1:]:
            top = jnp.maximum(top, v)
        own = merge_rows(top + jnp.log2(sum(jnp.exp2(v - top) for v in parts)))
        for q in range(4):
            col1[it, quad, q:q + 1, :] = own[:, q * LANE:(q + 1) * LANE]
        exchange(col1.at[it], quad, quad_peers, c1_send.at[it], c1_recv.at[it])
        col2[it, z] = merge(col1[it])
        exchange(col2.at[it], z, z_peers, c2_send.at[it], c2_recv.at[it])
        g = -(math.log2(n_total) + merge(col2[it]))

    npot_ref[...] = f * (EPS / LOG2E)
    lpot_ref[...] = g * (EPS / LOG2E)

    LOW, HIGH = slice(0, HALF), slice(HALF, BLK)
    gw = wide(g)

    def weights(cols):
        for b in range(4):
            rows = slice(b * LANE, (b + 1) * LANE)
            w = m_total * jnp.exp2((f_rows[b] + gw[:, cols]) - cross[rows, cols])
            wt[core, cols, rows] = w.T.astype(BF16)

    def wcopy(j, src, dst, dev):
        return rc(src, dst, w_send.at[j], w_recv.at[j], dev)

    low, high = pl.ds(0, HALF), pl.ds(HALF, HALF)
    copies = []
    weights(HIGH)
    copies.append(wcopy(0, wt.at[core, high], wx.at[core], other_xl))
    copies[-1].start()
    weights(LOW)
    copies.append(wcopy(1, wt.at[core, low], wt.at[core, low], other_core))
    copies[-1].start()
    copies.append(wcopy(2, wt.at[core, high], wt.at[core, high], other_core))
    copies[-1].start()
    for q in range(2):
        rc(no.at[:, :, pl.ds(q * LANE, LANE)], no.at[:, :, pl.ds(q * LANE, LANE)],
           o_send.at[q], o_recv.at[q], other_core).wait_recv()
    wcopy(1, wt.at[core, low], wt.at[1 - core, low], other_core).wait_recv()

    def mine(d, q):
        return nz[d, :, pl.ds(pl.multiple_of(q * 256 + core * LANE, LANE), LANE)]

    def theirs(d, q):
        return no[d, :, pl.ds(pl.multiple_of(q * LANE, LANE), LANE)]

    def partial(rel):
        d = (z + rel) % Z
        part[rel] = jnp.dot(
            wt[core, LOW, :], jnp.concatenate([mine(d, q) for q in (1 - xl, xl)], axis=1),
            preferred_element_type=F32,
        ) + jnp.dot(
            wt[1 - core, LOW, :], jnp.concatenate([theirs(d, q) for q in (1 - xl, xl)], axis=1),
            preferred_element_type=F32,
        )

    def partial_high(rel):
        d = (z + rel) % Z
        parth[rel] = (
            jnp.dot(wt[core, HIGH, :], mine(d, xl), preferred_element_type=F32)
            + jnp.dot(wt[1 - core, HIGH, :], theirs(d, xl), preferred_element_type=F32)
        ) + (
            jnp.dot(wx[0], nx[0, d], preferred_element_type=F32)
            + jnp.dot(wx[1], nx[1, d], preferred_element_type=F32)
        )

    def piece(k, bufs, dr, s):
        ref = bufs[1].at[dr, 4 - s] if k == 2 else bufs[0].at[dr, 4 - s, k]
        return ref.at[pl.ds(dr * LANE, LANE)] if s == 4 else ref

    def ring_copy(k, dr, s):
        ss, rs = (t_send.at[dr, 4 - s], t_recv.at[dr, 4 - s]) if k == 2 else (
            s_send.at[dr, 4 - s, k], s_recv.at[dr, 4 - s, k])
        return rc(
            piece(k, (stage, stageh), dr, s), piece(k, (land, landh), dr, s), ss, rs,
            z_dn if dr == 0 else z_up,
        )

    def own_part(k, rel, rows):
        return parth[rel, rows, :] if k == 2 else part[rel, rows, k * LANE:(k + 1) * LANE]

    def got(k, dr, s, rows):
        v = landh[dr, 4 - s, rows, :] if k == 2 else land[dr, 4 - s, k, rows, :]
        return v.astype(F32)

    def put(k, dr, s, rows, v):
        if k == 2:
            stageh[dr, 4 - s, rows, :] = v.astype(BF16)
        else:
            stage[dr, 4 - s, k, rows, :] = v.astype(BF16)

    ALL = slice(0, HALF)

    def ring_step(k, s):
        for dr in range(2):
            rel = Z - s if dr == 0 else s
            first = slice(dr * LANE, (dr + 1) * LANE)
            other = slice((1 - dr) * LANE, (2 - dr) * LANE)
            if s == 4:
                put(k, dr, s, first, own_part(k, 4, first))
            else:
                ring_copy(k, dr, s + 1).wait_recv()
                if s == 3:
                    put(k, dr, s, first, own_part(k, rel, first) + got(k, dr, 4, first))
                    put(k, dr, s, other, own_part(k, rel, other))
                else:
                    put(k, dr, s, ALL, own_part(k, rel, ALL) + got(k, dr, s + 1, ALL))
            c = ring_copy(k, dr, s)
            c.start()
            sent.append(c)

    def total(k):
        for dr in range(2):
            ring_copy(k, dr, 1).wait_recv()
        return own_part(k, 0, ALL) + (got(k, 0, 1, ALL) + got(k, 1, 1, ALL))

    partial(4)
    ring_step(0, 4)
    ring_step(1, 4)
    partial(5)
    partial(3)
    ring_step(0, 3)
    ring_step(1, 3)
    partial(6)
    partial(2)
    ring_step(0, 2)
    ring_step(1, 2)
    wcopy(0, wt.at[core, high], wx.at[core], other_xl).wait_recv()
    copies.append(wcopy(3, wx.at[core], wx.at[core], other_core))
    copies[-1].start()
    partial(7)
    partial(1)
    wcopy(2, wt.at[core, high], wt.at[1 - core, high], other_core).wait_recv()
    for c in range(2):
        for slot in range(Z):
            rc(nx.at[c, slot], nx.at[c, slot], p_send.at[0, slot], p_recv.at[c, slot], other_xl).wait_recv()
    wcopy(3, wx.at[core], wx.at[1 - core], other_core).wait_recv()
    partial_high(4)
    ring_step(2, 4)
    ring_step(0, 1)
    ring_step(1, 1)
    partial_high(5)
    partial_high(3)
    ring_step(2, 3)
    partial_high(6)
    partial_high(2)
    ring_step(2, 2)
    partial(0)
    xs[...] = total(0)
    xc = rc(xs, xr, x_send.at[0], x_recv.at[0], other_xl)
    xc.start()
    copies.append(xc)
    partial_high(7)
    partial_high(1)
    ring_step(2, 1)
    partial_high(0)
    kept = total(1)
    xc.wait_recv()
    out_ref[:, LOW] = (kept + xr[...]).T
    out_ref[:, HIGH] = total(2).T
    sent.extend(copies)

    for c in sent:
        c.wait_send()
    for it in range(ITERS):
        for buf, k, ssem, rsem in (
            (rowx, 7, r_send, r_recv), (col1, 3, c1_send, c1_recv), (col2, 7, c2_send, c2_recv)
        ):
            ref = buf.at[it, pl.ds(0, k)]
            rc(ref, ref, ssem.at[it], rsem.at[it], z_up).wait_send()


def per_device(n_total, m_total, noise_draw, latent_code, start_potential):
    anyspace = pl.BlockSpec(memory_space=pltpu.HBM)
    vmem = pl.BlockSpec(memory_space=pltpu.VMEM)
    width = 4096
    dma = pltpu.SemaphoreType.DMA

    def body(*refs):
        kernel(n_total, m_total, width, *refs)

    npot, lpot, out = pl.pallas_call(
        body,
        out_shape=(
            jax.ShapeDtypeStruct((4, LANE), F32),
            jax.ShapeDtypeStruct((4, LANE), F32),
            jax.ShapeDtypeStruct((LANE, BLK), F32),
        ),
        in_specs=[anyspace, anyspace, vmem],
        out_specs=(vmem, vmem, vmem),
        scratch_shapes=[
            pltpu.VMEM((8, BLK, BLK), BF16),
            pltpu.VMEM((Z, 2, 2, BLK, LANE), BF16),
            pltpu.VMEM((8, BLK, 2 * LANE), BF16),
            pltpu.VMEM((2, 2, 2, BLK // 4, BLK), BF16),
            pltpu.VMEM((BLK, BLK), F32),
            pltpu.VMEM((BLK, LANE), F32),
            pltpu.VMEM((BLK, LANE), F32),
            pltpu.VMEM((2, BLK, BLK), BF16),
            pltpu.VMEM((2, HALF, BLK), BF16),
            pltpu.VMEM((2, Z, BLK, LANE), BF16),
            pltpu.VMEM((Z, HALF, 2 * LANE), F32),
            pltpu.VMEM((Z, HALF, LANE), F32),
            pltpu.VMEM((2, 4, 2, HALF, LANE), BF16),
            pltpu.VMEM((2, 4, 2, HALF, LANE), BF16),
            pltpu.VMEM((2, 4, HALF, LANE), BF16),
            pltpu.VMEM((2, 4, HALF, LANE), BF16),
            pltpu.VMEM((HALF, LANE), F32),
            pltpu.VMEM((HALF, LANE), F32),
            pltpu.VMEM((ITERS, 8, 4, LANE), F32),
            pltpu.VMEM((ITERS, 4, 4, LANE), F32),
            pltpu.VMEM((ITERS, 8, 4, LANE), F32),
            dma((10,)), dma((10,)),
            dma((2, 2, 2, 2)), dma((2, 2, 2, 2)),
            dma((19,)), dma((19,)),
            dma((2,)), dma((2,)),
            dma((4,)), dma((4,)),
            dma((2, Z)), dma((2, Z)),
            dma((ITERS,)), dma((ITERS,)),
            dma((ITERS,)), dma((ITERS,)),
            dma((ITERS,)), dma((ITERS,)),
            dma((2, 4, 2)), dma((2, 4, 2)),
            dma((2, 4)), dma((2, 4)),
            dma((1,)), dma((1,)),
            dma((2,)),
        ],
        compiler_params=pltpu.CompilerParams(
            collective_id=0, has_side_effects=True, vmem_limit_bytes=32 * 1024 * 1024
        ),
    )(noise_draw, latent_code, start_potential.reshape(4, LANE))
    return npot.reshape(BLK), lpot.reshape(BLK), out


def solution(mesh):
    in_specs = (P("row", "col"), P("col", "row"), P("col"))
    out_specs = (P("row"), P("col"), P("row", "col"))

    def whole(noise_draw, latent_code, start_potential):
        def block(a, b, c):
            return per_device(noise_draw.shape[0], latent_code.shape[0], a, b, c)

        return jax.shard_map(
            block, mesh=mesh, in_specs=in_specs, out_specs=out_specs, check_vma=False
        )(noise_draw, latent_code, start_potential)

    return whole
```

```python
import math

import jax
import jax.numpy as jnp
from jax import lax
from jax.experimental import pallas as pl
from jax.experimental.pallas import tpu as pltpu
from jax.sharding import PartitionSpec as P

ITERS = 3
EPS = 0.01
LOG2E = math.log2(math.e)
MESH = pl.DeviceIdType.MESH
F32 = jnp.float32
BF16 = jnp.bfloat16

Z, Y = 8, 4
LANE = 128
BLK = 512
HALF = BLK // 2


def kernel(
    n_total, m_total, width,
    noise_ref, latent_ref, start_ref,
    npot_ref, lpot_ref, out_ref,
    nz, lt, no, relay, cross, nsq, lsq, wt, wx, nx, part, parth, stage, land, stageh, landh, xs, xr, rowx, col2,
    n_send, n_recv, h_send, h_recv, l_send, l_recv, o_send, o_recv, w_send, w_recv,
    p_send, p_recv, r_send, r_recv, c2_send, c2_recv,
    s_send, s_recv, t_send, t_recv, x_send, x_recv, loc,
):
    row = lax.axis_index("row")
    col = lax.axis_index("col")
    z = row // 4
    xl = (row // 2) % 2
    core = row % 2
    y = col // 2
    xh = col % 2
    quad = row % 4

    def ring_z(d):
        return (z + d + Z) % Z

    def ring_y(d):
        return (y + d + Y) % Y

    other_core = (row + 1 - 2 * core, col)
    other_xl = (row + 2 - 4 * xl, col)
    flip_col = col + 1 - 2 * xh
    diagonal = (row + 2 - 4 * xl, flip_col)
    z_up = (ring_z(1) * 4 + quad, col)
    z_dn = (ring_z(-1) * 4 + quad, col)
    y_up = (row, ring_y(1) * 2 + xh)
    y_dn = (row, ring_y(-1) * 2 + xh)
    col_peers = [
        (row, ring_y(dy) * 2 + (1 - xh if dx else xh))
        for dy, dx in ((2, 1), (1, 1), (-1, 1), (2, 0), (0, 1), (1, 0), (-1, 0))
    ]
    across = (row + 2 - 4 * xl) // 2 * 2
    across_quad = ((across + 1 - core) % 4, (across + core) % 4, (quad // 2) * 2 + 1 - core, quad)
    row_peers = [
        (ring_z(d) * 4 + q, col)
        for d in (4, 3, -3, 2, -2, 1, -1, 0) for q in across_quad[:3 if d == 0 else 4]
    ]
    peers = col_peers + row_peers + [(across, flip_col), (across + 1, flip_col)]

    own_n = pltpu.make_async_copy(noise_ref, nz.at[col], loc.at[0])
    own_l = pltpu.make_async_copy(latent_ref, lt.at[z, core, xl], loc.at[1])
    own_n.start()
    own_l.start()

    barrier = pltpu.get_barrier_semaphore()
    for peer in peers:
        pl.semaphore_signal(barrier, inc=1, device_id=peer, device_id_type=MESH)
    cross[...] = jnp.zeros_like(cross)
    nsq[...] = jnp.zeros_like(nsq)
    lsq[...] = jnp.zeros_like(lsq)
    own_n.wait()
    own_l.wait()
    pl.semaphore_wait(barrier, len(peers))

    def rc(src, dst, ssem, rsem, dev):
        return pltpu.make_async_remote_copy(
            src_ref=src, dst_ref=dst, send_sem=ssem, recv_sem=rsem,
            device_id=dev, device_id_type=MESH,
        )

    def nsl(slot, h):
        return nz.at[slot, pl.ds(h * HALF, HALF), :]

    sent = []

    def nsend(slot, h, idx, dev):
        c = rc(nsl(slot, h), nsl(slot, h), n_send.at[idx], n_recv.at[idx], dev)
        c.start()
        sent.append(c)

    def nwait(slot, h, idx):
        rc(nsl(slot, h), nsl(slot, h), n_send.at[idx], n_recv.at[idx], y_up).wait_recv()

    def lsend(ref, idx, dev):
        c = rc(ref, ref, l_send.at[idx], l_recv.at[idx], dev)
        c.start()
        sent.append(c)

    def lwait(ref, idx):
        rc(ref, ref, l_send.at[idx], l_recv.at[idx], z_up).wait_recv()

    QUART = HALF // 2

    def slot_of(yy, s):
        return yy * 2 + (xh if s == 0 else 1 - xh)

    def quarter(slot, path, p):
        return nz.at[slot, pl.ds(path * HALF + p * QUART, QUART), :]

    def relay_start(t, path, p):
        ref = quarter(slot_of(ring_y(2 * t), 0), path, p)
        c = rc(ref, relay.at[t, path, p], h_send.at[0, t, path, p], h_recv.at[0, t, path, p],
               other_xl if path == 0 else diagonal)
        c.start()
        sent.append(c)

    def relay_forward(t, path, p):
        ref = quarter(slot_of(ring_y(2 * t), path), path, p)
        dev = diagonal if path == 0 else other_xl
        buf = relay.at[t, path, p]
        rc(buf, buf, h_send.at[0, t, path, p], h_recv.at[0, t, path, p], dev).wait_recv()
        c = rc(buf, ref, h_send.at[1, t, path, p], h_recv.at[1, t, path, p], dev)
        c.start()
        sent.append(c)

    def relay_end(t, path):
        for p in range(2):
            ref = quarter(slot_of(ring_y(2 * t), 1), path, p)
            rc(ref, ref, h_send.at[1, t, path, p], h_recv.at[1, t, path, p], diagonal).wait_recv()

    own_pair = lt.at[z, core]
    lsend(lt.at[z, core, xl], 0, other_xl)
    relay_start(0, 0, 0)
    relay_start(0, 1, 0)
    nsend(col, 0, 0, y_up)
    nsend(col, 1, 3, y_dn)
    lsend(lt.at[z, core, xl], 1, z_up)
    lsend(lt.at[z, core, xl], 6, z_dn)
    relay_start(0, 0, 1)
    relay_start(0, 1, 1)
    nsend(col, 1, 1, y_up)
    nsend(col, 0, 2, y_dn)

    lwait(lt.at[z, core, 1 - xl], 0)
    lsend(lt.at[z, core, 1 - xl], 2, z_up)
    lsend(lt.at[z, core, 1 - xl], 7, z_dn)
    lsend(own_pair, 11, other_core)
    relay_forward(0, 0, 0)
    relay_forward(0, 1, 0)

    for sgn, base, dev in ((-1, 1, z_up), (1, 6, z_dn)):
        zz = ring_z(sgn)
        lwait(lt.at[zz, core, xl], base)
        lwait(lt.at[zz, core, 1 - xl], base + 1)
        lsend(lt.at[zz, core], base + 2, dev)
        lsend(lt.at[zz, core], 12 + (base == 6), other_core)

    relay_forward(0, 0, 1)
    relay_forward(0, 1, 1)
    dn, up = slot_of(ring_y(-1), 0), slot_of(ring_y(1), 0)
    nwait(dn, 0, 0)
    nsend(dn, 0, 4, y_up)
    nwait(up, 1, 3)
    nsend(up, 1, 5, y_dn)

    for sgn, base, dev in ((-1, 1, z_up), (1, 6, z_dn)):
        zz = ring_z(2 * sgn)
        lwait(lt.at[zz, core], base + 2)
        lsend(lt.at[zz, core], base + 3, dev)
        lsend(lt.at[zz, core], 14 + (base == 6), other_core)

    relay_end(0, 0)
    nsend(flip_col, 0, 6, y_up)
    nsend(flip_col, 0, 8, y_dn)
    relay_end(0, 1)
    nsend(flip_col, 1, 9, y_dn)
    nsend(flip_col, 1, 7, y_up)

    nwait(slot_of(ring_y(2), 0), 0, 4)
    relay_start(1, 0, 0)
    relay_start(1, 0, 1)
    nwait(slot_of(ring_y(2), 0), 1, 5)
    relay_start(1, 1, 0)
    relay_start(1, 1, 1)

    for sgn, base, dev in ((-1, 1, z_up), (1, 6, z_dn)):
        zz = ring_z(3 * sgn)
        lwait(lt.at[zz, core], base + 3)
        lsend(lt.at[zz, core, int(base == 6)], base + 4, dev)
        lsend(lt.at[zz, core], 16 + (base == 6), other_core)
    far = ring_z(4)
    lwait(lt.at[far, core, 0], 5)
    lwait(lt.at[far, core, 1], 10)
    lsend(lt.at[far, core], 18, other_core)
    for p in range(2):
        for path in range(2):
            relay_forward(1, path, p)
    for j, d in enumerate((0, -1, 1, -2, 2, -3, 3, 4)):
        lwait(lt.at[ring_z(d), 1 - core], 11 + j)

    def accumulate(slot):
        a = nz[slot]
        b = jnp.concatenate([lt[slot, 0, 0], lt[slot, 1, 0], lt[slot, 0, 1], lt[slot, 1, 1]], axis=1)
        cross[...] += lax.dot_general(a, b, (((1,), (1,)), ((), ())), preferred_element_type=F32)
        a2 = jnp.square(a.astype(F32))
        nsq[...] += (a2[:, 0:128] + a2[:, 128:256]) + (a2[:, 256:384] + a2[:, 384:512])
        b2 = jnp.square(b.astype(F32))
        lsq[...] += (b2[:, 0:128] + b2[:, 128:256]) + (b2[:, 256:384] + b2[:, 384:512])

    def wait_rest(s):
        dn, up = slot_of(ring_y(-1), s), slot_of(ring_y(1), s)
        nwait(dn, 1, 6 * s + 1)
        nwait(up, 0, 6 * s + 2)

    wait_rest(0)

    def set0(k, carry):
        accumulate(((y + k) % Y) * 2 + xh)
        return carry

    lax.fori_loop(0, Y, set0, 0)
    accumulate(flip_col)
    dn, up = slot_of(ring_y(-1), 1), slot_of(ring_y(1), 1)
    nwait(dn, 0, 6)
    nwait(up, 1, 9)
    wait_rest(1)
    accumulate(dn)
    accumulate(up)
    relay_end(1, 0)
    relay_end(1, 1)
    accumulate(slot_of(ring_y(2), 1))

    for q in range(2):
        c = rc(
            nz.at[:, :, pl.ds(pl.multiple_of(q * 256 + (1 - core) * LANE, LANE), LANE)],
            no.at[:, :, pl.ds(q * LANE, LANE)],
            o_send.at[q], o_recv.at[q], other_core,
        )
        c.start()
        sent.append(c)

    eye = (
        lax.broadcasted_iota(jnp.int32, (LANE, LANE), 0)
        == lax.broadcasted_iota(jnp.int32, (LANE, LANE), 1)
    )

    def to_lanes(v):
        return jnp.sum(jnp.where(eye, v, 0.0), axis=0, keepdims=True)

    def to_rows(v):
        return jnp.sum(jnp.where(eye, v, 0.0), axis=1, keepdims=True)

    def wide(v):
        return jnp.concatenate([v[q:q + 1, :] for q in range(4)], axis=1)

    scale = LOG2E / (width * EPS)
    lq = jnp.concatenate(
        [to_lanes(jnp.sum(lsq[q * LANE:(q + 1) * LANE, :], axis=1, keepdims=True)) for q in range(4)],
        axis=1,
    )
    for b in range(4):
        rows = slice(b * LANE, (b + 1) * LANE)
        nq = jnp.sum(nsq[rows, :], axis=1, keepdims=True)
        cross[rows, :] = (nq + lq - 2.0 * cross[rows, :]) * scale

    def merge(parts):
        best = jnp.max(parts, axis=0)
        return best + jnp.log2(jnp.sum(jnp.exp2(parts - best[None]), axis=0))

    def merge_rows(parts):
        best = jnp.max(parts, axis=0, keepdims=True)
        return best + jnp.log2(jnp.sum(jnp.exp2(parts - best), axis=0, keepdims=True))

    def lend(step):
        k, zz = step % 2, step // 2
        lanes = pl.ds(pl.multiple_of((1 - xl) * 256 + k * LANE, LANE), LANE)
        for slot, dev in ((zz, (across + k, col)), (zz + 4, (across + k, flip_col))):
            c = rc(nz.at[slot, :, lanes], nx.at[core, slot], p_send.at[k, slot], p_recv.at[core, slot], dev)
            c.start()
            sent.append(c)

    steps = iter(range(6))

    def exchange(buf, mine, peers, ssem, rsem):
        for peer in peers:
            rc(buf.at[mine], buf.at[mine], ssem, rsem, peer).start()
        step = next(steps)
        for piece_at in range(step * 8 // 6, (step + 1) * 8 // 6):
            lend(piece_at)
        k = len(peers)
        rc(buf.at[pl.ds(0, k)], buf.at[pl.ds(0, k)], ssem, rsem, peers[0]).wait_recv()

    g = start_ref[...] * (LOG2E / EPS)
    f = None
    f_rows = None
    for it in range(ITERS):
        for b in range(4):
            parts = []
            for r in range(b * LANE, (b + 1) * LANE, 32):
                s = [g[q:q + 1, :] - cross[r:r + 32, q * LANE:(q + 1) * LANE] for q in range(4)]
                top = jnp.maximum(jnp.maximum(s[0], s[1]), jnp.maximum(s[2], s[3]))
                e = [jnp.exp2(v - top) for v in s]
                parts.append(top + jnp.log2((e[0] + e[1]) + (e[2] + e[3])))
            rowx[it, col, b:b + 1, :] = merge_rows(jnp.concatenate(parts, axis=0).T)
        exchange(rowx.at[it], col, col_peers, r_send.at[it], r_recv.at[it])
        f = -(math.log2(m_total) + merge(rowx[it]))
        f_rows = [to_rows(f[b:b + 1, :]) for b in range(4)]
        parts = []
        for r in range(0, BLK, 64):
            fr = f_rows[r // LANE][r % LANE:r % LANE + 64]
            s = (fr - cross[r:r + 64, :]).reshape(8, 8, BLK)
            top = jnp.max(s, axis=0)
            parts.append(top + jnp.log2(jnp.sum(jnp.exp2(s - top[None]), axis=0)))
        top = parts[0]
        for v in parts[1:]:
            top = jnp.maximum(top, v)
        own = merge_rows(top + jnp.log2(sum(jnp.exp2(v - top) for v in parts)))
        for q in range(4):
            col2[it, row, q:q + 1, :] = own[:, q * LANE:(q + 1) * LANE]
        exchange(col2.at[it], row, row_peers, c2_send.at[it], c2_recv.at[it])
        g = -(math.log2(n_total) + merge(col2[it]))

    npot_ref[...] = f * (EPS / LOG2E)
    lpot_ref[...] = g * (EPS / LOG2E)

    LOW, HIGH = slice(0, HALF), slice(HALF, BLK)
    gw = wide(g)

    def weights(cols):
        for b in range(4):
            rows = slice(b * LANE, (b + 1) * LANE)
            w = m_total * jnp.exp2((f_rows[b] + gw[:, cols]) - cross[rows, cols])
            wt[core, cols, rows] = w.T.astype(BF16)

    def wcopy(j, src, dst, dev):
        return rc(src, dst, w_send.at[j], w_recv.at[j], dev)

    low, high = pl.ds(0, HALF), pl.ds(HALF, HALF)
    copies = []
    weights(HIGH)
    copies.append(wcopy(0, wt.at[core, high], wx.at[core], other_xl))
    copies[-1].start()
    weights(LOW)
    copies.append(wcopy(1, wt.at[core, low], wt.at[core, low], other_core))
    copies[-1].start()
    copies.append(wcopy(2, wt.at[core, high], wt.at[core, high], other_core))
    copies[-1].start()
    for q in range(2):
        rc(no.at[:, :, pl.ds(q * LANE, LANE)], no.at[:, :, pl.ds(q * LANE, LANE)],
           o_send.at[q], o_recv.at[q], other_core).wait_recv()
    wcopy(1, wt.at[core, low], wt.at[1 - core, low], other_core).wait_recv()

    def mine(d, q):
        return nz[d, :, pl.ds(pl.multiple_of(q * 256 + core * LANE, LANE), LANE)]

    def theirs(d, q):
        return no[d, :, pl.ds(pl.multiple_of(q * LANE, LANE), LANE)]

    def partial(rel):
        d = (z + rel) % Z
        part[rel] = jnp.dot(
            wt[core, LOW, :], jnp.concatenate([mine(d, q) for q in (1 - xl, xl)], axis=1),
            preferred_element_type=F32,
        ) + jnp.dot(
            wt[1 - core, LOW, :], jnp.concatenate([theirs(d, q) for q in (1 - xl, xl)], axis=1),
            preferred_element_type=F32,
        )

    def partial_high(rel):
        d = (z + rel) % Z
        parth[rel] = (
            jnp.dot(wt[core, HIGH, :], mine(d, xl), preferred_element_type=F32)
            + jnp.dot(wt[1 - core, HIGH, :], theirs(d, xl), preferred_element_type=F32)
        ) + (
            jnp.dot(wx[0], nx[0, d], preferred_element_type=F32)
            + jnp.dot(wx[1], nx[1, d], preferred_element_type=F32)
        )

    def piece(k, bufs, dr, s):
        ref = bufs[1].at[dr, 4 - s] if k == 2 else bufs[0].at[dr, 4 - s, k]
        return ref.at[pl.ds(dr * LANE, LANE)] if s == 4 else ref

    def ring_copy(k, dr, s):
        ss, rs = (t_send.at[dr, 4 - s], t_recv.at[dr, 4 - s]) if k == 2 else (
            s_send.at[dr, 4 - s, k], s_recv.at[dr, 4 - s, k])
        return rc(
            piece(k, (stage, stageh), dr, s), piece(k, (land, landh), dr, s), ss, rs,
            z_dn if dr == 0 else z_up,
        )

    def own_part(k, rel, rows):
        return parth[rel, rows, :] if k == 2 else part[rel, rows, k * LANE:(k + 1) * LANE]

    def got(k, dr, s, rows):
        v = landh[dr, 4 - s, rows, :] if k == 2 else land[dr, 4 - s, k, rows, :]
        return v.astype(F32)

    def put(k, dr, s, rows, v):
        if k == 2:
            stageh[dr, 4 - s, rows, :] = v.astype(BF16)
        else:
            stage[dr, 4 - s, k, rows, :] = v.astype(BF16)

    ALL = slice(0, HALF)

    def ring_step(k, s):
        for dr in range(2):
            rel = Z - s if dr == 0 else s
            first = slice(dr * LANE, (dr + 1) * LANE)
            other = slice((1 - dr) * LANE, (2 - dr) * LANE)
            if s == 4:
                put(k, dr, s, first, own_part(k, 4, first))
            else:
                ring_copy(k, dr, s + 1).wait_recv()
                if s == 3:
                    put(k, dr, s, first, own_part(k, rel, first) + got(k, dr, 4, first))
                    put(k, dr, s, other, own_part(k, rel, other))
                else:
                    put(k, dr, s, ALL, own_part(k, rel, ALL) + got(k, dr, s + 1, ALL))
            c = ring_copy(k, dr, s)
            c.start()
            sent.append(c)

    def total(k):
        for dr in range(2):
            ring_copy(k, dr, 1).wait_recv()
        return own_part(k, 0, ALL) + (got(k, 0, 1, ALL) + got(k, 1, 1, ALL))

    partial(4)
    ring_step(0, 4)
    ring_step(1, 4)
    partial(5)
    partial(3)
    ring_step(0, 3)
    ring_step(1, 3)
    partial(6)
    partial(2)
    ring_step(0, 2)
    ring_step(1, 2)
    wcopy(0, wt.at[core, high], wx.at[core], other_xl).wait_recv()
    copies.append(wcopy(3, wx.at[core], wx.at[core], other_core))
    copies[-1].start()
    partial(7)
    partial(1)
    wcopy(2, wt.at[core, high], wt.at[1 - core, high], other_core).wait_recv()
    for c in range(2):
        for slot in range(Z):
            rc(nx.at[c, slot], nx.at[c, slot], p_send.at[0, slot], p_recv.at[c, slot], other_xl).wait_recv()
    wcopy(3, wx.at[core], wx.at[1 - core], other_core).wait_recv()
    partial_high(4)
    ring_step(2, 4)
    ring_step(0, 1)
    ring_step(1, 1)
    partial_high(5)
    partial_high(3)
    ring_step(2, 3)
    partial_high(6)
    partial_high(2)
    ring_step(2, 2)
    partial(0)
    xs[...] = total(0)
    xc = rc(xs, xr, x_send.at[0], x_recv.at[0], other_xl)
    xc.start()
    copies.append(xc)
    partial_high(7)
    partial_high(1)
    ring_step(2, 1)
    partial_high(0)
    kept = total(1)
    xc.wait_recv()
    out_ref[:, LOW] = (kept + xr[...]).T
    out_ref[:, HIGH] = total(2).T
    sent.extend(copies)

    for c in sent:
        c.wait_send()
    for it in range(ITERS):
        for buf, k, ssem, rsem in (
            (rowx, 7, r_send, r_recv), (col2, 31, c2_send, c2_recv)
        ):
            ref = buf.at[it, pl.ds(0, k)]
            rc(ref, ref, ssem.at[it], rsem.at[it], z_up).wait_send()


def per_device(n_total, m_total, noise_draw, latent_code, start_potential):
    anyspace = pl.BlockSpec(memory_space=pltpu.HBM)
    vmem = pl.BlockSpec(memory_space=pltpu.VMEM)
    width = 4096
    dma = pltpu.SemaphoreType.DMA

    def body(*refs):
        kernel(n_total, m_total, width, *refs)

    npot, lpot, out = pl.pallas_call(
        body,
        out_shape=(
            jax.ShapeDtypeStruct((4, LANE), F32),
            jax.ShapeDtypeStruct((4, LANE), F32),
            jax.ShapeDtypeStruct((LANE, BLK), F32),
        ),
        in_specs=[anyspace, anyspace, vmem],
        out_specs=(vmem, vmem, vmem),
        scratch_shapes=[
            pltpu.VMEM((8, BLK, BLK), BF16),
            pltpu.VMEM((Z, 2, 2, BLK, LANE), BF16),
            pltpu.VMEM((8, BLK, 2 * LANE), BF16),
            pltpu.VMEM((2, 2, 2, BLK // 4, BLK), BF16),
            pltpu.VMEM((BLK, BLK), F32),
            pltpu.VMEM((BLK, LANE), F32),
            pltpu.VMEM((BLK, LANE), F32),
            pltpu.VMEM((2, BLK, BLK), BF16),
            pltpu.VMEM((2, HALF, BLK), BF16),
            pltpu.VMEM((2, Z, BLK, LANE), BF16),
            pltpu.VMEM((Z, HALF, 2 * LANE), F32),
            pltpu.VMEM((Z, HALF, LANE), F32),
            pltpu.VMEM((2, 4, 2, HALF, LANE), BF16),
            pltpu.VMEM((2, 4, 2, HALF, LANE), BF16),
            pltpu.VMEM((2, 4, HALF, LANE), BF16),
            pltpu.VMEM((2, 4, HALF, LANE), BF16),
            pltpu.VMEM((HALF, LANE), F32),
            pltpu.VMEM((HALF, LANE), F32),
            pltpu.VMEM((ITERS, 8, 4, LANE), F32),
            pltpu.VMEM((ITERS, 32, 4, LANE), F32),
            dma((10,)), dma((10,)),
            dma((2, 2, 2, 2)), dma((2, 2, 2, 2)),
            dma((19,)), dma((19,)),
            dma((2,)), dma((2,)),
            dma((4,)), dma((4,)),
            dma((2, Z)), dma((2, Z)),
            dma((ITERS,)), dma((ITERS,)),
            dma((ITERS,)), dma((ITERS,)),
            dma((2, 4, 2)), dma((2, 4, 2)),
            dma((2, 4)), dma((2, 4)),
            dma((1,)), dma((1,)),
            dma((2,)),
        ],
        compiler_params=pltpu.CompilerParams(
            collective_id=0, has_side_effects=True, vmem_limit_bytes=32 * 1024 * 1024
        ),
    )(noise_draw, latent_code, start_potential.reshape(4, LANE))
    return npot.reshape(BLK), lpot.reshape(BLK), out


def solution(mesh):
    in_specs = (P("row", "col"), P("col", "row"), P("col"))
    out_specs = (P("row"), P("col"), P("row", "col"))

    def whole(noise_draw, latent_code, start_potential):
        def block(a, b, c):
            return per_device(noise_draw.shape[0], latent_code.shape[0], a, b, c)

        return jax.shard_map(
            block, mesh=mesh, in_specs=in_specs, out_specs=out_specs, check_vma=False
        )(noise_draw, latent_code, start_potential)

    return whole
```

```python
import math

import jax
import jax.numpy as jnp
from jax import lax
from jax.experimental import pallas as pl
from jax.experimental.pallas import tpu as pltpu
from jax.sharding import PartitionSpec as P

ITERS = 3
EPS = 0.01
LOG2E = math.log2(math.e)
MESH = pl.DeviceIdType.MESH
F32 = jnp.float32
BF16 = jnp.bfloat16

Z, Y = 8, 4
LANE = 128
BLK = 512
HALF = BLK // 2


def kernel(
    n_total, m_total, width,
    noise_ref, latent_ref, start_ref,
    npot_ref, lpot_ref, out_ref,
    nz, lt, no, relay, cross, nsq, lsq, wt, wx, nx, part, parth, stage, land, stageh, landh, xs, xr, rowx, col2,
    n_send, n_recv, h_send, h_recv, l_send, l_recv, o_send, o_recv, w_send, w_recv,
    p_send, p_recv, r_send, r_recv, c2_send, c2_recv,
    s_send, s_recv, t_send, t_recv, x_send, x_recv, loc,
):
    row = lax.axis_index("row")
    col = lax.axis_index("col")
    z = row // 4
    xl = (row // 2) % 2
    core = row % 2
    y = col // 2
    xh = col % 2
    quad = row % 4

    def ring_z(d):
        return (z + d + Z) % Z

    def ring_y(d):
        return (y + d + Y) % Y

    other_core = (row + 1 - 2 * core, col)
    other_xl = (row + 2 - 4 * xl, col)
    flip_col = col + 1 - 2 * xh
    diagonal = (row + 2 - 4 * xl, flip_col)
    z_up = (ring_z(1) * 4 + quad, col)
    z_dn = (ring_z(-1) * 4 + quad, col)
    y_up = (row, ring_y(1) * 2 + xh)
    y_dn = (row, ring_y(-1) * 2 + xh)
    col_peers = [
        (row, ring_y(dy) * 2 + (1 - xh if dx else xh))
        for dy, dx in ((2, 1), (1, 1), (-1, 1), (2, 0), (0, 1), (1, 0), (-1, 0))
    ]
    across = (row + 2 - 4 * xl) // 2 * 2
    across_quad = ((across + 1 - core) % 4, (across + core) % 4, (quad // 2) * 2 + 1 - core, quad)
    row_peers = [
        (ring_z(d) * 4 + q, col)
        for d in (4, 3, -3, 2, -2, 1, -1, 0) for q in across_quad[:3 if d == 0 else 4]
    ]
    peers = col_peers + row_peers + [(across, flip_col), (across + 1, flip_col)]

    own_n = pltpu.make_async_copy(noise_ref, nz.at[col], loc.at[0])
    own_l = pltpu.make_async_copy(latent_ref, lt.at[z, core, xl], loc.at[1])
    own_n.start()
    own_l.start()

    barrier = pltpu.get_barrier_semaphore()
    for peer in peers:
        pl.semaphore_signal(barrier, inc=1, device_id=peer, device_id_type=MESH)
    cross[...] = jnp.zeros_like(cross)
    nsq[...] = jnp.zeros_like(nsq)
    lsq[...] = jnp.zeros_like(lsq)
    pl.semaphore_wait(barrier, len(peers))

    def rc(src, dst, ssem, rsem, dev):
        return pltpu.make_async_remote_copy(
            src_ref=src, dst_ref=dst, send_sem=ssem, recv_sem=rsem,
            device_id=dev, device_id_type=MESH,
        )

    def nsl(slot, h):
        return nz.at[slot, pl.ds(h * HALF, HALF), :]

    sent = []

    def nsend(slot, h, idx, dev, src=None):
        src = nsl(slot, h) if src is None else src
        c = rc(src, nsl(slot, h), n_send.at[idx], n_recv.at[idx], dev)
        c.start()
        return c

    def own_half(h):
        return noise_ref.at[pl.ds(h * HALF, HALF), :]

    def nwait(slot, h, idx):
        rc(nsl(slot, h), nsl(slot, h), n_send.at[idx], n_recv.at[idx], y_up).wait_recv()

    def lsend(ref, idx, dev, src=None):
        c = rc(ref if src is None else src, ref, l_send.at[idx], l_recv.at[idx], dev)
        c.start()
        sent.append(c)

    def lwait(ref, idx):
        rc(ref, ref, l_send.at[idx], l_recv.at[idx], z_up).wait_recv()

    QUART = HALF // 2

    def slot_of(yy, s):
        return yy * 2 + (xh if s == 0 else 1 - xh)

    def quarter(slot, path, p):
        return nz.at[slot, pl.ds(path * HALF + p * QUART, QUART), :]

    def relay_start(t, path, p):
        if t == 0:
            ref = noise_ref.at[pl.ds(path * HALF + p * QUART, QUART), :]
        else:
            ref = quarter(slot_of(ring_y(2), 0), path, p)
        c = rc(ref, relay.at[t, path, p], h_send.at[0, t, path, p], h_recv.at[0, t, path, p],
               other_xl if path == 0 else diagonal)
        c.start()
        sent.append(c)

    def relay_forward(t, path, p):
        ref = quarter(slot_of(ring_y(2 * t), path), path, p)
        dev = diagonal if path == 0 else other_xl
        buf = relay.at[t, path, p]
        rc(buf, buf, h_send.at[0, t, path, p], h_recv.at[0, t, path, p], dev).wait_recv()
        c = rc(buf, ref, h_send.at[1, t, path, p], h_recv.at[1, t, path, p], dev)
        c.start()
        sent.append(c)

    def relay_end(t, path):
        for p in range(2):
            ref = quarter(slot_of(ring_y(2 * t), 1), path, p)
            rc(ref, ref, h_send.at[1, t, path, p], h_recv.at[1, t, path, p], diagonal).wait_recv()

    own_pair = lt.at[z, core]
    own_block = lt.at[z, core, xl]
    lsend(own_block, 0, other_xl, latent_ref)
    for p in range(2):
        relay_start(0, 0, p)
        relay_start(0, 1, p)
    sent.append(nsend(col, 0, 0, y_up, own_half(0)))
    sent.append(nsend(col, 1, 3, y_dn, own_half(1)))
    lsend(own_block, 1, z_up, latent_ref)
    lsend(own_block, 6, z_dn, latent_ref)

    lwait(lt.at[z, core, 1 - xl], 0)
    lsend(lt.at[z, core, 1 - xl], 2, z_up)
    lsend(lt.at[z, core, 1 - xl], 7, z_dn)
    own_l.wait()
    lsend(own_pair, 11, other_core)

    dn, up = slot_of(ring_y(-1), 0), slot_of(ring_y(1), 0)
    nwait(dn, 0, 0)
    onward_up = nsend(dn, 0, 4, y_up)
    nwait(up, 1, 3)
    onward_dn = nsend(up, 1, 5, y_dn)
    for p in range(2):
        relay_forward(0, 0, p)
        relay_forward(0, 1, p)

    for sgn, base, dev in ((-1, 1, z_up), (1, 6, z_dn)):
        zz = ring_z(sgn)
        lwait(lt.at[zz, core, xl], base)
        lwait(lt.at[zz, core, 1 - xl], base + 1)
        lsend(lt.at[zz, core], base + 2, dev)
        lsend(lt.at[zz, core], 12 + (base == 6), other_core)

    onward_up.wait_send()
    sent.append(nsend(col, 1, 1, y_up, own_half(1)))
    onward_dn.wait_send()
    sent.append(nsend(col, 0, 2, y_dn, own_half(0)))

    nwait(slot_of(ring_y(2), 0), 0, 4)
    relay_start(1, 0, 0)
    relay_start(1, 0, 1)
    nwait(slot_of(ring_y(2), 0), 1, 5)
    relay_start(1, 1, 0)
    relay_start(1, 1, 1)

    for sgn, base, dev in ((-1, 1, z_up), (1, 6, z_dn)):
        zz = ring_z(2 * sgn)
        lwait(lt.at[zz, core], base + 2)
        lsend(lt.at[zz, core], base + 3, dev)
        lsend(lt.at[zz, core], 14 + (base == 6), other_core)

    relay_end(0, 0)
    sent.append(nsend(flip_col, 0, 6, y_up))
    sent.append(nsend(flip_col, 0, 8, y_dn))
    relay_end(0, 1)
    sent.append(nsend(flip_col, 1, 9, y_dn))
    sent.append(nsend(flip_col, 1, 7, y_up))

    for sgn, base, dev in ((-1, 1, z_up), (1, 6, z_dn)):
        zz = ring_z(3 * sgn)
        lwait(lt.at[zz, core], base + 3)
        lsend(lt.at[zz, core, int(base == 6)], base + 4, dev)
        lsend(lt.at[zz, core], 16 + (base == 6), other_core)
    far = ring_z(4)
    lwait(lt.at[far, core, 0], 5)
    lwait(lt.at[far, core, 1], 10)
    lsend(lt.at[far, core], 18, other_core)
    for p in range(2):
        for path in range(2):
            relay_forward(1, path, p)
    for j, d in enumerate((0, -1, 1, -2, 2, -3, 3, 4)):
        lwait(lt.at[ring_z(d), 1 - core], 11 + j)

    def accumulate(slot):
        a = nz[slot]
        b = jnp.concatenate([lt[slot, 0, 0], lt[slot, 1, 0], lt[slot, 0, 1], lt[slot, 1, 1]], axis=1)
        cross[...] += lax.dot_general(a, b, (((1,), (1,)), ((), ())), preferred_element_type=F32)
        a2 = jnp.square(a.astype(F32))
        nsq[...] += (a2[:, 0:128] + a2[:, 128:256]) + (a2[:, 256:384] + a2[:, 384:512])
        b2 = jnp.square(b.astype(F32))
        lsq[...] += (b2[:, 0:128] + b2[:, 128:256]) + (b2[:, 256:384] + b2[:, 384:512])

    def wait_rest(s):
        dn, up = slot_of(ring_y(-1), s), slot_of(ring_y(1), s)
        nwait(dn, 1, 6 * s + 1)
        nwait(up, 0, 6 * s + 2)

    own_n.wait()
    wait_rest(0)

    def set0(k, carry):
        accumulate(((y + k) % Y) * 2 + xh)
        return carry

    lax.fori_loop(0, Y, set0, 0)
    accumulate(flip_col)
    relay_end(1, 0)
    relay_end(1, 1)
    accumulate(slot_of(ring_y(2), 1))
    dn, up = slot_of(ring_y(-1), 1), slot_of(ring_y(1), 1)
    nwait(dn, 0, 6)
    nwait(up, 1, 9)
    wait_rest(1)
    accumulate(dn)
    accumulate(up)

    for q in range(2):
        c = rc(
            nz.at[:, :, pl.ds(pl.multiple_of(q * 256 + (1 - core) * LANE, LANE), LANE)],
            no.at[:, :, pl.ds(q * LANE, LANE)],
            o_send.at[q], o_recv.at[q], other_core,
        )
        c.start()
        sent.append(c)

    eye = (
        lax.broadcasted_iota(jnp.int32, (LANE, LANE), 0)
        == lax.broadcasted_iota(jnp.int32, (LANE, LANE), 1)
    )

    def to_lanes(v):
        return jnp.sum(jnp.where(eye, v, 0.0), axis=0, keepdims=True)

    def to_rows(v):
        return jnp.sum(jnp.where(eye, v, 0.0), axis=1, keepdims=True)

    def wide(v):
        return jnp.concatenate([v[q:q + 1, :] for q in range(4)], axis=1)

    scale = LOG2E / (width * EPS)
    lq = jnp.concatenate(
        [to_lanes(jnp.sum(lsq[q * LANE:(q + 1) * LANE, :], axis=1, keepdims=True)) for q in range(4)],
        axis=1,
    )
    for b in range(4):
        rows = slice(b * LANE, (b + 1) * LANE)
        nq = jnp.sum(nsq[rows, :], axis=1, keepdims=True)
        cross[rows, :] = (nq + lq - 2.0 * cross[rows, :]) * scale

    def merge(parts):
        best = jnp.max(parts, axis=0)
        return best + jnp.log2(jnp.sum(jnp.exp2(parts - best[None]), axis=0))

    def merge_rows(parts):
        best = jnp.max(parts, axis=0, keepdims=True)
        return best + jnp.log2(jnp.sum(jnp.exp2(parts - best), axis=0, keepdims=True))

    def lend(step):
        k, zz = step % 2, step // 2
        lanes = pl.ds(pl.multiple_of((1 - xl) * 256 + k * LANE, LANE), LANE)
        for slot, dev in ((zz, (across + k, col)), (zz + 4, (across + k, flip_col))):
            c = rc(nz.at[slot, :, lanes], nx.at[core, slot], p_send.at[k, slot], p_recv.at[core, slot], dev)
            c.start()
            sent.append(c)

    steps = iter(range(6))

    def exchange(buf, mine, peers, ssem, rsem):
        for peer in peers:
            rc(buf.at[mine], buf.at[mine], ssem, rsem, peer).start()
        step = next(steps)
        for piece_at in range(step * 8 // 6, (step + 1) * 8 // 6):
            lend(piece_at)
        k = len(peers)
        rc(buf.at[pl.ds(0, k)], buf.at[pl.ds(0, k)], ssem, rsem, peers[0]).wait_recv()

    g = start_ref[...] * (LOG2E / EPS)
    f = None
    f_rows = None
    for it in range(ITERS):
        for b in range(4):
            parts = []
            for r in range(b * LANE, (b + 1) * LANE, 32):
                s = [g[q:q + 1, :] - cross[r:r + 32, q * LANE:(q + 1) * LANE] for q in range(4)]
                top = jnp.maximum(jnp.maximum(s[0], s[1]), jnp.maximum(s[2], s[3]))
                e = [jnp.exp2(v - top) for v in s]
                parts.append(top + jnp.log2((e[0] + e[1]) + (e[2] + e[3])))
            rowx[it, col, b:b + 1, :] = merge_rows(jnp.concatenate(parts, axis=0).T)
        exchange(rowx.at[it], col, col_peers, r_send.at[it], r_recv.at[it])
        f = -(math.log2(m_total) + merge(rowx[it]))
        f_rows = [to_rows(f[b:b + 1, :]) for b in range(4)]
        parts = []
        for r in range(0, BLK, 64):
            fr = f_rows[r // LANE][r % LANE:r % LANE + 64]
            s = (fr - cross[r:r + 64, :]).reshape(8, 8, BLK)
            top = jnp.max(s, axis=0)
            parts.append(top + jnp.log2(jnp.sum(jnp.exp2(s - top[None]), axis=0)))
        top = parts[0]
        for v in parts[1:]:
            top = jnp.maximum(top, v)
        own = merge_rows(top + jnp.log2(sum(jnp.exp2(v - top) for v in parts)))
        for q in range(4):
            col2[it, row, q:q + 1, :] = own[:, q * LANE:(q + 1) * LANE]
        exchange(col2.at[it], row, row_peers, c2_send.at[it], c2_recv.at[it])
        g = -(math.log2(n_total) + merge(col2[it]))

    npot_ref[...] = f * (EPS / LOG2E)
    lpot_ref[...] = g * (EPS / LOG2E)

    LOW, HIGH = slice(0, HALF), slice(HALF, BLK)
    gw = wide(g)

    def weights(cols):
        for b in range(4):
            rows = slice(b * LANE, (b + 1) * LANE)
            w = m_total * jnp.exp2((f_rows[b] + gw[:, cols]) - cross[rows, cols])
            wt[core, cols, rows] = w.T.astype(BF16)

    def wcopy(j, src, dst, dev):
        return rc(src, dst, w_send.at[j], w_recv.at[j], dev)

    low, high = pl.ds(0, HALF), pl.ds(HALF, HALF)
    copies = []
    weights(HIGH)
    copies.append(wcopy(0, wt.at[core, high], wx.at[core], other_xl))
    copies[-1].start()
    weights(LOW)
    copies.append(wcopy(1, wt.at[core, low], wt.at[core, low], other_core))
    copies[-1].start()
    copies.append(wcopy(2, wt.at[core, high], wt.at[core, high], other_core))
    copies[-1].start()
    for q in range(2):
        rc(no.at[:, :, pl.ds(q * LANE, LANE)], no.at[:, :, pl.ds(q * LANE, LANE)],
           o_send.at[q], o_recv.at[q], other_core).wait_recv()
    wcopy(1, wt.at[core, low], wt.at[1 - core, low], other_core).wait_recv()

    def mine(d, q):
        return nz[d, :, pl.ds(pl.multiple_of(q * 256 + core * LANE, LANE), LANE)]

    def theirs(d, q):
        return no[d, :, pl.ds(pl.multiple_of(q * LANE, LANE), LANE)]

    def partial(rel):
        d = (z + rel) % Z
        part[rel] = jnp.dot(
            wt[core, LOW, :], jnp.concatenate([mine(d, q) for q in (1 - xl, xl)], axis=1),
            preferred_element_type=F32,
        ) + jnp.dot(
            wt[1 - core, LOW, :], jnp.concatenate([theirs(d, q) for q in (1 - xl, xl)], axis=1),
            preferred_element_type=F32,
        )

    def partial_high(rel):
        d = (z + rel) % Z
        parth[rel] = (
            jnp.dot(wt[core, HIGH, :], mine(d, xl), preferred_element_type=F32)
            + jnp.dot(wt[1 - core, HIGH, :], theirs(d, xl), preferred_element_type=F32)
        ) + (
            jnp.dot(wx[0], nx[0, d], preferred_element_type=F32)
            + jnp.dot(wx[1], nx[1, d], preferred_element_type=F32)
        )

    def piece(k, bufs, dr, s):
        ref = bufs[1].at[dr, 4 - s] if k == 2 else bufs[0].at[dr, 4 - s, k]
        return ref.at[pl.ds(dr * LANE, LANE)] if s == 4 else ref

    def ring_copy(k, dr, s):
        ss, rs = (t_send.at[dr, 4 - s], t_recv.at[dr, 4 - s]) if k == 2 else (
            s_send.at[dr, 4 - s, k], s_recv.at[dr, 4 - s, k])
        return rc(
            piece(k, (stage, stageh), dr, s), piece(k, (land, landh), dr, s), ss, rs,
            z_dn if dr == 0 else z_up,
        )

    def own_part(k, rel, rows):
        return parth[rel, rows, :] if k == 2 else part[rel, rows, k * LANE:(k + 1) * LANE]

    def got(k, dr, s, rows):
        v = landh[dr, 4 - s, rows, :] if k == 2 else land[dr, 4 - s, k, rows, :]
        return v.astype(F32)

    def put(k, dr, s, rows, v):
        if k == 2:
            stageh[dr, 4 - s, rows, :] = v.astype(BF16)
        else:
            stage[dr, 4 - s, k, rows, :] = v.astype(BF16)

    ALL = slice(0, HALF)

    def ring_step(k, s):
        for dr in range(2):
            rel = Z - s if dr == 0 else s
            first = slice(dr * LANE, (dr + 1) * LANE)
            other = slice((1 - dr) * LANE, (2 - dr) * LANE)
            if s == 4:
                put(k, dr, s, first, own_part(k, 4, first))
            else:
                ring_copy(k, dr, s + 1).wait_recv()
                if s == 3:
                    put(k, dr, s, first, own_part(k, rel, first) + got(k, dr, 4, first))
                    put(k, dr, s, other, own_part(k, rel, other))
                else:
                    put(k, dr, s, ALL, own_part(k, rel, ALL) + got(k, dr, s + 1, ALL))
            c = ring_copy(k, dr, s)
            c.start()
            sent.append(c)

    def total(k):
        for dr in range(2):
            ring_copy(k, dr, 1).wait_recv()
        return own_part(k, 0, ALL) + (got(k, 0, 1, ALL) + got(k, 1, 1, ALL))

    partial(4)
    ring_step(0, 4)
    ring_step(1, 4)
    partial(5)
    partial(3)
    ring_step(0, 3)
    ring_step(1, 3)
    partial(6)
    partial(2)
    ring_step(0, 2)
    ring_step(1, 2)
    wcopy(0, wt.at[core, high], wx.at[core], other_xl).wait_recv()
    copies.append(wcopy(3, wx.at[core], wx.at[core], other_core))
    copies[-1].start()
    partial(7)
    partial(1)
    wcopy(2, wt.at[core, high], wt.at[1 - core, high], other_core).wait_recv()
    for c in range(2):
        for slot in range(Z):
            rc(nx.at[c, slot], nx.at[c, slot], p_send.at[0, slot], p_recv.at[c, slot], other_xl).wait_recv()
    wcopy(3, wx.at[core], wx.at[1 - core], other_core).wait_recv()
    partial_high(4)
    ring_step(2, 4)
    ring_step(0, 1)
    ring_step(1, 1)
    partial_high(5)
    partial_high(3)
    ring_step(2, 3)
    partial_high(6)
    partial_high(2)
    ring_step(2, 2)
    partial(0)
    xs[...] = total(0)
    xc = rc(xs, xr, x_send.at[0], x_recv.at[0], other_xl)
    xc.start()
    copies.append(xc)
    partial_high(7)
    partial_high(1)
    ring_step(2, 1)
    partial_high(0)
    kept = total(1)
    xc.wait_recv()
    out_ref[:, LOW] = (kept + xr[...]).T
    out_ref[:, HIGH] = total(2).T
    sent.extend(copies)

    for c in sent:
        c.wait_send()
    for it in range(ITERS):
        for buf, k, ssem, rsem in (
            (rowx, 7, r_send, r_recv), (col2, 31, c2_send, c2_recv)
        ):
            ref = buf.at[it, pl.ds(0, k)]
            rc(ref, ref, ssem.at[it], rsem.at[it], z_up).wait_send()


def per_device(n_total, m_total, noise_draw, latent_code, start_potential):
    anyspace = pl.BlockSpec(memory_space=pltpu.HBM)
    vmem = pl.BlockSpec(memory_space=pltpu.VMEM)
    width = 4096
    dma = pltpu.SemaphoreType.DMA

    def body(*refs):
        kernel(n_total, m_total, width, *refs)

    npot, lpot, out = pl.pallas_call(
        body,
        out_shape=(
            jax.ShapeDtypeStruct((4, LANE), F32),
            jax.ShapeDtypeStruct((4, LANE), F32),
            jax.ShapeDtypeStruct((LANE, BLK), F32),
        ),
        in_specs=[anyspace, anyspace, vmem],
        out_specs=(vmem, vmem, vmem),
        scratch_shapes=[
            pltpu.VMEM((8, BLK, BLK), BF16),
            pltpu.VMEM((Z, 2, 2, BLK, LANE), BF16),
            pltpu.VMEM((8, BLK, 2 * LANE), BF16),
            pltpu.VMEM((2, 2, 2, BLK // 4, BLK), BF16),
            pltpu.VMEM((BLK, BLK), F32),
            pltpu.VMEM((BLK, LANE), F32),
            pltpu.VMEM((BLK, LANE), F32),
            pltpu.VMEM((2, BLK, BLK), BF16),
            pltpu.VMEM((2, HALF, BLK), BF16),
            pltpu.VMEM((2, Z, BLK, LANE), BF16),
            pltpu.VMEM((Z, HALF, 2 * LANE), F32),
            pltpu.VMEM((Z, HALF, LANE), F32),
            pltpu.VMEM((2, 4, 2, HALF, LANE), BF16),
            pltpu.VMEM((2, 4, 2, HALF, LANE), BF16),
            pltpu.VMEM((2, 4, HALF, LANE), BF16),
            pltpu.VMEM((2, 4, HALF, LANE), BF16),
            pltpu.VMEM((HALF, LANE), F32),
            pltpu.VMEM((HALF, LANE), F32),
            pltpu.VMEM((ITERS, 8, 4, LANE), F32),
            pltpu.VMEM((ITERS, 32, 4, LANE), F32),
            dma((10,)), dma((10,)),
            dma((2, 2, 2, 2)), dma((2, 2, 2, 2)),
            dma((19,)), dma((19,)),
            dma((2,)), dma((2,)),
            dma((4,)), dma((4,)),
            dma((2, Z)), dma((2, Z)),
            dma((ITERS,)), dma((ITERS,)),
            dma((ITERS,)), dma((ITERS,)),
            dma((2, 4, 2)), dma((2, 4, 2)),
            dma((2, 4)), dma((2, 4)),
            dma((1,)), dma((1,)),
            dma((2,)),
        ],
        compiler_params=pltpu.CompilerParams(
            collective_id=0, has_side_effects=True, vmem_limit_bytes=54656 * 1024
        ),
    )(noise_draw, latent_code, start_potential.reshape(4, LANE))
    return npot.reshape(BLK), lpot.reshape(BLK), out


def solution(mesh):
    in_specs = (P("row", "col"), P("col", "row"), P("col"))
    out_specs = (P("row"), P("col"), P("row", "col"))

    def whole(noise_draw, latent_code, start_potential):
        def block(a, b, c):
            return per_device(noise_draw.shape[0], latent_code.shape[0], a, b, c)

        return jax.shard_map(
            block, mesh=mesh, in_specs=in_specs, out_specs=out_specs, check_vma=False
        )(noise_draw, latent_code, start_potential)

    return whole
```

```python
import math

import jax
import jax.numpy as jnp
from jax import lax
from jax.experimental import pallas as pl
from jax.experimental.pallas import tpu as pltpu
from jax.sharding import PartitionSpec as P

ITERS = 3
EPS = 0.01
LOG2E = math.log2(math.e)
MESH = pl.DeviceIdType.MESH
F32 = jnp.float32
BF16 = jnp.bfloat16

Z, Y = 8, 4
LANE = 128
BLK = 512
HALF = BLK // 2


def kernel(
    n_total, m_total, width,
    noise_ref, latent_ref, start_ref,
    npot_ref, lpot_ref, out_ref,
    nz, lt, no, relay, cross, nsq, lsq, wt, wx, nx, part, parth, stage, land, stageh, landh, xs, xr, rowx, col2,
    n_send, n_recv, h_send, h_recv, l_send, l_recv, o_send, o_recv, w_send, w_recv,
    p_send, p_recv, r_send, r_recv, c2_send, c2_recv,
    s_send, s_recv, t_send, t_recv, x_send, x_recv, loc,
):
    row = lax.axis_index("row")
    col = lax.axis_index("col")
    z = row // 4
    xl = (row // 2) % 2
    core = row % 2
    y = col // 2
    xh = col % 2
    quad = row % 4

    def ring_z(d):
        return (z + d + Z) % Z

    def ring_y(d):
        return (y + d + Y) % Y

    other_core = (row + 1 - 2 * core, col)
    other_xl = (row + 2 - 4 * xl, col)
    flip_col = col + 1 - 2 * xh
    diagonal = (row + 2 - 4 * xl, flip_col)
    z_up = (ring_z(1) * 4 + quad, col)
    z_dn = (ring_z(-1) * 4 + quad, col)
    y_up = (row, ring_y(1) * 2 + xh)
    y_dn = (row, ring_y(-1) * 2 + xh)
    col_peers = [
        (row, ring_y(dy) * 2 + (1 - xh if dx else xh))
        for dy, dx in ((2, 1), (1, 1), (-1, 1), (2, 0), (0, 1), (1, 0), (-1, 0))
    ]
    across = (row + 2 - 4 * xl) // 2 * 2
    across_quad = ((across + 1 - core) % 4, (across + core) % 4, (quad // 2) * 2 + 1 - core, quad)
    row_peers = [
        (ring_z(d) * 4 + q, col)
        for d in (4, 3, -3, 2, -2, 1, -1, 0) for q in across_quad[:3 if d == 0 else 4]
    ]
    peers = col_peers + row_peers + [(across, flip_col), (across + 1, flip_col)]

    own_n = pltpu.make_async_copy(noise_ref, nz.at[col], loc.at[0])
    own_l = pltpu.make_async_copy(latent_ref, lt.at[z, core, xl], loc.at[1])
    own_n.start()
    own_l.start()

    barrier = pltpu.get_barrier_semaphore()
    for peer in peers:
        pl.semaphore_signal(barrier, inc=1, device_id=peer, device_id_type=MESH)
    cross[...] = jnp.zeros_like(cross)
    nsq[...] = jnp.zeros_like(nsq)
    lsq[...] = jnp.zeros_like(lsq)
    pl.semaphore_wait(barrier, len(peers))

    def rc(src, dst, ssem, rsem, dev):
        return pltpu.make_async_remote_copy(
            src_ref=src, dst_ref=dst, send_sem=ssem, recv_sem=rsem,
            device_id=dev, device_id_type=MESH,
        )

    def nsl(slot, h):
        return nz.at[slot, pl.ds(h * HALF, HALF), :]

    sent = []

    def nsend(slot, h, idx, dev, src=None):
        src = nsl(slot, h) if src is None else src
        c = rc(src, nsl(slot, h), n_send.at[idx], n_recv.at[idx], dev)
        c.start()
        return c

    def own_half(h):
        return noise_ref.at[pl.ds(h * HALF, HALF), :]

    def nwait(slot, h, idx):
        rc(nsl(slot, h), nsl(slot, h), n_send.at[idx], n_recv.at[idx], y_up).wait_recv()

    def lsend(ref, idx, dev, src=None):
        c = rc(ref if src is None else src, ref, l_send.at[idx], l_recv.at[idx], dev)
        c.start()
        sent.append(c)

    def lwait(ref, idx):
        rc(ref, ref, l_send.at[idx], l_recv.at[idx], z_up).wait_recv()

    QUART = HALF // 2

    def slot_of(yy, s):
        return yy * 2 + (xh if s == 0 else 1 - xh)

    def quarter(slot, path, p):
        return nz.at[slot, pl.ds(path * HALF + p * QUART, QUART), :]

    def relay_start(t, path, p):
        if t == 0:
            ref = noise_ref.at[pl.ds(path * HALF + p * QUART, QUART), :]
        else:
            ref = quarter(slot_of(ring_y(2), 0), path, p)
        c = rc(ref, relay.at[t, path, p], h_send.at[0, t, path, p], h_recv.at[0, t, path, p],
               other_xl if path == 0 else diagonal)
        c.start()
        sent.append(c)

    def relay_forward(t, path, p):
        ref = quarter(slot_of(ring_y(2 * t), path), path, p)
        dev = diagonal if path == 0 else other_xl
        buf = relay.at[t, path, p]
        rc(buf, buf, h_send.at[0, t, path, p], h_recv.at[0, t, path, p], dev).wait_recv()
        c = rc(buf, ref, h_send.at[1, t, path, p], h_recv.at[1, t, path, p], dev)
        c.start()
        sent.append(c)

    def relay_end(t, path):
        for p in range(2):
            ref = quarter(slot_of(ring_y(2 * t), 1), path, p)
            rc(ref, ref, h_send.at[1, t, path, p], h_recv.at[1, t, path, p], diagonal).wait_recv()

    own_pair = lt.at[z, core]
    own_block = lt.at[z, core, xl]
    z_dirs = ((0, -1, z_up), (1, 1, z_dn))

    def lat(d, part):
        return lt.at[ring_z(d), core, xl if part == 0 else 1 - xl]

    def lat_forward(step, part, dirs):
        for dr, sgn, dev in dirs:
            block = lat(sgn * step, part)
            lwait(block, 1 + 8 * dr + 2 * (step - 1) + part)
            if step < 3 or part == dr:
                lsend(block, 1 + 8 * dr + 2 * step + part, dev)

    def lat_share(step):
        for dr, sgn, _ in z_dirs:
            lsend(lt.at[ring_z(sgn * step), core], 16 + 2 * step + dr, other_core)

    lsend(own_block, 0, other_xl, latent_ref)
    lsend(own_block, 1, z_up, latent_ref)
    lsend(own_block, 9, z_dn, latent_ref)
    sent.append(nsend(col, 0, 0, y_up, own_half(0)))
    sent.append(nsend(col, 1, 3, y_dn, own_half(1)))

    lwait(lat(0, 1), 0)
    lsend(lat(0, 1), 2, z_up)
    lsend(lat(0, 1), 10, z_dn)
    for p in range(2):
        relay_start(0, 0, p)
        relay_start(0, 1, p)
    lat_forward(1, 0, z_dirs)
    own_l.wait()
    lsend(own_pair, 17, other_core)

    dn, up = slot_of(ring_y(-1), 0), slot_of(ring_y(1), 0)
    nwait(dn, 0, 0)
    onward_up = nsend(dn, 0, 4, y_up)
    nwait(up, 1, 3)
    onward_dn = nsend(up, 1, 5, y_dn)

    lat_forward(1, 1, z_dirs)
    lat_share(1)
    lat_forward(2, 0, z_dirs)
    for p in range(2):
        relay_forward(0, 0, p)
        relay_forward(0, 1, p)
    lat_forward(2, 1, z_dirs)
    lat_share(2)

    onward_up.wait_send()
    sent.append(nsend(col, 1, 1, y_up, own_half(1)))
    onward_dn.wait_send()
    sent.append(nsend(col, 0, 2, y_dn, own_half(0)))

    nwait(slot_of(ring_y(2), 0), 0, 4)
    relay_start(1, 0, 0)
    relay_start(1, 0, 1)
    nwait(slot_of(ring_y(2), 0), 1, 5)
    relay_start(1, 1, 0)
    relay_start(1, 1, 1)

    lat_forward(3, 0, z_dirs)

    relay_end(0, 0)
    sent.append(nsend(flip_col, 0, 6, y_up))
    sent.append(nsend(flip_col, 0, 8, y_dn))
    relay_end(0, 1)
    sent.append(nsend(flip_col, 1, 9, y_dn))
    sent.append(nsend(flip_col, 1, 7, y_up))

    lat_forward(3, 1, z_dirs)
    lat_share(3)
    for p in range(2):
        for path in range(2):
            relay_forward(1, path, p)
    lwait(lat(4, 0), 7)
    lwait(lat(4, 1), 16)
    lsend(lt.at[ring_z(4), core], 24, other_core)
    for j, d in enumerate((0, -1, 1, -2, 2, -3, 3, 4)):
        lwait(lt.at[ring_z(d), 1 - core], 17 + j)

    def accumulate(slot):
        a = nz[slot]
        b = jnp.concatenate([lt[slot, 0, 0], lt[slot, 1, 0], lt[slot, 0, 1], lt[slot, 1, 1]], axis=1)
        cross[...] += lax.dot_general(a, b, (((1,), (1,)), ((), ())), preferred_element_type=F32)
        a2 = jnp.square(a.astype(F32))
        nsq[...] += (a2[:, 0:128] + a2[:, 128:256]) + (a2[:, 256:384] + a2[:, 384:512])
        b2 = jnp.square(b.astype(F32))
        lsq[...] += (b2[:, 0:128] + b2[:, 128:256]) + (b2[:, 256:384] + b2[:, 384:512])

    def wait_rest(s):
        dn, up = slot_of(ring_y(-1), s), slot_of(ring_y(1), s)
        nwait(dn, 1, 6 * s + 1)
        nwait(up, 0, 6 * s + 2)

    own_n.wait()
    wait_rest(0)

    def set0(k, carry):
        accumulate(((y + k) % Y) * 2 + xh)
        return carry

    lax.fori_loop(0, Y, set0, 0)
    accumulate(flip_col)
    relay_end(1, 0)
    relay_end(1, 1)
    accumulate(slot_of(ring_y(2), 1))
    dn, up = slot_of(ring_y(-1), 1), slot_of(ring_y(1), 1)
    nwait(dn, 0, 6)
    nwait(up, 1, 9)
    wait_rest(1)
    accumulate(dn)
    accumulate(up)

    for q in range(2):
        c = rc(
            nz.at[:, :, pl.ds(pl.multiple_of(q * 256 + (1 - core) * LANE, LANE), LANE)],
            no.at[:, :, pl.ds(q * LANE, LANE)],
            o_send.at[q], o_recv.at[q], other_core,
        )
        c.start()
        sent.append(c)

    eye = (
        lax.broadcasted_iota(jnp.int32, (LANE, LANE), 0)
        == lax.broadcasted_iota(jnp.int32, (LANE, LANE), 1)
    )

    def to_lanes(v):
        return jnp.sum(jnp.where(eye, v, 0.0), axis=0, keepdims=True)

    def to_rows(v):
        return jnp.sum(jnp.where(eye, v, 0.0), axis=1, keepdims=True)

    def wide(v):
        return jnp.concatenate([v[q:q + 1, :] for q in range(4)], axis=1)

    scale = LOG2E / (width * EPS)
    lq = jnp.concatenate(
        [to_lanes(jnp.sum(lsq[q * LANE:(q + 1) * LANE, :], axis=1, keepdims=True)) for q in range(4)],
        axis=1,
    )
    for b in range(4):
        rows = slice(b * LANE, (b + 1) * LANE)
        nq = jnp.sum(nsq[rows, :], axis=1, keepdims=True)
        cross[rows, :] = (nq + lq - 2.0 * cross[rows, :]) * scale

    def merge(parts):
        best = jnp.max(parts, axis=0)
        return best + jnp.log2(jnp.sum(jnp.exp2(parts - best[None]), axis=0))

    def merge_rows(parts):
        best = jnp.max(parts, axis=0, keepdims=True)
        return best + jnp.log2(jnp.sum(jnp.exp2(parts - best), axis=0, keepdims=True))

    def lend(step):
        k, zz = step % 2, step // 2
        lanes = pl.ds(pl.multiple_of((1 - xl) * 256 + k * LANE, LANE), LANE)
        for slot, dev in ((zz, (across + k, col)), (zz + 4, (across + k, flip_col))):
            c = rc(nz.at[slot, :, lanes], nx.at[core, slot], p_send.at[k, slot], p_recv.at[core, slot], dev)
            c.start()
            sent.append(c)

    steps = iter(range(6))

    def exchange(buf, mine, peers, ssem, rsem):
        for peer in peers:
            rc(buf.at[mine], buf.at[mine], ssem, rsem, peer).start()
        step = next(steps)
        for piece_at in range(step * 8 // 6, (step + 1) * 8 // 6):
            lend(piece_at)
        k = len(peers)
        rc(buf.at[pl.ds(0, k)], buf.at[pl.ds(0, k)], ssem, rsem, peers[0]).wait_recv()

    g = start_ref[...] * (LOG2E / EPS)
    f = None
    f_rows = None
    for it in range(ITERS):
        for b in range(4):
            parts = []
            for r in range(b * LANE, (b + 1) * LANE, 32):
                s = [g[q:q + 1, :] - cross[r:r + 32, q * LANE:(q + 1) * LANE] for q in range(4)]
                top = jnp.maximum(jnp.maximum(s[0], s[1]), jnp.maximum(s[2], s[3]))
                e = [jnp.exp2(v - top) for v in s]
                parts.append(top + jnp.log2((e[0] + e[1]) + (e[2] + e[3])))
            rowx[it, col, b:b + 1, :] = merge_rows(jnp.concatenate(parts, axis=0).T)
        exchange(rowx.at[it], col, col_peers, r_send.at[it], r_recv.at[it])
        f = -(math.log2(m_total) + merge(rowx[it]))
        f_rows = [to_rows(f[b:b + 1, :]) for b in range(4)]
        parts = []
        for r in range(0, BLK, 64):
            fr = f_rows[r // LANE][r % LANE:r % LANE + 64]
            s = (fr - cross[r:r + 64, :]).reshape(8, 8, BLK)
            top = jnp.max(s, axis=0)
            parts.append(top + jnp.log2(jnp.sum(jnp.exp2(s - top[None]), axis=0)))
        top = parts[0]
        for v in parts[1:]:
            top = jnp.maximum(top, v)
        own = merge_rows(top + jnp.log2(sum(jnp.exp2(v - top) for v in parts)))
        for q in range(4):
            col2[it, row, q:q + 1, :] = own[:, q * LANE:(q + 1) * LANE]
        exchange(col2.at[it], row, row_peers, c2_send.at[it], c2_recv.at[it])
        g = -(math.log2(n_total) + merge(col2[it]))

    npot_ref[...] = f * (EPS / LOG2E)
    lpot_ref[...] = g * (EPS / LOG2E)

    LOW, HIGH = slice(0, HALF), slice(HALF, BLK)
    gw = wide(g)

    def weights(cols):
        for b in range(4):
            rows = slice(b * LANE, (b + 1) * LANE)
            w = m_total * jnp.exp2((f_rows[b] + gw[:, cols]) - cross[rows, cols])
            wt[core, cols, rows] = w.T.astype(BF16)

    def wcopy(j, src, dst, dev):
        return rc(src, dst, w_send.at[j], w_recv.at[j], dev)

    low, high = pl.ds(0, HALF), pl.ds(HALF, HALF)
    copies = []
    weights(HIGH)
    copies.append(wcopy(0, wt.at[core, high], wx.at[core], other_xl))
    copies[-1].start()
    weights(LOW)
    copies.append(wcopy(1, wt.at[core, low], wt.at[core, low], other_core))
    copies[-1].start()
    copies.append(wcopy(2, wt.at[core, high], wt.at[core, high], other_core))
    copies[-1].start()
    for q in range(2):
        rc(no.at[:, :, pl.ds(q * LANE, LANE)], no.at[:, :, pl.ds(q * LANE, LANE)],
           o_send.at[q], o_recv.at[q], other_core).wait_recv()
    wcopy(1, wt.at[core, low], wt.at[1 - core, low], other_core).wait_recv()

    def mine(d, q):
        return nz[d, :, pl.ds(pl.multiple_of(q * 256 + core * LANE, LANE), LANE)]

    def theirs(d, q):
        return no[d, :, pl.ds(pl.multiple_of(q * LANE, LANE), LANE)]

    def partial(rel):
        d = (z + rel) % Z
        part[rel] = jnp.dot(
            wt[core, LOW, :], jnp.concatenate([mine(d, q) for q in (1 - xl, xl)], axis=1),
            preferred_element_type=F32,
        ) + jnp.dot(
            wt[1 - core, LOW, :], jnp.concatenate([theirs(d, q) for q in (1 - xl, xl)], axis=1),
            preferred_element_type=F32,
        )

    def partial_high(rel):
        d = (z + rel) % Z
        parth[rel] = (
            jnp.dot(wt[core, HIGH, :], mine(d, xl), preferred_element_type=F32)
            + jnp.dot(wt[1 - core, HIGH, :], theirs(d, xl), preferred_element_type=F32)
        ) + (
            jnp.dot(wx[0], nx[0, d], preferred_element_type=F32)
            + jnp.dot(wx[1], nx[1, d], preferred_element_type=F32)
        )

    def piece(k, bufs, dr, s):
        ref = bufs[1].at[dr, 4 - s] if k == 2 else bufs[0].at[dr, 4 - s, k]
        return ref.at[pl.ds(dr * LANE, LANE)] if s == 4 else ref

    def ring_copy(k, dr, s):
        ss, rs = (t_send.at[dr, 4 - s], t_recv.at[dr, 4 - s]) if k == 2 else (
            s_send.at[dr, 4 - s, k], s_recv.at[dr, 4 - s, k])
        return rc(
            piece(k, (stage, stageh), dr, s), piece(k, (land, landh), dr, s), ss, rs,
            z_dn if dr == 0 else z_up,
        )

    def own_part(k, rel, rows):
        return parth[rel, rows, :] if k == 2 else part[rel, rows, k * LANE:(k + 1) * LANE]

    def got(k, dr, s, rows):
        v = landh[dr, 4 - s, rows, :] if k == 2 else land[dr, 4 - s, k, rows, :]
        return v.astype(F32)

    def put(k, dr, s, rows, v):
        if k == 2:
            stageh[dr, 4 - s, rows, :] = v.astype(BF16)
        else:
            stage[dr, 4 - s, k, rows, :] = v.astype(BF16)

    ALL = slice(0, HALF)

    def ring_step(k, s):
        for dr in range(2):
            rel = Z - s if dr == 0 else s
            first = slice(dr * LANE, (dr + 1) * LANE)
            other = slice((1 - dr) * LANE, (2 - dr) * LANE)
            if s == 4:
                put(k, dr, s, first, own_part(k, 4, first))
            else:
                ring_copy(k, dr, s + 1).wait_recv()
                if s == 3:
                    put(k, dr, s, first, own_part(k, rel, first) + got(k, dr, 4, first))
                    put(k, dr, s, other, own_part(k, rel, other))
                else:
                    put(k, dr, s, ALL, own_part(k, rel, ALL) + got(k, dr, s + 1, ALL))
            c = ring_copy(k, dr, s)
            c.start()
            sent.append(c)

    def total(k):
        for dr in range(2):
            ring_copy(k, dr, 1).wait_recv()
        return own_part(k, 0, ALL) + (got(k, 0, 1, ALL) + got(k, 1, 1, ALL))

    partial(4)
    ring_step(0, 4)
    ring_step(1, 4)
    partial(5)
    partial(3)
    ring_step(0, 3)
    ring_step(1, 3)
    partial(6)
    partial(2)
    ring_step(0, 2)
    ring_step(1, 2)
    wcopy(0, wt.at[core, high], wx.at[core], other_xl).wait_recv()
    copies.append(wcopy(3, wx.at[core], wx.at[core], other_core))
    copies[-1].start()
    partial(7)
    partial(1)
    wcopy(2, wt.at[core, high], wt.at[1 - core, high], other_core).wait_recv()
    for c in range(2):
        for slot in range(Z):
            rc(nx.at[c, slot], nx.at[c, slot], p_send.at[0, slot], p_recv.at[c, slot], other_xl).wait_recv()
    wcopy(3, wx.at[core], wx.at[1 - core], other_core).wait_recv()
    partial_high(4)
    ring_step(2, 4)
    ring_step(0, 1)
    ring_step(1, 1)
    partial_high(5)
    partial_high(3)
    ring_step(2, 3)
    partial_high(6)
    partial_high(2)
    ring_step(2, 2)
    partial(0)
    xs[...] = total(0)
    xc = rc(xs, xr, x_send.at[0], x_recv.at[0], other_xl)
    xc.start()
    copies.append(xc)
    partial_high(7)
    partial_high(1)
    ring_step(2, 1)
    partial_high(0)
    kept = total(1)
    xc.wait_recv()
    out_ref[:, LOW] = (kept + xr[...]).T
    out_ref[:, HIGH] = total(2).T
    sent.extend(copies)

    for c in sent:
        c.wait_send()
    for it in range(ITERS):
        for buf, k, ssem, rsem in (
            (rowx, 7, r_send, r_recv), (col2, 31, c2_send, c2_recv)
        ):
            ref = buf.at[it, pl.ds(0, k)]
            rc(ref, ref, ssem.at[it], rsem.at[it], z_up).wait_send()


def per_device(n_total, m_total, noise_draw, latent_code, start_potential):
    anyspace = pl.BlockSpec(memory_space=pltpu.HBM)
    vmem = pl.BlockSpec(memory_space=pltpu.VMEM)
    width = 4096
    dma = pltpu.SemaphoreType.DMA

    def body(*refs):
        kernel(n_total, m_total, width, *refs)

    npot, lpot, out = pl.pallas_call(
        body,
        out_shape=(
            jax.ShapeDtypeStruct((4, LANE), F32),
            jax.ShapeDtypeStruct((4, LANE), F32),
            jax.ShapeDtypeStruct((LANE, BLK), F32),
        ),
        in_specs=[anyspace, anyspace, vmem],
        out_specs=(vmem, vmem, vmem),
        scratch_shapes=[
            pltpu.VMEM((8, BLK, BLK), BF16),
            pltpu.VMEM((Z, 2, 2, BLK, LANE), BF16),
            pltpu.VMEM((8, BLK, 2 * LANE), BF16),
            pltpu.VMEM((2, 2, 2, BLK // 4, BLK), BF16),
            pltpu.VMEM((BLK, BLK), F32),
            pltpu.VMEM((BLK, LANE), F32),
            pltpu.VMEM((BLK, LANE), F32),
            pltpu.VMEM((2, BLK, BLK), BF16),
            pltpu.VMEM((2, HALF, BLK), BF16),
            pltpu.VMEM((2, Z, BLK, LANE), BF16),
            pltpu.VMEM((Z, HALF, 2 * LANE), F32),
            pltpu.VMEM((Z, HALF, LANE), F32),
            pltpu.VMEM((2, 4, 2, HALF, LANE), BF16),
            pltpu.VMEM((2, 4, 2, HALF, LANE), BF16),
            pltpu.VMEM((2, 4, HALF, LANE), BF16),
            pltpu.VMEM((2, 4, HALF, LANE), BF16),
            pltpu.VMEM((HALF, LANE), F32),
            pltpu.VMEM((HALF, LANE), F32),
            pltpu.VMEM((ITERS, 8, 4, LANE), F32),
            pltpu.VMEM((ITERS, 32, 4, LANE), F32),
            dma((10,)), dma((10,)),
            dma((2, 2, 2, 2)), dma((2, 2, 2, 2)),
            dma((25,)), dma((25,)),
            dma((2,)), dma((2,)),
            dma((4,)), dma((4,)),
            dma((2, Z)), dma((2, Z)),
            dma((ITERS,)), dma((ITERS,)),
            dma((ITERS,)), dma((ITERS,)),
            dma((2, 4, 2)), dma((2, 4, 2)),
            dma((2, 4)), dma((2, 4)),
            dma((1,)), dma((1,)),
            dma((2,)),
        ],
        compiler_params=pltpu.CompilerParams(
            collective_id=0, has_side_effects=True, vmem_limit_bytes=54656 * 1024
        ),
    )(noise_draw, latent_code, start_potential.reshape(4, LANE))
    return npot.reshape(BLK), lpot.reshape(BLK), out


def solution(mesh):
    in_specs = (P("row", "col"), P("col", "row"), P("col"))
    out_specs = (P("row"), P("col"), P("row", "col"))

    def whole(noise_draw, latent_code, start_potential):
        def block(a, b, c):
            return per_device(noise_draw.shape[0], latent_code.shape[0], a, b, c)

        return jax.shard_map(
            block, mesh=mesh, in_specs=in_specs, out_specs=out_specs, check_vma=False
        )(noise_draw, latent_code, start_potential)

    return whole
```

```python
import math

import jax
import jax.numpy as jnp
from jax import lax
from jax.experimental import pallas as pl
from jax.experimental.pallas import tpu as pltpu
from jax.sharding import PartitionSpec as P

ITERS = 3
EPS = 0.01
LOG2E = math.log2(math.e)
MESH = pl.DeviceIdType.MESH
F32 = jnp.float32
BF16 = jnp.bfloat16

Z, Y = 8, 4
LANE = 128
BLK = 512
HALF = BLK // 2


def kernel(
    n_total, m_total, width,
    noise_ref, latent_ref, start_ref,
    npot_ref, lpot_ref, out_ref,
    nz, lt, no, relay, cross, nsq, lsq, wt, wx, nx, part, parth, stage, land, stageh, landh, xs, xr, rowx, col2,
    q_send, q_recv, n_send, n_recv, h_send, h_recv, l_send, l_recv, o_send, o_recv, w_send, w_recv,
    p_send, p_recv, r_send, r_recv, c2_send, c2_recv,
    s_send, s_recv, t_send, t_recv, x_send, x_recv, loc,
):
    row = lax.axis_index("row")
    col = lax.axis_index("col")
    z = row // 4
    xl = (row // 2) % 2
    core = row % 2
    y = col // 2
    xh = col % 2
    quad = row % 4

    def ring_z(d):
        return (z + d + Z) % Z

    def ring_y(d):
        return (y + d + Y) % Y

    other_core = (row + 1 - 2 * core, col)
    other_xl = (row + 2 - 4 * xl, col)
    flip_col = col + 1 - 2 * xh
    diagonal = (row + 2 - 4 * xl, flip_col)
    z_up = (ring_z(1) * 4 + quad, col)
    z_dn = (ring_z(-1) * 4 + quad, col)
    y_up = (row, ring_y(1) * 2 + xh)
    y_dn = (row, ring_y(-1) * 2 + xh)
    col_peers = [
        (row, ring_y(dy) * 2 + (1 - xh if dx else xh))
        for dy, dx in ((2, 1), (1, 1), (-1, 1), (2, 0), (0, 1), (1, 0), (-1, 0))
    ]
    across = (row + 2 - 4 * xl) // 2 * 2
    across_quad = ((across + 1 - core) % 4, (across + core) % 4, (quad // 2) * 2 + 1 - core, quad)
    row_peers = [
        (ring_z(d) * 4 + q, col)
        for d in (4, 3, -3, 2, -2, 1, -1, 0) for q in across_quad[:3 if d == 0 else 4]
    ]
    peers = col_peers + row_peers + [(across, flip_col), (across + 1, flip_col)]

    own_n = pltpu.make_async_copy(noise_ref, nz.at[col], loc.at[0])
    own_l = pltpu.make_async_copy(latent_ref, lt.at[z, core, xl], loc.at[1])
    own_n.start()
    own_l.start()

    barrier = pltpu.get_barrier_semaphore()
    for peer in peers:
        pl.semaphore_signal(barrier, inc=1, device_id=peer, device_id_type=MESH)
    cross[...] = jnp.zeros_like(cross)
    pl.semaphore_wait(barrier, len(peers))

    def rc(src, dst, ssem, rsem, dev):
        return pltpu.make_async_remote_copy(
            src_ref=src, dst_ref=dst, send_sem=ssem, recv_sem=rsem,
            device_id=dev, device_id_type=MESH,
        )

    def nsl(slot, h):
        return nz.at[slot, pl.ds(h * HALF, HALF), :]

    sent = []

    def nsend(slot, h, idx, dev, src=None):
        src = nsl(slot, h) if src is None else src
        c = rc(src, nsl(slot, h), n_send.at[idx], n_recv.at[idx], dev)
        c.start()
        return c

    def own_half(h):
        return noise_ref.at[pl.ds(h * HALF, HALF), :]

    def nwait(slot, h, idx):
        rc(nsl(slot, h), nsl(slot, h), n_send.at[idx], n_recv.at[idx], y_up).wait_recv()

    def lsend(ref, idx, dev, src=None):
        c = rc(ref if src is None else src, ref, l_send.at[idx], l_recv.at[idx], dev)
        c.start()
        sent.append(c)

    def lwait(ref, idx):
        rc(ref, ref, l_send.at[idx], l_recv.at[idx], z_up).wait_recv()

    QUART = HALF // 2

    def slot_of(yy, s):
        return yy * 2 + (xh if s == 0 else 1 - xh)

    def quarter(slot, path, p):
        return nz.at[slot, pl.ds(path * HALF + p * QUART, QUART), :]

    def relay_start(t, path, p):
        if t == 0:
            ref = noise_ref.at[pl.ds(path * HALF + p * QUART, QUART), :]
        else:
            ref = quarter(slot_of(ring_y(2), 0), path, p)
        c = rc(ref, relay.at[t, path, p], h_send.at[0, t, path, p], h_recv.at[0, t, path, p],
               other_xl if path == 0 else diagonal)
        c.start()
        sent.append(c)

    def relay_forward(t, path, p):
        ref = quarter(slot_of(ring_y(2 * t), path), path, p)
        dev = diagonal if path == 0 else other_xl
        buf = relay.at[t, path, p]
        rc(buf, buf, h_send.at[0, t, path, p], h_recv.at[0, t, path, p], dev).wait_recv()
        c = rc(buf, ref, h_send.at[1, t, path, p], h_recv.at[1, t, path, p], dev)
        c.start()
        sent.append(c)

    def relay_end(t, path):
        for p in range(2):
            ref = quarter(slot_of(ring_y(2 * t), 1), path, p)
            rc(ref, ref, h_send.at[1, t, path, p], h_recv.at[1, t, path, p], diagonal).wait_recv()

    own_pair = lt.at[z, core]
    own_block = lt.at[z, core, xl]
    z_dirs = ((0, -1, z_up), (1, 1, z_dn))

    def lat(d, part):
        return lt.at[ring_z(d), core, xl if part == 0 else 1 - xl]

    def lat_forward(step, part, dirs):
        for dr, sgn, dev in dirs:
            block = lat(sgn * step, part)
            lwait(block, 1 + 8 * dr + 2 * (step - 1) + part)
            if step < 3 or part == dr:
                lsend(block, 1 + 8 * dr + 2 * step + part, dev)

    def lat_share(step):
        for dr, sgn, _ in z_dirs:
            lsend(lt.at[ring_z(sgn * step), core], 16 + 2 * step + dr, other_core)

    lsend(own_block, 0, other_xl, latent_ref)
    lsend(own_block, 1, z_up, latent_ref)
    lsend(own_block, 9, z_dn, latent_ref)
    sent.append(nsend(col, 0, 0, y_up, own_half(0)))
    sent.append(nsend(col, 1, 3, y_dn, own_half(1)))

    own_n.wait()
    own_l.wait()
    for b in range(4):
        rows = slice(b * LANE, (b + 1) * LANE)
        n2 = jnp.square(nz[col, rows, :].astype(F32))
        n2 = (n2[:, 0:128] + n2[:, 128:256]) + (n2[:, 256:384] + n2[:, 384:512])
        nsq[col, b:b + 1, :] = jnp.sum(n2.T, axis=0, keepdims=True)
        l2 = jnp.square(lt[z, core, xl, rows, :].astype(F32))
        lsq[row, b:b + 1, :] = jnp.sum(l2.T, axis=0, keepdims=True)

    lwait(lat(0, 1), 0)
    lsend(lat(0, 1), 2, z_up)
    lsend(lat(0, 1), 10, z_dn)
    for p in range(2):
        relay_start(0, 0, p)
        relay_start(0, 1, p)
    lat_forward(1, 0, z_dirs)
    lsend(own_pair, 17, other_core)

    dn, up = slot_of(ring_y(-1), 0), slot_of(ring_y(1), 0)
    nwait(dn, 0, 0)
    onward_up = nsend(dn, 0, 4, y_up)
    nwait(up, 1, 3)
    onward_dn = nsend(up, 1, 5, y_dn)

    lat_forward(1, 1, z_dirs)
    lat_share(1)
    for peer in col_peers:
        rc(nsq.at[col], nsq.at[col], q_send.at[0], q_recv.at[0], peer).start()
    for peer in row_peers:
        rc(lsq.at[row], lsq.at[row], q_send.at[1], q_recv.at[1], peer).start()
    lat_forward(2, 0, z_dirs)
    for p in range(2):
        relay_forward(0, 0, p)
        relay_forward(0, 1, p)
    lat_forward(2, 1, z_dirs)
    lat_share(2)

    onward_up.wait_send()
    sent.append(nsend(col, 1, 1, y_up, own_half(1)))
    onward_dn.wait_send()
    sent.append(nsend(col, 0, 2, y_dn, own_half(0)))

    nwait(slot_of(ring_y(2), 0), 0, 4)
    relay_start(1, 0, 0)
    relay_start(1, 0, 1)
    nwait(slot_of(ring_y(2), 0), 1, 5)
    relay_start(1, 1, 0)
    relay_start(1, 1, 1)

    lat_forward(3, 0, z_dirs)

    relay_end(0, 0)
    sent.append(nsend(flip_col, 0, 6, y_up))
    sent.append(nsend(flip_col, 0, 8, y_dn))
    relay_end(0, 1)
    sent.append(nsend(flip_col, 1, 9, y_dn))
    sent.append(nsend(flip_col, 1, 7, y_up))

    lat_forward(3, 1, z_dirs)
    lat_share(3)
    for p in range(2):
        for path in range(2):
            relay_forward(1, path, p)
    lwait(lat(4, 0), 7)
    lwait(lat(4, 1), 16)
    lsend(lt.at[ring_z(4), core], 24, other_core)
    for j, d in enumerate((0, -1, 1, -2, 2, -3, 3, 4)):
        lwait(lt.at[ring_z(d), 1 - core], 17 + j)

    def accumulate(slot):
        a = nz[slot]
        b = jnp.concatenate([lt[slot, 0, 0], lt[slot, 1, 0], lt[slot, 0, 1], lt[slot, 1, 1]], axis=1)
        cross[...] += lax.dot_general(a, b, (((1,), (1,)), ((), ())), preferred_element_type=F32)

    def wait_rest(s):
        dn, up = slot_of(ring_y(-1), s), slot_of(ring_y(1), s)
        nwait(dn, 1, 6 * s + 1)
        nwait(up, 0, 6 * s + 2)

    wait_rest(0)

    def set0(k, carry):
        accumulate(((y + k) % Y) * 2 + xh)
        return carry

    lax.fori_loop(0, Y, set0, 0)
    accumulate(flip_col)
    relay_end(1, 0)
    relay_end(1, 1)
    accumulate(slot_of(ring_y(2), 1))
    dn, up = slot_of(ring_y(-1), 1), slot_of(ring_y(1), 1)
    nwait(dn, 0, 6)
    nwait(up, 1, 9)
    wait_rest(1)
    accumulate(dn)
    accumulate(up)

    for q in range(2):
        c = rc(
            nz.at[:, :, pl.ds(pl.multiple_of(q * 256 + (1 - core) * LANE, LANE), LANE)],
            no.at[:, :, pl.ds(q * LANE, LANE)],
            o_send.at[q], o_recv.at[q], other_core,
        )
        c.start()
        sent.append(c)

    eye = (
        lax.broadcasted_iota(jnp.int32, (LANE, LANE), 0)
        == lax.broadcasted_iota(jnp.int32, (LANE, LANE), 1)
    )

    def to_rows(v):
        return jnp.sum(jnp.where(eye, v, 0.0), axis=1, keepdims=True)

    def wide(v):
        return jnp.concatenate([v[q:q + 1, :] for q in range(4)], axis=1)

    scale = LOG2E / (width * EPS)
    rc(nsq.at[pl.ds(0, 7)], nsq.at[pl.ds(0, 7)], q_send.at[0], q_recv.at[0], z_up).wait_recv()
    rc(lsq.at[pl.ds(0, 31)], lsq.at[pl.ds(0, 31)], q_send.at[1], q_recv.at[1], z_up).wait_recv()
    nq = jnp.sum(nsq[...], axis=0)
    lq = wide(jnp.sum(lsq[...], axis=0))
    for b in range(4):
        rows = slice(b * LANE, (b + 1) * LANE)
        cross[rows, :] = (to_rows(nq[b:b + 1, :]) + lq - 2.0 * cross[rows, :]) * scale

    def merge(parts):
        best = jnp.max(parts, axis=0)
        return best + jnp.log2(jnp.sum(jnp.exp2(parts - best[None]), axis=0))

    def merge_rows(parts):
        best = jnp.max(parts, axis=0, keepdims=True)
        return best + jnp.log2(jnp.sum(jnp.exp2(parts - best), axis=0, keepdims=True))

    def lend(step):
        k, zz = step % 2, step // 2
        lanes = pl.ds(pl.multiple_of((1 - xl) * 256 + k * LANE, LANE), LANE)
        for slot, dev in ((zz, (across + k, col)), (zz + 4, (across + k, flip_col))):
            c = rc(nz.at[slot, :, lanes], nx.at[core, slot], p_send.at[k, slot], p_recv.at[core, slot], dev)
            c.start()
            sent.append(c)

    steps = iter(range(6))

    def exchange(buf, mine, peers, ssem, rsem):
        for peer in peers:
            rc(buf.at[mine], buf.at[mine], ssem, rsem, peer).start()
        step = next(steps)
        for piece_at in range(step * 8 // 6, (step + 1) * 8 // 6):
            lend(piece_at)
        k = len(peers)
        rc(buf.at[pl.ds(0, k)], buf.at[pl.ds(0, k)], ssem, rsem, peers[0]).wait_recv()

    g = start_ref[...] * (LOG2E / EPS)
    f = None
    f_rows = None
    for it in range(ITERS):
        for b in range(4):
            parts = []
            for r in range(b * LANE, (b + 1) * LANE, 32):
                s = [g[q:q + 1, :] - cross[r:r + 32, q * LANE:(q + 1) * LANE] for q in range(4)]
                top = jnp.maximum(jnp.maximum(s[0], s[1]), jnp.maximum(s[2], s[3]))
                e = [jnp.exp2(v - top) for v in s]
                parts.append(top + jnp.log2((e[0] + e[1]) + (e[2] + e[3])))
            rowx[it, col, b:b + 1, :] = merge_rows(jnp.concatenate(parts, axis=0).T)
        exchange(rowx.at[it], col, col_peers, r_send.at[it], r_recv.at[it])
        f = -(math.log2(m_total) + merge(rowx[it]))
        f_rows = [to_rows(f[b:b + 1, :]) for b in range(4)]
        parts = []
        for r in range(0, BLK, 64):
            fr = f_rows[r // LANE][r % LANE:r % LANE + 64]
            s = (fr - cross[r:r + 64, :]).reshape(8, 8, BLK)
            top = jnp.max(s, axis=0)
            parts.append(top + jnp.log2(jnp.sum(jnp.exp2(s - top[None]), axis=0)))
        top = parts[0]
        for v in parts[1:]:
            top = jnp.maximum(top, v)
        own = merge_rows(top + jnp.log2(sum(jnp.exp2(v - top) for v in parts)))
        for q in range(4):
            col2[it, row, q:q + 1, :] = own[:, q * LANE:(q + 1) * LANE]
        exchange(col2.at[it], row, row_peers, c2_send.at[it], c2_recv.at[it])
        g = -(math.log2(n_total) + merge(col2[it]))

    npot_ref[...] = f * (EPS / LOG2E)
    lpot_ref[...] = g * (EPS / LOG2E)

    LOW, HIGH = slice(0, HALF), slice(HALF, BLK)
    gw = wide(g)

    def weights(cols):
        for b in range(4):
            rows = slice(b * LANE, (b + 1) * LANE)
            w = m_total * jnp.exp2((f_rows[b] + gw[:, cols]) - cross[rows, cols])
            wt[core, cols, rows] = w.T.astype(BF16)

    def wcopy(j, src, dst, dev):
        return rc(src, dst, w_send.at[j], w_recv.at[j], dev)

    low, high = pl.ds(0, HALF), pl.ds(HALF, HALF)
    copies = []
    weights(LOW)
    copies.append(wcopy(1, wt.at[core, low], wt.at[core, low], other_core))
    copies[-1].start()
    weights(HIGH)
    copies.append(wcopy(0, wt.at[core, high], wx.at[core], other_xl))
    copies[-1].start()
    copies.append(wcopy(2, wt.at[core, high], wt.at[core, high], other_core))
    copies[-1].start()

    def mine(d, q):
        return nz[d, :, pl.ds(pl.multiple_of(q * 256 + core * LANE, LANE), LANE)]

    def theirs(d, q):
        return no[d, :, pl.ds(pl.multiple_of(q * LANE, LANE), LANE)]

    def partial_own(rel):
        d = (z + rel) % Z
        part[rel] = jnp.dot(
            wt[core, LOW, :], jnp.concatenate([mine(d, q) for q in (1 - xl, xl)], axis=1),
            preferred_element_type=F32,
        )

    def partial_other(rel):
        d = (z + rel) % Z
        part[rel] += jnp.dot(
            wt[1 - core, LOW, :], jnp.concatenate([theirs(d, q) for q in (1 - xl, xl)], axis=1),
            preferred_element_type=F32,
        )

    def partial(rel):
        partial_own(rel)
        partial_other(rel)

    def partial_high(rel):
        d = (z + rel) % Z
        parth[rel] = (
            jnp.dot(wt[core, HIGH, :], mine(d, xl), preferred_element_type=F32)
            + jnp.dot(wt[1 - core, HIGH, :], theirs(d, xl), preferred_element_type=F32)
        ) + (
            jnp.dot(wx[0], nx[0, d], preferred_element_type=F32)
            + jnp.dot(wx[1], nx[1, d], preferred_element_type=F32)
        )

    def piece(k, bufs, dr, s):
        ref = bufs[1].at[dr, 4 - s] if k == 2 else bufs[0].at[dr, 4 - s, k]
        return ref.at[pl.ds(dr * LANE, LANE)] if s == 4 else ref

    def ring_copy(k, dr, s):
        ss, rs = (t_send.at[dr, 4 - s], t_recv.at[dr, 4 - s]) if k == 2 else (
            s_send.at[dr, 4 - s, k], s_recv.at[dr, 4 - s, k])
        return rc(
            piece(k, (stage, stageh), dr, s), piece(k, (land, landh), dr, s), ss, rs,
            z_dn if dr == 0 else z_up,
        )

    def own_part(k, rel, rows):
        return parth[rel, rows, :] if k == 2 else part[rel, rows, k * LANE:(k + 1) * LANE]

    def got(k, dr, s, rows):
        v = landh[dr, 4 - s, rows, :] if k == 2 else land[dr, 4 - s, k, rows, :]
        return v.astype(F32)

    def put(k, dr, s, rows, v):
        if k == 2:
            stageh[dr, 4 - s, rows, :] = v.astype(BF16)
        else:
            stage[dr, 4 - s, k, rows, :] = v.astype(BF16)

    ALL = slice(0, HALF)

    def ring_step(k, s):
        for dr in range(2):
            rel = Z - s if dr == 0 else s
            first = slice(dr * LANE, (dr + 1) * LANE)
            other = slice((1 - dr) * LANE, (2 - dr) * LANE)
            if s == 4:
                put(k, dr, s, first, own_part(k, 4, first))
            else:
                ring_copy(k, dr, s + 1).wait_recv()
                if s == 3:
                    put(k, dr, s, first, own_part(k, rel, first) + got(k, dr, 4, first))
                    put(k, dr, s, other, own_part(k, rel, other))
                else:
                    put(k, dr, s, ALL, own_part(k, rel, ALL) + got(k, dr, s + 1, ALL))
            c = ring_copy(k, dr, s)
            c.start()
            sent.append(c)

    def total(k):
        for dr in range(2):
            ring_copy(k, dr, 1).wait_recv()
        return own_part(k, 0, ALL) + (got(k, 0, 1, ALL) + got(k, 1, 1, ALL))

    for rel in (4, 5, 3):
        partial_own(rel)
    for q in range(2):
        rc(no.at[:, :, pl.ds(q * LANE, LANE)], no.at[:, :, pl.ds(q * LANE, LANE)],
           o_send.at[q], o_recv.at[q], other_core).wait_recv()
    wcopy(1, wt.at[core, low], wt.at[1 - core, low], other_core).wait_recv()
    partial_other(4)
    ring_step(0, 4)
    ring_step(1, 4)
    partial_other(5)
    partial_other(3)
    ring_step(0, 3)
    ring_step(1, 3)
    partial(6)
    partial(2)
    ring_step(0, 2)
    ring_step(1, 2)
    wcopy(0, wt.at[core, high], wx.at[core], other_xl).wait_recv()
    copies.append(wcopy(3, wx.at[core], wx.at[core], other_core))
    copies[-1].start()
    partial(7)
    partial(1)
    wcopy(2, wt.at[core, high], wt.at[1 - core, high], other_core).wait_recv()
    for c in range(2):
        for slot in range(Z):
            rc(nx.at[c, slot], nx.at[c, slot], p_send.at[0, slot], p_recv.at[c, slot], other_xl).wait_recv()
    wcopy(3, wx.at[core], wx.at[1 - core], other_core).wait_recv()
    partial_high(4)
    ring_step(2, 4)
    ring_step(0, 1)
    ring_step(1, 1)
    partial_high(5)
    partial_high(3)
    ring_step(2, 3)
    partial_high(6)
    partial_high(2)
    ring_step(2, 2)
    partial(0)
    xs[...] = total(0)
    xc = rc(xs, xr, x_send.at[0], x_recv.at[0], other_xl)
    xc.start()
    copies.append(xc)
    partial_high(7)
    partial_high(1)
    ring_step(2, 1)
    partial_high(0)
    kept = total(1)
    xc.wait_recv()
    out_ref[:, LOW] = (kept + xr[...]).T
    out_ref[:, HIGH] = total(2).T
    sent.extend(copies)

    for j, (buf, k) in enumerate(((nsq, 7), (lsq, 31))):
        ref = buf.at[pl.ds(0, k)]
        rc(ref, ref, q_send.at[j], q_recv.at[j], z_up).wait_send()
    for c in sent:
        c.wait_send()
    for it in range(ITERS):
        for buf, k, ssem, rsem in (
            (rowx, 7, r_send, r_recv), (col2, 31, c2_send, c2_recv)
        ):
            ref = buf.at[it, pl.ds(0, k)]
            rc(ref, ref, ssem.at[it], rsem.at[it], z_up).wait_send()


def per_device(n_total, m_total, noise_draw, latent_code, start_potential):
    anyspace = pl.BlockSpec(memory_space=pltpu.HBM)
    vmem = pl.BlockSpec(memory_space=pltpu.VMEM)
    width = 4096
    dma = pltpu.SemaphoreType.DMA

    def body(*refs):
        kernel(n_total, m_total, width, *refs)

    npot, lpot, out = pl.pallas_call(
        body,
        out_shape=(
            jax.ShapeDtypeStruct((4, LANE), F32),
            jax.ShapeDtypeStruct((4, LANE), F32),
            jax.ShapeDtypeStruct((LANE, BLK), F32),
        ),
        in_specs=[anyspace, anyspace, vmem],
        out_specs=(vmem, vmem, vmem),
        scratch_shapes=[
            pltpu.VMEM((8, BLK, BLK), BF16),
            pltpu.VMEM((Z, 2, 2, BLK, LANE), BF16),
            pltpu.VMEM((8, BLK, 2 * LANE), BF16),
            pltpu.VMEM((2, 2, 2, BLK // 4, BLK), BF16),
            pltpu.VMEM((BLK, BLK), F32),
            pltpu.VMEM((8, 4, LANE), F32),
            pltpu.VMEM((32, 4, LANE), F32),
            pltpu.VMEM((2, BLK, BLK), BF16),
            pltpu.VMEM((2, HALF, BLK), BF16),
            pltpu.VMEM((2, Z, BLK, LANE), BF16),
            pltpu.VMEM((Z, HALF, 2 * LANE), F32),
            pltpu.VMEM((Z, HALF, LANE), F32),
            pltpu.VMEM((2, 4, 2, HALF, LANE), BF16),
            pltpu.VMEM((2, 4, 2, HALF, LANE), BF16),
            pltpu.VMEM((2, 4, HALF, LANE), BF16),
            pltpu.VMEM((2, 4, HALF, LANE), BF16),
            pltpu.VMEM((HALF, LANE), F32),
            pltpu.VMEM((HALF, LANE), F32),
            pltpu.VMEM((ITERS, 8, 4, LANE), F32),
            pltpu.VMEM((ITERS, 32, 4, LANE), F32),
            dma((2,)), dma((2,)),
            dma((10,)), dma((10,)),
            dma((2, 2, 2, 2)), dma((2, 2, 2, 2)),
            dma((25,)), dma((25,)),
            dma((2,)), dma((2,)),
            dma((4,)), dma((4,)),
            dma((2, Z)), dma((2, Z)),
            dma((ITERS,)), dma((ITERS,)),
            dma((ITERS,)), dma((ITERS,)),
            dma((2, 4, 2)), dma((2, 4, 2)),
            dma((2, 4)), dma((2, 4)),
            dma((1,)), dma((1,)),
            dma((2,)),
        ],
        compiler_params=pltpu.CompilerParams(
            collective_id=0, has_side_effects=True, vmem_limit_bytes=54656 * 1024
        ),
    )(noise_draw, latent_code, start_potential.reshape(4, LANE))
    return npot.reshape(BLK), lpot.reshape(BLK), out


def solution(mesh):
    in_specs = (P("row", "col"), P("col", "row"), P("col"))
    out_specs = (P("row"), P("col"), P("row", "col"))

    def whole(noise_draw, latent_code, start_potential):
        def block(a, b, c):
            return per_device(noise_draw.shape[0], latent_code.shape[0], a, b, c)

        return jax.shard_map(
            block, mesh=mesh, in_specs=in_specs, out_specs=out_specs, check_vma=False
        )(noise_draw, latent_code, start_potential)

    return whole
```

```python
import math

import jax
import jax.numpy as jnp
from jax import lax
from jax.experimental import pallas as pl
from jax.experimental.pallas import tpu as pltpu
from jax.sharding import PartitionSpec as P

ITERS = 3
EPS = 0.01
LOG2E = math.log2(math.e)
MESH = pl.DeviceIdType.MESH
F32 = jnp.float32
BF16 = jnp.bfloat16

Z, Y = 8, 4
LANE = 128
BLK = 512
HALF = BLK // 2
SPLIT = 384
REST = BLK - SPLIT


def kernel(
    n_total, m_total, width,
    noise_ref, latent_ref, start_ref,
    npot_ref, lpot_ref, out_ref,
    nz, lt, no, cross, nsq, lsq, wt, wx, nx, part, parth, stage, land, stageh, landh, xs, xr, rowx, col2,
    q_send, q_recv, n_send, n_recv, h_send, h_recv, l_send, l_recv, o_send, o_recv, w_send, w_recv,
    p_send, p_recv, r_send, r_recv, c2_send, c2_recv,
    s_send, s_recv, t_send, t_recv, x_send, x_recv, loc,
):
    row = lax.axis_index("row")
    col = lax.axis_index("col")
    z = row // 4
    xl = (row // 2) % 2
    core = row % 2
    y = col // 2
    xh = col % 2
    quad = row % 4

    def ring_z(d):
        return (z + d + Z) % Z

    def ring_y(d):
        return (y + d + Y) % Y

    other_core = (row + 1 - 2 * core, col)
    other_xl = (row + 2 - 4 * xl, col)
    flip_col = col + 1 - 2 * xh
    other_xh = (row, flip_col)
    z_up = (ring_z(1) * 4 + quad, col)
    z_dn = (ring_z(-1) * 4 + quad, col)
    y_up = (row, ring_y(1) * 2 + xh)
    y_dn = (row, ring_y(-1) * 2 + xh)
    col_peers = [
        (row, ring_y(dy) * 2 + (1 - xh if dx else xh))
        for dy, dx in ((2, 1), (1, 1), (-1, 1), (2, 0), (0, 1), (1, 0), (-1, 0))
    ]
    across = (row + 2 - 4 * xl) // 2 * 2
    across_quad = ((across + 1 - core) % 4, (across + core) % 4, (quad // 2) * 2 + 1 - core, quad)
    row_peers = [
        (ring_z(d) * 4 + q, col)
        for d in (4, 3, -3, 2, -2, 1, -1, 0) for q in across_quad[:3 if d == 0 else 4]
    ]
    peers = col_peers + row_peers + [(across, flip_col), (across + 1, flip_col)]

    own_n = pltpu.make_async_copy(noise_ref, nz.at[col], loc.at[0])
    own_l = pltpu.make_async_copy(latent_ref, lt.at[z, core, xl], loc.at[1])
    own_n.start()
    own_l.start()

    barrier = pltpu.get_barrier_semaphore()
    for peer in peers:
        pl.semaphore_signal(barrier, inc=1, device_id=peer, device_id_type=MESH)
    cross[...] = jnp.zeros_like(cross)
    pl.semaphore_wait(barrier, len(peers))

    def rc(src, dst, ssem, rsem, dev):
        return pltpu.make_async_remote_copy(
            src_ref=src, dst_ref=dst, send_sem=ssem, recv_sem=rsem,
            device_id=dev, device_id_type=MESH,
        )

    def nsl(slot, h):
        return nz.at[slot, pl.ds(h * HALF, HALF), :]

    QUART = HALF // 2
    sent = []

    def nsend(slot, h, idx, dev, src=None):
        src = nsl(slot, h) if src is None else src
        c = rc(src, nsl(slot, h), n_send.at[idx], n_recv.at[idx], dev)
        c.start()
        return c

    def own_half(h):
        return noise_ref.at[pl.ds(h * HALF, HALF), :]

    def nwait(slot, h, idx):
        rc(nsl(slot, h), nsl(slot, h), n_send.at[idx], n_recv.at[idx], y_up).wait_recv()

    def lsend(ref, idx, dev, src=None):
        c = rc(ref if src is None else src, ref, l_send.at[idx], l_recv.at[idx], dev)
        c.start()
        sent.append(c)

    def lwait(ref, idx):
        rc(ref, ref, l_send.at[idx], l_recv.at[idx], z_up).wait_recv()

    def slot_of(yy, s):
        return yy * 2 + (xh if s == 0 else 1 - xh)

    def xh_copy(t, h, src, slot):
        return rc(src, nsl(slot, h), h_send.at[t, h], h_recv.at[t, h], other_xh)

    def xh_send(t, h):
        far0 = slot_of(ring_y(2), 0)
        c = xh_copy(t, h, own_half(h), col) if t == 0 else xh_copy(t, h, nsl(far0, h), far0)
        c.start()
        sent.append(c)

    def xh_wait(t, h):
        slot = flip_col if t == 0 else slot_of(ring_y(2), 1)
        xh_copy(t, h, nsl(slot, h), slot).wait_recv()

    own_pair = lt.at[z, core]
    own_block = lt.at[z, core, xl]
    z_dirs = ((0, -1, z_up), (1, 1, z_dn))

    def lat(d, part):
        return lt.at[ring_z(d), core, xl if part == 0 else 1 - xl]

    def lat_forward(step, part, dirs):
        for dr, sgn, dev in dirs:
            block = lat(sgn * step, part)
            lwait(block, 1 + 8 * dr + 2 * (step - 1) + part)
            if step < 3 or part == dr:
                lsend(block, 1 + 8 * dr + 2 * step + part, dev)

    def lat_share(step):
        for dr, sgn, _ in z_dirs:
            lsend(lt.at[ring_z(sgn * step), core], 16 + 2 * step + dr, other_core)

    lsend(own_block, 0, other_xl, latent_ref)
    lsend(own_block, 1, z_up, latent_ref)
    lsend(own_block, 9, z_dn, latent_ref)
    first_up = nsend(col, 0, 0, y_up, own_half(0))
    first_dn = nsend(col, 1, 3, y_dn, own_half(1))
    xh_send(0, 0)
    xh_send(0, 1)

    own_n.wait()
    own_l.wait()
    for b in range(4):
        rows = slice(b * LANE, (b + 1) * LANE)
        n2 = jnp.square(nz[col, rows, :].astype(F32))
        n2 = (n2[:, 0:128] + n2[:, 128:256]) + (n2[:, 256:384] + n2[:, 384:512])
        nsq[col, b:b + 1, :] = jnp.sum(n2.T, axis=0, keepdims=True)
        l2 = jnp.square(lt[z, core, xl, rows, :].astype(F32))
        lsq[row, b:b + 1, :] = jnp.sum(l2.T, axis=0, keepdims=True)

    lwait(lat(0, 1), 0)
    lsend(lat(0, 1), 2, z_up)
    lsend(lat(0, 1), 10, z_dn)
    lat_forward(1, 0, z_dirs)
    lsend(own_pair, 17, other_core)

    def own_quarter(h, p, idx, dev):
        at = pl.ds(h * HALF + p * QUART, QUART)
        c = rc(noise_ref.at[at, :], nz.at[col, at, :], n_send.at[idx], n_recv.at[idx], dev)
        c.start()
        sent.append(c)

    first_up.wait_send()
    own_quarter(1, 0, 1, y_up)
    first_dn.wait_send()
    own_quarter(0, 0, 2, y_dn)

    dn, up = slot_of(ring_y(-1), 0), slot_of(ring_y(1), 0)
    nwait(dn, 0, 0)
    onward_up = nsend(dn, 0, 4, y_up)
    nwait(up, 1, 3)
    onward_dn = nsend(up, 1, 5, y_dn)

    lat_forward(1, 1, z_dirs)
    lat_share(1)
    for peer in col_peers:
        rc(nsq.at[col], nsq.at[col], q_send.at[0], q_recv.at[0], peer).start()
    for peer in row_peers:
        rc(lsq.at[row], lsq.at[row], q_send.at[1], q_recv.at[1], peer).start()
    lat_forward(2, 0, z_dirs)
    lat_forward(2, 1, z_dirs)
    lat_share(2)

    onward_up.wait_send()
    own_quarter(1, 1, 10, y_up)
    onward_dn.wait_send()
    own_quarter(0, 1, 11, y_dn)

    nwait(slot_of(ring_y(2), 0), 0, 4)
    xh_send(1, 0)
    nwait(slot_of(ring_y(2), 0), 1, 5)
    xh_send(1, 1)

    lat_forward(3, 0, z_dirs)

    xh_wait(0, 0)
    sent.append(nsend(flip_col, 0, 6, y_up))
    sent.append(nsend(flip_col, 0, 8, y_dn))
    xh_wait(0, 1)
    sent.append(nsend(flip_col, 1, 9, y_dn))
    sent.append(nsend(flip_col, 1, 7, y_up))

    lat_forward(3, 1, z_dirs)
    lat_share(3)
    lwait(lat(4, 0), 7)
    lwait(lat(4, 1), 16)
    lsend(lt.at[ring_z(4), core], 24, other_core)
    for j, d in enumerate((0, -1, 1, -2, 2, -3, 3, 4)):
        lwait(lt.at[ring_z(d), 1 - core], 17 + j)

    def accumulate(slot):
        a = nz[slot]
        b = jnp.concatenate([lt[slot, 0, 0], lt[slot, 1, 0], lt[slot, 0, 1], lt[slot, 1, 1]], axis=1)
        cross[...] += lax.dot_general(a, b, (((1,), (1,)), ((), ())), preferred_element_type=F32)

    dn, up = slot_of(ring_y(-1), 0), slot_of(ring_y(1), 0)
    for slot, h, idxs in ((dn, 1, (1, 10)), (up, 0, (2, 11))):
        for p in range(2):
            ref = nz.at[slot, pl.ds(h * HALF + p * QUART, QUART), :]
            rc(ref, ref, n_send.at[idxs[p]], n_recv.at[idxs[p]], y_up).wait_recv()

    def set0(k, carry):
        accumulate(((y + k) % Y) * 2 + xh)
        return carry

    lax.fori_loop(0, Y, set0, 0)
    accumulate(flip_col)
    xh_wait(1, 0)
    xh_wait(1, 1)
    accumulate(slot_of(ring_y(2), 1))
    dn, up = slot_of(ring_y(-1), 1), slot_of(ring_y(1), 1)
    nwait(dn, 0, 6)
    nwait(up, 1, 9)
    nwait(dn, 1, 7)
    nwait(up, 0, 8)
    accumulate(dn)
    accumulate(up)

    for q in range(2):
        c = rc(
            nz.at[:, :, pl.ds(pl.multiple_of(q * 256 + (1 - core) * LANE, LANE), LANE)],
            no.at[:, :, pl.ds(q * LANE, LANE)],
            o_send.at[q], o_recv.at[q], other_core,
        )
        c.start()
        sent.append(c)

    eye = (
        lax.broadcasted_iota(jnp.int32, (LANE, LANE), 0)
        == lax.broadcasted_iota(jnp.int32, (LANE, LANE), 1)
    )

    def to_rows(v):
        return jnp.sum(jnp.where(eye, v, 0.0), axis=1, keepdims=True)

    def wide(v):
        return jnp.concatenate([v[q:q + 1, :] for q in range(4)], axis=1)

    scale = LOG2E / (width * EPS)
    rc(nsq.at[pl.ds(0, 7)], nsq.at[pl.ds(0, 7)], q_send.at[0], q_recv.at[0], z_up).wait_recv()
    rc(lsq.at[pl.ds(0, 31)], lsq.at[pl.ds(0, 31)], q_send.at[1], q_recv.at[1], z_up).wait_recv()
    nq = jnp.sum(nsq[...], axis=0)
    lq = wide(jnp.sum(lsq[...], axis=0))
    for b in range(4):
        rows = slice(b * LANE, (b + 1) * LANE)
        cross[rows, :] = (to_rows(nq[b:b + 1, :]) + lq - 2.0 * cross[rows, :]) * scale

    def merge(parts):
        best = jnp.max(parts, axis=0)
        return best + jnp.log2(jnp.sum(jnp.exp2(parts - best[None]), axis=0))

    def merge_rows(parts):
        best = jnp.max(parts, axis=0, keepdims=True)
        return best + jnp.log2(jnp.sum(jnp.exp2(parts - best), axis=0, keepdims=True))

    def lend(step):
        k, zz = step % 2, step // 2
        lanes = pl.ds(pl.multiple_of((1 - xl) * 256 + k * LANE, LANE), LANE)
        for slot, dev in ((zz, (across + k, col)), (zz + 4, (across + k, flip_col))):
            c = rc(nz.at[slot, :, lanes], nx.at[core, slot], p_send.at[k, slot], p_recv.at[core, slot], dev)
            c.start()
            sent.append(c)

    steps = iter(range(6))

    def exchange(buf, mine, peers, ssem, rsem):
        for peer in peers:
            rc(buf.at[mine], buf.at[mine], ssem, rsem, peer).start()
        step = next(steps)
        for piece_at in range(step * 8 // 6, (step + 1) * 8 // 6):
            lend(piece_at)
        k = len(peers)
        rc(buf.at[pl.ds(0, k)], buf.at[pl.ds(0, k)], ssem, rsem, peers[0]).wait_recv()

    g = start_ref[...] * (LOG2E / EPS)
    f = None
    f_rows = None
    for it in range(ITERS):
        for b in range(4):
            parts = []
            for r in range(b * LANE, (b + 1) * LANE, 32):
                s = [g[q:q + 1, :] - cross[r:r + 32, q * LANE:(q + 1) * LANE] for q in range(4)]
                top = jnp.maximum(jnp.maximum(s[0], s[1]), jnp.maximum(s[2], s[3]))
                e = [jnp.exp2(v - top) for v in s]
                parts.append(top + jnp.log2((e[0] + e[1]) + (e[2] + e[3])))
            rowx[it, col, b:b + 1, :] = merge_rows(jnp.concatenate(parts, axis=0).T)
        exchange(rowx.at[it], col, col_peers, r_send.at[it], r_recv.at[it])
        f = -(math.log2(m_total) + merge(rowx[it]))
        f_rows = [to_rows(f[b:b + 1, :]) for b in range(4)]
        parts = []
        for r in range(0, BLK, 64):
            fr = f_rows[r // LANE][r % LANE:r % LANE + 64]
            s = (fr - cross[r:r + 64, :]).reshape(8, 8, BLK)
            top = jnp.max(s, axis=0)
            parts.append(top + jnp.log2(jnp.sum(jnp.exp2(s - top[None]), axis=0)))
        top = parts[0]
        for v in parts[1:]:
            top = jnp.maximum(top, v)
        own = merge_rows(top + jnp.log2(sum(jnp.exp2(v - top) for v in parts)))
        for q in range(4):
            col2[it, row, q:q + 1, :] = own[:, q * LANE:(q + 1) * LANE]
        exchange(col2.at[it], row, row_peers, c2_send.at[it], c2_recv.at[it])
        g = -(math.log2(n_total) + merge(col2[it]))

    npot_ref[...] = f * (EPS / LOG2E)
    lpot_ref[...] = g * (EPS / LOG2E)

    LOW, HIGH = slice(0, SPLIT), slice(SPLIT, BLK)
    gw = wide(g)

    def weights(cols):
        for b in range(4):
            rows = slice(b * LANE, (b + 1) * LANE)
            w = m_total * jnp.exp2((f_rows[b] + gw[:, cols]) - cross[rows, cols])
            wt[core, cols, rows] = w.T.astype(BF16)

    def wcopy(j, src, dst, dev, r=None):
        return rc(src, dst, w_send.at[j], w_recv.at[j if r is None else 3 * r], dev)

    low, high = pl.ds(0, SPLIT), pl.ds(SPLIT, REST)
    copies = []
    weights(HIGH)
    for k in range(2):
        copies.append(wcopy(3 * k, wt.at[core, high], wx.at[core], (across + k, col), core))
        copies[-1].start()
    weights(LOW)
    copies.append(wcopy(1, wt.at[core, low], wt.at[core, low], other_core))
    copies[-1].start()
    copies.append(wcopy(2, wt.at[core, high], wt.at[core, high], other_core))
    copies[-1].start()

    def mine(d, q):
        return nz[d, :, pl.ds(pl.multiple_of(q * 256 + core * LANE, LANE), LANE)]

    def theirs(d, q):
        return no[d, :, pl.ds(pl.multiple_of(q * LANE, LANE), LANE)]

    def partial_own(rel):
        d = (z + rel) % Z
        part[rel] = jnp.dot(
            wt[core, LOW, :], jnp.concatenate([mine(d, q) for q in (1 - xl, xl)], axis=1),
            preferred_element_type=F32,
        )

    def partial_other(rel):
        d = (z + rel) % Z
        part[rel] += jnp.dot(
            wt[1 - core, LOW, :], jnp.concatenate([theirs(d, q) for q in (1 - xl, xl)], axis=1),
            preferred_element_type=F32,
        )

    def partial(rel):
        partial_own(rel)
        partial_other(rel)

    def partial_high(rel):
        d = (z + rel) % Z
        parth[rel] = (
            jnp.dot(wt[core, HIGH, :], mine(d, xl), preferred_element_type=F32)
            + jnp.dot(wt[1 - core, HIGH, :], theirs(d, xl), preferred_element_type=F32)
        ) + (
            jnp.dot(wx[0], nx[0, d], preferred_element_type=F32)
            + jnp.dot(wx[1], nx[1, d], preferred_element_type=F32)
        )

    def size(k):
        return REST if k == 2 else SPLIT

    def piece(k, bufs, dr, s):
        ref = bufs[1].at[dr, 4 - s] if k == 2 else bufs[0].at[dr, 4 - s, k]
        h = size(k) // 2
        return ref.at[pl.ds(dr * h, h)] if s == 4 else ref

    def ring_copy(k, dr, s):
        ss, rs = (t_send.at[dr, 4 - s], t_recv.at[dr, 4 - s]) if k == 2 else (
            s_send.at[dr, 4 - s, k], s_recv.at[dr, 4 - s, k])
        return rc(
            piece(k, (stage, stageh), dr, s), piece(k, (land, landh), dr, s), ss, rs,
            z_dn if dr == 0 else z_up,
        )

    def own_part(k, rel, rows):
        return parth[rel, rows, :] if k == 2 else part[rel, rows, k * LANE:(k + 1) * LANE]

    def got(k, dr, s, rows):
        v = landh[dr, 4 - s, rows, :] if k == 2 else land[dr, 4 - s, k, rows, :]
        return v.astype(F32)

    def put(k, dr, s, rows, v):
        if k == 2:
            stageh[dr, 4 - s, rows, :] = v.astype(BF16)
        else:
            stage[dr, 4 - s, k, rows, :] = v.astype(BF16)

    def ring_step(k, s):
        h = size(k) // 2
        both = slice(0, 2 * h)
        for dr in range(2):
            rel = Z - s if dr == 0 else s
            first = slice(dr * h, (dr + 1) * h)
            other = slice((1 - dr) * h, (2 - dr) * h)
            if s == 4:
                put(k, dr, s, first, own_part(k, 4, first))
            else:
                ring_copy(k, dr, s + 1).wait_recv()
                if s == 3:
                    put(k, dr, s, first, own_part(k, rel, first) + got(k, dr, 4, first))
                    put(k, dr, s, other, own_part(k, rel, other))
                else:
                    put(k, dr, s, both, own_part(k, rel, both) + got(k, dr, s + 1, both))
            c = ring_copy(k, dr, s)
            c.start()
            sent.append(c)

    def total(k):
        both = slice(0, size(k))
        for dr in range(2):
            ring_copy(k, dr, 1).wait_recv()
        return own_part(k, 0, both) + (got(k, 0, 1, both) + got(k, 1, 1, both))

    for rel in (4, 5, 3):
        partial_own(rel)
    for q in range(2):
        rc(no.at[:, :, pl.ds(q * LANE, LANE)], no.at[:, :, pl.ds(q * LANE, LANE)],
           o_send.at[q], o_recv.at[q], other_core).wait_recv()
    wcopy(1, wt.at[core, low], wt.at[1 - core, low], other_core).wait_recv()
    partial_other(4)
    ring_step(0, 4)
    ring_step(1, 4)
    partial_other(5)
    partial_other(3)
    wcopy(2, wt.at[core, high], wt.at[1 - core, high], other_core).wait_recv()
    for c in range(2):
        for slot in range(Z):
            rc(nx.at[c, slot], nx.at[c, slot], p_send.at[0, slot], p_recv.at[c, slot], other_xl).wait_recv()
    ring_step(0, 3)
    ring_step(1, 3)
    for c in range(2):
        wcopy(0, wt.at[core, high], wx.at[c], other_xl, c).wait_recv()
    partial_high(4)
    ring_step(2, 4)
    for rel in (6, 2):
        partial(rel)
    for rel in (5, 3):
        partial_high(rel)
    ring_step(0, 2)
    ring_step(1, 2)
    ring_step(2, 3)
    for rel in (7, 1, 0):
        partial(rel)
    for rel in (6, 2):
        partial_high(rel)
    ring_step(0, 1)
    ring_step(1, 1)
    ring_step(2, 2)
    for rel in (7, 1, 0):
        partial_high(rel)
    xs[...] = total(0)
    xc = rc(xs, xr, x_send.at[0], x_recv.at[0], other_xl)
    xc.start()
    copies.append(xc)
    ring_step(2, 1)
    kept = total(1)
    out_ref[:, HIGH] = total(2).T
    xc.wait_recv()
    out_ref[:, LOW] = (kept + xr[...]).T
    sent.extend(copies)

    for j, (buf, k) in enumerate(((nsq, 7), (lsq, 31))):
        ref = buf.at[pl.ds(0, k)]
        rc(ref, ref, q_send.at[j], q_recv.at[j], z_up).wait_send()
    for c in sent:
        c.wait_send()
    for it in range(ITERS):
        for buf, k, ssem, rsem in (
            (rowx, 7, r_send, r_recv), (col2, 31, c2_send, c2_recv)
        ):
            ref = buf.at[it, pl.ds(0, k)]
            rc(ref, ref, ssem.at[it], rsem.at[it], z_up).wait_send()


def per_device(n_total, m_total, noise_draw, latent_code, start_potential):
    anyspace = pl.BlockSpec(memory_space=pltpu.HBM)
    vmem = pl.BlockSpec(memory_space=pltpu.VMEM)
    width = 4096
    dma = pltpu.SemaphoreType.DMA

    def body(*refs):
        kernel(n_total, m_total, width, *refs)

    npot, lpot, out = pl.pallas_call(
        body,
        out_shape=(
            jax.ShapeDtypeStruct((4, LANE), F32),
            jax.ShapeDtypeStruct((4, LANE), F32),
            jax.ShapeDtypeStruct((LANE, BLK), F32),
        ),
        in_specs=[anyspace, anyspace, vmem],
        out_specs=(vmem, vmem, vmem),
        scratch_shapes=[
            pltpu.VMEM((8, BLK, BLK), BF16),
            pltpu.VMEM((Z, 2, 2, BLK, LANE), BF16),
            pltpu.VMEM((8, BLK, 2 * LANE), BF16),
            pltpu.VMEM((BLK, BLK), F32),
            pltpu.VMEM((8, 4, LANE), F32),
            pltpu.VMEM((32, 4, LANE), F32),
            pltpu.VMEM((2, BLK, BLK), BF16),
            pltpu.VMEM((2, REST, BLK), BF16),
            pltpu.VMEM((2, Z, BLK, LANE), BF16),
            pltpu.VMEM((Z, SPLIT, 2 * LANE), F32),
            pltpu.VMEM((Z, REST, LANE), F32),
            pltpu.VMEM((2, 4, 2, SPLIT, LANE), BF16),
            pltpu.VMEM((2, 4, 2, SPLIT, LANE), BF16),
            pltpu.VMEM((2, 4, REST, LANE), BF16),
            pltpu.VMEM((2, 4, REST, LANE), BF16),
            pltpu.VMEM((SPLIT, LANE), F32),
            pltpu.VMEM((SPLIT, LANE), F32),
            pltpu.VMEM((ITERS, 8, 4, LANE), F32),
            pltpu.VMEM((ITERS, 32, 4, LANE), F32),
            dma((2,)), dma((2,)),
            dma((12,)), dma((12,)),
            dma((2, 2)), dma((2, 2)),
            dma((25,)), dma((25,)),
            dma((2,)), dma((2,)),
            dma((4,)), dma((4,)),
            dma((2, Z)), dma((2, Z)),
            dma((ITERS,)), dma((ITERS,)),
            dma((ITERS,)), dma((ITERS,)),
            dma((2, 4, 2)), dma((2, 4, 2)),
            dma((2, 4)), dma((2, 4)),
            dma((1,)), dma((1,)),
            dma((2,)),
        ],
        compiler_params=pltpu.CompilerParams(
            collective_id=0, has_side_effects=True, vmem_limit_bytes=54656 * 1024
        ),
    )(noise_draw, latent_code, start_potential.reshape(4, LANE))
    return npot.reshape(BLK), lpot.reshape(BLK), out


def solution(mesh):
    in_specs = (P("row", "col"), P("col", "row"), P("col"))
    out_specs = (P("row"), P("col"), P("row", "col"))

    def whole(noise_draw, latent_code, start_potential):
        def block(a, b, c):
            return per_device(noise_draw.shape[0], latent_code.shape[0], a, b, c)

        return jax.shard_map(
            block, mesh=mesh, in_specs=in_specs, out_specs=out_specs, check_vma=False
        )(noise_draw, latent_code, start_potential)

    return whole
```

```python
import math

import jax
import jax.numpy as jnp
from jax import lax
from jax.experimental import pallas as pl
from jax.experimental.pallas import tpu as pltpu
from jax.sharding import PartitionSpec as P

ITERS = 3
EPS = 0.01
LOG2E = math.log2(math.e)
MESH = pl.DeviceIdType.MESH
F32 = jnp.float32
BF16 = jnp.bfloat16

Z, Y = 8, 4
LANE = 128
BLK = 512
HALF = BLK // 2
SPLIT = 384
REST = BLK - SPLIT


def kernel(
    n_total, m_total, width,
    noise_ref, latent_ref, start_ref,
    npot_ref, lpot_ref, out_ref,
    nz, lt, no, cross, nsq, lsq, wt, wx, nx, part, parth, stage, land, stageh, landh, xs, xr, rowx, col2,
    q_send, q_recv, n_send, n_recv, h_send, h_recv, l_send, l_recv, o_send, o_recv, w_send, w_recv,
    p_send, p_recv, r_send, r_recv, c2_send, c2_recv,
    s_send, s_recv, t_send, t_recv, x_send, x_recv, loc,
):
    row = lax.axis_index("row")
    col = lax.axis_index("col")
    z = row // 4
    xl = (row // 2) % 2
    core = row % 2
    y = col // 2
    xh = col % 2
    quad = row % 4

    def ring_z(d):
        return (z + d + Z) % Z

    def ring_y(d):
        return (y + d + Y) % Y

    other_core = (row + 1 - 2 * core, col)
    other_xl = (row + 2 - 4 * xl, col)
    flip_col = col + 1 - 2 * xh
    other_xh = (row, flip_col)
    z_up = (ring_z(1) * 4 + quad, col)
    z_dn = (ring_z(-1) * 4 + quad, col)
    y_up = (row, ring_y(1) * 2 + xh)
    y_dn = (row, ring_y(-1) * 2 + xh)
    col_peers = [
        (row, ring_y(dy) * 2 + (1 - xh if dx else xh))
        for dy, dx in ((2, 1), (1, 1), (-1, 1), (2, 0), (0, 1), (1, 0), (-1, 0))
    ]
    across = (row + 2 - 4 * xl) // 2 * 2
    across_quad = ((across + 1 - core) % 4, (across + core) % 4, (quad // 2) * 2 + 1 - core, quad)
    row_peers = [
        (ring_z(d) * 4 + q, col)
        for d in (4, 3, -3, 2, -2, 1, -1, 0) for q in across_quad[:3 if d == 0 else 4]
    ]
    peers = col_peers + row_peers + [(across, flip_col), (across + 1, flip_col)]

    own_n = pltpu.make_async_copy(noise_ref, nz.at[col], loc.at[0])
    own_l = pltpu.make_async_copy(latent_ref, lt.at[z, core, xl], loc.at[1])
    own_n.start()
    own_l.start()

    barrier = pltpu.get_barrier_semaphore()
    for peer in peers:
        pl.semaphore_signal(barrier, inc=1, device_id=peer, device_id_type=MESH)
    cross[...] = jnp.zeros_like(cross)
    pl.semaphore_wait(barrier, len(peers))

    def rc(src, dst, ssem, rsem, dev):
        return pltpu.make_async_remote_copy(
            src_ref=src, dst_ref=dst, send_sem=ssem, recv_sem=rsem,
            device_id=dev, device_id_type=MESH,
        )

    def nsl(slot, h):
        return nz.at[slot, pl.ds(h * HALF, HALF), :]

    QUART = HALF // 2
    sent = []

    def nsend(slot, h, idx, dev, src=None):
        src = nsl(slot, h) if src is None else src
        c = rc(src, nsl(slot, h), n_send.at[idx], n_recv.at[idx], dev)
        c.start()
        return c

    def own_half(h):
        return noise_ref.at[pl.ds(h * HALF, HALF), :]

    def nwait(slot, h, idx):
        rc(nsl(slot, h), nsl(slot, h), n_send.at[idx], n_recv.at[idx], y_up).wait_recv()

    def lsend(ref, idx, dev, src=None):
        c = rc(ref if src is None else src, ref, l_send.at[idx], l_recv.at[idx], dev)
        c.start()
        sent.append(c)

    def lwait(ref, idx):
        rc(ref, ref, l_send.at[idx], l_recv.at[idx], z_up).wait_recv()

    def slot_of(yy, s):
        return yy * 2 + (xh if s == 0 else 1 - xh)

    def xh_copy(t, h, src, slot):
        return rc(src, nsl(slot, h), h_send.at[t, h], h_recv.at[t, h], other_xh)

    def xh_send(t, h):
        far0 = slot_of(ring_y(2), 0)
        c = xh_copy(t, h, own_half(h), col) if t == 0 else xh_copy(t, h, nsl(far0, h), far0)
        c.start()
        sent.append(c)

    def xh_wait(t, h):
        slot = flip_col if t == 0 else slot_of(ring_y(2), 1)
        xh_copy(t, h, nsl(slot, h), slot).wait_recv()

    own_pair = lt.at[z, core]
    own_block = lt.at[z, core, xl]
    z_dirs = ((0, -1, z_up), (1, 1, z_dn))

    def lat(d, part):
        return lt.at[ring_z(d), core, xl if part == 0 else 1 - xl]

    def lat_forward(step, part, dirs):
        for dr, sgn, dev in dirs:
            block = lat(sgn * step, part)
            lwait(block, 1 + 8 * dr + 2 * (step - 1) + part)
            if step < 3 or part == dr:
                lsend(block, 1 + 8 * dr + 2 * step + part, dev)

    def lat_share(step):
        for dr, sgn, _ in z_dirs:
            lsend(lt.at[ring_z(sgn * step), core], 16 + 2 * step + dr, other_core)

    lat_x = rc(latent_ref, own_block, l_send.at[0], l_recv.at[0], other_xl)
    lat_x.start()
    lsend(own_block, 1, z_up, latent_ref)
    lsend(own_block, 9, z_dn, latent_ref)
    first_up = nsend(col, 0, 0, y_up, own_half(0))
    first_dn = nsend(col, 1, 3, y_dn, own_half(1))

    lat_x.wait_send()
    xh_send(0, 0)
    xh_send(0, 1)

    own_n.wait()
    own_l.wait()
    for b in range(4):
        rows = slice(b * LANE, (b + 1) * LANE)
        n2 = jnp.square(nz[col, rows, :].astype(F32))
        n2 = (n2[:, 0:128] + n2[:, 128:256]) + (n2[:, 256:384] + n2[:, 384:512])
        nsq[col, b:b + 1, :] = jnp.sum(n2.T, axis=0, keepdims=True)
        l2 = jnp.square(lt[z, core, xl, rows, :].astype(F32))
        lsq[row, b:b + 1, :] = jnp.sum(l2.T, axis=0, keepdims=True)

    lwait(lat(0, 1), 0)
    lsend(lat(0, 1), 2, z_up)
    lsend(lat(0, 1), 10, z_dn)
    lat_forward(1, 0, z_dirs)
    lsend(own_pair, 17, other_core)

    def own_quarter(h, p, idx, dev):
        at = pl.ds(h * HALF + p * QUART, QUART)
        c = rc(noise_ref.at[at, :], nz.at[col, at, :], n_send.at[idx], n_recv.at[idx], dev)
        c.start()
        sent.append(c)

    first_up.wait_send()
    own_quarter(1, 0, 1, y_up)
    first_dn.wait_send()
    own_quarter(0, 0, 2, y_dn)

    dn, up = slot_of(ring_y(-1), 0), slot_of(ring_y(1), 0)
    nwait(dn, 0, 0)
    onward_up = nsend(dn, 0, 4, y_up)
    nwait(up, 1, 3)
    onward_dn = nsend(up, 1, 5, y_dn)

    lat_forward(1, 1, z_dirs)
    lat_share(1)
    for peer in col_peers:
        rc(nsq.at[col], nsq.at[col], q_send.at[0], q_recv.at[0], peer).start()
    for peer in row_peers:
        rc(lsq.at[row], lsq.at[row], q_send.at[1], q_recv.at[1], peer).start()
    lat_forward(2, 0, z_dirs)
    lat_forward(2, 1, z_dirs)
    lat_share(2)

    onward_up.wait_send()
    own_quarter(1, 1, 10, y_up)
    onward_dn.wait_send()
    own_quarter(0, 1, 11, y_dn)

    nwait(slot_of(ring_y(2), 0), 0, 4)
    xh_send(1, 0)
    nwait(slot_of(ring_y(2), 0), 1, 5)
    xh_send(1, 1)

    lat_forward(3, 0, z_dirs)

    xh_wait(0, 0)
    sent.append(nsend(flip_col, 0, 6, y_up))
    sent.append(nsend(flip_col, 0, 8, y_dn))
    xh_wait(0, 1)
    sent.append(nsend(flip_col, 1, 9, y_dn))
    sent.append(nsend(flip_col, 1, 7, y_up))

    lat_forward(3, 1, z_dirs)
    lat_share(3)
    lwait(lat(4, 0), 7)
    lwait(lat(4, 1), 16)
    lsend(lt.at[ring_z(4), core], 24, other_core)
    for j, d in enumerate((0, -1, 1, -2, 2, -3, 3, 4)):
        lwait(lt.at[ring_z(d), 1 - core], 17 + j)

    def accumulate(slot):
        a = nz[slot]
        b = jnp.concatenate([lt[slot, 0, 0], lt[slot, 1, 0], lt[slot, 0, 1], lt[slot, 1, 1]], axis=1)
        cross[...] += lax.dot_general(a, b, (((1,), (1,)), ((), ())), preferred_element_type=F32)

    dn, up = slot_of(ring_y(-1), 0), slot_of(ring_y(1), 0)
    for slot, h, idxs in ((dn, 1, (1, 10)), (up, 0, (2, 11))):
        for p in range(2):
            ref = nz.at[slot, pl.ds(h * HALF + p * QUART, QUART), :]
            rc(ref, ref, n_send.at[idxs[p]], n_recv.at[idxs[p]], y_up).wait_recv()

    def set0(k, carry):
        accumulate(((y + k) % Y) * 2 + xh)
        return carry

    lax.fori_loop(0, Y, set0, 0)
    accumulate(flip_col)
    xh_wait(1, 0)
    xh_wait(1, 1)
    accumulate(slot_of(ring_y(2), 1))
    dn, up = slot_of(ring_y(-1), 1), slot_of(ring_y(1), 1)
    nwait(dn, 0, 6)
    nwait(up, 1, 9)
    nwait(dn, 1, 7)
    nwait(up, 0, 8)
    accumulate(dn)
    accumulate(up)

    for q in range(2):
        c = rc(
            nz.at[:, :, pl.ds(pl.multiple_of(q * 256 + (1 - core) * LANE, LANE), LANE)],
            no.at[:, :, pl.ds(q * LANE, LANE)],
            o_send.at[q], o_recv.at[q], other_core,
        )
        c.start()
        sent.append(c)

    eye = (
        lax.broadcasted_iota(jnp.int32, (LANE, LANE), 0)
        == lax.broadcasted_iota(jnp.int32, (LANE, LANE), 1)
    )

    def to_rows(v):
        return jnp.sum(jnp.where(eye, v, 0.0), axis=1, keepdims=True)

    def wide(v):
        return jnp.concatenate([v[q:q + 1, :] for q in range(4)], axis=1)

    scale = LOG2E / (width * EPS)
    rc(nsq.at[pl.ds(0, 7)], nsq.at[pl.ds(0, 7)], q_send.at[0], q_recv.at[0], z_up).wait_recv()
    rc(lsq.at[pl.ds(0, 31)], lsq.at[pl.ds(0, 31)], q_send.at[1], q_recv.at[1], z_up).wait_recv()
    nq = jnp.sum(nsq[...], axis=0)
    lq = wide(jnp.sum(lsq[...], axis=0))
    for b in range(4):
        rows = slice(b * LANE, (b + 1) * LANE)
        cross[rows, :] = (to_rows(nq[b:b + 1, :]) + lq - 2.0 * cross[rows, :]) * scale

    def merge(parts):
        best = jnp.max(parts, axis=0)
        return best + jnp.log2(jnp.sum(jnp.exp2(parts - best[None]), axis=0))

    def merge_rows(parts):
        best = jnp.max(parts, axis=0, keepdims=True)
        return best + jnp.log2(jnp.sum(jnp.exp2(parts - best), axis=0, keepdims=True))

    def lend(step):
        k, zz = step % 2, step // 2
        lanes = pl.ds(pl.multiple_of((1 - xl) * 256 + k * LANE, LANE), LANE)
        for slot, dev in ((zz, (across + k, col)), (zz + 4, (across + k, flip_col))):
            c = rc(nz.at[slot, :, lanes], nx.at[core, slot], p_send.at[k, slot], p_recv.at[core, slot], dev)
            c.start()
            sent.append(c)

    steps = iter(range(6))

    def exchange(buf, mine, peers, ssem, rsem):
        for peer in peers:
            rc(buf.at[mine], buf.at[mine], ssem, rsem, peer).start()
        step = next(steps)
        for piece_at in range(*((0, 2), (2, 4), (4, 6), (6, 7), (7, 8), (8, 8))[step]):
            lend(piece_at)
        k = len(peers)
        rc(buf.at[pl.ds(0, k)], buf.at[pl.ds(0, k)], ssem, rsem, peers[0]).wait_recv()

    g = start_ref[...] * (LOG2E / EPS)
    f = None
    f_rows = None
    for it in range(ITERS):
        for b in range(4):
            parts = []
            for r in range(b * LANE, (b + 1) * LANE, 32):
                s = [g[q:q + 1, :] - cross[r:r + 32, q * LANE:(q + 1) * LANE] for q in range(4)]
                top = jnp.maximum(jnp.maximum(s[0], s[1]), jnp.maximum(s[2], s[3]))
                e = [jnp.exp2(v - top) for v in s]
                parts.append(top + jnp.log2((e[0] + e[1]) + (e[2] + e[3])))
            rowx[it, col, b:b + 1, :] = merge_rows(jnp.concatenate(parts, axis=0).T)
        exchange(rowx.at[it], col, col_peers, r_send.at[it], r_recv.at[it])
        f = -(math.log2(m_total) + merge(rowx[it]))
        f_rows = [to_rows(f[b:b + 1, :]) for b in range(4)]
        parts = []
        for r in range(0, BLK, 64):
            fr = f_rows[r // LANE][r % LANE:r % LANE + 64]
            s = (fr - cross[r:r + 64, :]).reshape(8, 8, BLK)
            top = jnp.max(s, axis=0)
            parts.append(top + jnp.log2(jnp.sum(jnp.exp2(s - top[None]), axis=0)))
        top = parts[0]
        for v in parts[1:]:
            top = jnp.maximum(top, v)
        own = merge_rows(top + jnp.log2(sum(jnp.exp2(v - top) for v in parts)))
        for q in range(4):
            col2[it, row, q:q + 1, :] = own[:, q * LANE:(q + 1) * LANE]
        exchange(col2.at[it], row, row_peers, c2_send.at[it], c2_recv.at[it])
        g = -(math.log2(n_total) + merge(col2[it]))

    npot_ref[...] = f * (EPS / LOG2E)
    lpot_ref[...] = g * (EPS / LOG2E)

    LOW, HIGH = slice(0, SPLIT), slice(SPLIT, BLK)
    gw = wide(g)

    def weights(cols):
        for b in range(4):
            rows = slice(b * LANE, (b + 1) * LANE)
            w = m_total * jnp.exp2((f_rows[b] + gw[:, cols]) - cross[rows, cols])
            wt[core, cols, rows] = w.T.astype(BF16)

    def wcopy(j, src, dst, dev, r=None):
        return rc(src, dst, w_send.at[j], w_recv.at[j if r is None else 3 * r], dev)

    low, high = pl.ds(0, SPLIT), pl.ds(SPLIT, REST)
    copies = []
    weights(HIGH)
    for k in range(2):
        copies.append(wcopy(3 * k, wt.at[core, high], wx.at[core], (across + k, col), core))
        copies[-1].start()
    weights(LOW)
    copies.append(wcopy(1, wt.at[core, low], wt.at[core, low], other_core))
    copies[-1].start()
    copies.append(wcopy(2, wt.at[core, high], wt.at[core, high], other_core))
    copies[-1].start()

    def mine(d, q):
        return nz[d, :, pl.ds(pl.multiple_of(q * 256 + core * LANE, LANE), LANE)]

    def theirs(d, q):
        return no[d, :, pl.ds(pl.multiple_of(q * LANE, LANE), LANE)]

    def partial_own(rel):
        d = (z + rel) % Z
        part[rel] = jnp.dot(
            wt[core, LOW, :], jnp.concatenate([mine(d, q) for q in (1 - xl, xl)], axis=1),
            preferred_element_type=F32,
        )

    def partial_other(rel):
        d = (z + rel) % Z
        part[rel] += jnp.dot(
            wt[1 - core, LOW, :], jnp.concatenate([theirs(d, q) for q in (1 - xl, xl)], axis=1),
            preferred_element_type=F32,
        )

    def partial(rel):
        partial_own(rel)
        partial_other(rel)

    def partial_high(rel):
        d = (z + rel) % Z
        parth[rel] = (
            jnp.dot(wt[core, HIGH, :], mine(d, xl), preferred_element_type=F32)
            + jnp.dot(wt[1 - core, HIGH, :], theirs(d, xl), preferred_element_type=F32)
        ) + (
            jnp.dot(wx[0], nx[0, d], preferred_element_type=F32)
            + jnp.dot(wx[1], nx[1, d], preferred_element_type=F32)
        )

    def size(k):
        return REST if k == 2 else SPLIT

    def piece(k, bufs, dr, s):
        ref = bufs[1].at[dr, 4 - s] if k == 2 else bufs[0].at[dr, 4 - s, k]
        h = size(k) // 2
        return ref.at[pl.ds(dr * h, h)] if s == 4 else ref

    def ring_copy(k, dr, s):
        ss, rs = (t_send.at[dr, 4 - s], t_recv.at[dr, 4 - s]) if k == 2 else (
            s_send.at[dr, 4 - s, k], s_recv.at[dr, 4 - s, k])
        return rc(
            piece(k, (stage, stageh), dr, s), piece(k, (land, landh), dr, s), ss, rs,
            z_dn if dr == 0 else z_up,
        )

    def own_part(k, rel, rows):
        return parth[rel, rows, :] if k == 2 else part[rel, rows, k * LANE:(k + 1) * LANE]

    def got(k, dr, s, rows):
        v = landh[dr, 4 - s, rows, :] if k == 2 else land[dr, 4 - s, k, rows, :]
        return v.astype(F32)

    def put(k, dr, s, rows, v):
        if k == 2:
            stageh[dr, 4 - s, rows, :] = v.astype(BF16)
        else:
            stage[dr, 4 - s, k, rows, :] = v.astype(BF16)

    leaving = {}

    def ring_step(k, s):
        h = size(k) // 2
        both = slice(0, 2 * h)
        for dr in range(2):
            rel = Z - s if dr == 0 else s
            first = slice(dr * h, (dr + 1) * h)
            other = slice((1 - dr) * h, (2 - dr) * h)
            if s == 4:
                put(k, dr, s, first, own_part(k, 4, first))
            else:
                ring_copy(k, dr, s + 1).wait_recv()
                if s == 3:
                    put(k, dr, s, first, own_part(k, rel, first) + got(k, dr, 4, first))
                    put(k, dr, s, other, own_part(k, rel, other))
                else:
                    put(k, dr, s, both, own_part(k, rel, both) + got(k, dr, s + 1, both))
            if dr in leaving:
                leaving[dr].wait_send()
            leaving[dr] = ring_copy(k, dr, s)
            leaving[dr].start()

    def total(k):
        both = slice(0, size(k))
        for dr in range(2):
            ring_copy(k, dr, 1).wait_recv()
        return own_part(k, 0, both) + (got(k, 0, 1, both) + got(k, 1, 1, both))

    for rel in (4, 5, 3):
        partial_own(rel)
    for q in range(2):
        rc(no.at[:, :, pl.ds(q * LANE, LANE)], no.at[:, :, pl.ds(q * LANE, LANE)],
           o_send.at[q], o_recv.at[q], other_core).wait_recv()
    wcopy(1, wt.at[core, low], wt.at[1 - core, low], other_core).wait_recv()
    partial_other(4)
    ring_step(0, 4)
    partial_other(5)
    partial_other(3)
    ring_step(1, 4)
    wcopy(2, wt.at[core, high], wt.at[1 - core, high], other_core).wait_recv()
    for c in range(2):
        for slot in range(Z):
            rc(nx.at[c, slot], nx.at[c, slot], p_send.at[0, slot], p_recv.at[c, slot], other_xl).wait_recv()
    ring_step(0, 3)
    for c in range(2):
        wcopy(0, wt.at[core, high], wx.at[c], other_xl, c).wait_recv()
    partial_high(4)
    ring_step(1, 3)
    partial(6)
    partial(2)
    ring_step(2, 4)
    ring_step(0, 2)
    partial_high(5)
    partial_high(3)
    ring_step(1, 2)
    partial(7)
    partial(1)
    ring_step(2, 3)
    ring_step(0, 1)
    partial(0)
    partial_high(6)
    partial_high(2)
    ring_step(1, 1)
    ring_step(2, 2)
    xs[...] = total(0)
    xc = rc(xs, xr, x_send.at[0], x_recv.at[0], other_xl)
    xc.start()
    copies.append(xc)
    for rel in (7, 1, 0):
        partial_high(rel)
    ring_step(2, 1)
    kept = total(1)
    out_ref[:, HIGH] = total(2).T
    xc.wait_recv()
    out_ref[:, LOW] = (kept + xr[...]).T
    sent.extend(copies)
    sent.extend(leaving.values())

    for j, (buf, k) in enumerate(((nsq, 7), (lsq, 31))):
        ref = buf.at[pl.ds(0, k)]
        rc(ref, ref, q_send.at[j], q_recv.at[j], z_up).wait_send()
    for c in sent:
        c.wait_send()
    for it in range(ITERS):
        for buf, k, ssem, rsem in (
            (rowx, 7, r_send, r_recv), (col2, 31, c2_send, c2_recv)
        ):
            ref = buf.at[it, pl.ds(0, k)]
            rc(ref, ref, ssem.at[it], rsem.at[it], z_up).wait_send()


def per_device(n_total, m_total, noise_draw, latent_code, start_potential):
    anyspace = pl.BlockSpec(memory_space=pltpu.HBM)
    vmem = pl.BlockSpec(memory_space=pltpu.VMEM)
    width = 4096
    dma = pltpu.SemaphoreType.DMA

    def body(*refs):
        kernel(n_total, m_total, width, *refs)

    npot, lpot, out = pl.pallas_call(
        body,
        out_shape=(
            jax.ShapeDtypeStruct((4, LANE), F32),
            jax.ShapeDtypeStruct((4, LANE), F32),
            jax.ShapeDtypeStruct((LANE, BLK), F32),
        ),
        in_specs=[anyspace, anyspace, vmem],
        out_specs=(vmem, vmem, vmem),
        scratch_shapes=[
            pltpu.VMEM((8, BLK, BLK), BF16),
            pltpu.VMEM((Z, 2, 2, BLK, LANE), BF16),
            pltpu.VMEM((8, BLK, 2 * LANE), BF16),
            pltpu.VMEM((BLK, BLK), F32),
            pltpu.VMEM((8, 4, LANE), F32),
            pltpu.VMEM((32, 4, LANE), F32),
            pltpu.VMEM((2, BLK, BLK), BF16),
            pltpu.VMEM((2, REST, BLK), BF16),
            pltpu.VMEM((2, Z, BLK, LANE), BF16),
            pltpu.VMEM((Z, SPLIT, 2 * LANE), F32),
            pltpu.VMEM((Z, REST, LANE), F32),
            pltpu.VMEM((2, 4, 2, SPLIT, LANE), BF16),
            pltpu.VMEM((2, 4, 2, SPLIT, LANE), BF16),
            pltpu.VMEM((2, 4, REST, LANE), BF16),
            pltpu.VMEM((2, 4, REST, LANE), BF16),
            pltpu.VMEM((SPLIT, LANE), F32),
            pltpu.VMEM((SPLIT, LANE), F32),
            pltpu.VMEM((ITERS, 8, 4, LANE), F32),
            pltpu.VMEM((ITERS, 32, 4, LANE), F32),
            dma((2,)), dma((2,)),
            dma((12,)), dma((12,)),
            dma((2, 2)), dma((2, 2)),
            dma((25,)), dma((25,)),
            dma((2,)), dma((2,)),
            dma((4,)), dma((4,)),
            dma((2, Z)), dma((2, Z)),
            dma((ITERS,)), dma((ITERS,)),
            dma((ITERS,)), dma((ITERS,)),
            dma((2, 4, 2)), dma((2, 4, 2)),
            dma((2, 4)), dma((2, 4)),
            dma((1,)), dma((1,)),
            dma((2,)),
        ],
        compiler_params=pltpu.CompilerParams(
            collective_id=0, has_side_effects=True, vmem_limit_bytes=54656 * 1024
        ),
    )(noise_draw, latent_code, start_potential.reshape(4, LANE))
    return npot.reshape(BLK), lpot.reshape(BLK), out


def solution(mesh):
    in_specs = (P("row", "col"), P("col", "row"), P("col"))
    out_specs = (P("row"), P("col"), P("row", "col"))

    def whole(noise_draw, latent_code, start_potential):
        def block(a, b, c):
            return per_device(noise_draw.shape[0], latent_code.shape[0], a, b, c)

        return jax.shard_map(
            block, mesh=mesh, in_specs=in_specs, out_specs=out_specs, check_vma=False
        )(noise_draw, latent_code, start_potential)

    return whole
```

```python
import math

import jax
import jax.numpy as jnp
from jax import lax
from jax.experimental import pallas as pl
from jax.experimental.pallas import tpu as pltpu
from jax.sharding import PartitionSpec as P

ITERS = 3
EPS = 0.01
LOG2E = math.log2(math.e)
MESH = pl.DeviceIdType.MESH
F32 = jnp.float32
BF16 = jnp.bfloat16

Z, Y = 8, 4
LANE = 128
BLK = 512
HALF = BLK // 2
SPLIT = 384
REST = BLK - SPLIT


def kernel(
    n_total, m_total, width,
    noise_ref, latent_ref, start_ref,
    npot_ref, lpot_ref, out_ref,
    nz, lt, no, cross, nsq, lsq, wt, wx, nx, part, parth, stage, land, stageh, landh, xs, xr, rowx, col2,
    q_send, q_recv, n_send, n_recv, h_send, h_recv, l_send, l_recv, o_send, o_recv, w_send, w_recv,
    p_send, p_recv, r_send, r_recv, c2_send, c2_recv,
    s_send, s_recv, t_send, t_recv, x_send, x_recv, loc,
):
    row = lax.axis_index("row")
    col = lax.axis_index("col")
    z = row // 4
    xl = (row // 2) % 2
    core = row % 2
    y = col // 2
    xh = col % 2
    quad = row % 4

    def ring_z(d):
        return (z + d + Z) % Z

    def ring_y(d):
        return (y + d + Y) % Y

    other_core = (row + 1 - 2 * core, col)
    other_xl = (row + 2 - 4 * xl, col)
    flip_col = col + 1 - 2 * xh
    other_xh = (row, flip_col)
    z_up = (ring_z(1) * 4 + quad, col)
    z_dn = (ring_z(-1) * 4 + quad, col)
    y_up = (row, ring_y(1) * 2 + xh)
    y_dn = (row, ring_y(-1) * 2 + xh)
    col_peers = [
        (row, ring_y(dy) * 2 + (1 - xh if dx else xh))
        for dy, dx in ((2, 1), (1, 1), (-1, 1), (2, 0), (0, 1), (1, 0), (-1, 0))
    ]
    across = (row + 2 - 4 * xl) // 2 * 2
    across_quad = ((across + 1 - core) % 4, (across + core) % 4, (quad // 2) * 2 + 1 - core, quad)
    row_peers = [
        (ring_z(d) * 4 + q, col)
        for d in (4, 3, -3, 2, -2, 1, -1, 0) for q in across_quad[:3 if d == 0 else 4]
    ]
    peers = col_peers + row_peers + [(across, flip_col), (across + 1, flip_col)]

    own_n = pltpu.make_async_copy(noise_ref, nz.at[col], loc.at[0])
    own_l = pltpu.make_async_copy(latent_ref, lt.at[z, core, xl], loc.at[1])
    own_n.start()
    own_l.start()

    barrier = pltpu.get_barrier_semaphore()
    for peer in peers:
        pl.semaphore_signal(barrier, inc=1, device_id=peer, device_id_type=MESH)
    cross[...] = jnp.zeros_like(cross)
    pl.semaphore_wait(barrier, len(peers))

    def rc(src, dst, ssem, rsem, dev):
        return pltpu.make_async_remote_copy(
            src_ref=src, dst_ref=dst, send_sem=ssem, recv_sem=rsem,
            device_id=dev, device_id_type=MESH,
        )

    def nsl(slot, h):
        return nz.at[slot, pl.ds(h * HALF, HALF), :]

    QUART = HALF // 2
    sent = []

    def nsend(slot, h, idx, dev, src=None):
        src = nsl(slot, h) if src is None else src
        c = rc(src, nsl(slot, h), n_send.at[idx], n_recv.at[idx], dev)
        c.start()
        return c

    def own_half(h):
        return noise_ref.at[pl.ds(h * HALF, HALF), :]

    def nwait(slot, h, idx):
        rc(nsl(slot, h), nsl(slot, h), n_send.at[idx], n_recv.at[idx], y_up).wait_recv()

    def lsend(ref, idx, dev, src=None):
        c = rc(ref if src is None else src, ref, l_send.at[idx], l_recv.at[idx], dev)
        c.start()
        sent.append(c)

    def lwait(ref, idx):
        rc(ref, ref, l_send.at[idx], l_recv.at[idx], z_up).wait_recv()

    def slot_of(yy, s):
        return yy * 2 + (xh if s == 0 else 1 - xh)

    def xh_copy(t, h, src, slot):
        return rc(src, nsl(slot, h), h_send.at[t, h], h_recv.at[t, h], other_xh)

    def xh_send(t, h):
        far0 = slot_of(ring_y(2), 0)
        c = xh_copy(t, h, own_half(h), col) if t == 0 else xh_copy(t, h, nsl(far0, h), far0)
        c.start()
        sent.append(c)

    def xh_wait(t, h):
        slot = flip_col if t == 0 else slot_of(ring_y(2), 1)
        xh_copy(t, h, nsl(slot, h), slot).wait_recv()

    own_pair = lt.at[z, core]
    own_block = lt.at[z, core, xl]
    z_dirs = ((0, -1, z_up), (1, 1, z_dn))

    def lat(d, part):
        return lt.at[ring_z(d), core, xl if part == 0 else 1 - xl]

    def lat_forward(step, part, dirs):
        for dr, sgn, dev in dirs:
            block = lat(sgn * step, part)
            lwait(block, 1 + 8 * dr + 2 * (step - 1) + part)
            if step < 3 or part == dr:
                lsend(block, 1 + 8 * dr + 2 * step + part, dev)

    def lat_share(step):
        for dr, sgn, _ in z_dirs:
            lsend(lt.at[ring_z(sgn * step), core], 16 + 2 * step + dr, other_core)

    lat_x = rc(latent_ref, own_block, l_send.at[0], l_recv.at[0], other_xl)
    lat_x.start()
    lsend(own_block, 1, z_up, latent_ref)
    lsend(own_block, 9, z_dn, latent_ref)
    first_up = nsend(col, 0, 0, y_up, own_half(0))
    first_dn = nsend(col, 1, 3, y_dn, own_half(1))

    sent.append(lat_x)
    xh_send(0, 0)
    xh_send(0, 1)

    own_n.wait()
    own_l.wait()
    for b in range(4):
        rows = slice(b * LANE, (b + 1) * LANE)
        n2 = jnp.square(nz[col, rows, :].astype(F32))
        n2 = (n2[:, 0:128] + n2[:, 128:256]) + (n2[:, 256:384] + n2[:, 384:512])
        nsq[col, b:b + 1, :] = jnp.sum(n2.T, axis=0, keepdims=True)
        l2 = jnp.square(lt[z, core, xl, rows, :].astype(F32))
        lsq[row, b:b + 1, :] = jnp.sum(l2.T, axis=0, keepdims=True)

    lwait(lat(0, 1), 0)
    lsend(lat(0, 1), 2, z_up)
    lsend(lat(0, 1), 10, z_dn)
    lat_forward(1, 0, z_dirs)
    lsend(own_pair, 17, other_core)

    def own_quarter(h, p, idx, dev):
        at = pl.ds(h * HALF + p * QUART, QUART)
        c = rc(noise_ref.at[at, :], nz.at[col, at, :], n_send.at[idx], n_recv.at[idx], dev)
        c.start()
        sent.append(c)

    first_up.wait_send()
    own_quarter(1, 0, 1, y_up)
    first_dn.wait_send()
    own_quarter(0, 0, 2, y_dn)

    dn, up = slot_of(ring_y(-1), 0), slot_of(ring_y(1), 0)
    nwait(dn, 0, 0)
    onward_up = nsend(dn, 0, 4, y_up)
    nwait(up, 1, 3)
    onward_dn = nsend(up, 1, 5, y_dn)

    lat_forward(1, 1, z_dirs)
    lat_share(1)
    for peer in col_peers:
        rc(nsq.at[col], nsq.at[col], q_send.at[0], q_recv.at[0], peer).start()
    for peer in row_peers:
        rc(lsq.at[row], lsq.at[row], q_send.at[1], q_recv.at[1], peer).start()
    lat_forward(2, 0, z_dirs)
    lat_forward(2, 1, z_dirs)
    lat_share(2)

    onward_up.wait_send()
    own_quarter(1, 1, 10, y_up)
    onward_dn.wait_send()
    own_quarter(0, 1, 11, y_dn)

    nwait(slot_of(ring_y(2), 0), 0, 4)
    xh_send(1, 0)
    nwait(slot_of(ring_y(2), 0), 1, 5)
    xh_send(1, 1)

    lat_forward(3, 0, z_dirs)

    xh_wait(0, 0)
    sent.append(nsend(flip_col, 0, 6, y_up))
    sent.append(nsend(flip_col, 0, 8, y_dn))
    xh_wait(0, 1)
    sent.append(nsend(flip_col, 1, 9, y_dn))
    sent.append(nsend(flip_col, 1, 7, y_up))

    lat_forward(3, 1, z_dirs)
    lat_share(3)
    lwait(lat(4, 0), 7)
    lwait(lat(4, 1), 16)
    lsend(lt.at[ring_z(4), core], 24, other_core)
    for j, d in enumerate((0, -1, 1, -2, 2, -3, 3, 4)):
        lwait(lt.at[ring_z(d), 1 - core], 17 + j)

    def accumulate(slot):
        a = nz[slot]
        b = jnp.concatenate([lt[slot, 0, 0], lt[slot, 1, 0], lt[slot, 0, 1], lt[slot, 1, 1]], axis=1)
        cross[...] += lax.dot_general(a, b, (((1,), (1,)), ((), ())), preferred_element_type=F32)

    dn, up = slot_of(ring_y(-1), 0), slot_of(ring_y(1), 0)
    for slot, h, idxs in ((dn, 1, (1, 10)), (up, 0, (2, 11))):
        for p in range(2):
            ref = nz.at[slot, pl.ds(h * HALF + p * QUART, QUART), :]
            rc(ref, ref, n_send.at[idxs[p]], n_recv.at[idxs[p]], y_up).wait_recv()

    def set0(k, carry):
        accumulate(((y + k) % Y) * 2 + xh)
        return carry

    lax.fori_loop(0, Y, set0, 0)
    accumulate(flip_col)
    xh_wait(1, 0)
    xh_wait(1, 1)
    accumulate(slot_of(ring_y(2), 1))
    dn, up = slot_of(ring_y(-1), 1), slot_of(ring_y(1), 1)
    nwait(dn, 0, 6)
    nwait(up, 1, 9)
    nwait(dn, 1, 7)
    nwait(up, 0, 8)
    accumulate(dn)
    accumulate(up)

    for q in range(2):
        c = rc(
            nz.at[:, :, pl.ds(pl.multiple_of(q * 256 + (1 - core) * LANE, LANE), LANE)],
            no.at[:, :, pl.ds(q * LANE, LANE)],
            o_send.at[q], o_recv.at[q], other_core,
        )
        c.start()
        sent.append(c)

    eye = (
        lax.broadcasted_iota(jnp.int32, (LANE, LANE), 0)
        == lax.broadcasted_iota(jnp.int32, (LANE, LANE), 1)
    )

    def to_rows(v):
        return jnp.sum(jnp.where(eye, v, 0.0), axis=1, keepdims=True)

    def wide(v):
        return jnp.concatenate([v[q:q + 1, :] for q in range(4)], axis=1)

    scale = LOG2E / (width * EPS)
    rc(nsq.at[pl.ds(0, 7)], nsq.at[pl.ds(0, 7)], q_send.at[0], q_recv.at[0], z_up).wait_recv()
    rc(lsq.at[pl.ds(0, 31)], lsq.at[pl.ds(0, 31)], q_send.at[1], q_recv.at[1], z_up).wait_recv()
    nq = jnp.sum(nsq[...], axis=0)
    lq = wide(jnp.sum(lsq[...], axis=0))
    for b in range(4):
        rows = slice(b * LANE, (b + 1) * LANE)
        cross[rows, :] = (to_rows(nq[b:b + 1, :]) + lq - 2.0 * cross[rows, :]) * scale

    def merge(parts):
        best = jnp.max(parts, axis=0)
        return best + jnp.log2(jnp.sum(jnp.exp2(parts - best[None]), axis=0))

    def merge_rows(parts):
        best = jnp.max(parts, axis=0, keepdims=True)
        return best + jnp.log2(jnp.sum(jnp.exp2(parts - best), axis=0, keepdims=True))

    def lend(step):
        k, zz = step % 2, step // 2
        lanes = pl.ds(pl.multiple_of((1 - xl) * 256 + k * LANE, LANE), LANE)
        for slot, dev in ((zz, (across + k, col)), (zz + 4, (across + k, flip_col))):
            c = rc(nz.at[slot, :, lanes], nx.at[core, slot], p_send.at[k, slot], p_recv.at[core, slot], dev)
            c.start()
            sent.append(c)

    steps = iter(range(6))

    def exchange(buf, mine, peers, ssem, rsem):
        for peer in peers:
            rc(buf.at[mine], buf.at[mine], ssem, rsem, peer).start()
        step = next(steps)
        for piece_at in range(*((0, 2), (2, 4), (4, 6), (6, 7), (7, 8), (8, 8))[step]):
            lend(piece_at)
        k = len(peers)
        rc(buf.at[pl.ds(0, k)], buf.at[pl.ds(0, k)], ssem, rsem, peers[0]).wait_recv()

    g = start_ref[...] * (LOG2E / EPS)
    f = None
    f_rows = None
    for it in range(ITERS):
        for b in range(4):
            parts = []
            for r in range(b * LANE, (b + 1) * LANE, 32):
                s = [g[q:q + 1, :] - cross[r:r + 32, q * LANE:(q + 1) * LANE] for q in range(4)]
                top = jnp.maximum(jnp.maximum(s[0], s[1]), jnp.maximum(s[2], s[3]))
                e = [jnp.exp2(v - top) for v in s]
                parts.append(top + jnp.log2((e[0] + e[1]) + (e[2] + e[3])))
            rowx[it, col, b:b + 1, :] = merge_rows(jnp.concatenate(parts, axis=0).T)
        exchange(rowx.at[it], col, col_peers, r_send.at[it], r_recv.at[it])
        f = -(math.log2(m_total) + merge(rowx[it]))
        f_rows = [to_rows(f[b:b + 1, :]) for b in range(4)]
        parts = []
        for r in range(0, BLK, 64):
            fr = f_rows[r // LANE][r % LANE:r % LANE + 64]
            s = (fr - cross[r:r + 64, :]).reshape(8, 8, BLK)
            top = jnp.max(s, axis=0)
            parts.append(top + jnp.log2(jnp.sum(jnp.exp2(s - top[None]), axis=0)))
        top = parts[0]
        for v in parts[1:]:
            top = jnp.maximum(top, v)
        own = merge_rows(top + jnp.log2(sum(jnp.exp2(v - top) for v in parts)))
        for q in range(4):
            col2[it, row, q:q + 1, :] = own[:, q * LANE:(q + 1) * LANE]
        exchange(col2.at[it], row, row_peers, c2_send.at[it], c2_recv.at[it])
        g = -(math.log2(n_total) + merge(col2[it]))

    npot_ref[...] = f * (EPS / LOG2E)
    lpot_ref[...] = g * (EPS / LOG2E)

    LOW, HIGH = slice(0, SPLIT), slice(SPLIT, BLK)
    gw = wide(g)

    def weights(cols):
        for b in range(4):
            rows = slice(b * LANE, (b + 1) * LANE)
            w = m_total * jnp.exp2((f_rows[b] + gw[:, cols]) - cross[rows, cols])
            wt[core, cols, rows] = w.T.astype(BF16)

    def wcopy(j, src, dst, dev, r=None):
        return rc(src, dst, w_send.at[j], w_recv.at[j if r is None else 3 * r], dev)

    low, high = pl.ds(0, SPLIT), pl.ds(SPLIT, REST)
    copies = []
    weights(HIGH)
    for k in range(2):
        copies.append(wcopy(3 * k, wt.at[core, high], wx.at[core], (across + k, col), core))
        copies[-1].start()
    weights(LOW)
    copies.append(wcopy(1, wt.at[core, low], wt.at[core, low], other_core))
    copies[-1].start()
    copies.append(wcopy(2, wt.at[core, high], wt.at[core, high], other_core))
    copies[-1].start()

    def mine(d, q):
        return nz[d, :, pl.ds(pl.multiple_of(q * 256 + core * LANE, LANE), LANE)]

    def theirs(d, q):
        return no[d, :, pl.ds(pl.multiple_of(q * LANE, LANE), LANE)]

    def partial_own(rel):
        d = (z + rel) % Z
        part[rel] = jnp.dot(
            wt[core, LOW, :], jnp.concatenate([mine(d, q) for q in (1 - xl, xl)], axis=1),
            preferred_element_type=F32,
        )

    def partial_other(rel):
        d = (z + rel) % Z
        part[rel] += jnp.dot(
            wt[1 - core, LOW, :], jnp.concatenate([theirs(d, q) for q in (1 - xl, xl)], axis=1),
            preferred_element_type=F32,
        )

    def partial(rel):
        partial_own(rel)
        partial_other(rel)

    def partial_high(rel):
        d = (z + rel) % Z
        parth[rel] = (
            jnp.dot(wt[core, HIGH, :], mine(d, xl), preferred_element_type=F32)
            + jnp.dot(wt[1 - core, HIGH, :], theirs(d, xl), preferred_element_type=F32)
        ) + (
            jnp.dot(wx[0], nx[0, d], preferred_element_type=F32)
            + jnp.dot(wx[1], nx[1, d], preferred_element_type=F32)
        )

    def size(k):
        return REST if k == 2 else SPLIT

    def piece(k, bufs, dr, s):
        ref = bufs[1].at[dr, 4 - s] if k == 2 else bufs[0].at[dr, 4 - s, k]
        h = size(k) // 2
        return ref.at[pl.ds(dr * h, h)] if s == 4 else ref

    def ring_copy(k, dr, s):
        ss, rs = (t_send.at[dr, 4 - s], t_recv.at[dr, 4 - s]) if k == 2 else (
            s_send.at[dr, 4 - s, k], s_recv.at[dr, 4 - s, k])
        return rc(
            piece(k, (stage, stageh), dr, s), piece(k, (land, landh), dr, s), ss, rs,
            z_dn if dr == 0 else z_up,
        )

    def own_part(k, rel, rows):
        return parth[rel, rows, :] if k == 2 else part[rel, rows, k * LANE:(k + 1) * LANE]

    def got(k, dr, s, rows):
        v = landh[dr, 4 - s, rows, :] if k == 2 else land[dr, 4 - s, k, rows, :]
        return v.astype(F32)

    def put(k, dr, s, rows, v):
        if k == 2:
            stageh[dr, 4 - s, rows, :] = v.astype(BF16)
        else:
            stage[dr, 4 - s, k, rows, :] = v.astype(BF16)

    def ring_step(k, s):
        h = size(k) // 2
        both = slice(0, 2 * h)
        for dr in range(2):
            rel = Z - s if dr == 0 else s
            first = slice(dr * h, (dr + 1) * h)
            other = slice((1 - dr) * h, (2 - dr) * h)
            if s == 4:
                put(k, dr, s, first, own_part(k, 4, first))
            else:
                ring_copy(k, dr, s + 1).wait_recv()
                if s == 3:
                    put(k, dr, s, first, own_part(k, rel, first) + got(k, dr, 4, first))
                    put(k, dr, s, other, own_part(k, rel, other))
                else:
                    put(k, dr, s, both, own_part(k, rel, both) + got(k, dr, s + 1, both))
            c = ring_copy(k, dr, s)
            c.start()
            sent.append(c)

    def total(k):
        both = slice(0, size(k))
        for dr in range(2):
            ring_copy(k, dr, 1).wait_recv()
        return own_part(k, 0, both) + (got(k, 0, 1, both) + got(k, 1, 1, both))

    for rel in (4, 5, 3):
        partial_own(rel)
    for q in range(2):
        rc(no.at[:, :, pl.ds(q * LANE, LANE)], no.at[:, :, pl.ds(q * LANE, LANE)],
           o_send.at[q], o_recv.at[q], other_core).wait_recv()
    wcopy(1, wt.at[core, low], wt.at[1 - core, low], other_core).wait_recv()
    partial_other(4)
    ring_step(0, 4)
    partial_other(5)
    partial_other(3)
    ring_step(1, 4)
    wcopy(2, wt.at[core, high], wt.at[1 - core, high], other_core).wait_recv()
    for c in range(2):
        for slot in range(Z):
            rc(nx.at[c, slot], nx.at[c, slot], p_send.at[0, slot], p_recv.at[c, slot], other_xl).wait_recv()
    ring_step(0, 3)
    for c in range(2):
        wcopy(0, wt.at[core, high], wx.at[c], other_xl, c).wait_recv()
    partial_high(4)
    ring_step(1, 3)
    partial(6)
    partial(2)
    ring_step(2, 4)
    ring_step(0, 2)
    partial_high(5)
    partial_high(3)
    ring_step(1, 2)
    partial(7)
    partial(1)
    ring_step(2, 3)
    ring_step(0, 1)
    partial(0)
    partial_high(6)
    partial_high(2)
    ring_step(1, 1)
    ring_step(2, 2)
    xs[...] = total(0)
    xc = rc(xs, xr, x_send.at[0], x_recv.at[0], other_xl)
    xc.start()
    copies.append(xc)
    for rel in (7, 1, 0):
        partial_high(rel)
    ring_step(2, 1)
    kept = total(1)
    out_ref[:, HIGH] = total(2).T
    xc.wait_recv()
    out_ref[:, LOW] = (kept + xr[...]).T
    sent.extend(copies)

    for j, (buf, k) in enumerate(((nsq, 7), (lsq, 31))):
        ref = buf.at[pl.ds(0, k)]
        rc(ref, ref, q_send.at[j], q_recv.at[j], z_up).wait_send()
    for c in sent:
        c.wait_send()
    for it in range(ITERS):
        for buf, k, ssem, rsem in (
            (rowx, 7, r_send, r_recv), (col2, 31, c2_send, c2_recv)
        ):
            ref = buf.at[it, pl.ds(0, k)]
            rc(ref, ref, ssem.at[it], rsem.at[it], z_up).wait_send()


def per_device(n_total, m_total, noise_draw, latent_code, start_potential):
    anyspace = pl.BlockSpec(memory_space=pltpu.HBM)
    vmem = pl.BlockSpec(memory_space=pltpu.VMEM)
    width = 4096
    dma = pltpu.SemaphoreType.DMA

    def body(*refs):
        kernel(n_total, m_total, width, *refs)

    npot, lpot, out = pl.pallas_call(
        body,
        out_shape=(
            jax.ShapeDtypeStruct((4, LANE), F32),
            jax.ShapeDtypeStruct((4, LANE), F32),
            jax.ShapeDtypeStruct((LANE, BLK), F32),
        ),
        in_specs=[anyspace, anyspace, vmem],
        out_specs=(vmem, vmem, vmem),
        scratch_shapes=[
            pltpu.VMEM((8, BLK, BLK), BF16),
            pltpu.VMEM((Z, 2, 2, BLK, LANE), BF16),
            pltpu.VMEM((8, BLK, 2 * LANE), BF16),
            pltpu.VMEM((BLK, BLK), F32),
            pltpu.VMEM((8, 4, LANE), F32),
            pltpu.VMEM((32, 4, LANE), F32),
            pltpu.VMEM((2, BLK, BLK), BF16),
            pltpu.VMEM((2, REST, BLK), BF16),
            pltpu.VMEM((2, Z, BLK, LANE), BF16),
            pltpu.VMEM((Z, SPLIT, 2 * LANE), F32),
            pltpu.VMEM((Z, REST, LANE), F32),
            pltpu.VMEM((2, 4, 2, SPLIT, LANE), BF16),
            pltpu.VMEM((2, 4, 2, SPLIT, LANE), BF16),
            pltpu.VMEM((2, 4, REST, LANE), BF16),
            pltpu.VMEM((2, 4, REST, LANE), BF16),
            pltpu.VMEM((SPLIT, LANE), F32),
            pltpu.VMEM((SPLIT, LANE), F32),
            pltpu.VMEM((ITERS, 8, 4, LANE), F32),
            pltpu.VMEM((ITERS, 32, 4, LANE), F32),
            dma((2,)), dma((2,)),
            dma((12,)), dma((12,)),
            dma((2, 2)), dma((2, 2)),
            dma((25,)), dma((25,)),
            dma((2,)), dma((2,)),
            dma((4,)), dma((4,)),
            dma((2, Z)), dma((2, Z)),
            dma((ITERS,)), dma((ITERS,)),
            dma((ITERS,)), dma((ITERS,)),
            dma((2, 4, 2)), dma((2, 4, 2)),
            dma((2, 4)), dma((2, 4)),
            dma((1,)), dma((1,)),
            dma((2,)),
        ],
        compiler_params=pltpu.CompilerParams(
            collective_id=0, has_side_effects=True, vmem_limit_bytes=54656 * 1024
        ),
    )(noise_draw, latent_code, start_potential.reshape(4, LANE))
    return npot.reshape(BLK), lpot.reshape(BLK), out


def solution(mesh):
    in_specs = (P("row", "col"), P("col", "row"), P("col"))
    out_specs = (P("row"), P("col"), P("row", "col"))

    def whole(noise_draw, latent_code, start_potential):
        def block(a, b, c):
            return per_device(noise_draw.shape[0], latent_code.shape[0], a, b, c)

        return jax.shard_map(
            block, mesh=mesh, in_specs=in_specs, out_specs=out_specs, check_vma=False
        )(noise_draw, latent_code, start_potential)

    return whole
```

```python
import math

import jax
import jax.numpy as jnp
from jax import lax
from jax.experimental import pallas as pl
from jax.experimental.pallas import tpu as pltpu
from jax.sharding import PartitionSpec as P

ITERS = 3
EPS = 0.01
LOG2E = math.log2(math.e)
MESH = pl.DeviceIdType.MESH
F32 = jnp.float32
BF16 = jnp.bfloat16

Z, Y = 8, 4
LANE = 128
BLK = 512
HALF = BLK // 2
SPLIT = 384
REST = BLK - SPLIT


def kernel(
    n_total, m_total, width,
    noise_ref, latent_ref, start_ref,
    npot_ref, lpot_ref, out_ref,
    nz, lt, no, cross, nsq, lsq, wt, wx, nx, part, parth, stage, land, stageh, landh, xs, xr, rowx, col2,
    q_send, q_recv, n_send, n_recv, h_send, h_recv, l_send, l_recv, o_send, o_recv, w_send, w_recv,
    p_send, p_recv, r_send, r_recv, c2_send, c2_recv,
    s_send, s_recv, t_send, t_recv, x_send, x_recv, loc,
):
    row = lax.axis_index("row")
    col = lax.axis_index("col")
    z = row // 4
    xl = (row // 2) % 2
    core = row % 2
    y = col // 2
    xh = col % 2
    quad = row % 4

    def ring_z(d):
        return (z + d + Z) % Z

    def ring_y(d):
        return (y + d + Y) % Y

    other_core = (row + 1 - 2 * core, col)
    other_xl = (row + 2 - 4 * xl, col)
    flip_col = col + 1 - 2 * xh
    other_xh = (row, flip_col)
    z_up = (ring_z(1) * 4 + quad, col)
    z_dn = (ring_z(-1) * 4 + quad, col)
    y_up = (row, ring_y(1) * 2 + xh)
    y_dn = (row, ring_y(-1) * 2 + xh)
    col_peers = [
        (row, ring_y(dy) * 2 + (1 - xh if dx else xh))
        for dy, dx in ((2, 1), (1, 1), (-1, 1), (2, 0), (0, 1), (1, 0), (-1, 0))
    ]
    across = (row + 2 - 4 * xl) // 2 * 2
    across_quad = ((across + 1 - core) % 4, (across + core) % 4, (quad // 2) * 2 + 1 - core, quad)
    row_peers = [
        (ring_z(d) * 4 + q, col)
        for d in (4, 3, -3, 2, -2, 1, -1, 0) for q in across_quad[:3 if d == 0 else 4]
    ]
    peers = col_peers + row_peers + [(across, flip_col), (across + 1, flip_col)]

    own_n = pltpu.make_async_copy(noise_ref, nz.at[col], loc.at[0])
    own_l = pltpu.make_async_copy(latent_ref, lt.at[z, core, xl], loc.at[1])
    own_n.start()
    own_l.start()

    barrier = pltpu.get_barrier_semaphore()
    for peer in peers:
        pl.semaphore_signal(barrier, inc=1, device_id=peer, device_id_type=MESH)
    cross[...] = jnp.zeros_like(cross)
    pl.semaphore_wait(barrier, len(peers))

    def rc(src, dst, ssem, rsem, dev):
        return pltpu.make_async_remote_copy(
            src_ref=src, dst_ref=dst, send_sem=ssem, recv_sem=rsem,
            device_id=dev, device_id_type=MESH,
        )

    def nsl(slot, h):
        return nz.at[slot, pl.ds(h * HALF, HALF), :]

    QUART = HALF // 2
    sent = []

    def nsend(slot, h, idx, dev, src=None):
        src = nsl(slot, h) if src is None else src
        c = rc(src, nsl(slot, h), n_send.at[idx], n_recv.at[idx], dev)
        c.start()
        return c

    def own_half(h):
        return noise_ref.at[pl.ds(h * HALF, HALF), :]

    def nwait(slot, h, idx):
        rc(nsl(slot, h), nsl(slot, h), n_send.at[idx], n_recv.at[idx], y_up).wait_recv()

    def lsend(ref, idx, dev, src=None):
        c = rc(ref if src is None else src, ref, l_send.at[idx], l_recv.at[idx], dev)
        c.start()
        sent.append(c)

    def lwait(ref, idx):
        rc(ref, ref, l_send.at[idx], l_recv.at[idx], z_up).wait_recv()

    def slot_of(yy, s):
        return yy * 2 + (xh if s == 0 else 1 - xh)

    def xh_copy(t, h, src, slot):
        return rc(src, nsl(slot, h), h_send.at[t, h], h_recv.at[t, h], other_xh)

    def xh_send(t, h):
        far0 = slot_of(ring_y(2), 0)
        c = xh_copy(t, h, own_half(h), col) if t == 0 else xh_copy(t, h, nsl(far0, h), far0)
        c.start()
        sent.append(c)

    def xh_wait(t, h):
        slot = flip_col if t == 0 else slot_of(ring_y(2), 1)
        xh_copy(t, h, nsl(slot, h), slot).wait_recv()

    own_pair = lt.at[z, core]
    own_block = lt.at[z, core, xl]
    z_dirs = ((0, -1, z_up), (1, 1, z_dn))

    def lat(d, part):
        return lt.at[ring_z(d), core, xl if part == 0 else 1 - xl]

    def lat_forward(step, part, dirs):
        for dr, sgn, dev in dirs:
            block = lat(sgn * step, part)
            lwait(block, 1 + 8 * dr + 2 * (step - 1) + part)
            if step < 3 or part == dr:
                lsend(block, 1 + 8 * dr + 2 * step + part, dev)

    def lat_share(step):
        for dr, sgn, _ in z_dirs:
            lsend(lt.at[ring_z(sgn * step), core], 16 + 2 * step + dr, other_core)

    lat_x = rc(latent_ref, own_block, l_send.at[0], l_recv.at[0], other_xl)
    lat_x.start()
    lsend(own_block, 1, z_up, latent_ref)
    lsend(own_block, 9, z_dn, latent_ref)
    first_up = nsend(col, 0, 0, y_up, own_half(0))
    first_dn = nsend(col, 1, 3, y_dn, own_half(1))

    sent.append(lat_x)

    own_n.wait()
    own_l.wait()
    for b in range(4):
        rows = slice(b * LANE, (b + 1) * LANE)
        n2 = jnp.square(nz[col, rows, :].astype(F32))
        n2 = (n2[:, 0:128] + n2[:, 128:256]) + (n2[:, 256:384] + n2[:, 384:512])
        nsq[col, b:b + 1, :] = jnp.sum(n2.T, axis=0, keepdims=True)
        l2 = jnp.square(lt[z, core, xl, rows, :].astype(F32))
        lsq[row, b:b + 1, :] = jnp.sum(l2.T, axis=0, keepdims=True)

    lwait(lat(0, 1), 0)
    lsend(lat(0, 1), 2, z_up)
    lsend(lat(0, 1), 10, z_dn)
    xh_send(0, 0)
    xh_send(0, 1)
    lat_forward(1, 0, z_dirs)
    lsend(own_pair, 17, other_core)

    def own_quarter(h, p, idx, dev):
        at = pl.ds(h * HALF + p * QUART, QUART)
        c = rc(noise_ref.at[at, :], nz.at[col, at, :], n_send.at[idx], n_recv.at[idx], dev)
        c.start()
        sent.append(c)

    first_up.wait_send()
    own_quarter(1, 0, 1, y_up)
    first_dn.wait_send()
    own_quarter(0, 0, 2, y_dn)

    dn, up = slot_of(ring_y(-1), 0), slot_of(ring_y(1), 0)
    nwait(dn, 0, 0)
    onward_up = nsend(dn, 0, 4, y_up)
    nwait(up, 1, 3)
    onward_dn = nsend(up, 1, 5, y_dn)

    lat_forward(1, 1, z_dirs)
    lat_share(1)
    for peer in col_peers:
        rc(nsq.at[col], nsq.at[col], q_send.at[0], q_recv.at[0], peer).start()
    for peer in row_peers:
        rc(lsq.at[row], lsq.at[row], q_send.at[1], q_recv.at[1], peer).start()
    lat_forward(2, 0, z_dirs)
    lat_forward(2, 1, z_dirs)
    lat_share(2)

    onward_up.wait_send()
    own_quarter(1, 1, 10, y_up)
    onward_dn.wait_send()
    own_quarter(0, 1, 11, y_dn)

    nwait(slot_of(ring_y(2), 0), 0, 4)
    xh_send(1, 0)
    nwait(slot_of(ring_y(2), 0), 1, 5)
    xh_send(1, 1)

    lat_forward(3, 0, z_dirs)

    xh_wait(0, 0)
    sent.append(nsend(flip_col, 0, 6, y_up))
    sent.append(nsend(flip_col, 0, 8, y_dn))
    xh_wait(0, 1)
    sent.append(nsend(flip_col, 1, 9, y_dn))
    sent.append(nsend(flip_col, 1, 7, y_up))

    lat_forward(3, 1, z_dirs)
    lat_share(3)
    lwait(lat(4, 0), 7)
    lwait(lat(4, 1), 16)
    lsend(lt.at[ring_z(4), core], 24, other_core)
    for j, d in enumerate((0, -1, 1, -2, 2, -3, 3, 4)):
        lwait(lt.at[ring_z(d), 1 - core], 17 + j)

    def accumulate(slot):
        a = nz[slot]
        b = jnp.concatenate([lt[slot, 0, 0], lt[slot, 1, 0], lt[slot, 0, 1], lt[slot, 1, 1]], axis=1)
        cross[...] += lax.dot_general(a, b, (((1,), (1,)), ((), ())), preferred_element_type=F32)

    dn, up = slot_of(ring_y(-1), 0), slot_of(ring_y(1), 0)
    for slot, h, idxs in ((dn, 1, (1, 10)), (up, 0, (2, 11))):
        for p in range(2):
            ref = nz.at[slot, pl.ds(h * HALF + p * QUART, QUART), :]
            rc(ref, ref, n_send.at[idxs[p]], n_recv.at[idxs[p]], y_up).wait_recv()

    def set0(k, carry):
        accumulate(((y + k) % Y) * 2 + xh)
        return carry

    lax.fori_loop(0, Y, set0, 0)
    accumulate(flip_col)
    xh_wait(1, 0)
    xh_wait(1, 1)
    accumulate(slot_of(ring_y(2), 1))
    dn, up = slot_of(ring_y(-1), 1), slot_of(ring_y(1), 1)
    nwait(dn, 0, 6)
    nwait(up, 1, 9)
    nwait(dn, 1, 7)
    nwait(up, 0, 8)
    accumulate(dn)
    accumulate(up)

    for q in range(2):
        c = rc(
            nz.at[:, :, pl.ds(pl.multiple_of(q * 256 + (1 - core) * LANE, LANE), LANE)],
            no.at[:, :, pl.ds(q * LANE, LANE)],
            o_send.at[q], o_recv.at[q], other_core,
        )
        c.start()
        sent.append(c)

    eye = (
        lax.broadcasted_iota(jnp.int32, (LANE, LANE), 0)
        == lax.broadcasted_iota(jnp.int32, (LANE, LANE), 1)
    )

    def to_rows(v):
        return jnp.sum(jnp.where(eye, v, 0.0), axis=1, keepdims=True)

    def wide(v):
        return jnp.concatenate([v[q:q + 1, :] for q in range(4)], axis=1)

    scale = LOG2E / (width * EPS)
    rc(nsq.at[pl.ds(0, 7)], nsq.at[pl.ds(0, 7)], q_send.at[0], q_recv.at[0], z_up).wait_recv()
    rc(lsq.at[pl.ds(0, 31)], lsq.at[pl.ds(0, 31)], q_send.at[1], q_recv.at[1], z_up).wait_recv()
    nq = jnp.sum(nsq[...], axis=0)
    lq = wide(jnp.sum(lsq[...], axis=0))
    for b in range(4):
        rows = slice(b * LANE, (b + 1) * LANE)
        cross[rows, :] = (to_rows(nq[b:b + 1, :]) + lq - 2.0 * cross[rows, :]) * scale

    def merge(parts):
        best = jnp.max(parts, axis=0)
        return best + jnp.log2(jnp.sum(jnp.exp2(parts - best[None]), axis=0))

    def merge_rows(parts):
        best = jnp.max(parts, axis=0, keepdims=True)
        return best + jnp.log2(jnp.sum(jnp.exp2(parts - best), axis=0, keepdims=True))

    def lend(step):
        k, zz = step % 2, step // 2
        lanes = pl.ds(pl.multiple_of((1 - xl) * 256 + k * LANE, LANE), LANE)
        for slot, dev in ((zz, (across + k, col)), (zz + 4, (across + k, flip_col))):
            c = rc(nz.at[slot, :, lanes], nx.at[core, slot], p_send.at[k, slot], p_recv.at[core, slot], dev)
            c.start()
            sent.append(c)

    steps = iter(range(6))

    def exchange(buf, mine, peers, ssem, rsem):
        for peer in peers:
            rc(buf.at[mine], buf.at[mine], ssem, rsem, peer).start()
        step = next(steps)
        for piece_at in range(*((0, 2), (2, 4), (4, 6), (6, 7), (7, 8), (8, 8))[step]):
            lend(piece_at)
        k = len(peers)
        rc(buf.at[pl.ds(0, k)], buf.at[pl.ds(0, k)], ssem, rsem, peers[0]).wait_recv()

    g = start_ref[...] * (LOG2E / EPS)
    f = None
    f_rows = None
    for it in range(ITERS):
        for b in range(4):
            parts = []
            for r in range(b * LANE, (b + 1) * LANE, 32):
                s = [g[q:q + 1, :] - cross[r:r + 32, q * LANE:(q + 1) * LANE] for q in range(4)]
                top = jnp.maximum(jnp.maximum(s[0], s[1]), jnp.maximum(s[2], s[3]))
                e = [jnp.exp2(v - top) for v in s]
                parts.append(top + jnp.log2((e[0] + e[1]) + (e[2] + e[3])))
            rowx[it, col, b:b + 1, :] = merge_rows(jnp.concatenate(parts, axis=0).T)
        exchange(rowx.at[it], col, col_peers, r_send.at[it], r_recv.at[it])
        f = -(math.log2(m_total) + merge(rowx[it]))
        f_rows = [to_rows(f[b:b + 1, :]) for b in range(4)]
        parts = []
        for r in range(0, BLK, 64):
            fr = f_rows[r // LANE][r % LANE:r % LANE + 64]
            s = (fr - cross[r:r + 64, :]).reshape(8, 8, BLK)
            top = jnp.max(s, axis=0)
            parts.append(top + jnp.log2(jnp.sum(jnp.exp2(s - top[None]), axis=0)))
        top = parts[0]
        for v in parts[1:]:
            top = jnp.maximum(top, v)
        own = merge_rows(top + jnp.log2(sum(jnp.exp2(v - top) for v in parts)))
        for q in range(4):
            col2[it, row, q:q + 1, :] = own[:, q * LANE:(q + 1) * LANE]
        exchange(col2.at[it], row, row_peers, c2_send.at[it], c2_recv.at[it])
        g = -(math.log2(n_total) + merge(col2[it]))

    npot_ref[...] = f * (EPS / LOG2E)
    lpot_ref[...] = g * (EPS / LOG2E)

    LOW, HIGH = slice(0, SPLIT), slice(SPLIT, BLK)
    gw = wide(g)

    def weights(cols):
        for b in range(4):
            rows = slice(b * LANE, (b + 1) * LANE)
            w = m_total * jnp.exp2((f_rows[b] + gw[:, cols]) - cross[rows, cols])
            wt[core, cols, rows] = w.T.astype(BF16)

    def wcopy(j, src, dst, dev, r=None):
        return rc(src, dst, w_send.at[j], w_recv.at[j if r is None else 3 * r], dev)

    low, high = pl.ds(0, SPLIT), pl.ds(SPLIT, REST)
    copies = []
    weights(HIGH)
    for k in range(2):
        copies.append(wcopy(3 * k, wt.at[core, high], wx.at[core], (across + k, col), core))
        copies[-1].start()
    weights(LOW)
    copies.append(wcopy(1, wt.at[core, low], wt.at[core, low], other_core))
    copies[-1].start()
    copies.append(wcopy(2, wt.at[core, high], wt.at[core, high], other_core))
    copies[-1].start()

    def mine(d, q):
        return nz[d, :, pl.ds(pl.multiple_of(q * 256 + core * LANE, LANE), LANE)]

    def theirs(d, q):
        return no[d, :, pl.ds(pl.multiple_of(q * LANE, LANE), LANE)]

    def partial_own(rel):
        d = (z + rel) % Z
        part[rel] = jnp.dot(
            wt[core, LOW, :], jnp.concatenate([mine(d, q) for q in (1 - xl, xl)], axis=1),
            preferred_element_type=F32,
        )

    def partial_other(rel):
        d = (z + rel) % Z
        part[rel] += jnp.dot(
            wt[1 - core, LOW, :], jnp.concatenate([theirs(d, q) for q in (1 - xl, xl)], axis=1),
            preferred_element_type=F32,
        )

    def partial(rel):
        partial_own(rel)
        partial_other(rel)

    def partial_high(rel):
        d = (z + rel) % Z
        parth[rel] = (
            jnp.dot(wt[core, HIGH, :], mine(d, xl), preferred_element_type=F32)
            + jnp.dot(wt[1 - core, HIGH, :], theirs(d, xl), preferred_element_type=F32)
        ) + (
            jnp.dot(wx[0], nx[0, d], preferred_element_type=F32)
            + jnp.dot(wx[1], nx[1, d], preferred_element_type=F32)
        )

    def size(k):
        return REST if k == 2 else SPLIT

    def piece(k, bufs, dr, s):
        ref = bufs[1].at[dr, 4 - s] if k == 2 else bufs[0].at[dr, 4 - s, k]
        h = size(k) // 2
        return ref.at[pl.ds(dr * h, h)] if s == 4 else ref

    def ring_copy(k, dr, s):
        ss, rs = (t_send.at[dr, 4 - s], t_recv.at[dr, 4 - s]) if k == 2 else (
            s_send.at[dr, 4 - s, k], s_recv.at[dr, 4 - s, k])
        return rc(
            piece(k, (stage, stageh), dr, s), piece(k, (land, landh), dr, s), ss, rs,
            z_dn if dr == 0 else z_up,
        )

    def own_part(k, rel, rows):
        return parth[rel, rows, :] if k == 2 else part[rel, rows, k * LANE:(k + 1) * LANE]

    def got(k, dr, s, rows):
        v = landh[dr, 4 - s, rows, :] if k == 2 else land[dr, 4 - s, k, rows, :]
        return v.astype(F32)

    def put(k, dr, s, rows, v):
        if k == 2:
            stageh[dr, 4 - s, rows, :] = v.astype(BF16)
        else:
            stage[dr, 4 - s, k, rows, :] = v.astype(BF16)

    def ring_step(k, s):
        h = size(k) // 2
        both = slice(0, 2 * h)
        for dr in range(2):
            rel = Z - s if dr == 0 else s
            first = slice(dr * h, (dr + 1) * h)
            other = slice((1 - dr) * h, (2 - dr) * h)
            if s == 4:
                put(k, dr, s, first, own_part(k, 4, first))
            else:
                ring_copy(k, dr, s + 1).wait_recv()
                if s == 3:
                    put(k, dr, s, first, own_part(k, rel, first) + got(k, dr, 4, first))
                    put(k, dr, s, other, own_part(k, rel, other))
                else:
                    put(k, dr, s, both, own_part(k, rel, both) + got(k, dr, s + 1, both))
            c = ring_copy(k, dr, s)
            c.start()
            sent.append(c)

    def total(k):
        both = slice(0, size(k))
        for dr in range(2):
            ring_copy(k, dr, 1).wait_recv()
        return own_part(k, 0, both) + (got(k, 0, 1, both) + got(k, 1, 1, both))

    for rel in (4, 5, 3):
        partial_own(rel)
    for q in range(2):
        rc(no.at[:, :, pl.ds(q * LANE, LANE)], no.at[:, :, pl.ds(q * LANE, LANE)],
           o_send.at[q], o_recv.at[q], other_core).wait_recv()
    wcopy(1, wt.at[core, low], wt.at[1 - core, low], other_core).wait_recv()
    partial_other(4)
    ring_step(0, 4)
    partial_other(5)
    partial_other(3)
    ring_step(1, 4)
    wcopy(2, wt.at[core, high], wt.at[1 - core, high], other_core).wait_recv()
    for c in range(2):
        for slot in range(Z):
            rc(nx.at[c, slot], nx.at[c, slot], p_send.at[0, slot], p_recv.at[c, slot], other_xl).wait_recv()
    ring_step(0, 3)
    for c in range(2):
        wcopy(0, wt.at[core, high], wx.at[c], other_xl, c).wait_recv()
    partial_high(4)
    ring_step(1, 3)
    partial(6)
    partial(2)
    ring_step(2, 4)
    ring_step(0, 2)
    partial_high(5)
    partial_high(3)
    ring_step(1, 2)
    partial(7)
    partial(1)
    ring_step(2, 3)
    ring_step(0, 1)
    partial(0)
    partial_high(6)
    partial_high(2)
    ring_step(1, 1)
    ring_step(2, 2)
    xs[...] = total(0)
    xc = rc(xs, xr, x_send.at[0], x_recv.at[0], other_xl)
    xc.start()
    copies.append(xc)
    for rel in (7, 1, 0):
        partial_high(rel)
    ring_step(2, 1)
    kept = total(1)
    out_ref[:, HIGH] = total(2).T
    xc.wait_recv()
    out_ref[:, LOW] = (kept + xr[...]).T
    sent.extend(copies)

    for j, (buf, k) in enumerate(((nsq, 7), (lsq, 31))):
        ref = buf.at[pl.ds(0, k)]
        rc(ref, ref, q_send.at[j], q_recv.at[j], z_up).wait_send()
    for c in sent:
        c.wait_send()
    for it in range(ITERS):
        for buf, k, ssem, rsem in (
            (rowx, 7, r_send, r_recv), (col2, 31, c2_send, c2_recv)
        ):
            ref = buf.at[it, pl.ds(0, k)]
            rc(ref, ref, ssem.at[it], rsem.at[it], z_up).wait_send()


def per_device(n_total, m_total, noise_draw, latent_code, start_potential):
    anyspace = pl.BlockSpec(memory_space=pltpu.HBM)
    vmem = pl.BlockSpec(memory_space=pltpu.VMEM)
    width = 4096
    dma = pltpu.SemaphoreType.DMA

    def body(*refs):
        kernel(n_total, m_total, width, *refs)

    npot, lpot, out = pl.pallas_call(
        body,
        out_shape=(
            jax.ShapeDtypeStruct((4, LANE), F32),
            jax.ShapeDtypeStruct((4, LANE), F32),
            jax.ShapeDtypeStruct((LANE, BLK), F32),
        ),
        in_specs=[anyspace, anyspace, vmem],
        out_specs=(vmem, vmem, vmem),
        scratch_shapes=[
            pltpu.VMEM((8, BLK, BLK), BF16),
            pltpu.VMEM((Z, 2, 2, BLK, LANE), BF16),
            pltpu.VMEM((8, BLK, 2 * LANE), BF16),
            pltpu.VMEM((BLK, BLK), F32),
            pltpu.VMEM((8, 4, LANE), F32),
            pltpu.VMEM((32, 4, LANE), F32),
            pltpu.VMEM((2, BLK, BLK), BF16),
            pltpu.VMEM((2, REST, BLK), BF16),
            pltpu.VMEM((2, Z, BLK, LANE), BF16),
            pltpu.VMEM((Z, SPLIT, 2 * LANE), F32),
            pltpu.VMEM((Z, REST, LANE), F32),
            pltpu.VMEM((2, 4, 2, SPLIT, LANE), BF16),
            pltpu.VMEM((2, 4, 2, SPLIT, LANE), BF16),
            pltpu.VMEM((2, 4, REST, LANE), BF16),
            pltpu.VMEM((2, 4, REST, LANE), BF16),
            pltpu.VMEM((SPLIT, LANE), F32),
            pltpu.VMEM((SPLIT, LANE), F32),
            pltpu.VMEM((ITERS, 8, 4, LANE), F32),
            pltpu.VMEM((ITERS, 32, 4, LANE), F32),
            dma((2,)), dma((2,)),
            dma((12,)), dma((12,)),
            dma((2, 2)), dma((2, 2)),
            dma((25,)), dma((25,)),
            dma((2,)), dma((2,)),
            dma((4,)), dma((4,)),
            dma((2, Z)), dma((2, Z)),
            dma((ITERS,)), dma((ITERS,)),
            dma((ITERS,)), dma((ITERS,)),
            dma((2, 4, 2)), dma((2, 4, 2)),
            dma((2, 4)), dma((2, 4)),
            dma((1,)), dma((1,)),
            dma((2,)),
        ],
        compiler_params=pltpu.CompilerParams(
            collective_id=0, has_side_effects=True, vmem_limit_bytes=54656 * 1024
        ),
    )(noise_draw, latent_code, start_potential.reshape(4, LANE))
    return npot.reshape(BLK), lpot.reshape(BLK), out


def solution(mesh):
    in_specs = (P("row", "col"), P("col", "row"), P("col"))
    out_specs = (P("row"), P("col"), P("row", "col"))

    def whole(noise_draw, latent_code, start_potential):
        def block(a, b, c):
            return per_device(noise_draw.shape[0], latent_code.shape[0], a, b, c)

        return jax.shard_map(
            block, mesh=mesh, in_specs=in_specs, out_specs=out_specs, check_vma=False
        )(noise_draw, latent_code, start_potential)

    return whole
```

```python
import math

import jax
import jax.numpy as jnp
from jax import lax
from jax.experimental import pallas as pl
from jax.experimental.pallas import tpu as pltpu
from jax.sharding import PartitionSpec as P

ITERS = 3
EPS = 0.01
LOG2E = math.log2(math.e)
MESH = pl.DeviceIdType.MESH
F32 = jnp.float32
BF16 = jnp.bfloat16

Z, Y = 8, 4
LANE = 128
BLK = 512
HALF = BLK // 2
SPLIT = 384
REST = BLK - SPLIT


def kernel(
    n_total, m_total, width,
    noise_ref, latent_ref, start_ref,
    npot_ref, lpot_ref, out_ref,
    nz, lt, no, cross, nsq, lsq, wt, wx, nx, part, parth, stage, land, stageh, landh, xs, xr, rowx, col2,
    q_send, q_recv, n_send, n_recv, h_send, h_recv, l_send, l_recv, o_send, o_recv, w_send, w_recv,
    p_send, p_recv, r_send, r_recv, c2_send, c2_recv,
    s_send, s_recv, t_send, t_recv, x_send, x_recv, loc,
):
    row = lax.axis_index("row")
    col = lax.axis_index("col")
    z = row // 4
    xl = (row // 2) % 2
    core = row % 2
    y = col // 2
    xh = col % 2
    quad = row % 4

    def ring_z(d):
        return (z + d + Z) % Z

    def ring_y(d):
        return (y + d + Y) % Y

    other_core = (row + 1 - 2 * core, col)
    other_xl = (row + 2 - 4 * xl, col)
    flip_col = col + 1 - 2 * xh
    other_xh = (row, flip_col)
    z_up = (ring_z(1) * 4 + quad, col)
    z_dn = (ring_z(-1) * 4 + quad, col)
    y_up = (row, ring_y(1) * 2 + xh)
    y_dn = (row, ring_y(-1) * 2 + xh)
    col_peers = [
        (row, ring_y(dy) * 2 + (1 - xh if dx else xh))
        for dy, dx in ((2, 1), (1, 1), (-1, 1), (2, 0), (0, 1), (1, 0), (-1, 0))
    ]
    across = (row + 2 - 4 * xl) // 2 * 2
    across_quad = ((across + 1 - core) % 4, (across + core) % 4, (quad // 2) * 2 + 1 - core, quad)
    row_peers = [
        (ring_z(d) * 4 + q, col)
        for d in (4, 3, -3, 2, -2, 1, -1, 0) for q in across_quad[:3 if d == 0 else 4]
    ]
    peers = col_peers + row_peers + [(across, flip_col), (across + 1, flip_col)]

    own_n = pltpu.make_async_copy(noise_ref, nz.at[col], loc.at[0])
    own_l = pltpu.make_async_copy(latent_ref, lt.at[z, core, xl], loc.at[1])
    own_n.start()
    own_l.start()

    barrier = pltpu.get_barrier_semaphore()
    for peer in peers:
        pl.semaphore_signal(barrier, inc=1, device_id=peer, device_id_type=MESH)
    cross[...] = jnp.zeros_like(cross)
    pl.semaphore_wait(barrier, len(peers))

    def rc(src, dst, ssem, rsem, dev):
        return pltpu.make_async_remote_copy(
            src_ref=src, dst_ref=dst, send_sem=ssem, recv_sem=rsem,
            device_id=dev, device_id_type=MESH,
        )

    def nsl(slot, h):
        return nz.at[slot, pl.ds(h * HALF, HALF), :]

    QUART = HALF // 2
    sent = []

    def nsend(slot, h, idx, dev, src=None):
        src = nsl(slot, h) if src is None else src
        c = rc(src, nsl(slot, h), n_send.at[idx], n_recv.at[idx], dev)
        c.start()
        return c

    def own_half(h):
        return noise_ref.at[pl.ds(h * HALF, HALF), :]

    def nwait(slot, h, idx):
        rc(nsl(slot, h), nsl(slot, h), n_send.at[idx], n_recv.at[idx], y_up).wait_recv()

    def lsend(ref, idx, dev, src=None):
        c = rc(ref if src is None else src, ref, l_send.at[idx], l_recv.at[idx], dev)
        c.start()
        sent.append(c)

    def lwait(ref, idx):
        rc(ref, ref, l_send.at[idx], l_recv.at[idx], z_up).wait_recv()

    def slot_of(yy, s):
        return yy * 2 + (xh if s == 0 else 1 - xh)

    def xh_copy(t, h, src, slot):
        return rc(src, nsl(slot, h), h_send.at[t, h], h_recv.at[t, h], other_xh)

    def xh_send(t, h):
        far0 = slot_of(ring_y(2), 0)
        c = xh_copy(t, h, own_half(h), col) if t == 0 else xh_copy(t, h, nsl(far0, h), far0)
        c.start()
        sent.append(c)

    def xh_wait(t, h):
        slot = flip_col if t == 0 else slot_of(ring_y(2), 1)
        xh_copy(t, h, nsl(slot, h), slot).wait_recv()

    own_pair = lt.at[z, core]
    own_block = lt.at[z, core, xl]
    z_dirs = ((0, -1, z_up), (1, 1, z_dn))

    def lat(d, part):
        return lt.at[ring_z(d), core, xl if part == 0 else 1 - xl]

    def lat_forward(step, part, dirs):
        for dr, sgn, dev in dirs:
            block = lat(sgn * step, part)
            lwait(block, 1 + 8 * dr + 2 * (step - 1) + part)
            if step < 3 or part == dr:
                lsend(block, 1 + 8 * dr + 2 * step + part, dev)
            if step == 3 and part == dr:
                lsend(block, 24 + part, (dev[0] + 1 - 2 * core, col))

    def lat_share(step):
        for dr, sgn, _ in z_dirs:
            lsend(lt.at[ring_z(sgn * step), core], 16 + 2 * step + dr, other_core)

    lat_x = rc(latent_ref, own_block, l_send.at[0], l_recv.at[0], other_xl)
    lat_x.start()
    lsend(own_block, 1, z_up, latent_ref)
    lsend(own_block, 9, z_dn, latent_ref)
    first_up = nsend(col, 0, 0, y_up, own_half(0))
    first_dn = nsend(col, 1, 3, y_dn, own_half(1))

    sent.append(lat_x)
    xh_send(0, 0)

    own_n.wait()
    own_l.wait()
    for b in range(4):
        rows = slice(b * LANE, (b + 1) * LANE)
        n2 = jnp.square(nz[col, rows, :].astype(F32))
        n2 = (n2[:, 0:128] + n2[:, 128:256]) + (n2[:, 256:384] + n2[:, 384:512])
        nsq[col, b:b + 1, :] = jnp.sum(n2.T, axis=0, keepdims=True)
        l2 = jnp.square(lt[z, core, xl, rows, :].astype(F32))
        lsq[row, b:b + 1, :] = jnp.sum(l2.T, axis=0, keepdims=True)

    lwait(lat(0, 1), 0)
    lsend(lat(0, 1), 2, z_up)
    lsend(lat(0, 1), 10, z_dn)
    xh_send(0, 1)
    lat_forward(1, 0, z_dirs)
    lsend(own_pair, 17, other_core)

    def own_quarter(h, p, idx, dev):
        at = pl.ds(h * HALF + p * QUART, QUART)
        c = rc(noise_ref.at[at, :], nz.at[col, at, :], n_send.at[idx], n_recv.at[idx], dev)
        c.start()
        sent.append(c)

    first_up.wait_send()
    own_quarter(1, 0, 1, y_up)
    first_dn.wait_send()
    own_quarter(0, 0, 2, y_dn)

    dn, up = slot_of(ring_y(-1), 0), slot_of(ring_y(1), 0)
    nwait(dn, 0, 0)
    onward_up = nsend(dn, 0, 4, y_up)
    nwait(up, 1, 3)
    onward_dn = nsend(up, 1, 5, y_dn)

    lat_forward(1, 1, z_dirs)
    lat_share(1)
    for peer in col_peers:
        rc(nsq.at[col], nsq.at[col], q_send.at[0], q_recv.at[0], peer).start()
    for peer in row_peers:
        rc(lsq.at[row], lsq.at[row], q_send.at[1], q_recv.at[1], peer).start()
    lat_forward(2, 0, z_dirs)
    lat_forward(2, 1, z_dirs)
    lat_share(2)

    onward_up.wait_send()
    own_quarter(1, 1, 10, y_up)
    onward_dn.wait_send()
    own_quarter(0, 1, 11, y_dn)

    nwait(slot_of(ring_y(2), 0), 0, 4)
    xh_send(1, 0)
    nwait(slot_of(ring_y(2), 0), 1, 5)
    xh_send(1, 1)

    lat_forward(3, 0, z_dirs)

    xh_wait(0, 0)
    sent.append(nsend(flip_col, 0, 6, y_up))
    sent.append(nsend(flip_col, 0, 8, y_dn))
    xh_wait(0, 1)
    sent.append(nsend(flip_col, 1, 9, y_dn))
    sent.append(nsend(flip_col, 1, 7, y_up))

    lat_forward(3, 1, z_dirs)
    lat_share(3)
    lwait(lat(4, 0), 7)
    lwait(lat(4, 1), 16)
    for j, d in enumerate((0, -1, 1, -2, 2, -3, 3)):
        lwait(lt.at[ring_z(d), 1 - core], 17 + j)
    lwait(lt.at[ring_z(4), 1 - core, xl], 24)
    lwait(lt.at[ring_z(4), 1 - core, 1 - xl], 25)

    def accumulate(slot):
        a = nz[slot]
        b = jnp.concatenate([lt[slot, 0, 0], lt[slot, 1, 0], lt[slot, 0, 1], lt[slot, 1, 1]], axis=1)
        cross[...] += lax.dot_general(a, b, (((1,), (1,)), ((), ())), preferred_element_type=F32)

    dn, up = slot_of(ring_y(-1), 0), slot_of(ring_y(1), 0)
    for slot, h, idxs in ((dn, 1, (1, 10)), (up, 0, (2, 11))):
        for p in range(2):
            ref = nz.at[slot, pl.ds(h * HALF + p * QUART, QUART), :]
            rc(ref, ref, n_send.at[idxs[p]], n_recv.at[idxs[p]], y_up).wait_recv()

    def set0(k, carry):
        accumulate(((y + k) % Y) * 2 + xh)
        return carry

    lax.fori_loop(0, Y, set0, 0)
    accumulate(flip_col)
    xh_wait(1, 0)
    xh_wait(1, 1)
    accumulate(slot_of(ring_y(2), 1))
    dn, up = slot_of(ring_y(-1), 1), slot_of(ring_y(1), 1)
    nwait(dn, 0, 6)
    nwait(up, 1, 9)
    nwait(dn, 1, 7)
    nwait(up, 0, 8)
    accumulate(dn)
    accumulate(up)

    for q in range(2):
        c = rc(
            nz.at[:, :, pl.ds(pl.multiple_of(q * 256 + (1 - core) * LANE, LANE), LANE)],
            no.at[:, :, pl.ds(q * LANE, LANE)],
            o_send.at[q], o_recv.at[q], other_core,
        )
        c.start()
        sent.append(c)

    eye = (
        lax.broadcasted_iota(jnp.int32, (LANE, LANE), 0)
        == lax.broadcasted_iota(jnp.int32, (LANE, LANE), 1)
    )

    def to_rows(v):
        return jnp.sum(jnp.where(eye, v, 0.0), axis=1, keepdims=True)

    def wide(v):
        return jnp.concatenate([v[q:q + 1, :] for q in range(4)], axis=1)

    scale = LOG2E / (width * EPS)
    rc(nsq.at[pl.ds(0, 7)], nsq.at[pl.ds(0, 7)], q_send.at[0], q_recv.at[0], z_up).wait_recv()
    rc(lsq.at[pl.ds(0, 31)], lsq.at[pl.ds(0, 31)], q_send.at[1], q_recv.at[1], z_up).wait_recv()
    nq = jnp.sum(nsq[...], axis=0)
    lq = wide(jnp.sum(lsq[...], axis=0))
    for b in range(4):
        rows = slice(b * LANE, (b + 1) * LANE)
        cross[rows, :] = (to_rows(nq[b:b + 1, :]) + lq - 2.0 * cross[rows, :]) * scale

    def merge(parts):
        best = jnp.max(parts, axis=0)
        return best + jnp.log2(jnp.sum(jnp.exp2(parts - best[None]), axis=0))

    def merge_rows(parts):
        best = jnp.max(parts, axis=0, keepdims=True)
        return best + jnp.log2(jnp.sum(jnp.exp2(parts - best), axis=0, keepdims=True))

    def lend(step):
        k, zz = step % 2, step // 2
        lanes = pl.ds(pl.multiple_of((1 - xl) * 256 + k * LANE, LANE), LANE)
        for slot, dev in ((zz, (across + k, col)), (zz + 4, (across + k, flip_col))):
            c = rc(nz.at[slot, :, lanes], nx.at[core, slot], p_send.at[k, slot], p_recv.at[core, slot], dev)
            c.start()
            sent.append(c)

    steps = iter(range(6))

    def exchange(buf, mine, peers, ssem, rsem):
        for peer in peers:
            rc(buf.at[mine], buf.at[mine], ssem, rsem, peer).start()
        step = next(steps)
        for piece_at in range(*((0, 2), (2, 4), (4, 6), (6, 7), (7, 8), (8, 8))[step]):
            lend(piece_at)
        k = len(peers)
        rc(buf.at[pl.ds(0, k)], buf.at[pl.ds(0, k)], ssem, rsem, peers[0]).wait_recv()

    g = start_ref[...] * (LOG2E / EPS)
    f = None
    f_rows = None
    for it in range(ITERS):
        for b in range(4):
            parts = []
            for r in range(b * LANE, (b + 1) * LANE, 32):
                s = [g[q:q + 1, :] - cross[r:r + 32, q * LANE:(q + 1) * LANE] for q in range(4)]
                top = jnp.maximum(jnp.maximum(s[0], s[1]), jnp.maximum(s[2], s[3]))
                e = [jnp.exp2(v - top) for v in s]
                parts.append(top + jnp.log2((e[0] + e[1]) + (e[2] + e[3])))
            rowx[it, col, b:b + 1, :] = merge_rows(jnp.concatenate(parts, axis=0).T)
        exchange(rowx.at[it], col, col_peers, r_send.at[it], r_recv.at[it])
        f = -(math.log2(m_total) + merge(rowx[it]))
        f_rows = [to_rows(f[b:b + 1, :]) for b in range(4)]
        parts = []
        for r in range(0, BLK, 64):
            fr = f_rows[r // LANE][r % LANE:r % LANE + 64]
            s = (fr - cross[r:r + 64, :]).reshape(8, 8, BLK)
            top = jnp.max(s, axis=0)
            parts.append(top + jnp.log2(jnp.sum(jnp.exp2(s - top[None]), axis=0)))
        top = parts[0]
        for v in parts[1:]:
            top = jnp.maximum(top, v)
        own = merge_rows(top + jnp.log2(sum(jnp.exp2(v - top) for v in parts)))
        for q in range(4):
            col2[it, row, q:q + 1, :] = own[:, q * LANE:(q + 1) * LANE]
        exchange(col2.at[it], row, row_peers, c2_send.at[it], c2_recv.at[it])
        g = -(math.log2(n_total) + merge(col2[it]))

    npot_ref[...] = f * (EPS / LOG2E)
    lpot_ref[...] = g * (EPS / LOG2E)

    LOW, HIGH = slice(0, SPLIT), slice(SPLIT, BLK)
    gw = wide(g)

    def weights(cols):
        for b in range(4):
            rows = slice(b * LANE, (b + 1) * LANE)
            w = m_total * jnp.exp2((f_rows[b] + gw[:, cols]) - cross[rows, cols])
            wt[core, cols, rows] = w.T.astype(BF16)

    def wcopy(j, src, dst, dev, r=None):
        return rc(src, dst, w_send.at[j], w_recv.at[j if r is None else 3 * r], dev)

    low, high = pl.ds(0, SPLIT), pl.ds(SPLIT, REST)
    copies = []
    weights(HIGH)
    for k in range(2):
        copies.append(wcopy(3 * k, wt.at[core, high], wx.at[core], (across + k, col), core))
        copies[-1].start()
    weights(LOW)
    copies.append(wcopy(1, wt.at[core, low], wt.at[core, low], other_core))
    copies[-1].start()
    copies.append(wcopy(2, wt.at[core, high], wt.at[core, high], other_core))
    copies[-1].start()

    def mine(d, q):
        return nz[d, :, pl.ds(pl.multiple_of(q * 256 + core * LANE, LANE), LANE)]

    def theirs(d, q):
        return no[d, :, pl.ds(pl.multiple_of(q * LANE, LANE), LANE)]

    def partial_own(rel):
        d = (z + rel) % Z
        part[rel] = jnp.dot(
            wt[core, LOW, :], jnp.concatenate([mine(d, q) for q in (1 - xl, xl)], axis=1),
            preferred_element_type=F32,
        )

    def partial_other(rel):
        d = (z + rel) % Z
        part[rel] += jnp.dot(
            wt[1 - core, LOW, :], jnp.concatenate([theirs(d, q) for q in (1 - xl, xl)], axis=1),
            preferred_element_type=F32,
        )

    def partial(rel):
        partial_own(rel)
        partial_other(rel)

    def partial_high(rel):
        d = (z + rel) % Z
        parth[rel] = (
            jnp.dot(wt[core, HIGH, :], mine(d, xl), preferred_element_type=F32)
            + jnp.dot(wt[1 - core, HIGH, :], theirs(d, xl), preferred_element_type=F32)
        ) + (
            jnp.dot(wx[0], nx[0, d], preferred_element_type=F32)
            + jnp.dot(wx[1], nx[1, d], preferred_element_type=F32)
        )

    def size(k):
        return REST if k == 2 else SPLIT

    def piece(k, bufs, dr, s):
        ref = bufs[1].at[dr, 4 - s] if k == 2 else bufs[0].at[dr, 4 - s, k]
        h = size(k) // 2
        return ref.at[pl.ds(dr * h, h)] if s == 4 else ref

    def ring_copy(k, dr, s):
        ss, rs = (t_send.at[dr, 4 - s], t_recv.at[dr, 4 - s]) if k == 2 else (
            s_send.at[dr, 4 - s, k], s_recv.at[dr, 4 - s, k])
        return rc(
            piece(k, (stage, stageh), dr, s), piece(k, (land, landh), dr, s), ss, rs,
            z_dn if dr == 0 else z_up,
        )

    def own_part(k, rel, rows):
        return parth[rel, rows, :] if k == 2 else part[rel, rows, k * LANE:(k + 1) * LANE]

    def got(k, dr, s, rows):
        v = landh[dr, 4 - s, rows, :] if k == 2 else land[dr, 4 - s, k, rows, :]
        return v.astype(F32)

    def put(k, dr, s, rows, v):
        if k == 2:
            stageh[dr, 4 - s, rows, :] = v.astype(BF16)
        else:
            stage[dr, 4 - s, k, rows, :] = v.astype(BF16)

    def ring_step(k, s):
        h = size(k) // 2
        both = slice(0, 2 * h)
        for dr in range(2):
            rel = Z - s if dr == 0 else s
            first = slice(dr * h, (dr + 1) * h)
            other = slice((1 - dr) * h, (2 - dr) * h)
            if s == 4:
                put(k, dr, s, first, own_part(k, 4, first))
            else:
                ring_copy(k, dr, s + 1).wait_recv()
                if s == 3:
                    put(k, dr, s, first, own_part(k, rel, first) + got(k, dr, 4, first))
                    put(k, dr, s, other, own_part(k, rel, other))
                else:
                    put(k, dr, s, both, own_part(k, rel, both) + got(k, dr, s + 1, both))
            c = ring_copy(k, dr, s)
            c.start()
            sent.append(c)

    def total(k):
        both = slice(0, size(k))
        for dr in range(2):
            ring_copy(k, dr, 1).wait_recv()
        return own_part(k, 0, both) + (got(k, 0, 1, both) + got(k, 1, 1, both))

    for rel in (4, 5, 3):
        partial_own(rel)
    for q in range(2):
        rc(no.at[:, :, pl.ds(q * LANE, LANE)], no.at[:, :, pl.ds(q * LANE, LANE)],
           o_send.at[q], o_recv.at[q], other_core).wait_recv()
    wcopy(1, wt.at[core, low], wt.at[1 - core, low], other_core).wait_recv()
    partial_other(4)
    ring_step(0, 4)
    partial_other(5)
    partial_other(3)
    ring_step(1, 4)
    wcopy(2, wt.at[core, high], wt.at[1 - core, high], other_core).wait_recv()
    for c in range(2):
        for slot in range(Z):
            rc(nx.at[c, slot], nx.at[c, slot], p_send.at[0, slot], p_recv.at[c, slot], other_xl).wait_recv()
    ring_step(0, 3)
    for c in range(2):
        wcopy(0, wt.at[core, high], wx.at[c], other_xl, c).wait_recv()
    partial_high(4)
    ring_step(1, 3)
    partial(6)
    partial(2)
    ring_step(2, 4)
    ring_step(0, 2)
    partial_high(5)
    partial_high(3)
    ring_step(1, 2)
    partial(7)
    partial(1)
    ring_step(2, 3)
    ring_step(0, 1)
    partial(0)
    partial_high(6)
    partial_high(2)
    ring_step(1, 1)
    ring_step(2, 2)
    xs[...] = total(0)
    xc = rc(xs, xr, x_send.at[0], x_recv.at[0], other_xl)
    xc.start()
    copies.append(xc)
    for rel in (7, 1, 0):
        partial_high(rel)
    ring_step(2, 1)
    kept = total(1)
    out_ref[:, HIGH] = total(2).T
    xc.wait_recv()
    out_ref[:, LOW] = (kept + xr[...]).T
    sent.extend(copies)

    for j, (buf, k) in enumerate(((nsq, 7), (lsq, 31))):
        ref = buf.at[pl.ds(0, k)]
        rc(ref, ref, q_send.at[j], q_recv.at[j], z_up).wait_send()
    for c in sent:
        c.wait_send()
    for it in range(ITERS):
        for buf, k, ssem, rsem in (
            (rowx, 7, r_send, r_recv), (col2, 31, c2_send, c2_recv)
        ):
            ref = buf.at[it, pl.ds(0, k)]
            rc(ref, ref, ssem.at[it], rsem.at[it], z_up).wait_send()


def per_device(n_total, m_total, noise_draw, latent_code, start_potential):
    anyspace = pl.BlockSpec(memory_space=pltpu.HBM)
    vmem = pl.BlockSpec(memory_space=pltpu.VMEM)
    width = 4096
    dma = pltpu.SemaphoreType.DMA

    def body(*refs):
        kernel(n_total, m_total, width, *refs)

    npot, lpot, out = pl.pallas_call(
        body,
        out_shape=(
            jax.ShapeDtypeStruct((4, LANE), F32),
            jax.ShapeDtypeStruct((4, LANE), F32),
            jax.ShapeDtypeStruct((LANE, BLK), F32),
        ),
        in_specs=[anyspace, anyspace, vmem],
        out_specs=(vmem, vmem, vmem),
        scratch_shapes=[
            pltpu.VMEM((8, BLK, BLK), BF16),
            pltpu.VMEM((Z, 2, 2, BLK, LANE), BF16),
            pltpu.VMEM((8, BLK, 2 * LANE), BF16),
            pltpu.VMEM((BLK, BLK), F32),
            pltpu.VMEM((8, 4, LANE), F32),
            pltpu.VMEM((32, 4, LANE), F32),
            pltpu.VMEM((2, BLK, BLK), BF16),
            pltpu.VMEM((2, REST, BLK), BF16),
            pltpu.VMEM((2, Z, BLK, LANE), BF16),
            pltpu.VMEM((Z, SPLIT, 2 * LANE), F32),
            pltpu.VMEM((Z, REST, LANE), F32),
            pltpu.VMEM((2, 4, 2, SPLIT, LANE), BF16),
            pltpu.VMEM((2, 4, 2, SPLIT, LANE), BF16),
            pltpu.VMEM((2, 4, REST, LANE), BF16),
            pltpu.VMEM((2, 4, REST, LANE), BF16),
            pltpu.VMEM((SPLIT, LANE), F32),
            pltpu.VMEM((SPLIT, LANE), F32),
            pltpu.VMEM((ITERS, 8, 4, LANE), F32),
            pltpu.VMEM((ITERS, 32, 4, LANE), F32),
            dma((2,)), dma((2,)),
            dma((12,)), dma((12,)),
            dma((2, 2)), dma((2, 2)),
            dma((26,)), dma((26,)),
            dma((2,)), dma((2,)),
            dma((4,)), dma((4,)),
            dma((2, Z)), dma((2, Z)),
            dma((ITERS,)), dma((ITERS,)),
            dma((ITERS,)), dma((ITERS,)),
            dma((2, 4, 2)), dma((2, 4, 2)),
            dma((2, 4)), dma((2, 4)),
            dma((1,)), dma((1,)),
            dma((2,)),
        ],
        compiler_params=pltpu.CompilerParams(
            collective_id=0, has_side_effects=True, vmem_limit_bytes=54656 * 1024
        ),
    )(noise_draw, latent_code, start_potential.reshape(4, LANE))
    return npot.reshape(BLK), lpot.reshape(BLK), out


def solution(mesh):
    in_specs = (P("row", "col"), P("col", "row"), P("col"))
    out_specs = (P("row"), P("col"), P("row", "col"))

    def whole(noise_draw, latent_code, start_potential):
        def block(a, b, c):
            return per_device(noise_draw.shape[0], latent_code.shape[0], a, b, c)

        return jax.shard_map(
            block, mesh=mesh, in_specs=in_specs, out_specs=out_specs, check_vma=False
        )(noise_draw, latent_code, start_potential)

    return whole
```

```python
import math

import jax
import jax.numpy as jnp
from jax import lax
from jax.experimental import pallas as pl
from jax.experimental.pallas import tpu as pltpu
from jax.sharding import PartitionSpec as P

ITERS = 3
EPS = 0.01
LOG2E = math.log2(math.e)
MESH = pl.DeviceIdType.MESH
F32 = jnp.float32
BF16 = jnp.bfloat16

Z, Y = 8, 4
LANE = 128
BLK = 512
HALF = BLK // 2
SPLIT = 384
REST = BLK - SPLIT


def kernel(
    n_total, m_total, width,
    noise_ref, latent_ref, start_ref,
    npot_ref, lpot_ref, out_ref,
    nz, lt, no, cross, nsq, lsq, wt, wx, nx, part, parth, stage, land, stageh, landh, xs, xr, rowx, col2,
    q_send, q_recv, n_send, n_recv, h_send, h_recv, l_send, l_recv, o_send, o_recv, w_send, w_recv,
    p_send, p_recv, r_send, r_recv, c2_send, c2_recv,
    s_send, s_recv, t_send, t_recv, x_send, x_recv, loc,
):
    row = lax.axis_index("row")
    col = lax.axis_index("col")
    z = row // 4
    xl = (row // 2) % 2
    core = row % 2
    y = col // 2
    xh = col % 2
    quad = row % 4

    def ring_z(d):
        return (z + d + Z) % Z

    def ring_y(d):
        return (y + d + Y) % Y

    other_core = (row + 1 - 2 * core, col)
    other_xl = (row + 2 - 4 * xl, col)
    flip_col = col + 1 - 2 * xh
    other_xh = (row, flip_col)
    z_up = (ring_z(1) * 4 + quad, col)
    z_dn = (ring_z(-1) * 4 + quad, col)
    y_up = (row, ring_y(1) * 2 + xh)
    y_dn = (row, ring_y(-1) * 2 + xh)
    col_peers = [
        (row, ring_y(dy) * 2 + (1 - xh if dx else xh))
        for dy, dx in ((2, 1), (1, 1), (-1, 1), (2, 0), (0, 1), (1, 0), (-1, 0))
    ]
    across = (row + 2 - 4 * xl) // 2 * 2
    across_quad = ((across + 1 - core) % 4, (across + core) % 4, (quad // 2) * 2 + 1 - core, quad)
    row_peers = [
        (ring_z(d) * 4 + q, col)
        for d in (4, 3, -3, 2, -2, 1, -1, 0) for q in across_quad[:3 if d == 0 else 4]
    ]
    peers = col_peers + row_peers + [(across, flip_col), (across + 1, flip_col)]

    own_n = pltpu.make_async_copy(noise_ref, nz.at[col], loc.at[0])
    own_l = pltpu.make_async_copy(latent_ref, lt.at[z, core, xl], loc.at[1])
    own_n.start()
    own_l.start()

    barrier = pltpu.get_barrier_semaphore()
    for peer in peers:
        pl.semaphore_signal(barrier, inc=1, device_id=peer, device_id_type=MESH)
    cross[...] = jnp.zeros_like(cross)
    pl.semaphore_wait(barrier, len(peers))

    def rc(src, dst, ssem, rsem, dev):
        return pltpu.make_async_remote_copy(
            src_ref=src, dst_ref=dst, send_sem=ssem, recv_sem=rsem,
            device_id=dev, device_id_type=MESH,
        )

    def nsl(slot, h):
        return nz.at[slot, pl.ds(h * HALF, HALF), :]

    QUART = HALF // 2
    sent = []

    def nsend(slot, h, idx, dev, src=None):
        src = nsl(slot, h) if src is None else src
        c = rc(src, nsl(slot, h), n_send.at[idx], n_recv.at[idx], dev)
        c.start()
        return c

    def own_half(h):
        return noise_ref.at[pl.ds(h * HALF, HALF), :]

    def nwait(slot, h, idx):
        rc(nsl(slot, h), nsl(slot, h), n_send.at[idx], n_recv.at[idx], y_up).wait_recv()

    def lsend(ref, idx, dev, src=None):
        c = rc(ref if src is None else src, ref, l_send.at[idx], l_recv.at[idx], dev)
        c.start()
        sent.append(c)

    def lwait(ref, idx):
        rc(ref, ref, l_send.at[idx], l_recv.at[idx], z_up).wait_recv()

    def slot_of(yy, s):
        return yy * 2 + (xh if s == 0 else 1 - xh)

    def xh_copy(t, h, src, slot):
        return rc(src, nsl(slot, h), h_send.at[t, h], h_recv.at[t, h], other_xh)

    def xh_send(t, h):
        far0 = slot_of(ring_y(2), 0)
        c = xh_copy(t, h, own_half(h), col) if t == 0 else xh_copy(t, h, nsl(far0, h), far0)
        c.start()
        sent.append(c)

    def xh_wait(t, h):
        slot = flip_col if t == 0 else slot_of(ring_y(2), 1)
        xh_copy(t, h, nsl(slot, h), slot).wait_recv()

    own_pair = lt.at[z, core]
    own_block = lt.at[z, core, xl]
    z_dirs = ((0, -1, z_up), (1, 1, z_dn))

    def lat(d, part):
        return lt.at[ring_z(d), core, xl if part == 0 else 1 - xl]

    def lat_forward(step, part, dirs):
        for dr, sgn, dev in dirs:
            block = lat(sgn * step, part)
            lwait(block, 1 + 8 * dr + 2 * (step - 1) + part)
            if step < 3 or part == dr:
                lsend(block, 1 + 8 * dr + 2 * step + part, dev)
            if step == 3 and part == dr:
                lsend(block, 24 + part, (dev[0] + 1 - 2 * core, col))

    def lat_share(step):
        for dr, sgn, _ in z_dirs:
            lsend(lt.at[ring_z(sgn * step), core], 16 + 2 * step + dr, other_core)

    lat_x = rc(latent_ref, own_block, l_send.at[0], l_recv.at[0], other_xl)
    lat_x.start()
    lsend(own_block, 1, z_up, latent_ref)
    lsend(own_block, 9, z_dn, latent_ref)
    first_up = nsend(col, 0, 0, y_up, own_half(0))
    first_dn = nsend(col, 1, 3, y_dn, own_half(1))

    sent.append(lat_x)
    xh_send(0, 0)

    own_n.wait()
    own_l.wait()
    for b in range(4):
        rows = slice(b * LANE, (b + 1) * LANE)
        n2 = jnp.square(nz[col, rows, :].astype(F32))
        n2 = (n2[:, 0:128] + n2[:, 128:256]) + (n2[:, 256:384] + n2[:, 384:512])
        nsq[col, b:b + 1, :] = jnp.sum(n2.T, axis=0, keepdims=True)
        l2 = jnp.square(lt[z, core, xl, rows, :].astype(F32))
        lsq[row, b:b + 1, :] = jnp.sum(l2.T, axis=0, keepdims=True)

    lwait(lat(0, 1), 0)
    lsend(lat(0, 1), 2, z_up)
    lsend(lat(0, 1), 10, z_dn)
    xh_send(0, 1)
    lat_forward(1, 0, z_dirs)
    lsend(own_pair, 17, other_core)

    def own_quarter(h, p, idx, dev):
        at = pl.ds(h * HALF + p * QUART, QUART)
        c = rc(noise_ref.at[at, :], nz.at[col, at, :], n_send.at[idx], n_recv.at[idx], dev)
        c.start()
        sent.append(c)

    first_up.wait_send()
    own_quarter(1, 0, 1, y_up)
    first_dn.wait_send()
    own_quarter(0, 0, 2, y_dn)

    dn, up = slot_of(ring_y(-1), 0), slot_of(ring_y(1), 0)
    nwait(dn, 0, 0)
    onward_up = nsend(dn, 0, 4, y_up)
    nwait(up, 1, 3)
    onward_dn = nsend(up, 1, 5, y_dn)

    lat_forward(1, 1, z_dirs)
    lat_share(1)
    for peer in col_peers:
        rc(nsq.at[col], nsq.at[col], q_send.at[0], q_recv.at[0], peer).start()
    for peer in row_peers:
        rc(lsq.at[row], lsq.at[row], q_send.at[1], q_recv.at[1], peer).start()
    lat_forward(2, 0, z_dirs)
    lat_forward(2, 1, z_dirs)
    lat_share(2)

    onward_up.wait_send()
    own_quarter(1, 1, 10, y_up)
    onward_dn.wait_send()
    own_quarter(0, 1, 11, y_dn)

    nwait(slot_of(ring_y(2), 0), 0, 4)
    xh_send(1, 0)
    nwait(slot_of(ring_y(2), 0), 1, 5)
    xh_send(1, 1)

    lat_forward(3, 0, z_dirs)

    xh_wait(0, 0)
    sent.append(nsend(flip_col, 0, 6, y_up))
    sent.append(nsend(flip_col, 0, 8, y_dn))
    xh_wait(0, 1)
    sent.append(nsend(flip_col, 1, 9, y_dn))
    sent.append(nsend(flip_col, 1, 7, y_up))

    lat_forward(3, 1, z_dirs)
    lat_share(3)
    lwait(lat(4, 0), 7)
    lwait(lat(4, 1), 16)
    for j, d in enumerate((0, -1, 1, -2, 2, -3, 3)):
        lwait(lt.at[ring_z(d), 1 - core], 17 + j)
    lwait(lt.at[ring_z(4), 1 - core, xl], 24)
    lwait(lt.at[ring_z(4), 1 - core, 1 - xl], 25)

    def accumulate(slot):
        a = nz[slot]
        b = jnp.concatenate([lt[slot, 0, 0], lt[slot, 1, 0], lt[slot, 0, 1], lt[slot, 1, 1]], axis=1)
        cross[...] += lax.dot_general(a, b, (((1,), (1,)), ((), ())), preferred_element_type=F32)

    dn, up = slot_of(ring_y(-1), 0), slot_of(ring_y(1), 0)
    for slot, h, idxs in ((dn, 1, (1, 10)), (up, 0, (2, 11))):
        for p in range(2):
            ref = nz.at[slot, pl.ds(h * HALF + p * QUART, QUART), :]
            rc(ref, ref, n_send.at[idxs[p]], n_recv.at[idxs[p]], y_up).wait_recv()

    def set0(k, carry):
        accumulate(((y + k) % Y) * 2 + xh)
        return carry

    lax.fori_loop(0, Y, set0, 0)
    accumulate(flip_col)
    xh_wait(1, 0)
    xh_wait(1, 1)
    accumulate(slot_of(ring_y(2), 1))
    dn, up = slot_of(ring_y(-1), 1), slot_of(ring_y(1), 1)
    nwait(dn, 0, 6)
    nwait(up, 1, 9)
    nwait(dn, 1, 7)
    nwait(up, 0, 8)
    accumulate(dn)
    accumulate(up)

    for q in range(2):
        c = rc(
            nz.at[:, :, pl.ds(pl.multiple_of(q * 256 + (1 - core) * LANE, LANE), LANE)],
            no.at[:, :, pl.ds(q * LANE, LANE)],
            o_send.at[q], o_recv.at[q], other_core,
        )
        c.start()
        sent.append(c)

    eye = (
        lax.broadcasted_iota(jnp.int32, (LANE, LANE), 0)
        == lax.broadcasted_iota(jnp.int32, (LANE, LANE), 1)
    )

    def to_rows(v):
        return jnp.sum(jnp.where(eye, v, 0.0), axis=1, keepdims=True)

    def wide(v):
        return jnp.concatenate([v[q:q + 1, :] for q in range(4)], axis=1)

    scale = LOG2E / (width * EPS)
    rc(nsq.at[pl.ds(0, 7)], nsq.at[pl.ds(0, 7)], q_send.at[0], q_recv.at[0], z_up).wait_recv()
    rc(lsq.at[pl.ds(0, 31)], lsq.at[pl.ds(0, 31)], q_send.at[1], q_recv.at[1], z_up).wait_recv()
    nq = jnp.sum(nsq[...], axis=0)
    lq = wide(jnp.sum(lsq[...], axis=0))
    for b in range(4):
        rows = slice(b * LANE, (b + 1) * LANE)
        cross[rows, :] = (to_rows(nq[b:b + 1, :]) + lq - 2.0 * cross[rows, :]) * scale

    def merge(parts):
        best = jnp.max(parts, axis=0)
        return best + jnp.log2(jnp.sum(jnp.exp2(parts - best[None]), axis=0))

    def merge_rows(parts):
        best = jnp.max(parts, axis=0, keepdims=True)
        return best + jnp.log2(jnp.sum(jnp.exp2(parts - best), axis=0, keepdims=True))

    def lend_copies(k, zz):
        lanes = pl.ds(pl.multiple_of((1 - xl) * 256 + k * LANE, LANE), LANE)
        return [
            rc(nz.at[slot, :, lanes], nx.at[core, slot], p_send.at[k, slot], p_recv.at[core, slot], dev)
            for slot, dev in ((zz, (across + k, col)), (zz + 4, (across + k, flip_col)))
        ]

    def lend(zz):
        for k in range(2):
            for c in lend_copies(k, zz):
                c.start()

    def send_all(buf, mine, peers, ssem, rsem):
        for peer in peers:
            rc(buf.at[mine], buf.at[mine], ssem, rsem, peer).start()

    def wait_all(buf, k, ssem, rsem):
        rc(buf.at[pl.ds(0, k)], buf.at[pl.ds(0, k)], ssem, rsem, z_up).wait_recv()

    def iteration(it, carry):
        g = carry[1]
        for b in range(4):
            parts = []
            for r in range(b * LANE, (b + 1) * LANE, 32):
                s = [g[q:q + 1, :] - cross[r:r + 32, q * LANE:(q + 1) * LANE] for q in range(4)]
                top = jnp.maximum(jnp.maximum(s[0], s[1]), jnp.maximum(s[2], s[3]))
                e = [jnp.exp2(v - top) for v in s]
                parts.append(top + jnp.log2((e[0] + e[1]) + (e[2] + e[3])))
            rowx[it, col, b:b + 1, :] = merge_rows(jnp.concatenate(parts, axis=0).T)
        send_all(rowx.at[it], col, col_peers, r_send.at[it], r_recv.at[it])
        lend(it)
        wait_all(rowx.at[it], 7, r_send.at[it], r_recv.at[it])
        f = -(math.log2(m_total) + merge(rowx[it]))
        f_rows = [to_rows(f[b:b + 1, :]) for b in range(4)]
        parts = []
        for r in range(0, BLK, 64):
            fr = f_rows[r // LANE][r % LANE:r % LANE + 64]
            s = (fr - cross[r:r + 64, :]).reshape(8, 8, BLK)
            top = jnp.max(s, axis=0)
            parts.append(top + jnp.log2(jnp.sum(jnp.exp2(s - top[None]), axis=0)))
        top = parts[0]
        for v in parts[1:]:
            top = jnp.maximum(top, v)
        own = merge_rows(top + jnp.log2(sum(jnp.exp2(v - top) for v in parts)))
        for q in range(4):
            col2[it, row, q:q + 1, :] = own[:, q * LANE:(q + 1) * LANE]
        send_all(col2.at[it], row, row_peers, c2_send.at[it], c2_recv.at[it])
        wait_all(col2.at[it], 31, c2_send.at[it], c2_recv.at[it])
        g = -(math.log2(n_total) + merge(col2[it]))
        return f, g

    lend(3)
    g = start_ref[...] * (LOG2E / EPS)
    f, g = lax.fori_loop(0, ITERS, iteration, (jnp.zeros_like(g), g))
    f_rows = [to_rows(f[b:b + 1, :]) for b in range(4)]

    npot_ref[...] = f * (EPS / LOG2E)
    lpot_ref[...] = g * (EPS / LOG2E)

    LOW, HIGH = slice(0, SPLIT), slice(SPLIT, BLK)
    gw = wide(g)

    def weights(cols):
        for b in range(4):
            rows = slice(b * LANE, (b + 1) * LANE)
            w = m_total * jnp.exp2((f_rows[b] + gw[:, cols]) - cross[rows, cols])
            wt[core, cols, rows] = w.T.astype(BF16)

    def wcopy(j, src, dst, dev, r=None):
        return rc(src, dst, w_send.at[j], w_recv.at[j if r is None else 3 * r], dev)

    low, high = pl.ds(0, SPLIT), pl.ds(SPLIT, REST)
    copies = []
    weights(HIGH)
    for k in range(2):
        copies.append(wcopy(3 * k, wt.at[core, high], wx.at[core], (across + k, col), core))
        copies[-1].start()
    weights(LOW)
    copies.append(wcopy(1, wt.at[core, low], wt.at[core, low], other_core))
    copies[-1].start()
    copies.append(wcopy(2, wt.at[core, high], wt.at[core, high], other_core))
    copies[-1].start()

    def mine(d, q):
        return nz[d, :, pl.ds(pl.multiple_of(q * 256 + core * LANE, LANE), LANE)]

    def theirs(d, q):
        return no[d, :, pl.ds(pl.multiple_of(q * LANE, LANE), LANE)]

    def partial_own(rel):
        d = (z + rel) % Z
        part[rel] = jnp.dot(
            wt[core, LOW, :], jnp.concatenate([mine(d, q) for q in (1 - xl, xl)], axis=1),
            preferred_element_type=F32,
        )

    def partial_other(rel):
        d = (z + rel) % Z
        part[rel] += jnp.dot(
            wt[1 - core, LOW, :], jnp.concatenate([theirs(d, q) for q in (1 - xl, xl)], axis=1),
            preferred_element_type=F32,
        )

    def partial(rel):
        partial_own(rel)
        partial_other(rel)

    def partial_high(rel):
        d = (z + rel) % Z
        parth[rel] = (
            jnp.dot(wt[core, HIGH, :], mine(d, xl), preferred_element_type=F32)
            + jnp.dot(wt[1 - core, HIGH, :], theirs(d, xl), preferred_element_type=F32)
        ) + (
            jnp.dot(wx[0], nx[0, d], preferred_element_type=F32)
            + jnp.dot(wx[1], nx[1, d], preferred_element_type=F32)
        )

    def size(k):
        return REST if k == 2 else SPLIT

    def piece(k, bufs, dr, s):
        ref = bufs[1].at[dr, 4 - s] if k == 2 else bufs[0].at[dr, 4 - s, k]
        h = size(k) // 2
        return ref.at[pl.ds(dr * h, h)] if s == 4 else ref

    def ring_copy(k, dr, s):
        ss, rs = (t_send.at[dr, 4 - s], t_recv.at[dr, 4 - s]) if k == 2 else (
            s_send.at[dr, 4 - s, k], s_recv.at[dr, 4 - s, k])
        return rc(
            piece(k, (stage, stageh), dr, s), piece(k, (land, landh), dr, s), ss, rs,
            z_dn if dr == 0 else z_up,
        )

    def own_part(k, rel, rows):
        return parth[rel, rows, :] if k == 2 else part[rel, rows, k * LANE:(k + 1) * LANE]

    def got(k, dr, s, rows):
        v = landh[dr, 4 - s, rows, :] if k == 2 else land[dr, 4 - s, k, rows, :]
        return v.astype(F32)

    def put(k, dr, s, rows, v):
        if k == 2:
            stageh[dr, 4 - s, rows, :] = v.astype(BF16)
        else:
            stage[dr, 4 - s, k, rows, :] = v.astype(BF16)

    def ring_step(k, s):
        h = size(k) // 2
        both = slice(0, 2 * h)
        for dr in range(2):
            rel = Z - s if dr == 0 else s
            first = slice(dr * h, (dr + 1) * h)
            other = slice((1 - dr) * h, (2 - dr) * h)
            if s == 4:
                put(k, dr, s, first, own_part(k, 4, first))
            else:
                ring_copy(k, dr, s + 1).wait_recv()
                if s == 3:
                    put(k, dr, s, first, own_part(k, rel, first) + got(k, dr, 4, first))
                    put(k, dr, s, other, own_part(k, rel, other))
                else:
                    put(k, dr, s, both, own_part(k, rel, both) + got(k, dr, s + 1, both))
            c = ring_copy(k, dr, s)
            c.start()
            sent.append(c)

    def total(k):
        both = slice(0, size(k))
        for dr in range(2):
            ring_copy(k, dr, 1).wait_recv()
        return own_part(k, 0, both) + (got(k, 0, 1, both) + got(k, 1, 1, both))

    for rel in (4, 5, 3):
        partial_own(rel)
    for q in range(2):
        rc(no.at[:, :, pl.ds(q * LANE, LANE)], no.at[:, :, pl.ds(q * LANE, LANE)],
           o_send.at[q], o_recv.at[q], other_core).wait_recv()
    wcopy(1, wt.at[core, low], wt.at[1 - core, low], other_core).wait_recv()
    partial_other(4)
    ring_step(0, 4)
    partial_other(5)
    partial_other(3)
    ring_step(1, 4)
    wcopy(2, wt.at[core, high], wt.at[1 - core, high], other_core).wait_recv()
    for c in range(2):
        for slot in range(Z):
            rc(nx.at[c, slot], nx.at[c, slot], p_send.at[0, slot], p_recv.at[c, slot], other_xl).wait_recv()
    ring_step(0, 3)
    for c in range(2):
        wcopy(0, wt.at[core, high], wx.at[c], other_xl, c).wait_recv()
    partial_high(4)
    ring_step(1, 3)
    partial(6)
    partial(2)
    ring_step(2, 4)
    ring_step(0, 2)
    partial_high(5)
    partial_high(3)
    ring_step(1, 2)
    partial(7)
    partial(1)
    ring_step(2, 3)
    ring_step(0, 1)
    partial(0)
    partial_high(6)
    partial_high(2)
    ring_step(1, 1)
    ring_step(2, 2)
    xs[...] = total(0)
    xc = rc(xs, xr, x_send.at[0], x_recv.at[0], other_xl)
    xc.start()
    copies.append(xc)
    for rel in (7, 1, 0):
        partial_high(rel)
    ring_step(2, 1)
    kept = total(1)
    out_ref[:, HIGH] = total(2).T
    xc.wait_recv()
    out_ref[:, LOW] = (kept + xr[...]).T
    sent.extend(copies)

    for k in range(2):
        for zz in range(4):
            for c in lend_copies(k, zz):
                c.wait_send()
    for j, (buf, k) in enumerate(((nsq, 7), (lsq, 31))):
        ref = buf.at[pl.ds(0, k)]
        rc(ref, ref, q_send.at[j], q_recv.at[j], z_up).wait_send()
    for c in sent:
        c.wait_send()
    for it in range(ITERS):
        for buf, k, ssem, rsem in (
            (rowx, 7, r_send, r_recv), (col2, 31, c2_send, c2_recv)
        ):
            ref = buf.at[it, pl.ds(0, k)]
            rc(ref, ref, ssem.at[it], rsem.at[it], z_up).wait_send()


def per_device(n_total, m_total, noise_draw, latent_code, start_potential):
    anyspace = pl.BlockSpec(memory_space=pltpu.HBM)
    vmem = pl.BlockSpec(memory_space=pltpu.VMEM)
    width = 4096
    dma = pltpu.SemaphoreType.DMA

    def body(*refs):
        kernel(n_total, m_total, width, *refs)

    npot, lpot, out = pl.pallas_call(
        body,
        out_shape=(
            jax.ShapeDtypeStruct((4, LANE), F32),
            jax.ShapeDtypeStruct((4, LANE), F32),
            jax.ShapeDtypeStruct((LANE, BLK), F32),
        ),
        in_specs=[anyspace, anyspace, vmem],
        out_specs=(vmem, vmem, vmem),
        scratch_shapes=[
            pltpu.VMEM((8, BLK, BLK), BF16),
            pltpu.VMEM((Z, 2, 2, BLK, LANE), BF16),
            pltpu.VMEM((8, BLK, 2 * LANE), BF16),
            pltpu.VMEM((BLK, BLK), F32),
            pltpu.VMEM((8, 4, LANE), F32),
            pltpu.VMEM((32, 4, LANE), F32),
            pltpu.VMEM((2, BLK, BLK), BF16),
            pltpu.VMEM((2, REST, BLK), BF16),
            pltpu.VMEM((2, Z, BLK, LANE), BF16),
            pltpu.VMEM((Z, SPLIT, 2 * LANE), F32),
            pltpu.VMEM((Z, REST, LANE), F32),
            pltpu.VMEM((2, 4, 2, SPLIT, LANE), BF16),
            pltpu.VMEM((2, 4, 2, SPLIT, LANE), BF16),
            pltpu.VMEM((2, 4, REST, LANE), BF16),
            pltpu.VMEM((2, 4, REST, LANE), BF16),
            pltpu.VMEM((SPLIT, LANE), F32),
            pltpu.VMEM((SPLIT, LANE), F32),
            pltpu.VMEM((ITERS, 8, 4, LANE), F32),
            pltpu.VMEM((ITERS, 32, 4, LANE), F32),
            dma((2,)), dma((2,)),
            dma((12,)), dma((12,)),
            dma((2, 2)), dma((2, 2)),
            dma((26,)), dma((26,)),
            dma((2,)), dma((2,)),
            dma((4,)), dma((4,)),
            dma((2, Z)), dma((2, Z)),
            dma((ITERS,)), dma((ITERS,)),
            dma((ITERS,)), dma((ITERS,)),
            dma((2, 4, 2)), dma((2, 4, 2)),
            dma((2, 4)), dma((2, 4)),
            dma((1,)), dma((1,)),
            dma((2,)),
        ],
        compiler_params=pltpu.CompilerParams(
            collective_id=0, has_side_effects=True, vmem_limit_bytes=54656 * 1024
        ),
    )(noise_draw, latent_code, start_potential.reshape(4, LANE))
    return npot.reshape(BLK), lpot.reshape(BLK), out


def solution(mesh):
    in_specs = (P("row", "col"), P("col", "row"), P("col"))
    out_specs = (P("row"), P("col"), P("row", "col"))

    def whole(noise_draw, latent_code, start_potential):
        def block(a, b, c):
            return per_device(noise_draw.shape[0], latent_code.shape[0], a, b, c)

        return jax.shard_map(
            block, mesh=mesh, in_specs=in_specs, out_specs=out_specs, check_vma=False
        )(noise_draw, latent_code, start_potential)

    return whole
```

```python
import math

import jax
import jax.numpy as jnp
from jax import lax
from jax.experimental import pallas as pl
from jax.experimental.pallas import tpu as pltpu
from jax.sharding import PartitionSpec as P

ITERS = 3
EPS = 0.01
LOG2E = math.log2(math.e)
MESH = pl.DeviceIdType.MESH
F32 = jnp.float32
BF16 = jnp.bfloat16

Z, Y = 8, 4
LANE = 128
BLK = 512
HALF = BLK // 2
SPLIT = 384
REST = BLK - SPLIT


def kernel(
    n_total, m_total, width,
    noise_ref, latent_ref, start_ref,
    npot_ref, lpot_ref, out_ref,
    nz, lt, no, cross, nsq, lsq, wt, wx, nx, part, parth, stage, land, stageh, landh, xs, xr, rowx, col2,
    q_send, q_recv, n_send, n_recv, h_send, h_recv, l_send, l_recv, o_send, o_recv, w_send, w_recv,
    p_send, p_recv, r_send, r_recv, c2_send, c2_recv,
    s_send, s_recv, t_send, t_recv, x_send, x_recv, loc,
):
    row = lax.axis_index("row")
    col = lax.axis_index("col")
    z = row // 4
    xl = (row // 2) % 2
    core = row % 2
    y = col // 2
    xh = col % 2
    quad = row % 4

    def ring_z(d):
        return (z + d + Z) % Z

    def ring_y(d):
        return (y + d + Y) % Y

    other_core = (row + 1 - 2 * core, col)
    other_xl = (row + 2 - 4 * xl, col)
    flip_col = col + 1 - 2 * xh
    other_xh = (row, flip_col)
    z_up = (ring_z(1) * 4 + quad, col)
    z_dn = (ring_z(-1) * 4 + quad, col)
    y_up = (row, ring_y(1) * 2 + xh)
    y_dn = (row, ring_y(-1) * 2 + xh)
    col_peers = [
        (row, ring_y(dy) * 2 + (1 - xh if dx else xh))
        for dy, dx in ((2, 1), (1, 1), (-1, 1), (2, 0), (0, 1), (1, 0), (-1, 0))
    ]
    across = (row + 2 - 4 * xl) // 2 * 2
    across_quad = ((across + 1 - core) % 4, (across + core) % 4, (quad // 2) * 2 + 1 - core, quad)
    row_peers = [
        (ring_z(d) * 4 + q, col)
        for d in (4, 3, -3, 2, -2, 1, -1, 0) for q in across_quad[:3 if d == 0 else 4]
    ]
    peers = col_peers + row_peers + [(across, flip_col), (across + 1, flip_col)]

    own_n = pltpu.make_async_copy(noise_ref, nz.at[col], loc.at[0])
    own_l = pltpu.make_async_copy(latent_ref, lt.at[z, core, xl], loc.at[1])
    own_n.start()
    own_l.start()

    barrier = pltpu.get_barrier_semaphore()
    for peer in peers:
        pl.semaphore_signal(barrier, inc=1, device_id=peer, device_id_type=MESH)
    cross[...] = jnp.zeros_like(cross)
    pl.semaphore_wait(barrier, len(peers))

    def rc(src, dst, ssem, rsem, dev):
        return pltpu.make_async_remote_copy(
            src_ref=src, dst_ref=dst, send_sem=ssem, recv_sem=rsem,
            device_id=dev, device_id_type=MESH,
        )

    def nsl(slot, h):
        return nz.at[slot, pl.ds(h * HALF, HALF), :]

    QUART = HALF // 2
    sent = []

    def nsend(slot, h, idx, dev, src=None):
        src = nsl(slot, h) if src is None else src
        c = rc(src, nsl(slot, h), n_send.at[idx], n_recv.at[idx], dev)
        c.start()
        return c

    def own_half(h):
        return noise_ref.at[pl.ds(h * HALF, HALF), :]

    def nwait(slot, h, idx):
        rc(nsl(slot, h), nsl(slot, h), n_send.at[idx], n_recv.at[idx], y_up).wait_recv()

    def lsend(ref, idx, dev, src=None):
        c = rc(ref if src is None else src, ref, l_send.at[idx], l_recv.at[idx], dev)
        c.start()
        sent.append(c)

    def lwait(ref, idx):
        rc(ref, ref, l_send.at[idx], l_recv.at[idx], z_up).wait_recv()

    def slot_of(yy, s):
        return yy * 2 + (xh if s == 0 else 1 - xh)

    def xh_copy(t, h, src, slot):
        return rc(src, nsl(slot, h), h_send.at[t, h], h_recv.at[t, h], other_xh)

    def xh_send(t, h):
        far0 = slot_of(ring_y(2), 0)
        c = xh_copy(t, h, own_half(h), col) if t == 0 else xh_copy(t, h, nsl(far0, h), far0)
        c.start()
        sent.append(c)

    def xh_wait(t, h):
        slot = flip_col if t == 0 else slot_of(ring_y(2), 1)
        xh_copy(t, h, nsl(slot, h), slot).wait_recv()

    own_pair = lt.at[z, core]
    own_block = lt.at[z, core, xl]
    z_dirs = ((0, -1, z_up), (1, 1, z_dn))

    def lat(d, part):
        return lt.at[ring_z(d), core, xl if part == 0 else 1 - xl]

    def lat_forward(step, part, dirs):
        for dr, sgn, dev in dirs:
            block = lat(sgn * step, part)
            lwait(block, 1 + 8 * dr + 2 * (step - 1) + part)
            if step < 3 or part == dr:
                lsend(block, 1 + 8 * dr + 2 * step + part, dev)
            if step == 3 and part == dr:
                lsend(block, 24 + part, (dev[0] + 1 - 2 * core, col))

    def lat_share(step):
        for dr, sgn, _ in z_dirs:
            lsend(lt.at[ring_z(sgn * step), core], 16 + 2 * step + dr, other_core)

    lat_x = rc(latent_ref, own_block, l_send.at[0], l_recv.at[0], other_xl)
    lat_x.start()
    lsend(own_block, 1, z_up, latent_ref)
    lsend(own_block, 9, z_dn, latent_ref)
    first_up = nsend(col, 0, 0, y_up, own_half(0))
    first_dn = nsend(col, 1, 3, y_dn, own_half(1))

    sent.append(lat_x)
    xh_send(0, 0)

    own_n.wait()
    own_l.wait()
    for b in range(4):
        rows = slice(b * LANE, (b + 1) * LANE)
        n2 = jnp.square(nz[col, rows, :].astype(F32))
        n2 = (n2[:, 0:128] + n2[:, 128:256]) + (n2[:, 256:384] + n2[:, 384:512])
        nsq[col, b:b + 1, :] = jnp.sum(n2.T, axis=0, keepdims=True)
        l2 = jnp.square(lt[z, core, xl, rows, :].astype(F32))
        lsq[row, b:b + 1, :] = jnp.sum(l2.T, axis=0, keepdims=True)

    lwait(lat(0, 1), 0)
    lsend(lat(0, 1), 2, z_up)
    lsend(lat(0, 1), 10, z_dn)
    xh_send(0, 1)
    lat_forward(1, 0, z_dirs)
    lsend(own_pair, 17, other_core)

    def own_quarter(h, p, idx, dev):
        at = pl.ds(h * HALF + p * QUART, QUART)
        c = rc(noise_ref.at[at, :], nz.at[col, at, :], n_send.at[idx], n_recv.at[idx], dev)
        c.start()
        sent.append(c)

    first_up.wait_send()
    own_quarter(1, 0, 1, y_up)
    first_dn.wait_send()
    own_quarter(0, 0, 2, y_dn)

    dn, up = slot_of(ring_y(-1), 0), slot_of(ring_y(1), 0)
    nwait(dn, 0, 0)
    onward_up = nsend(dn, 0, 4, y_up)
    nwait(up, 1, 3)
    onward_dn = nsend(up, 1, 5, y_dn)

    lat_forward(1, 1, z_dirs)
    lat_share(1)
    lat_forward(2, 0, z_dirs)
    lat_forward(2, 1, z_dirs)
    lat_share(2)

    onward_up.wait_send()
    own_quarter(1, 1, 10, y_up)
    onward_dn.wait_send()
    own_quarter(0, 1, 11, y_dn)

    nwait(slot_of(ring_y(2), 0), 0, 4)
    xh_send(1, 0)
    nwait(slot_of(ring_y(2), 0), 1, 5)
    xh_send(1, 1)

    lat_forward(3, 0, z_dirs)

    xh_wait(0, 0)
    sent.append(nsend(flip_col, 0, 6, y_up))
    sent.append(nsend(flip_col, 0, 8, y_dn))
    xh_wait(0, 1)
    sent.append(nsend(flip_col, 1, 9, y_dn))
    sent.append(nsend(flip_col, 1, 7, y_up))

    lat_forward(3, 1, z_dirs)
    lat_share(3)
    for peer in col_peers:
        rc(nsq.at[col], nsq.at[col], q_send.at[0], q_recv.at[0], peer).start()
    for peer in row_peers:
        rc(lsq.at[row], lsq.at[row], q_send.at[1], q_recv.at[1], peer).start()
    lwait(lat(4, 0), 7)
    lwait(lat(4, 1), 16)
    for j, d in enumerate((0, -1, 1, -2, 2, -3, 3)):
        lwait(lt.at[ring_z(d), 1 - core], 17 + j)
    lwait(lt.at[ring_z(4), 1 - core, xl], 24)
    lwait(lt.at[ring_z(4), 1 - core, 1 - xl], 25)

    def accumulate(slot):
        a = nz[slot]
        b = jnp.concatenate([lt[slot, 0, 0], lt[slot, 1, 0], lt[slot, 0, 1], lt[slot, 1, 1]], axis=1)
        cross[...] += lax.dot_general(a, b, (((1,), (1,)), ((), ())), preferred_element_type=F32)

    dn, up = slot_of(ring_y(-1), 0), slot_of(ring_y(1), 0)
    for slot, h, idxs in ((dn, 1, (1, 10)), (up, 0, (2, 11))):
        for p in range(2):
            ref = nz.at[slot, pl.ds(h * HALF + p * QUART, QUART), :]
            rc(ref, ref, n_send.at[idxs[p]], n_recv.at[idxs[p]], y_up).wait_recv()

    def set0(k, carry):
        accumulate(((y + k) % Y) * 2 + xh)
        return carry

    lax.fori_loop(0, Y, set0, 0)
    accumulate(flip_col)
    xh_wait(1, 0)
    xh_wait(1, 1)
    accumulate(slot_of(ring_y(2), 1))
    dn, up = slot_of(ring_y(-1), 1), slot_of(ring_y(1), 1)
    nwait(dn, 0, 6)
    nwait(up, 1, 9)
    nwait(dn, 1, 7)
    nwait(up, 0, 8)
    accumulate(dn)
    accumulate(up)

    for q in range(2):
        c = rc(
            nz.at[:, :, pl.ds(pl.multiple_of(q * 256 + (1 - core) * LANE, LANE), LANE)],
            no.at[:, :, pl.ds(q * LANE, LANE)],
            o_send.at[q], o_recv.at[q], other_core,
        )
        c.start()
        sent.append(c)

    eye = (
        lax.broadcasted_iota(jnp.int32, (LANE, LANE), 0)
        == lax.broadcasted_iota(jnp.int32, (LANE, LANE), 1)
    )

    def to_rows(v):
        return jnp.sum(jnp.where(eye, v, 0.0), axis=1, keepdims=True)

    def wide(v):
        return jnp.concatenate([v[q:q + 1, :] for q in range(4)], axis=1)

    scale = LOG2E / (width * EPS)
    rc(nsq.at[pl.ds(0, 7)], nsq.at[pl.ds(0, 7)], q_send.at[0], q_recv.at[0], z_up).wait_recv()
    rc(lsq.at[pl.ds(0, 31)], lsq.at[pl.ds(0, 31)], q_send.at[1], q_recv.at[1], z_up).wait_recv()
    nq = jnp.sum(nsq[...], axis=0)
    lq = wide(jnp.sum(lsq[...], axis=0))
    for b in range(4):
        rows = slice(b * LANE, (b + 1) * LANE)
        cross[rows, :] = (to_rows(nq[b:b + 1, :]) + lq - 2.0 * cross[rows, :]) * scale

    def merge(parts):
        best = jnp.max(parts, axis=0)
        return best + jnp.log2(jnp.sum(jnp.exp2(parts - best[None]), axis=0))

    def merge_rows(parts):
        best = jnp.max(parts, axis=0, keepdims=True)
        return best + jnp.log2(jnp.sum(jnp.exp2(parts - best), axis=0, keepdims=True))

    def lend(step):
        k, zz = step % 2, step // 2
        lanes = pl.ds(pl.multiple_of((1 - xl) * 256 + k * LANE, LANE), LANE)
        for slot, dev in ((zz, (across + k, col)), (zz + 4, (across + k, flip_col))):
            c = rc(nz.at[slot, :, lanes], nx.at[core, slot], p_send.at[k, slot], p_recv.at[core, slot], dev)
            c.start()
            sent.append(c)

    steps = iter(range(6))

    def exchange(buf, mine, peers, ssem, rsem):
        for peer in peers:
            rc(buf.at[mine], buf.at[mine], ssem, rsem, peer).start()
        step = next(steps)
        for piece_at in range(*((0, 2), (2, 4), (4, 6), (6, 7), (7, 8), (8, 8))[step]):
            lend(piece_at)
        k = len(peers)
        rc(buf.at[pl.ds(0, k)], buf.at[pl.ds(0, k)], ssem, rsem, peers[0]).wait_recv()

    g = start_ref[...] * (LOG2E / EPS)
    f = None
    f_rows = None
    for it in range(ITERS):
        for b in range(4):
            parts = []
            for r in range(b * LANE, (b + 1) * LANE, 32):
                s = [g[q:q + 1, :] - cross[r:r + 32, q * LANE:(q + 1) * LANE] for q in range(4)]
                top = jnp.maximum(jnp.maximum(s[0], s[1]), jnp.maximum(s[2], s[3]))
                e = [jnp.exp2(v - top) for v in s]
                parts.append(top + jnp.log2((e[0] + e[1]) + (e[2] + e[3])))
            rowx[it, col, b:b + 1, :] = merge_rows(jnp.concatenate(parts, axis=0).T)
        exchange(rowx.at[it], col, col_peers, r_send.at[it], r_recv.at[it])
        f = -(math.log2(m_total) + merge(rowx[it]))
        f_rows = [to_rows(f[b:b + 1, :]) for b in range(4)]
        parts = []
        for r in range(0, BLK, 64):
            fr = f_rows[r // LANE][r % LANE:r % LANE + 64]
            s = (fr - cross[r:r + 64, :]).reshape(8, 8, BLK)
            top = jnp.max(s, axis=0)
            parts.append(top + jnp.log2(jnp.sum(jnp.exp2(s - top[None]), axis=0)))
        top = parts[0]
        for v in parts[1:]:
            top = jnp.maximum(top, v)
        own = merge_rows(top + jnp.log2(sum(jnp.exp2(v - top) for v in parts)))
        for q in range(4):
            col2[it, row, q:q + 1, :] = own[:, q * LANE:(q + 1) * LANE]
        exchange(col2.at[it], row, row_peers, c2_send.at[it], c2_recv.at[it])
        g = -(math.log2(n_total) + merge(col2[it]))

    npot_ref[...] = f * (EPS / LOG2E)
    lpot_ref[...] = g * (EPS / LOG2E)

    LOW, HIGH = slice(0, SPLIT), slice(SPLIT, BLK)
    gw = wide(g)

    def weights(cols):
        for b in range(4):
            rows = slice(b * LANE, (b + 1) * LANE)
            w = m_total * jnp.exp2((f_rows[b] + gw[:, cols]) - cross[rows, cols])
            wt[core, cols, rows] = w.T.astype(BF16)

    def wcopy(j, src, dst, dev, r=None):
        return rc(src, dst, w_send.at[j], w_recv.at[j if r is None else 3 * r], dev)

    low, high = pl.ds(0, SPLIT), pl.ds(SPLIT, REST)
    copies = []
    weights(HIGH)
    for k in range(2):
        copies.append(wcopy(3 * k, wt.at[core, high], wx.at[core], (across + k, col), core))
        copies[-1].start()
    weights(LOW)
    copies.append(wcopy(1, wt.at[core, low], wt.at[core, low], other_core))
    copies[-1].start()
    copies.append(wcopy(2, wt.at[core, high], wt.at[core, high], other_core))
    copies[-1].start()

    def mine(d, q):
        return nz[d, :, pl.ds(pl.multiple_of(q * 256 + core * LANE, LANE), LANE)]

    def theirs(d, q):
        return no[d, :, pl.ds(pl.multiple_of(q * LANE, LANE), LANE)]

    def partial_own(rel):
        d = (z + rel) % Z
        part[rel] = jnp.dot(
            wt[core, LOW, :], jnp.concatenate([mine(d, q) for q in (1 - xl, xl)], axis=1),
            preferred_element_type=F32,
        )

    def partial_other(rel):
        d = (z + rel) % Z
        part[rel] += jnp.dot(
            wt[1 - core, LOW, :], jnp.concatenate([theirs(d, q) for q in (1 - xl, xl)], axis=1),
            preferred_element_type=F32,
        )

    def partial(rel):
        partial_own(rel)
        partial_other(rel)

    def partial_high(rel):
        d = (z + rel) % Z
        parth[rel] = (
            jnp.dot(wt[core, HIGH, :], mine(d, xl), preferred_element_type=F32)
            + jnp.dot(wt[1 - core, HIGH, :], theirs(d, xl), preferred_element_type=F32)
        ) + (
            jnp.dot(wx[0], nx[0, d], preferred_element_type=F32)
            + jnp.dot(wx[1], nx[1, d], preferred_element_type=F32)
        )

    def size(k):
        return REST if k == 2 else SPLIT

    def piece(k, bufs, dr, s):
        ref = bufs[1].at[dr, 4 - s] if k == 2 else bufs[0].at[dr, 4 - s, k]
        h = size(k) // 2
        return ref.at[pl.ds(dr * h, h)] if s == 4 else ref

    def ring_copy(k, dr, s):
        ss, rs = (t_send.at[dr, 4 - s], t_recv.at[dr, 4 - s]) if k == 2 else (
            s_send.at[dr, 4 - s, k], s_recv.at[dr, 4 - s, k])
        return rc(
            piece(k, (stage, stageh), dr, s), piece(k, (land, landh), dr, s), ss, rs,
            z_dn if dr == 0 else z_up,
        )

    def own_part(k, rel, rows):
        return parth[rel, rows, :] if k == 2 else part[rel, rows, k * LANE:(k + 1) * LANE]

    def got(k, dr, s, rows):
        v = landh[dr, 4 - s, rows, :] if k == 2 else land[dr, 4 - s, k, rows, :]
        return v.astype(F32)

    def put(k, dr, s, rows, v):
        if k == 2:
            stageh[dr, 4 - s, rows, :] = v.astype(BF16)
        else:
            stage[dr, 4 - s, k, rows, :] = v.astype(BF16)

    def ring_step(k, s):
        h = size(k) // 2
        both = slice(0, 2 * h)
        for dr in range(2):
            rel = Z - s if dr == 0 else s
            first = slice(dr * h, (dr + 1) * h)
            other = slice((1 - dr) * h, (2 - dr) * h)
            if s == 4:
                put(k, dr, s, first, own_part(k, 4, first))
            else:
                ring_copy(k, dr, s + 1).wait_recv()
                if s == 3:
                    put(k, dr, s, first, own_part(k, rel, first) + got(k, dr, 4, first))
                    put(k, dr, s, other, own_part(k, rel, other))
                else:
                    put(k, dr, s, both, own_part(k, rel, both) + got(k, dr, s + 1, both))
            c = ring_copy(k, dr, s)
            c.start()
            sent.append(c)

    def total(k):
        both = slice(0, size(k))
        for dr in range(2):
            ring_copy(k, dr, 1).wait_recv()
        return own_part(k, 0, both) + (got(k, 0, 1, both) + got(k, 1, 1, both))

    for rel in (4, 5, 3):
        partial_own(rel)
    for q in range(2):
        rc(no.at[:, :, pl.ds(q * LANE, LANE)], no.at[:, :, pl.ds(q * LANE, LANE)],
           o_send.at[q], o_recv.at[q], other_core).wait_recv()
    wcopy(1, wt.at[core, low], wt.at[1 - core, low], other_core).wait_recv()
    partial_other(4)
    ring_step(0, 4)
    partial_other(5)
    partial_other(3)
    ring_step(1, 4)
    wcopy(2, wt.at[core, high], wt.at[1 - core, high], other_core).wait_recv()
    for c in range(2):
        for slot in range(Z):
            rc(nx.at[c, slot], nx.at[c, slot], p_send.at[0, slot], p_recv.at[c, slot], other_xl).wait_recv()
    ring_step(0, 3)
    for c in range(2):
        wcopy(0, wt.at[core, high], wx.at[c], other_xl, c).wait_recv()
    partial_high(4)
    ring_step(1, 3)
    partial(6)
    partial(2)
    ring_step(2, 4)
    ring_step(0, 2)
    partial_high(5)
    partial_high(3)
    ring_step(1, 2)
    partial(7)
    partial(1)
    ring_step(2, 3)
    ring_step(0, 1)
    partial(0)
    partial_high(6)
    partial_high(2)
    ring_step(1, 1)
    ring_step(2, 2)
    xs[...] = total(0)
    xc = rc(xs, xr, x_send.at[0], x_recv.at[0], other_xl)
    xc.start()
    copies.append(xc)
    for rel in (7, 1, 0):
        partial_high(rel)
    ring_step(2, 1)
    kept = total(1)
    out_ref[:, HIGH] = total(2).T
    xc.wait_recv()
    out_ref[:, LOW] = (kept + xr[...]).T
    sent.extend(copies)

    for j, (buf, k) in enumerate(((nsq, 7), (lsq, 31))):
        ref = buf.at[pl.ds(0, k)]
        rc(ref, ref, q_send.at[j], q_recv.at[j], z_up).wait_send()
    for c in sent:
        c.wait_send()
    for it in range(ITERS):
        for buf, k, ssem, rsem in (
            (rowx, 7, r_send, r_recv), (col2, 31, c2_send, c2_recv)
        ):
            ref = buf.at[it, pl.ds(0, k)]
            rc(ref, ref, ssem.at[it], rsem.at[it], z_up).wait_send()


def per_device(n_total, m_total, noise_draw, latent_code, start_potential):
    anyspace = pl.BlockSpec(memory_space=pltpu.HBM)
    vmem = pl.BlockSpec(memory_space=pltpu.VMEM)
    width = 4096
    dma = pltpu.SemaphoreType.DMA

    def body(*refs):
        kernel(n_total, m_total, width, *refs)

    npot, lpot, out = pl.pallas_call(
        body,
        out_shape=(
            jax.ShapeDtypeStruct((4, LANE), F32),
            jax.ShapeDtypeStruct((4, LANE), F32),
            jax.ShapeDtypeStruct((LANE, BLK), F32),
        ),
        in_specs=[anyspace, anyspace, vmem],
        out_specs=(vmem, vmem, vmem),
        scratch_shapes=[
            pltpu.VMEM((8, BLK, BLK), BF16),
            pltpu.VMEM((Z, 2, 2, BLK, LANE), BF16),
            pltpu.VMEM((8, BLK, 2 * LANE), BF16),
            pltpu.VMEM((BLK, BLK), F32),
            pltpu.VMEM((8, 4, LANE), F32),
            pltpu.VMEM((32, 4, LANE), F32),
            pltpu.VMEM((2, BLK, BLK), BF16),
            pltpu.VMEM((2, REST, BLK), BF16),
            pltpu.VMEM((2, Z, BLK, LANE), BF16),
            pltpu.VMEM((Z, SPLIT, 2 * LANE), F32),
            pltpu.VMEM((Z, REST, LANE), F32),
            pltpu.VMEM((2, 4, 2, SPLIT, LANE), BF16),
            pltpu.VMEM((2, 4, 2, SPLIT, LANE), BF16),
            pltpu.VMEM((2, 4, REST, LANE), BF16),
            pltpu.VMEM((2, 4, REST, LANE), BF16),
            pltpu.VMEM((SPLIT, LANE), F32),
            pltpu.VMEM((SPLIT, LANE), F32),
            pltpu.VMEM((ITERS, 8, 4, LANE), F32),
            pltpu.VMEM((ITERS, 32, 4, LANE), F32),
            dma((2,)), dma((2,)),
            dma((12,)), dma((12,)),
            dma((2, 2)), dma((2, 2)),
            dma((26,)), dma((26,)),
            dma((2,)), dma((2,)),
            dma((4,)), dma((4,)),
            dma((2, Z)), dma((2, Z)),
            dma((ITERS,)), dma((ITERS,)),
            dma((ITERS,)), dma((ITERS,)),
            dma((2, 4, 2)), dma((2, 4, 2)),
            dma((2, 4)), dma((2, 4)),
            dma((1,)), dma((1,)),
            dma((2,)),
        ],
        compiler_params=pltpu.CompilerParams(
            collective_id=0, has_side_effects=True, vmem_limit_bytes=54656 * 1024
        ),
    )(noise_draw, latent_code, start_potential.reshape(4, LANE))
    return npot.reshape(BLK), lpot.reshape(BLK), out


def solution(mesh):
    in_specs = (P("row", "col"), P("col", "row"), P("col"))
    out_specs = (P("row"), P("col"), P("row", "col"))

    def whole(noise_draw, latent_code, start_potential):
        def block(a, b, c):
            return per_device(noise_draw.shape[0], latent_code.shape[0], a, b, c)

        return jax.shard_map(
            block, mesh=mesh, in_specs=in_specs, out_specs=out_specs, check_vma=False
        )(noise_draw, latent_code, start_potential)

    return whole
```

```python
import math

import jax
import jax.numpy as jnp
from jax import lax
from jax.experimental import pallas as pl
from jax.experimental.pallas import tpu as pltpu
from jax.sharding import PartitionSpec as P

ITERS = 3
EPS = 0.01
LOG2E = math.log2(math.e)
MESH = pl.DeviceIdType.MESH
F32 = jnp.float32
BF16 = jnp.bfloat16

Z, Y = 8, 4
LANE = 128
BLK = 512
HALF = BLK // 2
SPLIT = 384
REST = BLK - SPLIT


def kernel(
    n_total, m_total, width,
    noise_ref, latent_ref, start_ref,
    npot_ref, lpot_ref, out_ref,
    nz, lt, no, cross, nsq, lsq, wt, wx, nx, part, parth, stage, land, stageh, landh, xs, xr, rowx, col2,
    q_send, q_recv, n_send, n_recv, h_send, h_recv, l_send, l_recv, o_send, o_recv, w_send, w_recv,
    p_send, p_recv, r_send, r_recv, c2_send, c2_recv,
    s_send, s_recv, t_send, t_recv, x_send, x_recv, loc,
):
    row = lax.axis_index("row")
    col = lax.axis_index("col")
    z = row // 4
    xl = (row // 2) % 2
    core = row % 2
    y = col // 2
    xh = col % 2
    quad = row % 4

    def ring_z(d):
        return (z + d + Z) % Z

    def ring_y(d):
        return (y + d + Y) % Y

    other_core = (row + 1 - 2 * core, col)
    other_xl = (row + 2 - 4 * xl, col)
    flip_col = col + 1 - 2 * xh
    other_xh = (row, flip_col)
    z_up = (ring_z(1) * 4 + quad, col)
    z_dn = (ring_z(-1) * 4 + quad, col)
    y_up = (row, ring_y(1) * 2 + xh)
    y_dn = (row, ring_y(-1) * 2 + xh)
    col_peers = [
        (row, ring_y(dy) * 2 + (1 - xh if dx else xh))
        for dy, dx in ((2, 1), (1, 1), (-1, 1), (2, 0), (0, 1), (1, 0), (-1, 0))
    ]
    across = (row + 2 - 4 * xl) // 2 * 2
    across_quad = ((across + 1 - core) % 4, (across + core) % 4, (quad // 2) * 2 + 1 - core, quad)
    row_peers = [
        (ring_z(d) * 4 + q, col)
        for d in (4, 3, -3, 2, -2, 1, -1, 0) for q in across_quad[:3 if d == 0 else 4]
    ]
    peers = col_peers + row_peers + [(across, flip_col), (across + 1, flip_col)]

    own_n = pltpu.make_async_copy(noise_ref, nz.at[col], loc.at[0])
    own_l = pltpu.make_async_copy(latent_ref, lt.at[z, core, xl], loc.at[1])
    own_n.start()
    own_l.start()

    barrier = pltpu.get_barrier_semaphore()
    for peer in peers:
        pl.semaphore_signal(barrier, inc=1, device_id=peer, device_id_type=MESH)
    cross[...] = jnp.zeros_like(cross)
    pl.semaphore_wait(barrier, len(peers))

    def rc(src, dst, ssem, rsem, dev):
        return pltpu.make_async_remote_copy(
            src_ref=src, dst_ref=dst, send_sem=ssem, recv_sem=rsem,
            device_id=dev, device_id_type=MESH,
        )

    def nsl(slot, h):
        return nz.at[slot, pl.ds(h * HALF, HALF), :]

    QUART = HALF // 2
    sent = []

    def nsend(slot, h, idx, dev, src=None):
        src = nsl(slot, h) if src is None else src
        c = rc(src, nsl(slot, h), n_send.at[idx], n_recv.at[idx], dev)
        c.start()
        return c

    def own_half(h):
        return noise_ref.at[pl.ds(h * HALF, HALF), :]

    def nwait(slot, h, idx):
        rc(nsl(slot, h), nsl(slot, h), n_send.at[idx], n_recv.at[idx], y_up).wait_recv()

    def lsend(ref, idx, dev, src=None):
        c = rc(ref if src is None else src, ref, l_send.at[idx], l_recv.at[idx], dev)
        c.start()
        sent.append(c)

    def lwait(ref, idx):
        rc(ref, ref, l_send.at[idx], l_recv.at[idx], z_up).wait_recv()

    def slot_of(yy, s):
        return yy * 2 + (xh if s == 0 else 1 - xh)

    def xh_copy(t, h, src, slot):
        return rc(src, nsl(slot, h), h_send.at[t, h], h_recv.at[t, h], other_xh)

    def xh_send(t, h):
        far0 = slot_of(ring_y(2), 0)
        c = xh_copy(t, h, own_half(h), col) if t == 0 else xh_copy(t, h, nsl(far0, h), far0)
        c.start()
        sent.append(c)

    def xh_wait(t, h):
        slot = flip_col if t == 0 else slot_of(ring_y(2), 1)
        xh_copy(t, h, nsl(slot, h), slot).wait_recv()

    own_pair = lt.at[z, core]
    own_block = lt.at[z, core, xl]
    z_dirs = ((0, -1, z_up), (1, 1, z_dn))

    def lat(d, part):
        return lt.at[ring_z(d), core, xl if part == 0 else 1 - xl]

    def lat_forward(step, part, dirs):
        for dr, sgn, dev in dirs:
            block = lat(sgn * step, part)
            lwait(block, 1 + 8 * dr + 2 * (step - 1) + part)
            if step < 3 or part == dr:
                lsend(block, 1 + 8 * dr + 2 * step + part, dev)
            if step == 3 and part == dr:
                lsend(block, 24 + part, (dev[0] + 1 - 2 * core, col))

    def lat_share(step):
        for dr, sgn, _ in z_dirs:
            lsend(lt.at[ring_z(sgn * step), core], 16 + 2 * step + dr, other_core)

    lat_x = rc(latent_ref, own_block, l_send.at[0], l_recv.at[0], other_xl)
    lat_x.start()
    lsend(own_block, 1, z_up, latent_ref)
    lsend(own_block, 9, z_dn, latent_ref)
    first_up = nsend(col, 0, 0, y_up, own_half(0))
    first_dn = nsend(col, 1, 3, y_dn, own_half(1))

    sent.append(lat_x)
    xh_send(0, 0)

    own_n.wait()
    own_l.wait()
    for b in range(4):
        rows = slice(b * LANE, (b + 1) * LANE)
        n2 = jnp.square(nz[col, rows, :].astype(F32))
        n2 = (n2[:, 0:128] + n2[:, 128:256]) + (n2[:, 256:384] + n2[:, 384:512])
        nsq[col, b:b + 1, :] = jnp.sum(n2.T, axis=0, keepdims=True)
        l2 = jnp.square(lt[z, core, xl, rows, :].astype(F32))
        lsq[row, b:b + 1, :] = jnp.sum(l2.T, axis=0, keepdims=True)

    lwait(lat(0, 1), 0)
    lsend(lat(0, 1), 2, z_up)
    lsend(lat(0, 1), 10, z_dn)
    xh_send(0, 1)
    lat_forward(1, 0, z_dirs)
    lsend(own_pair, 17, other_core)

    def own_quarter(h, p, idx, dev):
        at = pl.ds(h * HALF + p * QUART, QUART)
        c = rc(noise_ref.at[at, :], nz.at[col, at, :], n_send.at[idx], n_recv.at[idx], dev)
        c.start()
        sent.append(c)

    first_up.wait_send()
    own_quarter(1, 0, 1, y_up)
    first_dn.wait_send()
    own_quarter(0, 0, 2, y_dn)

    dn, up = slot_of(ring_y(-1), 0), slot_of(ring_y(1), 0)
    nwait(dn, 0, 0)
    onward_up = nsend(dn, 0, 4, y_up)
    nwait(up, 1, 3)
    onward_dn = nsend(up, 1, 5, y_dn)

    lat_forward(1, 1, z_dirs)
    lat_share(1)
    lat_forward(2, 0, z_dirs)
    lat_forward(2, 1, z_dirs)
    lat_share(2)

    onward_up.wait_send()
    own_quarter(1, 1, 10, y_up)
    onward_dn.wait_send()
    own_quarter(0, 1, 11, y_dn)

    nwait(slot_of(ring_y(2), 0), 0, 4)
    xh_send(1, 0)
    nwait(slot_of(ring_y(2), 0), 1, 5)
    xh_send(1, 1)

    lat_forward(3, 0, z_dirs)

    xh_wait(0, 0)
    sent.append(nsend(flip_col, 0, 6, y_up))
    sent.append(nsend(flip_col, 0, 8, y_dn))
    xh_wait(0, 1)
    sent.append(nsend(flip_col, 1, 9, y_dn))
    sent.append(nsend(flip_col, 1, 7, y_up))

    lat_forward(3, 1, z_dirs)
    lat_share(3)
    for peer in col_peers:
        rc(nsq.at[col], nsq.at[col], q_send.at[0], q_recv.at[0], peer).start()
    for peer in row_peers:
        rc(lsq.at[row], lsq.at[row], q_send.at[1], q_recv.at[1], peer).start()
    lwait(lat(4, 0), 7)
    lwait(lat(4, 1), 16)
    for j, d in enumerate((0, -1, 1, -2, 2, -3, 3)):
        lwait(lt.at[ring_z(d), 1 - core], 17 + j)
    lwait(lt.at[ring_z(4), 1 - core, xl], 24)
    lwait(lt.at[ring_z(4), 1 - core, 1 - xl], 25)

    def accumulate(slot):
        a = nz[slot]
        b = jnp.concatenate([lt[slot, 0, 0], lt[slot, 1, 0], lt[slot, 0, 1], lt[slot, 1, 1]], axis=1)
        cross[...] += lax.dot_general(a, b, (((1,), (1,)), ((), ())), preferred_element_type=F32)

    dn, up = slot_of(ring_y(-1), 0), slot_of(ring_y(1), 0)
    for slot, h, idxs in ((dn, 1, (1, 10)), (up, 0, (2, 11))):
        for p in range(2):
            ref = nz.at[slot, pl.ds(h * HALF + p * QUART, QUART), :]
            rc(ref, ref, n_send.at[idxs[p]], n_recv.at[idxs[p]], y_up).wait_recv()

    def set0(k, carry):
        accumulate(((y + k) % Y) * 2 + xh)
        return carry

    lax.fori_loop(0, Y, set0, 0)
    accumulate(flip_col)
    xh_wait(1, 0)
    xh_wait(1, 1)
    accumulate(slot_of(ring_y(2), 1))
    dn, up = slot_of(ring_y(-1), 1), slot_of(ring_y(1), 1)
    nwait(dn, 0, 6)
    nwait(up, 1, 9)
    nwait(dn, 1, 7)
    nwait(up, 0, 8)
    accumulate(dn)
    accumulate(up)

    for q in range(2):
        c = rc(
            nz.at[:, :, pl.ds(pl.multiple_of(q * 256 + (1 - core) * LANE, LANE), LANE)],
            no.at[:, :, pl.ds(q * LANE, LANE)],
            o_send.at[q], o_recv.at[q], other_core,
        )
        c.start()
        sent.append(c)

    eye = (
        lax.broadcasted_iota(jnp.int32, (LANE, LANE), 0)
        == lax.broadcasted_iota(jnp.int32, (LANE, LANE), 1)
    )

    def to_rows(v):
        return jnp.sum(jnp.where(eye, v, 0.0), axis=1, keepdims=True)

    def wide(v):
        return jnp.concatenate([v[q:q + 1, :] for q in range(4)], axis=1)

    scale = LOG2E / (width * EPS)
    rc(nsq.at[pl.ds(0, 7)], nsq.at[pl.ds(0, 7)], q_send.at[0], q_recv.at[0], z_up).wait_recv()
    rc(lsq.at[pl.ds(0, 31)], lsq.at[pl.ds(0, 31)], q_send.at[1], q_recv.at[1], z_up).wait_recv()
    nq = jnp.sum(nsq[...], axis=0)
    lq = wide(jnp.sum(lsq[...], axis=0))
    for b in range(4):
        rows = slice(b * LANE, (b + 1) * LANE)
        cross[rows, :] = (to_rows(nq[b:b + 1, :]) + lq - 2.0 * cross[rows, :]) * scale

    def merge(parts):
        best = jnp.max(parts, axis=0)
        return best + jnp.log2(jnp.sum(jnp.exp2(parts - best[None]), axis=0))

    def merge_rows(parts):
        best = jnp.max(parts, axis=0, keepdims=True)
        return best + jnp.log2(jnp.sum(jnp.exp2(parts - best), axis=0, keepdims=True))

    lent = []

    def lend():
        for k in range(2):
            lanes = pl.ds(pl.multiple_of((1 - xl) * 256 + k * LANE, LANE), LANE)
            for h, dev in ((0, (across + k, col)), (1, (across + k, flip_col))):
                at = pl.ds(4 * h, 4)
                c = rc(nz.at[at, :, lanes], nx.at[core, at], p_send.at[k, h], p_recv.at[core, h], dev)
                c.start()
                lent.append(c)

    def drain(keep=0):
        for c in sent[:len(sent) - keep]:
            c.wait_send()
        del sent[:len(sent) - keep]

    steps = iter(range(6))

    def exchange(buf, mine, peers, ssem, rsem):
        for peer in peers:
            rc(buf.at[mine], buf.at[mine], ssem, rsem, peer).start()
        step = next(steps)
        if step == 0:
            lend()
        if step == 1:
            drain()
        k = len(peers)
        rc(buf.at[pl.ds(0, k)], buf.at[pl.ds(0, k)], ssem, rsem, peers[0]).wait_recv()

    g = start_ref[...] * (LOG2E / EPS)
    f = None
    f_rows = None
    for it in range(ITERS):
        for b in range(4):
            parts = []
            for r in range(b * LANE, (b + 1) * LANE, 32):
                s = [g[q:q + 1, :] - cross[r:r + 32, q * LANE:(q + 1) * LANE] for q in range(4)]
                top = jnp.maximum(jnp.maximum(s[0], s[1]), jnp.maximum(s[2], s[3]))
                e = [jnp.exp2(v - top) for v in s]
                parts.append(top + jnp.log2((e[0] + e[1]) + (e[2] + e[3])))
            rowx[it, col, b:b + 1, :] = merge_rows(jnp.concatenate(parts, axis=0).T)
        exchange(rowx.at[it], col, col_peers, r_send.at[it], r_recv.at[it])
        f = -(math.log2(m_total) + merge(rowx[it]))
        f_rows = [to_rows(f[b:b + 1, :]) for b in range(4)]
        parts = []
        for r in range(0, BLK, 64):
            fr = f_rows[r // LANE][r % LANE:r % LANE + 64]
            s = (fr - cross[r:r + 64, :]).reshape(8, 8, BLK)
            top = jnp.max(s, axis=0)
            parts.append(top + jnp.log2(jnp.sum(jnp.exp2(s - top[None]), axis=0)))
        top = parts[0]
        for v in parts[1:]:
            top = jnp.maximum(top, v)
        own = merge_rows(top + jnp.log2(sum(jnp.exp2(v - top) for v in parts)))
        for q in range(4):
            col2[it, row, q:q + 1, :] = own[:, q * LANE:(q + 1) * LANE]
        exchange(col2.at[it], row, row_peers, c2_send.at[it], c2_recv.at[it])
        g = -(math.log2(n_total) + merge(col2[it]))

    npot_ref[...] = f * (EPS / LOG2E)
    lpot_ref[...] = g * (EPS / LOG2E)

    LOW, HIGH = slice(0, SPLIT), slice(SPLIT, BLK)
    gw = wide(g)

    def weights(cols):
        for b in range(4):
            rows = slice(b * LANE, (b + 1) * LANE)
            w = m_total * jnp.exp2((f_rows[b] + gw[:, cols]) - cross[rows, cols])
            wt[core, cols, rows] = w.T.astype(BF16)

    def wcopy(j, src, dst, dev, r=None):
        return rc(src, dst, w_send.at[j], w_recv.at[j if r is None else 3 * r], dev)

    low, high = pl.ds(0, SPLIT), pl.ds(SPLIT, REST)
    copies = []
    weights(HIGH)
    for k in range(2):
        copies.append(wcopy(3 * k, wt.at[core, high], wx.at[core], (across + k, col), core))
        copies[-1].start()
    weights(LOW)
    copies.append(wcopy(1, wt.at[core, low], wt.at[core, low], other_core))
    copies[-1].start()
    copies.append(wcopy(2, wt.at[core, high], wt.at[core, high], other_core))
    copies[-1].start()

    def mine(d, q):
        return nz[d, :, pl.ds(pl.multiple_of(q * 256 + core * LANE, LANE), LANE)]

    def theirs(d, q):
        return no[d, :, pl.ds(pl.multiple_of(q * LANE, LANE), LANE)]

    def partial_own(rel):
        d = (z + rel) % Z
        part[rel] = jnp.dot(
            wt[core, LOW, :], jnp.concatenate([mine(d, q) for q in (1 - xl, xl)], axis=1),
            preferred_element_type=F32,
        )

    def partial_other(rel):
        d = (z + rel) % Z
        part[rel] += jnp.dot(
            wt[1 - core, LOW, :], jnp.concatenate([theirs(d, q) for q in (1 - xl, xl)], axis=1),
            preferred_element_type=F32,
        )

    def partial(rel):
        partial_own(rel)
        partial_other(rel)

    def partial_high(rel):
        d = (z + rel) % Z
        parth[rel] = (
            jnp.dot(wt[core, HIGH, :], mine(d, xl), preferred_element_type=F32)
            + jnp.dot(wt[1 - core, HIGH, :], theirs(d, xl), preferred_element_type=F32)
        ) + (
            jnp.dot(wx[0], nx[0, d], preferred_element_type=F32)
            + jnp.dot(wx[1], nx[1, d], preferred_element_type=F32)
        )

    def size(k):
        return REST if k == 2 else SPLIT

    def piece(k, bufs, dr, s):
        ref = bufs[1].at[dr, 4 - s] if k == 2 else bufs[0].at[dr, 4 - s, k]
        h = size(k) // 2
        return ref.at[pl.ds(dr * h, h)] if s == 4 else ref

    def ring_copy(k, dr, s):
        ss, rs = (t_send.at[dr, 4 - s], t_recv.at[dr, 4 - s]) if k == 2 else (
            s_send.at[dr, 4 - s, k], s_recv.at[dr, 4 - s, k])
        return rc(
            piece(k, (stage, stageh), dr, s), piece(k, (land, landh), dr, s), ss, rs,
            z_dn if dr == 0 else z_up,
        )

    def own_part(k, rel, rows):
        return parth[rel, rows, :] if k == 2 else part[rel, rows, k * LANE:(k + 1) * LANE]

    def got(k, dr, s, rows):
        v = landh[dr, 4 - s, rows, :] if k == 2 else land[dr, 4 - s, k, rows, :]
        return v.astype(F32)

    def put(k, dr, s, rows, v):
        if k == 2:
            stageh[dr, 4 - s, rows, :] = v.astype(BF16)
        else:
            stage[dr, 4 - s, k, rows, :] = v.astype(BF16)

    def ring_step(k, s):
        h = size(k) // 2
        both = slice(0, 2 * h)
        for dr in range(2):
            rel = Z - s if dr == 0 else s
            first = slice(dr * h, (dr + 1) * h)
            other = slice((1 - dr) * h, (2 - dr) * h)
            if s == 4:
                put(k, dr, s, first, own_part(k, 4, first))
            else:
                ring_copy(k, dr, s + 1).wait_recv()
                if s == 3:
                    put(k, dr, s, first, own_part(k, rel, first) + got(k, dr, 4, first))
                    put(k, dr, s, other, own_part(k, rel, other))
                else:
                    put(k, dr, s, both, own_part(k, rel, both) + got(k, dr, s + 1, both))
            c = ring_copy(k, dr, s)
            c.start()
            sent.append(c)

    def total(k):
        both = slice(0, size(k))
        for dr in range(2):
            ring_copy(k, dr, 1).wait_recv()
        return own_part(k, 0, both) + (got(k, 0, 1, both) + got(k, 1, 1, both))

    for rel in (4, 5, 3):
        partial_own(rel)
    for q in range(2):
        rc(no.at[:, :, pl.ds(q * LANE, LANE)], no.at[:, :, pl.ds(q * LANE, LANE)],
           o_send.at[q], o_recv.at[q], other_core).wait_recv()
    wcopy(1, wt.at[core, low], wt.at[1 - core, low], other_core).wait_recv()
    partial_other(4)
    ring_step(0, 4)
    partial_other(5)
    partial_other(3)
    ring_step(1, 4)
    for j, (buf, k) in enumerate(((nsq, 7), (lsq, 31))):
        ref = buf.at[pl.ds(0, k)]
        rc(ref, ref, q_send.at[j], q_recv.at[j], z_up).wait_send()
    for it in range(ITERS):
        for buf, k, ssem, rsem in ((rowx, 7, r_send, r_recv), (col2, 31, c2_send, c2_recv)):
            ref = buf.at[it, pl.ds(0, k)]
            rc(ref, ref, ssem.at[it], rsem.at[it], z_up).wait_send()
    for c in lent:
        c.wait_send()
    wcopy(2, wt.at[core, high], wt.at[1 - core, high], other_core).wait_recv()
    for c in range(2):
        for h in range(2):
            ref = nx.at[c, pl.ds(4 * h, 4)]
            rc(ref, ref, p_send.at[0, h], p_recv.at[c, h], other_xl).wait_recv()
    ring_step(0, 3)
    for c in range(2):
        wcopy(0, wt.at[core, high], wx.at[c], other_xl, c).wait_recv()
    partial_high(4)
    ring_step(1, 3)
    partial(6)
    partial(2)
    ring_step(2, 4)
    ring_step(0, 2)
    partial_high(5)
    partial_high(3)
    ring_step(1, 2)
    partial(7)
    partial(1)
    ring_step(2, 3)
    ring_step(0, 1)
    partial(0)
    partial_high(6)
    partial_high(2)
    ring_step(1, 1)
    ring_step(2, 2)
    drain(6)
    xs[...] = total(0)
    xc = rc(xs, xr, x_send.at[0], x_recv.at[0], other_xl)
    xc.start()
    copies.append(xc)
    for rel in (7, 1, 0):
        partial_high(rel)
    ring_step(2, 1)
    kept = total(1)
    out_ref[:, HIGH] = total(2).T
    xc.wait_recv()
    out_ref[:, LOW] = (kept + xr[...]).T
    sent.extend(copies)

    drain()


def per_device(n_total, m_total, noise_draw, latent_code, start_potential):
    anyspace = pl.BlockSpec(memory_space=pltpu.HBM)
    vmem = pl.BlockSpec(memory_space=pltpu.VMEM)
    width = 4096
    dma = pltpu.SemaphoreType.DMA

    def body(*refs):
        kernel(n_total, m_total, width, *refs)

    npot, lpot, out = pl.pallas_call(
        body,
        out_shape=(
            jax.ShapeDtypeStruct((4, LANE), F32),
            jax.ShapeDtypeStruct((4, LANE), F32),
            jax.ShapeDtypeStruct((LANE, BLK), F32),
        ),
        in_specs=[anyspace, anyspace, vmem],
        out_specs=(vmem, vmem, vmem),
        scratch_shapes=[
            pltpu.VMEM((8, BLK, BLK), BF16),
            pltpu.VMEM((Z, 2, 2, BLK, LANE), BF16),
            pltpu.VMEM((8, BLK, 2 * LANE), BF16),
            pltpu.VMEM((BLK, BLK), F32),
            pltpu.VMEM((8, 4, LANE), F32),
            pltpu.VMEM((32, 4, LANE), F32),
            pltpu.VMEM((2, BLK, BLK), BF16),
            pltpu.VMEM((2, REST, BLK), BF16),
            pltpu.VMEM((2, Z, BLK, LANE), BF16),
            pltpu.VMEM((Z, SPLIT, 2 * LANE), F32),
            pltpu.VMEM((Z, REST, LANE), F32),
            pltpu.VMEM((2, 4, 2, SPLIT, LANE), BF16),
            pltpu.VMEM((2, 4, 2, SPLIT, LANE), BF16),
            pltpu.VMEM((2, 4, REST, LANE), BF16),
            pltpu.VMEM((2, 4, REST, LANE), BF16),
            pltpu.VMEM((SPLIT, LANE), F32),
            pltpu.VMEM((SPLIT, LANE), F32),
            pltpu.VMEM((ITERS, 8, 4, LANE), F32),
            pltpu.VMEM((ITERS, 32, 4, LANE), F32),
            dma((2,)), dma((2,)),
            dma((12,)), dma((12,)),
            dma((2, 2)), dma((2, 2)),
            dma((26,)), dma((26,)),
            dma((2,)), dma((2,)),
            dma((4,)), dma((4,)),
            dma((2, 2)), dma((2, 2)),
            dma((ITERS,)), dma((ITERS,)),
            dma((ITERS,)), dma((ITERS,)),
            dma((2, 4, 2)), dma((2, 4, 2)),
            dma((2, 4)), dma((2, 4)),
            dma((1,)), dma((1,)),
            dma((2,)),
        ],
        compiler_params=pltpu.CompilerParams(
            collective_id=0, has_side_effects=True, vmem_limit_bytes=54656 * 1024
        ),
    )(noise_draw, latent_code, start_potential.reshape(4, LANE))
    return npot.reshape(BLK), lpot.reshape(BLK), out


def solution(mesh):
    in_specs = (P("row", "col"), P("col", "row"), P("col"))
    out_specs = (P("row"), P("col"), P("row", "col"))

    def whole(noise_draw, latent_code, start_potential):
        def block(a, b, c):
            return per_device(noise_draw.shape[0], latent_code.shape[0], a, b, c)

        return jax.shard_map(
            block, mesh=mesh, in_specs=in_specs, out_specs=out_specs, check_vma=False
        )(noise_draw, latent_code, start_potential)

    return whole
```

```python
import math

import jax
import jax.numpy as jnp
from jax import lax
from jax.experimental import pallas as pl
from jax.experimental.pallas import tpu as pltpu
from jax.sharding import PartitionSpec as P

ITERS = 3
EPS = 0.01
LOG2E = math.log2(math.e)
MESH = pl.DeviceIdType.MESH
F32 = jnp.float32
BF16 = jnp.bfloat16

Z, Y = 8, 4
LANE = 128
BLK = 512
HALF = BLK // 2
SPLIT = 384
REST = BLK - SPLIT


def kernel(
    n_total, m_total, width,
    noise_ref, latent_ref, start_ref,
    npot_ref, lpot_ref, out_ref,
    nz, lt, no, cross, nsq, lsq, wt, wx, nx, part, parth, stage, land, stageh, landh, xs, xr, rowx, col2,
    q_send, q_recv, n_send, n_recv, h_send, h_recv, l_send, l_recv, o_send, o_recv, w_send, w_recv,
    p_send, p_recv, r_send, r_recv, c2_send, c2_recv,
    s_send, s_recv, t_send, t_recv, x_send, x_recv, loc,
):
    row = lax.axis_index("row")
    col = lax.axis_index("col")
    z = row // 4
    xl = (row // 2) % 2
    core = row % 2
    y = col // 2
    xh = col % 2
    quad = row % 4

    def ring_z(d):
        return (z + d + Z) % Z

    def ring_y(d):
        return (y + d + Y) % Y

    other_core = (row + 1 - 2 * core, col)
    other_xl = (row + 2 - 4 * xl, col)
    flip_col = col + 1 - 2 * xh
    other_xh = (row, flip_col)
    z_up = (ring_z(1) * 4 + quad, col)
    z_dn = (ring_z(-1) * 4 + quad, col)
    y_up = (row, ring_y(1) * 2 + xh)
    y_dn = (row, ring_y(-1) * 2 + xh)
    col_peers = [
        (row, ring_y(dy) * 2 + (1 - xh if dx else xh))
        for dy, dx in ((2, 1), (1, 1), (-1, 1), (2, 0), (0, 1), (1, 0), (-1, 0))
    ]
    across = (row + 2 - 4 * xl) // 2 * 2
    across_quad = ((across + 1 - core) % 4, (across + core) % 4, (quad // 2) * 2 + 1 - core, quad)
    row_peers = [
        (ring_z(d) * 4 + q, col)
        for d in (4, 3, -3, 2, -2, 1, -1, 0) for q in across_quad[:3 if d == 0 else 4]
    ]
    peers = col_peers + row_peers + [(across, flip_col), (across + 1, flip_col)]

    own_n = pltpu.make_async_copy(noise_ref, nz.at[col], loc.at[0])
    own_l = pltpu.make_async_copy(latent_ref, lt.at[z, core, xl], loc.at[1])
    own_n.start()
    own_l.start()

    barrier = pltpu.get_barrier_semaphore()
    for peer in peers:
        pl.semaphore_signal(barrier, inc=1, device_id=peer, device_id_type=MESH)
    cross[...] = jnp.zeros_like(cross)
    pl.semaphore_wait(barrier, len(peers))

    def rc(src, dst, ssem, rsem, dev):
        return pltpu.make_async_remote_copy(
            src_ref=src, dst_ref=dst, send_sem=ssem, recv_sem=rsem,
            device_id=dev, device_id_type=MESH,
        )

    def nsl(slot, h):
        return nz.at[slot, pl.ds(h * HALF, HALF), :]

    QUART = HALF // 2
    sent = []

    def nsend(slot, h, idx, dev, src=None):
        src = nsl(slot, h) if src is None else src
        c = rc(src, nsl(slot, h), n_send.at[idx], n_recv.at[idx], dev)
        c.start()
        return c

    def own_half(h):
        return noise_ref.at[pl.ds(h * HALF, HALF), :]

    def nwait(slot, h, idx):
        rc(nsl(slot, h), nsl(slot, h), n_send.at[idx], n_recv.at[idx], y_up).wait_recv()

    def lsend(ref, idx, dev, src=None):
        c = rc(ref if src is None else src, ref, l_send.at[idx], l_recv.at[idx], dev)
        c.start()
        sent.append(c)

    def lwait(ref, idx):
        rc(ref, ref, l_send.at[idx], l_recv.at[idx], z_up).wait_recv()

    def slot_of(yy, s):
        return yy * 2 + (xh if s == 0 else 1 - xh)

    def xh_copy(t, h, src, slot):
        return rc(src, nsl(slot, h), h_send.at[t, h], h_recv.at[t, h], other_xh)

    def xh_send(t, h):
        far0 = slot_of(ring_y(2), 0)
        c = xh_copy(t, h, own_half(h), col) if t == 0 else xh_copy(t, h, nsl(far0, h), far0)
        c.start()
        sent.append(c)

    def xh_wait(t, h):
        slot = flip_col if t == 0 else slot_of(ring_y(2), 1)
        xh_copy(t, h, nsl(slot, h), slot).wait_recv()

    own_pair = lt.at[z, core]
    own_block = lt.at[z, core, xl]
    z_dirs = ((0, -1, z_up), (1, 1, z_dn))

    def lat(d, part):
        return lt.at[ring_z(d), core, xl if part == 0 else 1 - xl]

    def lat_forward(step, part, dirs):
        for dr, sgn, dev in dirs:
            block = lat(sgn * step, part)
            lwait(block, 1 + 8 * dr + 2 * (step - 1) + part)
            if step < 3 or part == dr:
                lsend(block, 1 + 8 * dr + 2 * step + part, dev)
            if step == 3 and part == dr:
                lsend(block, 24 + part, (dev[0] + 1 - 2 * core, col))

    def lat_share(step):
        for dr, sgn, _ in z_dirs:
            lsend(lt.at[ring_z(sgn * step), core], 16 + 2 * step + dr, other_core)

    lat_x = rc(latent_ref, own_block, l_send.at[0], l_recv.at[0], other_xl)
    lat_x.start()
    lsend(own_block, 1, z_up, latent_ref)
    lsend(own_block, 9, z_dn, latent_ref)
    first_up = nsend(col, 0, 0, y_up, own_half(0))
    first_dn = nsend(col, 1, 3, y_dn, own_half(1))

    sent.append(lat_x)
    xh_send(0, 0)

    own_n.wait()
    own_l.wait()
    for b in range(4):
        rows = slice(b * LANE, (b + 1) * LANE)
        n2 = jnp.square(nz[col, rows, :].astype(F32))
        n2 = (n2[:, 0:128] + n2[:, 128:256]) + (n2[:, 256:384] + n2[:, 384:512])
        nsq[col, b:b + 1, :] = jnp.sum(n2.T, axis=0, keepdims=True)
        l2 = jnp.square(lt[z, core, xl, rows, :].astype(F32))
        lsq[row, b:b + 1, :] = jnp.sum(l2.T, axis=0, keepdims=True)

    lwait(lat(0, 1), 0)
    lsend(lat(0, 1), 2, z_up)
    lsend(lat(0, 1), 10, z_dn)
    xh_send(0, 1)
    lat_forward(1, 0, z_dirs)
    lsend(own_pair, 17, other_core)

    def own_quarter(h, p, idx, dev):
        at = pl.ds(h * HALF + p * QUART, QUART)
        c = rc(noise_ref.at[at, :], nz.at[col, at, :], n_send.at[idx], n_recv.at[idx], dev)
        c.start()
        sent.append(c)

    first_up.wait_send()
    own_quarter(1, 0, 1, y_up)
    first_dn.wait_send()
    own_quarter(0, 0, 2, y_dn)

    dn, up = slot_of(ring_y(-1), 0), slot_of(ring_y(1), 0)
    nwait(dn, 0, 0)
    onward_up = nsend(dn, 0, 4, y_up)
    nwait(up, 1, 3)
    onward_dn = nsend(up, 1, 5, y_dn)

    lat_forward(1, 1, z_dirs)
    lat_share(1)
    lat_forward(2, 0, z_dirs)
    lat_forward(2, 1, z_dirs)
    lat_share(2)

    onward_up.wait_send()
    own_quarter(1, 1, 10, y_up)
    onward_dn.wait_send()
    own_quarter(0, 1, 11, y_dn)

    nwait(slot_of(ring_y(2), 0), 0, 4)
    xh_send(1, 0)
    nwait(slot_of(ring_y(2), 0), 1, 5)
    xh_send(1, 1)

    lat_forward(3, 0, z_dirs)

    xh_wait(0, 0)
    sent.append(nsend(flip_col, 0, 6, y_up))
    sent.append(nsend(flip_col, 0, 8, y_dn))
    xh_wait(0, 1)
    sent.append(nsend(flip_col, 1, 9, y_dn))
    sent.append(nsend(flip_col, 1, 7, y_up))

    lat_forward(3, 1, z_dirs)
    lat_share(3)
    for peer in col_peers:
        rc(nsq.at[col], nsq.at[col], q_send.at[0], q_recv.at[0], peer).start()
    for peer in row_peers:
        rc(lsq.at[row], lsq.at[row], q_send.at[1], q_recv.at[1], peer).start()
    lwait(lat(4, 0), 7)
    lwait(lat(4, 1), 16)
    for j, d in enumerate((0, -1, 1, -2, 2, -3, 3)):
        lwait(lt.at[ring_z(d), 1 - core], 17 + j)
    lwait(lt.at[ring_z(4), 1 - core, xl], 24)
    lwait(lt.at[ring_z(4), 1 - core, 1 - xl], 25)

    def accumulate(slot):
        a = nz[slot]
        b = jnp.concatenate([lt[slot, 0, 0], lt[slot, 1, 0], lt[slot, 0, 1], lt[slot, 1, 1]], axis=1)
        cross[...] += lax.dot_general(a, b, (((1,), (1,)), ((), ())), preferred_element_type=F32)

    dn, up = slot_of(ring_y(-1), 0), slot_of(ring_y(1), 0)
    for slot, h, idxs in ((dn, 1, (1, 10)), (up, 0, (2, 11))):
        for p in range(2):
            ref = nz.at[slot, pl.ds(h * HALF + p * QUART, QUART), :]
            rc(ref, ref, n_send.at[idxs[p]], n_recv.at[idxs[p]], y_up).wait_recv()

    def set0(k, carry):
        accumulate(((y + k) % Y) * 2 + xh)
        return carry

    lax.fori_loop(0, Y, set0, 0)
    accumulate(flip_col)
    xh_wait(1, 0)
    xh_wait(1, 1)
    accumulate(slot_of(ring_y(2), 1))
    dn, up = slot_of(ring_y(-1), 1), slot_of(ring_y(1), 1)
    nwait(dn, 0, 6)
    nwait(up, 1, 9)
    nwait(dn, 1, 7)
    nwait(up, 0, 8)
    accumulate(dn)
    accumulate(up)

    for q in range(2):
        c = rc(
            nz.at[:, :, pl.ds(pl.multiple_of(q * 256 + (1 - core) * LANE, LANE), LANE)],
            no.at[:, :, pl.ds(q * LANE, LANE)],
            o_send.at[q], o_recv.at[q], other_core,
        )
        c.start()
        sent.append(c)

    eye = (
        lax.broadcasted_iota(jnp.int32, (LANE, LANE), 0)
        == lax.broadcasted_iota(jnp.int32, (LANE, LANE), 1)
    )

    def to_rows(v):
        return jnp.sum(jnp.where(eye, v, 0.0), axis=1, keepdims=True)

    def wide(v):
        return jnp.concatenate([v[q:q + 1, :] for q in range(4)], axis=1)

    scale = LOG2E / (width * EPS)
    rc(nsq.at[pl.ds(0, 7)], nsq.at[pl.ds(0, 7)], q_send.at[0], q_recv.at[0], z_up).wait_recv()
    rc(lsq.at[pl.ds(0, 31)], lsq.at[pl.ds(0, 31)], q_send.at[1], q_recv.at[1], z_up).wait_recv()
    nq = jnp.sum(nsq[...], axis=0)
    lq = wide(jnp.sum(lsq[...], axis=0))
    for b in range(4):
        rows = slice(b * LANE, (b + 1) * LANE)
        cross[rows, :] = (to_rows(nq[b:b + 1, :]) + lq - 2.0 * cross[rows, :]) * scale

    def merge(parts):
        best = jnp.max(parts, axis=0)
        return best + jnp.log2(jnp.sum(jnp.exp2(parts - best[None]), axis=0))

    def merge_rows(parts):
        best = jnp.max(parts, axis=0, keepdims=True)
        return best + jnp.log2(jnp.sum(jnp.exp2(parts - best), axis=0, keepdims=True))

    lent = []

    def lend(step):
        k, zz = step % 2, step // 2
        lanes = pl.ds(pl.multiple_of((1 - xl) * 256 + k * LANE, LANE), LANE)
        for slot, dev in ((zz, (across + k, col)), (zz + 4, (across + k, flip_col))):
            c = rc(nz.at[slot, :, lanes], nx.at[core, slot], p_send.at[k, slot], p_recv.at[core, slot], dev)
            c.start()
            lent.append(c)

    def drain(keep=0):
        for c in sent[:len(sent) - keep]:
            c.wait_send()
        del sent[:len(sent) - keep]

    steps = iter(range(6))

    def exchange(buf, mine, peers, ssem, rsem):
        for peer in peers:
            rc(buf.at[mine], buf.at[mine], ssem, rsem, peer).start()
        step = next(steps)
        for piece_at in range(*((0, 2), (2, 4), (4, 6), (6, 7), (7, 8), (8, 8))[step]):
            lend(piece_at)
        if step == 1:
            drain()
        k = len(peers)
        rc(buf.at[pl.ds(0, k)], buf.at[pl.ds(0, k)], ssem, rsem, peers[0]).wait_recv()

    g = start_ref[...] * (LOG2E / EPS)
    f = None
    f_rows = None
    for it in range(ITERS):
        for b in range(4):
            parts = []
            for r in range(b * LANE, (b + 1) * LANE, 32):
                s = [g[q:q + 1, :] - cross[r:r + 32, q * LANE:(q + 1) * LANE] for q in range(4)]
                top = jnp.maximum(jnp.maximum(s[0], s[1]), jnp.maximum(s[2], s[3]))
                e = [jnp.exp2(v - top) for v in s]
                parts.append(top + jnp.log2((e[0] + e[1]) + (e[2] + e[3])))
            rowx[it, col, b:b + 1, :] = merge_rows(jnp.concatenate(parts, axis=0).T)
        exchange(rowx.at[it], col, col_peers, r_send.at[it], r_recv.at[it])
        f = -(math.log2(m_total) + merge(rowx[it]))
        f_rows = [to_rows(f[b:b + 1, :]) for b in range(4)]
        parts = []
        for r in range(0, BLK, 64):
            fr = f_rows[r // LANE][r % LANE:r % LANE + 64]
            s = (fr - cross[r:r + 64, :]).reshape(8, 8, BLK)
            top = jnp.max(s, axis=0)
            parts.append(top + jnp.log2(jnp.sum(jnp.exp2(s - top[None]), axis=0)))
        top = parts[0]
        for v in parts[1:]:
            top = jnp.maximum(top, v)
        own = merge_rows(top + jnp.log2(sum(jnp.exp2(v - top) for v in parts)))
        for q in range(4):
            col2[it, row, q:q + 1, :] = own[:, q * LANE:(q + 1) * LANE]
        exchange(col2.at[it], row, row_peers, c2_send.at[it], c2_recv.at[it])
        g = -(math.log2(n_total) + merge(col2[it]))

    npot_ref[...] = f * (EPS / LOG2E)
    lpot_ref[...] = g * (EPS / LOG2E)

    LOW, HIGH = slice(0, SPLIT), slice(SPLIT, BLK)
    gw = wide(g)

    def weights(cols):
        for b in range(4):
            rows = slice(b * LANE, (b + 1) * LANE)
            w = m_total * jnp.exp2((f_rows[b] + gw[:, cols]) - cross[rows, cols])
            wt[core, cols, rows] = w.T.astype(BF16)

    def wcopy(j, src, dst, dev, r=None):
        return rc(src, dst, w_send.at[j], w_recv.at[j if r is None else 3 * r], dev)

    low, high = pl.ds(0, SPLIT), pl.ds(SPLIT, REST)
    copies = []
    weights(HIGH)
    for k in range(2):
        copies.append(wcopy(3 * k, wt.at[core, high], wx.at[core], (across + k, col), core))
        copies[-1].start()
    weights(LOW)
    copies.append(wcopy(1, wt.at[core, low], wt.at[core, low], other_core))
    copies[-1].start()
    copies.append(wcopy(2, wt.at[core, high], wt.at[core, high], other_core))
    copies[-1].start()

    def mine(d, q):
        return nz[d, :, pl.ds(pl.multiple_of(q * 256 + core * LANE, LANE), LANE)]

    def theirs(d, q):
        return no[d, :, pl.ds(pl.multiple_of(q * LANE, LANE), LANE)]

    def partial_own(rel):
        d = (z + rel) % Z
        part[rel] = jnp.dot(
            wt[core, LOW, :], jnp.concatenate([mine(d, q) for q in (1 - xl, xl)], axis=1),
            preferred_element_type=F32,
        )

    def partial_other(rel):
        d = (z + rel) % Z
        part[rel] += jnp.dot(
            wt[1 - core, LOW, :], jnp.concatenate([theirs(d, q) for q in (1 - xl, xl)], axis=1),
            preferred_element_type=F32,
        )

    def partial(rel):
        partial_own(rel)
        partial_other(rel)

    def partial_high(rel):
        d = (z + rel) % Z
        parth[rel] = (
            jnp.dot(wt[core, HIGH, :], mine(d, xl), preferred_element_type=F32)
            + jnp.dot(wt[1 - core, HIGH, :], theirs(d, xl), preferred_element_type=F32)
        ) + (
            jnp.dot(wx[0], nx[0, d], preferred_element_type=F32)
            + jnp.dot(wx[1], nx[1, d], preferred_element_type=F32)
        )

    def size(k):
        return REST if k == 2 else SPLIT

    def piece(k, bufs, dr, s):
        ref = bufs[1].at[dr, 4 - s] if k == 2 else bufs[0].at[dr, 4 - s, k]
        h = size(k) // 2
        return ref.at[pl.ds(dr * h, h)] if s == 4 else ref

    def ring_copy(k, dr, s):
        ss, rs = (t_send.at[dr, 4 - s], t_recv.at[dr, 4 - s]) if k == 2 else (
            s_send.at[dr, 4 - s, k], s_recv.at[dr, 4 - s, k])
        return rc(
            piece(k, (stage, stageh), dr, s), piece(k, (land, landh), dr, s), ss, rs,
            z_dn if dr == 0 else z_up,
        )

    def own_part(k, rel, rows):
        return parth[rel, rows, :] if k == 2 else part[rel, rows, k * LANE:(k + 1) * LANE]

    def got(k, dr, s, rows):
        v = landh[dr, 4 - s, rows, :] if k == 2 else land[dr, 4 - s, k, rows, :]
        return v.astype(F32)

    def put(k, dr, s, rows, v):
        if k == 2:
            stageh[dr, 4 - s, rows, :] = v.astype(BF16)
        else:
            stage[dr, 4 - s, k, rows, :] = v.astype(BF16)

    def ring_step(k, s):
        h = size(k) // 2
        both = slice(0, 2 * h)
        for dr in range(2):
            rel = Z - s if dr == 0 else s
            first = slice(dr * h, (dr + 1) * h)
            other = slice((1 - dr) * h, (2 - dr) * h)
            if s == 4:
                put(k, dr, s, first, own_part(k, 4, first))
            else:
                ring_copy(k, dr, s + 1).wait_recv()
                if s == 3:
                    put(k, dr, s, first, own_part(k, rel, first) + got(k, dr, 4, first))
                    put(k, dr, s, other, own_part(k, rel, other))
                else:
                    put(k, dr, s, both, own_part(k, rel, both) + got(k, dr, s + 1, both))
            c = ring_copy(k, dr, s)
            c.start()
            sent.append(c)

    def total(k):
        both = slice(0, size(k))
        for dr in range(2):
            ring_copy(k, dr, 1).wait_recv()
        return own_part(k, 0, both) + (got(k, 0, 1, both) + got(k, 1, 1, both))

    for rel in (4, 5, 3):
        partial_own(rel)
    for q in range(2):
        rc(no.at[:, :, pl.ds(q * LANE, LANE)], no.at[:, :, pl.ds(q * LANE, LANE)],
           o_send.at[q], o_recv.at[q], other_core).wait_recv()
    wcopy(1, wt.at[core, low], wt.at[1 - core, low], other_core).wait_recv()
    partial_other(4)
    ring_step(0, 4)
    partial_other(5)
    partial_other(3)
    ring_step(1, 4)
    for j, (buf, k) in enumerate(((nsq, 7), (lsq, 31))):
        ref = buf.at[pl.ds(0, k)]
        rc(ref, ref, q_send.at[j], q_recv.at[j], z_up).wait_send()
    for it in range(ITERS):
        for buf, k, ssem, rsem in ((rowx, 7, r_send, r_recv), (col2, 31, c2_send, c2_recv)):
            ref = buf.at[it, pl.ds(0, k)]
            rc(ref, ref, ssem.at[it], rsem.at[it], z_up).wait_send()
    for c in lent:
        c.wait_send()
    wcopy(2, wt.at[core, high], wt.at[1 - core, high], other_core).wait_recv()
    for c in range(2):
        for slot in range(Z):
            rc(nx.at[c, slot], nx.at[c, slot], p_send.at[0, slot], p_recv.at[c, slot], other_xl).wait_recv()
    ring_step(0, 3)
    for c in range(2):
        wcopy(0, wt.at[core, high], wx.at[c], other_xl, c).wait_recv()
    partial_high(4)
    ring_step(1, 3)
    partial(6)
    partial(2)
    ring_step(2, 4)
    ring_step(0, 2)
    partial_high(5)
    partial_high(3)
    ring_step(1, 2)
    partial(7)
    partial(1)
    ring_step(2, 3)
    ring_step(0, 1)
    partial(0)
    partial_high(6)
    partial_high(2)
    ring_step(1, 1)
    ring_step(2, 2)
    drain(6)
    xs[...] = total(0)
    xc = rc(xs, xr, x_send.at[0], x_recv.at[0], other_xl)
    xc.start()
    copies.append(xc)
    for rel in (7, 1, 0):
        partial_high(rel)
    ring_step(2, 1)
    kept = total(1)
    out_ref[:, HIGH] = total(2).T
    xc.wait_recv()
    out_ref[:, LOW] = (kept + xr[...]).T
    sent.extend(copies)

    drain()


def per_device(n_total, m_total, noise_draw, latent_code, start_potential):
    anyspace = pl.BlockSpec(memory_space=pltpu.HBM)
    vmem = pl.BlockSpec(memory_space=pltpu.VMEM)
    width = 4096
    dma = pltpu.SemaphoreType.DMA

    def body(*refs):
        kernel(n_total, m_total, width, *refs)

    npot, lpot, out = pl.pallas_call(
        body,
        out_shape=(
            jax.ShapeDtypeStruct((4, LANE), F32),
            jax.ShapeDtypeStruct((4, LANE), F32),
            jax.ShapeDtypeStruct((LANE, BLK), F32),
        ),
        in_specs=[anyspace, anyspace, vmem],
        out_specs=(vmem, vmem, vmem),
        scratch_shapes=[
            pltpu.VMEM((8, BLK, BLK), BF16),
            pltpu.VMEM((Z, 2, 2, BLK, LANE), BF16),
            pltpu.VMEM((8, BLK, 2 * LANE), BF16),
            pltpu.VMEM((BLK, BLK), F32),
            pltpu.VMEM((8, 4, LANE), F32),
            pltpu.VMEM((32, 4, LANE), F32),
            pltpu.VMEM((2, BLK, BLK), BF16),
            pltpu.VMEM((2, REST, BLK), BF16),
            pltpu.VMEM((2, Z, BLK, LANE), BF16),
            pltpu.VMEM((Z, SPLIT, 2 * LANE), F32),
            pltpu.VMEM((Z, REST, LANE), F32),
            pltpu.VMEM((2, 4, 2, SPLIT, LANE), BF16),
            pltpu.VMEM((2, 4, 2, SPLIT, LANE), BF16),
            pltpu.VMEM((2, 4, REST, LANE), BF16),
            pltpu.VMEM((2, 4, REST, LANE), BF16),
            pltpu.VMEM((SPLIT, LANE), F32),
            pltpu.VMEM((SPLIT, LANE), F32),
            pltpu.VMEM((ITERS, 8, 4, LANE), F32),
            pltpu.VMEM((ITERS, 32, 4, LANE), F32),
            dma((2,)), dma((2,)),
            dma((12,)), dma((12,)),
            dma((2, 2)), dma((2, 2)),
            dma((26,)), dma((26,)),
            dma((2,)), dma((2,)),
            dma((4,)), dma((4,)),
            dma((2, Z)), dma((2, Z)),
            dma((ITERS,)), dma((ITERS,)),
            dma((ITERS,)), dma((ITERS,)),
            dma((2, 4, 2)), dma((2, 4, 2)),
            dma((2, 4)), dma((2, 4)),
            dma((1,)), dma((1,)),
            dma((2,)),
        ],
        compiler_params=pltpu.CompilerParams(
            collective_id=0, has_side_effects=True, vmem_limit_bytes=54656 * 1024
        ),
    )(noise_draw, latent_code, start_potential.reshape(4, LANE))
    return npot.reshape(BLK), lpot.reshape(BLK), out


def solution(mesh):
    in_specs = (P("row", "col"), P("col", "row"), P("col"))
    out_specs = (P("row"), P("col"), P("row", "col"))

    def whole(noise_draw, latent_code, start_potential):
        def block(a, b, c):
            return per_device(noise_draw.shape[0], latent_code.shape[0], a, b, c)

        return jax.shard_map(
            block, mesh=mesh, in_specs=in_specs, out_specs=out_specs, check_vma=False
        )(noise_draw, latent_code, start_potential)

    return whole
```
